32 devices in a mesh: dp: 2 (over core), expert: 16 (over z, y, x).
Axes of the slice: x: 2, y: 2, z: 4, core: 2. Of those that a mesh axis runs over, the one named last changes fastest.
Arguments:
- hidden_in: bfloat16 [32768, 1024], P(('dp', 'expert')), may hold values from -6 to 6
- buckets: int32 [16384, 1], P(('dp', 'expert')), may hold values from 0 to 15; in each aligned block of 512 rows (0 to 511, 512 to 1023, ...) at most 64 rows name the same one
- expert_of_bucket: int32 [16], replicated, may hold values from 0 to 15, each once
- lengths: int32 [32, 3], P(('dp', 'expert')), may hold values from 1 to 384, 512 in all within a row
- norm1_gain: float32 [1024], replicated, may hold values from 0.25 to 1.75
- norm1_bias: float32 [1024], replicated, may hold values from -1.2 to 1.2
- w_qkv: bfloat16 [1024, 3072], replicated, may hold values from -0.1875 to 0.1875
- w_out: bfloat16 [1024, 1024], replicated, may hold values from -0.75 to 0.75
- norm2_gain: float32 [1024], replicated, may hold values from 0.25 to 1.75
- norm2_bias: float32 [1024], replicated, may hold values from -1.2 to 1.2
- w_up: bfloat16 [16, 1024, 4096], P('expert', None, 'dp'), may hold values from -0.1875 to 0.1875
- b_up: float32 [16, 4096], P('expert', 'dp'), may hold values from -1.8 to 1.8
- w_down: bfloat16 [16, 4096, 1024], P('expert', 'dp'), may hold values from -0.09375 to 0.09375
- b_down: float32 [16, 1024], P('expert'), may hold values from -1.8 to 1.8
- grad_out: bfloat16 [32768, 1024], P(('dp', 'expert')), may hold values from -6 to 6
Outputs:
- hidden_out: bfloat16 [32768, 1024], P(('dp', 'expert'))
- grad_in: bfloat16 [32768, 1024], P(('dp', 'expert'))
- grad_qkv: float32 [1024, 3072], P(('dp', 'expert'))
- grad_wout: float32 [1024, 1024], P(('dp', 'expert'))
- grad_norm1_gain: float32 [1024], P(('dp', 'expert'))
- grad_norm1_bias: float32 [1024], P(('dp', 'expert'))
- grad_norm2_gain: float32 [1024], P(('dp', 'expert'))
- grad_norm2_bias: float32 [1024], P(('dp', 'expert'))
- grad_up: float32 [16, 1024, 4096], P('expert', None, 'dp')
- grad_bup: float32 [16, 4096], P('expert', 'dp')
- grad_down: float32 [16, 4096, 1024], P('expert', 'dp')
- grad_bdown: float32 [16, 1024], P('expert', 'dp')
The draws below stay inside these ranges and needn't reach their ends.
Inputs may be any that keep to these rules, and one draw needn't show every extreme that they name: `buckets`: among the 512 tokens of one device no bucket appears more than 64 times, and in every draw some bucket appears exactly 64 times on some device. `expert_of_bucket`: each expert serves exactly one bucket. `lengths`: each row sums to 512 and its largest entry is 384.
All inputs are finite; a program needn't handle non-finite values.
Results may differ from the reference program's by a relative error of at most 0.014.
Values may be sent and summed in bfloat16 or wider, within the bound.
A program may use at most 192 MiB of HBM per device.

```python
import math
import jax
import jax.numpy as jnp
import numpy as np
from jax import lax

D = 1024
HEADS = 16
HEAD_DIM = 64
FF = 4096
TOK_DEV = 512
NSEG = 3
EXPERTS = 16
CAP = 64
SLOTS = 1024
SEQ_MOST = 384
TOKENS = 16384
ROWS = 32768
N_DP = 2
N_EXPERT = 16


def levels(stream_key, shape, shards, least, high):
    def one(position, blocks):
        steps = jax.random.uniform(jax.random.fold_in(jax.random.fold_in(stream_key, 6), position), (blocks,), jnp.float32, least / len(shards), high / len(shards))
        return jnp.repeat(jnp.exp(steps), shape[position] // blocks).reshape((-1,) + (1,) * (len(shape) - position - 1))

    factor_of = one(*shards[0])
    for cut in shards[1:]:
        factor_of = factor_of * one(*cut)
    return factor_of


def split_up(number_of, total, bound, slope):
    portions = [(1 << 20) // math.isqrt(rank ** slope) + 1 for rank in range(2, number_of + 1)]
    spare, holding = total - bound - (number_of - 1), [1] * (number_of - 1)
    while spare > 0:
        candidates = [i for i in range(number_of - 1) if holding[i] < bound]
        pool, budget = sum([portions[i] for i in candidates]), spare
        for i in candidates:
            extra = min(bound - holding[i], max(1, budget * portions[i] // pool), spare)
            holding[i] = holding[i] + extra
            spare = spare - extra
    return np.array([bound] + holding)


def uneven_parts(stream_key, count, total, limit, skew):
    if count == 2:
        one = jax.random.randint(stream_key, (), max(1, total - limit), min(limit, total - 1) + 1)
        return jnp.stack([one, total - one])
    sizes = jnp.asarray(split_up(count, total, limit, skew), jnp.int32)
    couples = (count - 1) // 2
    source_of, receiver = sizes[1:1 + 2 * couples:2], sizes[2:2 + 2 * couples:2]
    slack = jnp.minimum(source_of - 1, limit - receiver)
    moved = jax.random.randint(jax.random.fold_in(stream_key, 1), (couples,), 0, 1 << 20) % (slack + 1)
    sizes = sizes.at[1:1 + 2 * couples:2].set(source_of - moved).at[2:2 + 2 * couples:2].set(receiver + moved)
    return sizes[jax.random.permutation(jax.random.fold_in(stream_key, 2), count)]


def routed_block(key, own, number, rows, amount, top, most, skew):
    ranking = jax.random.permutation(key, amount)
    crowded, usual = shares(amount, rows * top, most, skew, True), shares(amount, rows * top, most, skew, False)
    places = jnp.arange(amount)

    def named(sizes, rotation):
        used = int((sizes > 0).sum())
        fixed = max(1, used // 4)
        moved = fixed + (places - fixed + rotation * (used - fixed)) % max(1, amount - fixed)
        return jnp.zeros((amount,), jnp.int32).at[ranking[jnp.where(places < fixed, places, moved)]].set(jnp.asarray(sizes, jnp.int32))

    sizes = jnp.where(number % 4 == 0, named(crowded, number // 4), named(usual, number - number // 4 - 1))
    mixed = jax.random.permutation(jax.random.fold_in(own, 3), amount)
    giver, sink = mixed[0:amount // 2 * 2:2], mixed[1:amount // 2 * 2:2]
    margin = jnp.minimum(sizes[giver] - 1, most - sizes[sink]) // 2
    margin = jnp.where((giver == ranking[0]) | (sink == ranking[0]) | (sizes[sink] == 0), 0, jnp.maximum(margin, 0))
    moved = jax.random.randint(jax.random.fold_in(own, 4), (amount // 2,), 0, 1 << 20) % (margin + 1)
    sizes = sizes.at[giver].add(-moved).at[sink].add(moved)
    items = jnp.searchsorted(jnp.cumsum(sizes), jnp.arange(rows * top), side="right").astype(jnp.int32)
    listing = items.reshape(top, rows).T
    listing = listing[jax.random.permutation(jax.random.fold_in(own, 1), rows)]
    rotation = jax.random.randint(jax.random.fold_in(own, 2), (rows, 1), 0, top)
    return jnp.take_along_axis(listing, (jnp.arange(top)[None, :] + rotation) % top, axis=1)


def shares(amount, total, reach, skew, full):
    weights = [(1 << 20) // math.isqrt(rank ** skew) + 1 for rank in range(1, amount + 1)]
    largest = reach if full else min(reach, max(-(-total // amount), total * weights[0] // sum(weights)))
    least = 1 if total - largest >= amount - 1 else 0
    holding, rest = [largest] + [least] * (amount - 1), total - largest - least * (amount - 1)
    while rest > 0:
        movable = [i for i in range(1, amount) if holding[i] < largest] or [i for i in range(1, amount) if holding[i] < reach]
        pool, left = sum([weights[i] for i in movable]), rest
        for i in movable:
            extra = min(reach - holding[i], max(1, left * weights[i] // pool), rest)
            holding[i] = holding[i] + extra
            rest = rest - extra
    return np.array(holding)


def bell_draw(own_key, extent, width, limit, cuts=(), held_as=jnp.bfloat16):
    values = width * jax.random.normal(own_key, extent, jnp.float32)
    if cuts:
        values = values * levels(own_key, extent, cuts, -0.22, 0.18)
    return jnp.clip(values, -limit, limit).astype(held_as)


def setup_inputs(seed: int = 0) -> dict:
    splits = jax.random.split(jax.random.key(seed), 16)
    hidden_in = bell_draw(splits[0], (ROWS, D), 1.0, 6.0, ((0, 32),))
    buckets_keys = jax.random.split(jax.random.fold_in(splits[1], 1), TOKENS // TOK_DEV)
    buckets_turns = jax.random.permutation(jax.random.fold_in(splits[1], 3), TOKENS // TOK_DEV)
    buckets = jax.vmap(lambda own, number: routed_block(jax.random.fold_in(splits[1], 2), own, number, TOK_DEV, EXPERTS, 1, CAP, 1))(buckets_keys, buckets_turns).reshape((TOKENS, 1))
    expert_of_bucket = jax.random.permutation(splits[2], EXPERTS).astype(jnp.int32)
    lengths = jax.vmap(lambda own: uneven_parts(own, NSEG, TOK_DEV, SEQ_MOST, 1))(jax.random.split(splits[3], (N_DP * N_EXPERT))).reshape((N_DP * N_EXPERT, NSEG)).astype(jnp.int32)
    norm1_gain = jnp.clip(1.0 + 0.15 * jax.random.normal(splits[4], (D,), jnp.float32), 0.25, 1.75)
    norm1_bias = bell_draw(splits[5], (D,), 0.2, 1.2, (), jnp.float32)
    w_qkv = bell_draw(splits[6], (D, 3 * D), D ** -0.5, 0.1875)
    w_out = bell_draw(splits[7], (D, D), (D // 16) ** -0.5, 0.75)
    norm2_gain = jnp.clip(1.0 + 0.15 * jax.random.normal(splits[8], (D,), jnp.float32), 0.25, 1.75)
    norm2_bias = bell_draw(splits[9], (D,), 0.2, 1.2, (), jnp.float32)
    w_up = bell_draw(splits[10], (EXPERTS, D, FF), D ** -0.5, 0.1875, ((0, 16), (2, 2)))
    b_up = bell_draw(splits[11], (EXPERTS, FF), 0.3, 1.8, ((0, 16), (1, 2)), jnp.float32)
    w_down = bell_draw(splits[12], (EXPERTS, FF, D), FF ** -0.5, 0.09375, ((0, 16), (1, 2)))
    b_down = bell_draw(splits[13], (EXPERTS, D), 0.3, 1.8, ((0, 16),), jnp.float32)
    grad_out = bell_draw(splits[14], (ROWS, D), 1.0, 6.0, ((0, 32),))
    return dict(hidden_in=hidden_in, buckets=buckets, expert_of_bucket=expert_of_bucket, lengths=lengths, norm1_gain=norm1_gain, norm1_bias=norm1_bias, w_qkv=w_qkv, w_out=w_out, norm2_gain=norm2_gain, norm2_bias=norm2_bias, w_up=w_up, b_up=b_up, w_down=w_down, b_down=b_down, grad_out=grad_out)


@jax.custom_vjp
def low(v):
    return lax.optimization_barrier(v.astype(jnp.bfloat16)).astype(jnp.float32)

@jax.custom_vjp
def low_back(v):
    return v

def low_keep(v):
    return (low(v), None)

def low_pass(kept, grad):
    return (grad,)

def back_keep(v):
    return (v, None)

def back_low(kept, grad):
    return (low(grad),)
low.defvjp(low_keep, low_pass)
low_back.defvjp(back_keep, back_low)
norm_eps = 1e-05
masked_score = -1e+30
highest = lax.Precision.HIGHEST

def both_ways(values):
    return low(low_back(values))

def layer_norm(values, gain_vec, bias_vec):
    mean_val = lax.optimization_barrier(jnp.mean(values, axis=-1, keepdims=True))
    centered = values - mean_val
    variance = lax.optimization_barrier(jnp.mean(centered * centered, axis=-1, keepdims=True))
    return centered * lax.rsqrt(variance + norm_eps) * gain_vec + bias_vec

def routing(buckets, expert_of_bucket, lengths):
    devices_all = N_DP * N_EXPERT
    expert_tok = expert_of_bucket[buckets[:, 0]].astype(jnp.int32).reshape(devices_all, TOK_DEV)
    labels = jnp.arange(EXPERTS, dtype=jnp.int32)
    expert_hot = (expert_tok[:, :, None] == labels[None, None, :]).astype(jnp.int32)
    before = jnp.cumsum(expert_hot, axis=1) - expert_hot
    rank_tok = lax.optimization_barrier(jnp.sum(before * expert_hot, axis=2))
    device_ids = jnp.arange(devices_all, dtype=jnp.int32)[:, None]
    group_ids = device_ids // N_EXPERT
    source_ids = device_ids % N_EXPERT
    slot_ids = ((group_ids * N_EXPERT + expert_tok) * N_EXPERT + source_ids) * CAP + rank_tok
    slot_ids = slot_ids.reshape(-1).astype(jnp.int32)
    live_rows = jnp.zeros((ROWS, 1), jnp.float32).at[slot_ids].set(1.0)
    seg_ends = jnp.cumsum(lengths, axis=1)
    positions = jnp.arange(TOK_DEV, dtype=jnp.int32)
    segment = lax.optimization_barrier(jnp.sum((positions[None, :, None] >= seg_ends[:, None, :]).astype(jnp.int32), axis=2))
    return (slot_ids, live_rows, segment)

def forward(hidden_f, norm1_gain, norm1_bias, w_qkv, w_out, norm2_gain, norm2_bias, w_up, b_up, w_down, b_down, slot_ids, live_rows, segment):
    tokens_f = low_back(hidden_f)[slot_ids]
    blocks = tokens_f.reshape(N_DP * N_EXPERT, TOK_DEV, D)
    scale_val = HEAD_DIM ** (-0.5)
    positions = jnp.arange(TOK_DEV, dtype=jnp.int32)
    causal = positions[None, :] <= positions[:, None]

    def attend(block_item):
        rows_in, seg_row = block_item
        normed = low(layer_norm(rows_in, norm1_gain, norm1_bias))
        proj_qkv = both_ways(jnp.dot(normed, w_qkv, precision=highest))
        queries = proj_qkv[:, :D].reshape(TOK_DEV, HEADS, HEAD_DIM)
        key_rows = proj_qkv[:, D:2 * D].reshape(TOK_DEV, HEADS, HEAD_DIM)
        values = proj_qkv[:, 2 * D:].reshape(TOK_DEV, HEADS, HEAD_DIM)
        scores = low_back(jnp.einsum('qhd,khd->hqk', queries, key_rows, precision=highest) * scale_val)
        allowed = jnp.logical_and(causal, seg_row[:, None] == seg_row[None, :])
        scores = jnp.where(allowed[None], scores, masked_score)
        attn_probs = low(jax.nn.softmax(scores, axis=-1))
        attended = jnp.einsum('hqk,khd->qhd', attn_probs, values, precision=highest).reshape(TOK_DEV, D)
        attended = both_ways(attended)
        return rows_in + jnp.dot(attended, w_out, precision=highest)
    residual_h = lax.map(jax.checkpoint(attend), (blocks, segment)).reshape(TOKENS, D)
    sent = both_ways(residual_h)
    expert_rows = jnp.zeros((ROWS, D), jnp.float32).at[slot_ids].set(sent)
    grouped = expert_rows.reshape(N_DP, EXPERTS, SLOTS, D).transpose(1, 0, 2, 3).reshape(EXPERTS, N_DP * SLOTS, D)

    def expert_ffn(block_item):
        rows_in, up_mat, up_bias, down_mat, down_bias = block_item
        normed = low(layer_norm(rows_in, norm2_gain, norm2_bias))
        hidden_pre = low_back(jnp.dot(normed, up_mat, precision=highest) + up_bias)
        hidden_act = low(jax.nn.gelu(hidden_pre, approximate=False))
        return rows_in + jnp.dot(hidden_act, down_mat, precision=highest) + down_bias
    result = lax.map(jax.checkpoint(expert_ffn), (grouped, w_up, b_up, w_down, b_down))
    result = result.reshape(EXPERTS, N_DP, SLOTS, D).transpose(1, 0, 2, 3).reshape(ROWS, D)
    return result * live_rows

def reference(hidden_in, buckets, expert_of_bucket, lengths, norm1_gain, norm1_bias, w_qkv, w_out, norm2_gain, norm2_bias, w_up, b_up, w_down, b_down, grad_out):
    slot_ids, live_rows, segment = routing(buckets, expert_of_bucket, lengths)
    floats = tuple((array_in.astype(jnp.float32) for array_in in (hidden_in, norm1_gain, norm1_bias, w_qkv, w_out, norm2_gain, norm2_bias, w_up, b_up, w_down, b_down)))

    def wrapped(*params):
        return forward(*params, slot_ids, live_rows, segment)
    result, pullback = jax.vjp(wrapped, *floats)
    gradients = pullback(grad_out.astype(jnp.float32))
    return (result.astype(jnp.bfloat16), gradients[0].astype(jnp.bfloat16), gradients[3], gradients[4], gradients[1], gradients[2], gradients[5], gradients[6], gradients[7], gradients[8], gradients[9], gradients[10])
```

```python
import functools

import jax
import jax.numpy as jnp
from jax import lax
from jax.experimental import pallas as pl
from jax.experimental.pallas import tpu as pltpu
from jax.sharding import PartitionSpec as P

HEADS = 16
HEAD_DIM = 64


norm_eps = 1e-05
masked_score = -1e30
root_half = 0.7071067811865476
inv_root_tau = 0.3989422804014327


def normalize(values):
    mean_val = jnp.mean(values, axis=-1, keepdims=True)
    centered = values - mean_val
    variance = jnp.mean(centered * centered, axis=-1, keepdims=True)
    inv_std = lax.rsqrt(variance + norm_eps)
    return (centered * inv_std, inv_std)


def norm_back(grad_normed, normed, inv_std, gain_vec):
    scaled = grad_normed * gain_vec
    mean_grad = jnp.mean(scaled, axis=-1, keepdims=True)
    mean_cross = jnp.mean(scaled * normed, axis=-1, keepdims=True)
    return inv_std * (scaled - mean_grad - normed * mean_cross)


def gelu_slope(values):
    return 0.5 * (1.0 + lax.erf(values * root_half)) + values * inv_root_tau * jnp.exp(
        -0.5 * values * values
    )


def local_routes(buckets, expert_of_bucket, slot_rows):
    experts_all = expert_of_bucket.shape[0]
    tok_rows = buckets.shape[0]
    capacity = slot_rows // experts_all
    labels = jnp.arange(experts_all, dtype=jnp.int32)
    bucket_hot = (buckets == labels[None, :]).astype(jnp.int32)
    expert_tok = jnp.sum(bucket_hot * expert_of_bucket[None, :], axis=1)
    expert_hot = (expert_tok[:, None] == labels[None, :]).astype(jnp.int32)
    before = jnp.cumsum(expert_hot, axis=0) - expert_hot
    rank_tok = jnp.sum(before * expert_hot, axis=1)
    slot_local = expert_tok * capacity + rank_tok
    source_of_slot = (
        jnp.full((slot_rows,), tok_rows, jnp.int32)
        .at[slot_local]
        .set(jnp.arange(tok_rows, dtype=jnp.int32))
    )
    return (slot_local, source_of_slot)


def to_slots(rows_low, source_of_slot, experts_all):
    model_width = rows_low.shape[1]
    padded = jnp.concatenate([rows_low, jnp.zeros((1, model_width), rows_low.dtype)], axis=0)
    picked = jnp.take(padded, source_of_slot, axis=0)
    return picked.reshape(experts_all, -1, model_width)


def block_scores(query_block, key_rows, allowed, scale_val):
    scores = (
        jnp.einsum("qhd,khd->hqk", query_block, key_rows, preferred_element_type=jnp.float32)
        * scale_val
    )
    return jnp.where(allowed[None], scores, masked_score)


MESH_ID = pl.DeviceIdType.MESH
PARTS = 4
UNITS = 256


def mm(a, b):
    return jnp.dot(a, b, preferred_element_type=jnp.float32)


def mm_nt(a, b):
    return lax.dot_general(a, b, (((1,), (1,)), ((), ())), preferred_element_type=jnp.float32)


def mm_tn(a, b):
    return lax.dot_general(a, b, (((0,), (0,)), ((), ())), preferred_element_type=jnp.float32)


def gelu_parts(pre):
    bell = jnp.exp(-0.5 * pre * pre)
    den = 1.0 + (0.3275911 * root_half) * jnp.abs(pre)
    t = pl.reciprocal(den, approx=True)
    t = t * (2.0 - den * t)
    tail = t * (
        0.5 * 0.254829592
        + t * (0.5 * -0.284496736 + t * (0.5 * 1.421413741 + t * (0.5 * -1.453152027 + t * (0.5 * 1.061405429))))
    )
    tail = tail * bell
    phi = jnp.where(pre >= 0.0, 1.0 - tail, tail)
    return pre * phi, phi + pre * (inv_root_tau * bell)


def greet(me_d, me_e, n):
    barrier = pltpu.get_barrier_semaphore()

    def signal(i, carry):
        pl.semaphore_signal(barrier, inc=1, device_id=(me_d, me_e ^ i), device_id_type=MESH_ID)
        return carry

    lax.fori_loop(1, n, signal, 0)
    pl.semaphore_signal(barrier, inc=1, device_id=(1 - me_d, me_e), device_id_type=MESH_ID)
    pl.semaphore_wait(barrier, n)


def expert_kernel(
    n,
    cap,
    sent,
    grads,
    live,
    up_hbm,
    up_bias,
    down_hbm,
    down_bias,
    gain,
    bias,
    returned,
    hidden_out,
    grad_up,
    grad_down,
    grad_bup,
    grad_bdown,
    grad_norm,
    rows_in,
    ffn_in,
    grad_rows,
    up,
    down,
    act,
    pre_grad,
    pre_tile,
    hid_tile,
    part_out,
    part_in,
    back,
    tile,
    tile_down,
    sem_send,
    sem_recv,
    sem_back_send,
    sem_back_recv,
    sem_pair,
    sem_load,
    sem_store,
):
    me_d = lax.axis_index("dp")
    me_e = lax.axis_index("expert")
    rows = rows_in.shape[0]
    width = rows_in.shape[1]
    units = up.shape[1]
    block = rows // PARTS
    many = n // PARTS
    partner = (1 - me_d, me_e)

    def base_of(part):
        return pl.multiple_of(((me_e // many) ^ part) * block, block)

    def slot_copy(i):
        peer = me_e ^ i
        return pltpu.make_async_remote_copy(
            src_ref=sent.at[pl.ds(pl.multiple_of(peer * cap, cap), cap)],
            dst_ref=rows_in.at[pl.ds(pl.multiple_of(me_e * cap, cap), cap)],
            send_sem=sem_send.at[i],
            recv_sem=sem_recv.at[i],
            device_id=(me_d, peer),
            device_id_type=MESH_ID,
        )

    def own_slots():
        own = pl.ds(pl.multiple_of(me_e * cap, cap), cap)
        return pltpu.make_async_copy(sent.at[own], rows_in.at[own], sem_recv.at[0])

    def back_copy(i):
        peer = me_e ^ i
        return pltpu.make_async_remote_copy(
            src_ref=back.at[pl.ds(pl.multiple_of(peer * cap, cap), cap)],
            dst_ref=returned.at[pl.ds(pl.multiple_of(me_e * cap, cap), cap)],
            send_sem=sem_back_send.at[i],
            recv_sem=sem_back_recv.at[i],
            device_id=(me_d, peer),
            device_id_type=MESH_ID,
        )

    def own_back():
        own = pl.ds(pl.multiple_of(me_e * cap, cap), cap)
        return pltpu.make_async_copy(back.at[own], returned.at[own], sem_back_recv.at[0])

    def pair_copy(src, dst, kind, part):
        return pltpu.make_async_remote_copy(
            src_ref=src,
            dst_ref=dst,
            send_sem=sem_pair.at[kind, 0, part],
            recv_sem=sem_pair.at[kind, 1, part],
            device_id=partner,
            device_id_type=MESH_ID,
        )

    def grads_pair(part):
        return pair_copy(
            grads.at[pl.ds(base_of(part), block)], grad_rows.at[part, pl.ds(block, block)], 0, part
        )

    def ffn_pair(part):
        return pair_copy(
            ffn_in.at[part, pl.ds(0, block)], ffn_in.at[part, pl.ds(block, block)], 1, part
        )

    def part_pair(part):
        return pair_copy(part_out.at[part], part_in.at[part], 2, part)

    def out_pair(part):
        return pair_copy(part_out.at[PARTS + part], part_in.at[PARTS + part], 3, part)

    def grads_load(part):
        return pltpu.make_async_copy(
            grads.at[pl.ds(base_of(part), block)], grad_rows.at[part, pl.ds(0, block)], sem_load.at[2 + part]
        )

    up_load = pltpu.make_async_copy(up_hbm, up, sem_load.at[0])
    down_load = pltpu.make_async_copy(down_hbm, down, sem_load.at[1])

    greet(me_d, me_e, n)
    own_slots().start()
    for part in range(PARTS):
        grads_pair(part).start()
        grads_load(part).start()
    down_load.start()
    up_load.start()

    def start_slots(i, carry):
        slot_copy(i).start()
        return carry

    lax.fori_loop(1, n, start_slots, 0)
    grad_norm[...] = jnp.zeros_like(grad_norm)
    down_load.wait()
    up_load.wait()

    def stats(base):
        x = rows_in[pl.ds(base, block), :].astype(jnp.float32)
        return normalize(x)

    def work(part, carry):
        base = base_of(part)

        @pl.when(part == 0)
        def _():
            own_slots().wait()

        @pl.when(part > 0)
        def _():
            slot_copy(part * many).wait()

        def wait_slots(j, c):
            slot_copy(part * many + j).wait()
            return c

        lax.fori_loop(1, many, wait_slots, 0)
        normed, _ = stats(base)
        ffn_in[part, 0:block, :] = (normed * gain[...] + bias[...]).astype(jnp.bfloat16)
        ffn_pair(part).start()
        grads_load(part).wait()
        grads_pair(part).wait()
        ffn_pair(part).wait()

        def hidden(f, c):
            cols = pl.ds(pl.multiple_of(f * UNITS, UNITS), UNITS)
            pre = mm(ffn_in[part], up[:, cols]) + up_bias[:, cols]
            hid = mm_nt(grad_rows[part], down[cols, :])
            a, slope = gelu_parts(pre)
            act[part, :, cols] = a.astype(jnp.bfloat16)
            pre_grad[part, :, cols] = (hid * slope).astype(jnp.bfloat16)
            return c

        lax.fori_loop(0, units // UNITS, hidden, 0)
        part_out[part] = mm_nt(pre_grad[part, block:, :], up[...]).astype(jnp.bfloat16)
        part_pair(part).start()
        mine = mm_nt(pre_grad[part, 0:block, :], up[...])
        part_pair(part).wait()
        grad_ffn = mine + part_in[part].astype(jnp.float32)
        normed, inv_std = stats(base)
        grad_norm[0:1, :] += jnp.sum(grad_ffn * normed, axis=0, keepdims=True)
        grad_norm[1:2, :] += jnp.sum(grad_ffn, axis=0, keepdims=True)
        result = grad_rows[part, 0:block, :].astype(jnp.float32) + norm_back(
            grad_ffn, normed, inv_std, gain[...]
        )
        back[pl.ds(base, block), :] = result.astype(jnp.bfloat16)

        @pl.when(part == 0)
        def _():
            own_back().start()

        @pl.when(part > 0)
        def _():
            back_copy(part * many).start()

        def start_back(j, c):
            back_copy(part * many + j).start()
            return c

        lax.fori_loop(1, many, start_back, 0)
        return carry

    lax.fori_loop(0, PARTS, work, 0)

    def output(part, carry):
        part_out[PARTS + part] = mm(act[part, block:, :], down[...]).astype(jnp.bfloat16)
        out_pair(part).start()
        return carry

    lax.fori_loop(0, PARTS, output, 0)

    def output_own(part, carry):
        base = base_of(part)
        here = pl.ds(base, block)
        mine = mm(act[part, 0:block, :], down[...])
        out_pair(part).wait()
        total = rows_in[here, :].astype(jnp.float32) + mine + part_in[PARTS + part].astype(jnp.float32) + down_bias[...]
        rows_in[here, :] = (total * live[here, :]).astype(jnp.bfloat16)
        pltpu.make_async_copy(rows_in.at[here], hidden_out.at[here], sem_store.at[part]).start()
        return carry

    lax.fori_loop(0, PARTS, output_own, 0)

    ones = jnp.ones((8, PARTS * 2 * block), jnp.bfloat16)
    all_act = act.reshape(PARTS * 2 * block, units)
    all_pre = pre_grad.reshape(PARTS * 2 * block, units)
    all_in = ffn_in.reshape(PARTS * 2 * block, width)
    all_grad = grad_rows.reshape(PARTS * 2 * block, width)
    grad_bup[...] = mm(ones, all_pre[...])
    grad_bdown[...] = mm(ones, all_grad[...])

    def up_store(f, slot):
        cols = pl.ds(pl.multiple_of(f * UNITS, UNITS), UNITS)
        return pltpu.make_async_copy(tile.at[slot], grad_up.at[:, cols], sem_store.at[PARTS + slot])

    def down_store(f, slot):
        cols = pl.ds(pl.multiple_of(f * UNITS, UNITS), UNITS)
        return pltpu.make_async_copy(
            tile_down.at[slot], grad_down.at[cols, :], sem_store.at[PARTS + 2 + slot]
        )

    def weights(f, carry):
        slot = lax.rem(f, 2)
        cols = pl.ds(pl.multiple_of(f * UNITS, UNITS), UNITS)

        @pl.when(f >= 2)
        def _():
            up_store(f, slot).wait()
            down_store(f, slot).wait()

        tile[slot] = mm_tn(all_in[...], all_pre[:, cols])
        up_store(f, slot).start()
        tile_down[slot] = mm_tn(all_act[:, cols], all_grad[...])
        down_store(f, slot).start()
        return carry

    lax.fori_loop(0, units // UNITS, weights, 0)
    for slot in range(2):
        up_store(0, slot).wait()
        down_store(0, slot).wait()
    for part in range(PARTS):
        pltpu.make_async_copy(
            rows_in.at[pl.ds(0, block)], hidden_out.at[pl.ds(0, block)], sem_store.at[part]
        ).wait()
    own_back().wait()

    def wait_back(i, carry):
        back_copy(i).wait()
        return carry

    lax.fori_loop(1, n, wait_back, 0)


def expert_block(sent, grads, live, up, up_bias, down, down_bias, gain, bias):
    n = lax.axis_size("expert")
    rows, width = sent.shape
    units = up.shape[1]
    cap = rows // n
    block = rows // PARTS
    vm = pl.BlockSpec(memory_space=pltpu.VMEM)
    hbm = pl.BlockSpec(memory_space=pl.ANY)
    f32, low = jnp.float32, jnp.bfloat16
    return pl.pallas_call(
        functools.partial(expert_kernel, n, cap),
        out_shape=(
            jax.ShapeDtypeStruct((rows, width), low),
            jax.ShapeDtypeStruct((rows, width), low),
            jax.ShapeDtypeStruct((width, units), f32),
            jax.ShapeDtypeStruct((units, width), f32),
            jax.ShapeDtypeStruct((8, units), f32),
            jax.ShapeDtypeStruct((8, width), f32),
            jax.ShapeDtypeStruct((8, width), f32),
        ),
        in_specs=[hbm, hbm, vm, hbm, vm, hbm, vm, vm, vm],
        out_specs=(hbm, hbm, hbm, hbm, vm, vm, vm),
        scratch_shapes=[
            pltpu.VMEM((rows, width), low),
            pltpu.VMEM((PARTS, 2 * block, width), low),
            pltpu.VMEM((PARTS, 2 * block, width), low),
            pltpu.VMEM((width, units), low),
            pltpu.VMEM((units, width), low),
            pltpu.VMEM((PARTS, 2 * block, units), low),
            pltpu.VMEM((PARTS, 2 * block, units), low),
            pltpu.VMEM((2, 2 * block, UNITS), f32),
            pltpu.VMEM((2, 2 * block, UNITS), f32),
            pltpu.VMEM((2 * PARTS, block, width), low),
            pltpu.VMEM((2 * PARTS, block, width), low),
            pltpu.VMEM((rows, width), low),
            pltpu.VMEM((2, width, UNITS), f32),
            pltpu.VMEM((2, UNITS, width), f32),
            pltpu.SemaphoreType.DMA((n,)),
            pltpu.SemaphoreType.DMA((n,)),
            pltpu.SemaphoreType.DMA((n,)),
            pltpu.SemaphoreType.DMA((n,)),
            pltpu.SemaphoreType.DMA((4, 2, PARTS)),
            pltpu.SemaphoreType.DMA((2 + PARTS,)),
            pltpu.SemaphoreType.DMA((PARTS + 4,)),
        ],
        compiler_params=pltpu.CompilerParams(
            collective_id=1, has_side_effects=True, vmem_limit_bytes=60 * 1024 * 1024
        ),
    )(sent, grads, live, up, up_bias, down, down_bias, gain, bias)


def on_device(
    hidden_in,
    buckets,
    expert_of_bucket,
    lengths,
    norm1_gain,
    norm1_bias,
    w_qkv,
    w_out,
    norm2_gain,
    norm2_bias,
    w_up,
    b_up,
    w_down,
    b_down,
    grad_out,
):
    experts_all = lax.axis_size("expert")
    slot_rows = hidden_in.shape[0]
    model_width = hidden_in.shape[1]
    capacity = slot_rows // experts_all
    tok_rows = buckets.shape[0]
    scale_val = HEAD_DIM ** (-0.5)
    slot_local, source_of_slot = local_routes(buckets, expert_of_bucket, slot_rows)
    taken_flags = (source_of_slot < tok_rows).astype(jnp.bfloat16).reshape(experts_all, capacity)
    arrived = lax.all_to_all(
        hidden_in.reshape(experts_all, capacity, model_width),
        "expert",
        split_axis=0,
        concat_axis=0,
        tiled=True,
    )
    tokens_in = jnp.take(arrived.reshape(slot_rows, model_width), slot_local, axis=0).astype(
        jnp.float32
    )
    seg_ends = jnp.cumsum(lengths[0])
    positions = jnp.arange(tok_rows, dtype=jnp.int32)
    segment = jnp.sum((positions[:, None] >= seg_ends[None, :]).astype(jnp.int32), axis=1)
    normed1, inv_std1 = normalize(tokens_in)
    attn_in = (normed1 * norm1_gain + norm1_bias).astype(jnp.bfloat16)
    proj_qkv = jnp.dot(attn_in, w_qkv, preferred_element_type=jnp.float32).astype(jnp.bfloat16)
    queries = proj_qkv[:, :model_width].reshape(tok_rows, HEADS, HEAD_DIM)
    key_rows = proj_qkv[:, model_width : 2 * model_width].reshape(tok_rows, HEADS, HEAD_DIM)
    values = proj_qkv[:, 2 * model_width :].reshape(tok_rows, HEADS, HEAD_DIM)
    block_rows = min(512, tok_rows)
    block_idx = 0
    row_start = block_idx * block_rows
    allowed = jnp.logical_and(
        positions[None, :] <= positions[row_start : row_start + block_rows, None],
        segment[None, :] == segment[row_start : row_start + block_rows, None],
    )
    scores = block_scores(queries, key_rows, allowed, scale_val)
    top_score = jnp.max(scores, axis=-1, keepdims=True)
    exp_scores = jnp.exp(scores - top_score)
    row_total = jnp.sum(exp_scores, axis=-1, keepdims=True)
    attended = jnp.einsum(
        "hqk,khd->qhd",
        (exp_scores / row_total).astype(jnp.bfloat16),
        values,
        preferred_element_type=jnp.float32,
    )
    outputs = attended.reshape(block_rows, model_width)
    log_totals = [top_score + jnp.log(row_total)]
    allowed_list = [allowed]
    attended_low = outputs.astype(jnp.bfloat16)
    residual_h = tokens_in + jnp.dot(attended_low, w_out, preferred_element_type=jnp.float32)
    sent_h = to_slots(residual_h.astype(jnp.bfloat16), source_of_slot, experts_all)
    live_part = lax.all_to_all(taken_flags, "expert", split_axis=0, concat_axis=0, tiled=True)
    live_rows = live_part.reshape(slot_rows, 1).astype(jnp.float32)
    grad_rows = (grad_out.astype(jnp.float32) * live_rows).astype(jnp.bfloat16)
    (
        returned,
        hidden_out,
        grad_up_half,
        grad_down_half,
        grad_bup,
        grad_bdown,
        grad_norm2,
    ) = expert_block(
        sent_h.reshape(slot_rows, model_width),
        grad_rows,
        live_rows,
        w_up[0],
        b_up,
        w_down[0],
        b_down,
        norm2_gain[None],
        norm2_bias[None],
    )
    grad_bup_half = grad_bup[0]
    half = model_width // lax.axis_size("dp")
    grad_bdown_half = lax.dynamic_slice_in_dim(grad_bdown[0], lax.axis_index("dp") * half, half)
    grad_gain2, grad_bias2 = grad_norm2[0], grad_norm2[1]
    grad_h = jnp.take(returned.reshape(slot_rows, model_width), slot_local, axis=0)
    grad_wout = jnp.einsum("td,te->de", attended_low, grad_h, preferred_element_type=jnp.float32)
    grad_attended = (
        jnp.einsum("te,de->td", grad_h, w_out, preferred_element_type=jnp.float32)
        .astype(jnp.bfloat16)
        .reshape(tok_rows, HEADS, HEAD_DIM)
    )
    block_idx = 0
    scores = block_scores(queries, key_rows, allowed_list[block_idx], scale_val)
    attn_probs = jnp.exp(scores - log_totals[block_idx])
    grad_probs = jnp.einsum(
        "qhd,khd->hqk", grad_attended, values, preferred_element_type=jnp.float32
    )
    row_dot = jnp.sum(attn_probs * grad_probs, axis=-1, keepdims=True)
    grad_scores = (attn_probs * (grad_probs - row_dot)).astype(jnp.bfloat16)
    query_grads = (
        jnp.einsum("hqk,khd->qhd", grad_scores, key_rows, preferred_element_type=jnp.float32)
        * scale_val
    )
    grad_keys = (
        jnp.einsum("hqk,qhd->khd", grad_scores, queries, preferred_element_type=jnp.float32)
        * scale_val
    )
    grad_values = jnp.einsum(
        "hqk,qhd->khd",
        attn_probs.astype(jnp.bfloat16),
        grad_attended,
        preferred_element_type=jnp.float32,
    )
    grad_proj = jnp.concatenate(
        [
            query_grads.reshape(tok_rows, model_width),
            grad_keys.reshape(tok_rows, model_width),
            grad_values.reshape(tok_rows, model_width),
        ],
        axis=1,
    ).astype(jnp.bfloat16)
    grad_wqkv = jnp.einsum("td,te->de", attn_in, grad_proj, preferred_element_type=jnp.float32)
    grad_attn = jnp.einsum("te,de->td", grad_proj, w_qkv, preferred_element_type=jnp.float32)
    grad_gain1 = jnp.sum(grad_attn * normed1, axis=0)
    grad_bias1 = jnp.sum(grad_attn, axis=0)
    grad_tokens = grad_h.astype(jnp.float32) + norm_back(grad_attn, normed1, inv_std1, norm1_gain)
    grad_in = lax.all_to_all(
        to_slots(grad_tokens.astype(jnp.bfloat16), source_of_slot, experts_all),
        "expert",
        split_axis=0,
        concat_axis=0,
        tiled=True,
    ).reshape(slot_rows, model_width)
    norm_terms = jnp.stack([grad_gain1, grad_bias1, grad_gain2, grad_bias2], axis=0)
    grad_qkv, grad_wout_part, norm_parts = (
        lax.psum_scatter(grad_wqkv, ("dp", "expert"), scatter_dimension=0, tiled=True),
        lax.psum_scatter(grad_wout, ("dp", "expert"), scatter_dimension=0, tiled=True),
        lax.psum_scatter(norm_terms, ("dp", "expert"), scatter_dimension=1, tiled=True),
    )
    return (
        hidden_out,
        grad_in,
        grad_qkv,
        grad_wout_part,
        norm_parts[0],
        norm_parts[1],
        norm_parts[2],
        norm_parts[3],
        grad_up_half[None],
        grad_bup_half[None],
        grad_down_half[None],
        grad_bdown_half[None],
    )


def solution(mesh):
    return jax.shard_map(
        on_device,
        mesh=mesh,
        in_specs=(
            P(("dp", "expert"), None),
            P(("dp", "expert"), None),
            P(),
            P(("dp", "expert"), None),
            P(),
            P(),
            P(),
            P(),
            P(),
            P(),
            P("expert", None, "dp"),
            P("expert", "dp"),
            P("expert", "dp", None),
            P("expert", None),
            P(("dp", "expert"), None),
        ),
        out_specs=(
            P(("dp", "expert"), None),
            P(("dp", "expert"), None),
            P(("dp", "expert"), None),
            P(("dp", "expert"), None),
            P(("dp", "expert")),
            P(("dp", "expert")),
            P(("dp", "expert")),
            P(("dp", "expert")),
            P("expert", None, "dp"),
            P("expert", "dp"),
            P("expert", "dp", None),
            P("expert", "dp"),
        ),
        check_vma=False,
    )
```

```python
import functools

import jax
import jax.numpy as jnp
from jax import lax
from jax.experimental import pallas as pl
from jax.experimental.pallas import tpu as pltpu
from jax.sharding import PartitionSpec as P

HEADS = 16
HEAD_DIM = 64


norm_eps = 1e-05
masked_score = -1e30
root_half = 0.7071067811865476
inv_root_tau = 0.3989422804014327


def normalize(values):
    mean_val = jnp.mean(values, axis=-1, keepdims=True)
    centered = values - mean_val
    variance = jnp.mean(centered * centered, axis=-1, keepdims=True)
    inv_std = lax.rsqrt(variance + norm_eps)
    return (centered * inv_std, inv_std)


def norm_back(grad_normed, normed, inv_std, gain_vec):
    scaled = grad_normed * gain_vec
    mean_grad = jnp.mean(scaled, axis=-1, keepdims=True)
    mean_cross = jnp.mean(scaled * normed, axis=-1, keepdims=True)
    return inv_std * (scaled - mean_grad - normed * mean_cross)


def gelu_slope(values):
    return 0.5 * (1.0 + lax.erf(values * root_half)) + values * inv_root_tau * jnp.exp(
        -0.5 * values * values
    )


def local_routes(buckets, expert_of_bucket, slot_rows):
    experts_all = expert_of_bucket.shape[0]
    tok_rows = buckets.shape[0]
    capacity = slot_rows // experts_all
    labels = jnp.arange(experts_all, dtype=jnp.int32)
    bucket_hot = (buckets == labels[None, :]).astype(jnp.int32)
    expert_tok = jnp.sum(bucket_hot * expert_of_bucket[None, :], axis=1)
    expert_hot = (expert_tok[:, None] == labels[None, :]).astype(jnp.int32)
    before = jnp.cumsum(expert_hot, axis=0) - expert_hot
    rank_tok = jnp.sum(before * expert_hot, axis=1)
    slot_local = expert_tok * capacity + rank_tok
    source_of_slot = (
        jnp.full((slot_rows,), tok_rows, jnp.int32)
        .at[slot_local]
        .set(jnp.arange(tok_rows, dtype=jnp.int32))
    )
    return (slot_local, source_of_slot)


def to_slots(rows_low, source_of_slot, experts_all):
    model_width = rows_low.shape[1]
    padded = jnp.concatenate([rows_low, jnp.zeros((1, model_width), rows_low.dtype)], axis=0)
    picked = jnp.take(padded, source_of_slot, axis=0)
    return picked.reshape(experts_all, -1, model_width)


def block_scores(query_block, key_rows, allowed, scale_val):
    scores = (
        jnp.einsum("qhd,khd->hqk", query_block, key_rows, preferred_element_type=jnp.float32)
        * scale_val
    )
    return jnp.where(allowed[None], scores, masked_score)


MESH_ID = pl.DeviceIdType.MESH
PARTS = 4
UNITS = 256


def mm(a, b):
    return jnp.dot(a, b, preferred_element_type=jnp.float32)


def mm_nt(a, b):
    return lax.dot_general(a, b, (((1,), (1,)), ((), ())), preferred_element_type=jnp.float32)


def mm_tn(a, b):
    return lax.dot_general(a, b, (((0,), (0,)), ((), ())), preferred_element_type=jnp.float32)


def gelu_parts(pre):
    bell = jnp.exp(-0.5 * pre * pre)
    den = 1.0 + (0.3275911 * root_half) * jnp.abs(pre)
    t = pl.reciprocal(den, approx=True)
    t = t * (2.0 - den * t)
    tail = t * (
        0.5 * 0.254829592
        + t * (0.5 * -0.284496736 + t * (0.5 * 1.421413741 + t * (0.5 * -1.453152027 + t * (0.5 * 1.061405429))))
    )
    tail = tail * bell
    phi = jnp.where(pre >= 0.0, 1.0 - tail, tail)
    return pre * phi, phi + pre * (inv_root_tau * bell)


def greet(me_d, me_e, n):
    barrier = pltpu.get_barrier_semaphore()

    def signal(i, carry):
        pl.semaphore_signal(barrier, inc=1, device_id=(me_d, me_e ^ i), device_id_type=MESH_ID)
        return carry

    lax.fori_loop(1, n, signal, 0)
    pl.semaphore_signal(barrier, inc=1, device_id=(1 - me_d, me_e), device_id_type=MESH_ID)
    pl.semaphore_wait(barrier, n)


def expert_kernel(
    n,
    cap,
    sent,
    grads,
    live,
    up_hbm,
    up_bias,
    down_hbm,
    down_bias,
    gain,
    bias,
    returned,
    hidden_out,
    grad_up,
    grad_down,
    grad_bup,
    grad_bdown,
    grad_norm,
    rows_in,
    ffn_in,
    grad_rows,
    up,
    down,
    act,
    pre_grad,
    pre_tile,
    hid_tile,
    part_out,
    part_in,
    back,
    tile,
    tile_down,
    sem_send,
    sem_recv,
    sem_back_send,
    sem_back_recv,
    sem_pair,
    sem_load,
    sem_store,
):
    me_d = lax.axis_index("dp")
    me_e = lax.axis_index("expert")
    rows = rows_in.shape[0]
    width = rows_in.shape[1]
    units = up.shape[1]
    block = rows // PARTS
    many = n // PARTS
    partner = (1 - me_d, me_e)

    def base_of(part):
        return pl.multiple_of(((me_e // many) ^ part) * block, block)

    def slot_copy(i):
        peer = me_e ^ i
        return pltpu.make_async_remote_copy(
            src_ref=sent.at[pl.ds(pl.multiple_of(peer * cap, cap), cap)],
            dst_ref=rows_in.at[pl.ds(pl.multiple_of(me_e * cap, cap), cap)],
            send_sem=sem_send.at[i],
            recv_sem=sem_recv.at[i],
            device_id=(me_d, peer),
            device_id_type=MESH_ID,
        )

    def own_slots():
        own = pl.ds(pl.multiple_of(me_e * cap, cap), cap)
        return pltpu.make_async_copy(sent.at[own], rows_in.at[own], sem_recv.at[0])

    def back_copy(i):
        peer = me_e ^ i
        return pltpu.make_async_remote_copy(
            src_ref=back.at[pl.ds(pl.multiple_of(peer * cap, cap), cap)],
            dst_ref=returned.at[pl.ds(pl.multiple_of(me_e * cap, cap), cap)],
            send_sem=sem_back_send.at[i],
            recv_sem=sem_back_recv.at[i],
            device_id=(me_d, peer),
            device_id_type=MESH_ID,
        )

    def own_back():
        own = pl.ds(pl.multiple_of(me_e * cap, cap), cap)
        return pltpu.make_async_copy(back.at[own], returned.at[own], sem_back_recv.at[0])

    def pair_copy(src, dst, kind, part):
        return pltpu.make_async_remote_copy(
            src_ref=src,
            dst_ref=dst,
            send_sem=sem_pair.at[kind, 0, part],
            recv_sem=sem_pair.at[kind, 1, part],
            device_id=partner,
            device_id_type=MESH_ID,
        )

    def grads_pair(part):
        return pair_copy(
            grads.at[pl.ds(base_of(part), block)], grad_rows.at[part, pl.ds(block, block)], 0, part
        )

    def ffn_pair(part):
        return pair_copy(
            ffn_in.at[part, pl.ds(0, block)], ffn_in.at[part, pl.ds(block, block)], 1, part
        )

    def part_pair(part):
        return pair_copy(part_out.at[part], part_in.at[part], 2, part)

    def out_pair(part):
        return pair_copy(part_out.at[PARTS + part], part_in.at[PARTS + part], 3, part)

    def grads_load(part):
        return pltpu.make_async_copy(
            grads.at[pl.ds(base_of(part), block)], grad_rows.at[part, pl.ds(0, block)], sem_load.at[2 + part]
        )

    up_load = pltpu.make_async_copy(up_hbm, up, sem_load.at[0])
    down_load = pltpu.make_async_copy(down_hbm, down, sem_load.at[1])

    greet(me_d, me_e, n)
    own_slots().start()
    for part in range(PARTS):
        grads_pair(part).start()
        grads_load(part).start()
    down_load.start()
    up_load.start()

    def start_slots(i, carry):
        slot_copy(i).start()
        return carry

    lax.fori_loop(1, n, start_slots, 0)
    grad_norm[...] = jnp.zeros_like(grad_norm)
    down_load.wait()
    up_load.wait()

    def stats(base):
        x = rows_in[pl.ds(base, block), :].astype(jnp.float32)
        return normalize(x)

    def work(part, carry):
        base = base_of(part)

        @pl.when(part == 0)
        def _():
            own_slots().wait()

        @pl.when(part > 0)
        def _():
            slot_copy(part * many).wait()

        def wait_slots(j, c):
            slot_copy(part * many + j).wait()
            return c

        lax.fori_loop(1, many, wait_slots, 0)
        normed, _ = stats(base)
        ffn_in[part, 0:block, :] = (normed * gain[...] + bias[...]).astype(jnp.bfloat16)
        ffn_pair(part).start()
        grads_load(part).wait()
        grads_pair(part).wait()
        ffn_pair(part).wait()

        def hidden(f, c):
            cols = pl.ds(pl.multiple_of(f * UNITS, UNITS), UNITS)
            pre = mm(ffn_in[part], up[:, cols]) + up_bias[:, cols]
            hid = mm_nt(grad_rows[part], down[cols, :])
            a, slope = gelu_parts(pre)
            act[part, :, cols] = a.astype(jnp.bfloat16)
            pre_grad[part, :, cols] = (hid * slope).astype(jnp.bfloat16)
            return c

        lax.fori_loop(0, units // UNITS, hidden, 0)
        part_out[part] = mm_nt(pre_grad[part, block:, :], up[...]).astype(jnp.bfloat16)
        part_pair(part).start()
        mine = mm_nt(pre_grad[part, 0:block, :], up[...])
        part_pair(part).wait()
        grad_ffn = mine + part_in[part].astype(jnp.float32)
        normed, inv_std = stats(base)
        grad_norm[0:1, :] += jnp.sum(grad_ffn * normed, axis=0, keepdims=True)
        grad_norm[1:2, :] += jnp.sum(grad_ffn, axis=0, keepdims=True)
        result = grad_rows[part, 0:block, :].astype(jnp.float32) + norm_back(
            grad_ffn, normed, inv_std, gain[...]
        )
        back[pl.ds(base, block), :] = result.astype(jnp.bfloat16)

        @pl.when(part == 0)
        def _():
            own_back().start()

        @pl.when(part > 0)
        def _():
            back_copy(part * many).start()

        def start_back(j, c):
            back_copy(part * many + j).start()
            return c

        lax.fori_loop(1, many, start_back, 0)
        return carry

    lax.fori_loop(0, PARTS, work, 0)

    def output(part, carry):
        part_out[PARTS + part] = mm(act[part, block:, :], down[...]).astype(jnp.bfloat16)
        out_pair(part).start()
        return carry

    lax.fori_loop(0, PARTS, output, 0)

    def output_own(part, carry):
        base = base_of(part)
        here = pl.ds(base, block)
        mine = mm(act[part, 0:block, :], down[...])
        out_pair(part).wait()
        total = rows_in[here, :].astype(jnp.float32) + mine + part_in[PARTS + part].astype(jnp.float32) + down_bias[...]
        rows_in[here, :] = (total * live[here, :]).astype(jnp.bfloat16)
        pltpu.make_async_copy(rows_in.at[here], hidden_out.at[here], sem_store.at[part]).start()
        return carry

    lax.fori_loop(0, PARTS, output_own, 0)

    ones = jnp.ones((8, PARTS * 2 * block), jnp.bfloat16)
    all_act = act.reshape(PARTS * 2 * block, units)
    all_pre = pre_grad.reshape(PARTS * 2 * block, units)
    all_in = ffn_in.reshape(PARTS * 2 * block, width)
    all_grad = grad_rows.reshape(PARTS * 2 * block, width)
    grad_bup[...] = mm(ones, all_pre[...])
    grad_bdown[...] = mm(ones, all_grad[...])

    def up_store(f, slot):
        cols = pl.ds(pl.multiple_of(f * UNITS, UNITS), UNITS)
        return pltpu.make_async_copy(tile.at[slot], grad_up.at[:, cols], sem_store.at[PARTS + slot])

    def down_store(f, slot):
        cols = pl.ds(pl.multiple_of(f * UNITS, UNITS), UNITS)
        return pltpu.make_async_copy(
            tile_down.at[slot], grad_down.at[cols, :], sem_store.at[PARTS + 2 + slot]
        )

    def weights(f, carry):
        slot = lax.rem(f, 2)
        cols = pl.ds(pl.multiple_of(f * UNITS, UNITS), UNITS)

        @pl.when(f >= 2)
        def _():
            up_store(f, slot).wait()
            down_store(f, slot).wait()

        tile[slot] = mm_tn(all_in[...], all_pre[:, cols])
        up_store(f, slot).start()
        tile_down[slot] = mm_tn(all_act[:, cols], all_grad[...])
        down_store(f, slot).start()
        return carry

    lax.fori_loop(0, units // UNITS, weights, 0)
    for slot in range(2):
        up_store(0, slot).wait()
        down_store(0, slot).wait()
    for part in range(PARTS):
        pltpu.make_async_copy(
            rows_in.at[pl.ds(0, block)], hidden_out.at[pl.ds(0, block)], sem_store.at[part]
        ).wait()
    own_back().wait()

    def wait_back(i, carry):
        back_copy(i).wait()
        return carry

    lax.fori_loop(1, n, wait_back, 0)


def expert_block(sent, grads, live, up, up_bias, down, down_bias, gain, bias):
    n = lax.axis_size("expert")
    rows, width = sent.shape
    units = up.shape[1]
    cap = rows // n
    block = rows // PARTS
    vm = pl.BlockSpec(memory_space=pltpu.VMEM)
    hbm = pl.BlockSpec(memory_space=pl.ANY)
    f32, low = jnp.float32, jnp.bfloat16
    return pl.pallas_call(
        functools.partial(expert_kernel, n, cap),
        out_shape=(
            jax.ShapeDtypeStruct((rows, width), low),
            jax.ShapeDtypeStruct((rows, width), low),
            jax.ShapeDtypeStruct((width, units), f32),
            jax.ShapeDtypeStruct((units, width), f32),
            jax.ShapeDtypeStruct((8, units), f32),
            jax.ShapeDtypeStruct((8, width), f32),
            jax.ShapeDtypeStruct((8, width), f32),
        ),
        in_specs=[hbm, hbm, vm, hbm, vm, hbm, vm, vm, vm],
        out_specs=(hbm, hbm, hbm, hbm, vm, vm, vm),
        scratch_shapes=[
            pltpu.VMEM((rows, width), low),
            pltpu.VMEM((PARTS, 2 * block, width), low),
            pltpu.VMEM((PARTS, 2 * block, width), low),
            pltpu.VMEM((width, units), low),
            pltpu.VMEM((units, width), low),
            pltpu.VMEM((PARTS, 2 * block, units), low),
            pltpu.VMEM((PARTS, 2 * block, units), low),
            pltpu.VMEM((2, 2 * block, UNITS), f32),
            pltpu.VMEM((2, 2 * block, UNITS), f32),
            pltpu.VMEM((2 * PARTS, block, width), low),
            pltpu.VMEM((2 * PARTS, block, width), low),
            pltpu.VMEM((rows, width), low),
            pltpu.VMEM((2, width, UNITS), f32),
            pltpu.VMEM((2, UNITS, width), f32),
            pltpu.SemaphoreType.DMA((n,)),
            pltpu.SemaphoreType.DMA((n,)),
            pltpu.SemaphoreType.DMA((n,)),
            pltpu.SemaphoreType.DMA((n,)),
            pltpu.SemaphoreType.DMA((4, 2, PARTS)),
            pltpu.SemaphoreType.DMA((2 + PARTS,)),
            pltpu.SemaphoreType.DMA((PARTS + 4,)),
        ],
        compiler_params=pltpu.CompilerParams(
            collective_id=1, has_side_effects=True, vmem_limit_bytes=60 * 1024 * 1024
        ),
    )(sent, grads, live, up, up_bias, down, down_bias, gain, bias)


STREAMS = 3


def ending_kernel(n, cap, sent, terms, grad_in, sums, own, total, landed, sem_send, sem_recv, sem_own, sem_pair, sem_step):
    me_d = lax.axis_index("dp")
    me_e = lax.axis_index("expert")
    partner = (1 - me_d, me_e)
    bits = n.bit_length() - 1
    half = n // 2
    wide = total.shape[-1]
    orders = []
    for s in range(STREAMS):
        first = s % bits
        orders.append([first] + [b for b in range(bits) if b != first])

    def cols(s):
        return pl.ds(s * wide, wide)

    def offset(s, p):
        k = 0
        for j, b in enumerate(orders[s]):
            k = k + lax.rem(p // (1 << (bits - 1 - j)), 2) * (1 << b)
        return k

    def slot_copy(i):
        peer = me_e ^ i
        return pltpu.make_async_remote_copy(
            src_ref=sent.at[pl.ds(pl.multiple_of(peer * cap, cap), cap)],
            dst_ref=grad_in.at[pl.ds(pl.multiple_of(me_e * cap, cap), cap)],
            send_sem=sem_send.at[i],
            recv_sem=sem_recv.at[i],
            device_id=(me_d, peer),
            device_id_type=MESH_ID,
        )

    def own_slots():
        here = pl.ds(pl.multiple_of(me_e * cap, cap), cap)
        return pltpu.make_async_copy(sent.at[here], grad_in.at[here], sem_recv.at[0])

    def pair_copy(s, p):
        return pltpu.make_async_remote_copy(
            src_ref=terms.at[(1 - me_d) * n + (me_e ^ offset(s, p)), :, cols(s)],
            dst_ref=landed.at[s, p],
            send_sem=sem_pair.at[0, s, p // half],
            recv_sem=sem_pair.at[1, s, p // half],
            device_id=partner,
            device_id_type=MESH_ID,
        )

    def pair_whole(s, q):
        here = landed.at[s, pl.ds(q * half, half)]
        return pltpu.make_async_remote_copy(
            src_ref=here,
            dst_ref=here,
            send_sem=sem_pair.at[0, s, q],
            recv_sem=sem_pair.at[1, s, q],
            device_id=partner,
            device_id_type=MESH_ID,
        )

    def step_copy(s, j):
        size = n >> (j + 1)
        start = n + sum(n >> (i + 1) for i in range(j))
        return (
            pltpu.make_async_remote_copy(
                src_ref=total.at[s, pl.ds(size, size)],
                dst_ref=landed.at[s, pl.ds(start, size)],
                send_sem=sem_step.at[0, s, j],
                recv_sem=sem_step.at[1, s, j],
                device_id=(me_d, me_e ^ (1 << orders[s][j])),
                device_id_type=MESH_ID,
            ),
            size,
            start,
        )

    greet(me_d, me_e, n)
    own_load = pltpu.make_async_copy(terms.at[pl.ds(me_d * n, n)], own, sem_own.at[0])
    own_load.start()
    own_slots().start()
    for q in (1, 0):
        for s in range(STREAMS):

            def start_pair(p, carry, s=s):
                pair_copy(s, p).start()
                return carry

            lax.fori_loop(q * half, q * half + half, start_pair, 0)

    def start_slots(i, carry):
        slot_copy(i).start()
        return carry

    lax.fori_loop(1, n, start_slots, 0)
    own_load.wait()
    for q in (1, 0):
        for s in range(STREAMS):
            pair_whole(s, q).wait()

            def add_pair(p, carry, s=s):
                mine = own[me_e ^ offset(s, p), :, cols(s)].astype(jnp.float32)
                total[s, p] = (mine + landed[s, p].astype(jnp.float32)).astype(jnp.bfloat16)
                return carry

            lax.fori_loop(q * half, q * half + half, add_pair, 0)
            if q == 1:
                step_copy(s, 0)[0].start()
    for j in range(bits):
        for s in range(STREAMS):
            copy, size, start = step_copy(s, j)
            copy.wait()
            if size > 1:

                def add_step(p, carry, s=s, start=start):
                    both = total[s, p].astype(jnp.float32) + landed[s, start + p].astype(jnp.float32)
                    total[s, p] = both.astype(jnp.bfloat16)
                    return carry

                lax.fori_loop(0, size, add_step, 0)
                step_copy(s, j + 1)[0].start()
            else:
                sums[:, cols(s)] = total[s, 0].astype(jnp.float32) + landed[s, start].astype(jnp.float32)
    own_slots().wait()

    def wait_slots(i, carry):
        slot_copy(i).wait()
        return carry

    lax.fori_loop(1, n, wait_slots, 0)


def ending(sent, terms):
    n = lax.axis_size("expert")
    rows, width = sent.shape
    owners, each, wide = terms.shape
    bits = n.bit_length() - 1
    low = jnp.bfloat16
    hbm = pl.BlockSpec(memory_space=pl.ANY)
    return pl.pallas_call(
        functools.partial(ending_kernel, n, rows // n),
        out_shape=(
            jax.ShapeDtypeStruct((rows, width), low),
            jax.ShapeDtypeStruct((each, wide), jnp.float32),
        ),
        in_specs=[hbm, hbm],
        out_specs=(hbm, pl.BlockSpec(memory_space=pltpu.VMEM)),
        scratch_shapes=[
            pltpu.VMEM((n, each, wide), low),
            pltpu.VMEM((STREAMS, n, each, wide // STREAMS), low),
            pltpu.VMEM((STREAMS, 2 * n, each, wide // STREAMS), low),
            pltpu.SemaphoreType.DMA((n,)),
            pltpu.SemaphoreType.DMA((n,)),
            pltpu.SemaphoreType.DMA((1,)),
            pltpu.SemaphoreType.DMA((2, STREAMS, 2)),
            pltpu.SemaphoreType.DMA((2, STREAMS, bits)),
        ],
        compiler_params=pltpu.CompilerParams(
            collective_id=2, has_side_effects=True, vmem_limit_bytes=60 * 1024 * 1024
        ),
    )(sent, terms)


def on_device(
    hidden_in,
    buckets,
    expert_of_bucket,
    lengths,
    norm1_gain,
    norm1_bias,
    w_qkv,
    w_out,
    norm2_gain,
    norm2_bias,
    w_up,
    b_up,
    w_down,
    b_down,
    grad_out,
):
    experts_all = lax.axis_size("expert")
    slot_rows = hidden_in.shape[0]
    model_width = hidden_in.shape[1]
    capacity = slot_rows // experts_all
    tok_rows = buckets.shape[0]
    scale_val = HEAD_DIM ** (-0.5)
    slot_local, source_of_slot = local_routes(buckets, expert_of_bucket, slot_rows)
    taken_flags = (source_of_slot < tok_rows).astype(jnp.bfloat16).reshape(experts_all, capacity)
    arrived = lax.all_to_all(
        hidden_in.reshape(experts_all, capacity, model_width),
        "expert",
        split_axis=0,
        concat_axis=0,
        tiled=True,
    )
    tokens_in = jnp.take(arrived.reshape(slot_rows, model_width), slot_local, axis=0).astype(
        jnp.float32
    )
    seg_ends = jnp.cumsum(lengths[0])
    positions = jnp.arange(tok_rows, dtype=jnp.int32)
    segment = jnp.sum((positions[:, None] >= seg_ends[None, :]).astype(jnp.int32), axis=1)
    normed1, inv_std1 = normalize(tokens_in)
    attn_in = (normed1 * norm1_gain + norm1_bias).astype(jnp.bfloat16)
    proj_qkv = jnp.dot(attn_in, w_qkv, preferred_element_type=jnp.float32).astype(jnp.bfloat16)
    queries = proj_qkv[:, :model_width].reshape(tok_rows, HEADS, HEAD_DIM)
    key_rows = proj_qkv[:, model_width : 2 * model_width].reshape(tok_rows, HEADS, HEAD_DIM)
    values = proj_qkv[:, 2 * model_width :].reshape(tok_rows, HEADS, HEAD_DIM)
    block_rows = min(512, tok_rows)
    block_idx = 0
    row_start = block_idx * block_rows
    allowed = jnp.logical_and(
        positions[None, :] <= positions[row_start : row_start + block_rows, None],
        segment[None, :] == segment[row_start : row_start + block_rows, None],
    )
    scores = block_scores(queries, key_rows, allowed, scale_val)
    top_score = jnp.max(scores, axis=-1, keepdims=True)
    exp_scores = jnp.exp(scores - top_score)
    row_total = jnp.sum(exp_scores, axis=-1, keepdims=True)
    attended = jnp.einsum(
        "hqk,khd->qhd",
        (exp_scores / row_total).astype(jnp.bfloat16),
        values,
        preferred_element_type=jnp.float32,
    )
    outputs = attended.reshape(block_rows, model_width)
    log_totals = [top_score + jnp.log(row_total)]
    allowed_list = [allowed]
    attended_low = outputs.astype(jnp.bfloat16)
    residual_h = tokens_in + jnp.dot(attended_low, w_out, preferred_element_type=jnp.float32)
    sent_h = to_slots(residual_h.astype(jnp.bfloat16), source_of_slot, experts_all)
    live_part = lax.all_to_all(taken_flags, "expert", split_axis=0, concat_axis=0, tiled=True)
    live_rows = live_part.reshape(slot_rows, 1).astype(jnp.float32)
    grad_rows = (grad_out.astype(jnp.float32) * live_rows).astype(jnp.bfloat16)
    (
        returned,
        hidden_out,
        grad_up_half,
        grad_down_half,
        grad_bup,
        grad_bdown,
        grad_norm2,
    ) = expert_block(
        sent_h.reshape(slot_rows, model_width),
        grad_rows,
        live_rows,
        w_up[0],
        b_up,
        w_down[0],
        b_down,
        norm2_gain[None],
        norm2_bias[None],
    )
    grad_bup_half = grad_bup[0]
    half = model_width // lax.axis_size("dp")
    grad_bdown_half = lax.dynamic_slice_in_dim(grad_bdown[0], lax.axis_index("dp") * half, half)
    grad_gain2, grad_bias2 = grad_norm2[0], grad_norm2[1]
    grad_h = jnp.take(returned.reshape(slot_rows, model_width), slot_local, axis=0)
    grad_wout = jnp.einsum("td,te->de", attended_low, grad_h, preferred_element_type=jnp.float32)
    grad_attended = (
        jnp.einsum("te,de->td", grad_h, w_out, preferred_element_type=jnp.float32)
        .astype(jnp.bfloat16)
        .reshape(tok_rows, HEADS, HEAD_DIM)
    )
    block_idx = 0
    scores = block_scores(queries, key_rows, allowed_list[block_idx], scale_val)
    attn_probs = jnp.exp(scores - log_totals[block_idx])
    grad_probs = jnp.einsum(
        "qhd,khd->hqk", grad_attended, values, preferred_element_type=jnp.float32
    )
    row_dot = jnp.sum(attn_probs * grad_probs, axis=-1, keepdims=True)
    grad_scores = (attn_probs * (grad_probs - row_dot)).astype(jnp.bfloat16)
    query_grads = (
        jnp.einsum("hqk,khd->qhd", grad_scores, key_rows, preferred_element_type=jnp.float32)
        * scale_val
    )
    grad_keys = (
        jnp.einsum("hqk,qhd->khd", grad_scores, queries, preferred_element_type=jnp.float32)
        * scale_val
    )
    grad_values = jnp.einsum(
        "hqk,qhd->khd",
        attn_probs.astype(jnp.bfloat16),
        grad_attended,
        preferred_element_type=jnp.float32,
    )
    grad_proj = jnp.concatenate(
        [
            query_grads.reshape(tok_rows, model_width),
            grad_keys.reshape(tok_rows, model_width),
            grad_values.reshape(tok_rows, model_width),
        ],
        axis=1,
    ).astype(jnp.bfloat16)
    grad_wqkv = jnp.einsum("td,te->de", attn_in, grad_proj, preferred_element_type=jnp.float32)
    grad_attn = jnp.einsum("te,de->td", grad_proj, w_qkv, preferred_element_type=jnp.float32)
    grad_gain1 = jnp.sum(grad_attn * normed1, axis=0)
    grad_bias1 = jnp.sum(grad_attn, axis=0)
    grad_tokens = grad_h.astype(jnp.float32) + norm_back(grad_attn, normed1, inv_std1, norm1_gain)
    sent_grad = to_slots(grad_tokens.astype(jnp.bfloat16), source_of_slot, experts_all)
    norm_terms = jnp.stack([grad_gain1, grad_bias1, grad_gain2, grad_bias2], axis=1)
    terms = jnp.concatenate(
        [
            grad_wqkv.astype(jnp.bfloat16),
            grad_wout.astype(jnp.bfloat16),
            jnp.pad(norm_terms, ((0, 0), (0, 124))).astype(jnp.bfloat16),
        ],
        axis=1,
    )
    owners = lax.axis_size("dp") * experts_all
    grad_in, sums = ending(
        sent_grad.reshape(slot_rows, model_width),
        terms.reshape(owners, model_width // owners, 4 * model_width + 128),
    )
    grad_qkv = sums[:, : 3 * model_width]
    grad_wout_part = sums[:, 3 * model_width : 4 * model_width]
    norm_parts = sums[:, 4 * model_width : 4 * model_width + 4].T
    return (
        hidden_out,
        grad_in,
        grad_qkv,
        grad_wout_part,
        norm_parts[0],
        norm_parts[1],
        norm_parts[2],
        norm_parts[3],
        grad_up_half[None],
        grad_bup_half[None],
        grad_down_half[None],
        grad_bdown_half[None],
    )


def solution(mesh):
    return jax.shard_map(
        on_device,
        mesh=mesh,
        in_specs=(
            P(("dp", "expert"), None),
            P(("dp", "expert"), None),
            P(),
            P(("dp", "expert"), None),
            P(),
            P(),
            P(),
            P(),
            P(),
            P(),
            P("expert", None, "dp"),
            P("expert", "dp"),
            P("expert", "dp", None),
            P("expert", None),
            P(("dp", "expert"), None),
        ),
        out_specs=(
            P(("dp", "expert"), None),
            P(("dp", "expert"), None),
            P(("dp", "expert"), None),
            P(("dp", "expert"), None),
            P(("dp", "expert")),
            P(("dp", "expert")),
            P(("dp", "expert")),
            P(("dp", "expert")),
            P("expert", None, "dp"),
            P("expert", "dp"),
            P("expert", "dp", None),
            P("expert", "dp"),
        ),
        check_vma=False,
    )
```

```python
import functools

import jax
import jax.numpy as jnp
from jax import lax
from jax.experimental import pallas as pl
from jax.experimental.pallas import tpu as pltpu
from jax.sharding import PartitionSpec as P

HEADS = 16
HEAD_DIM = 64


norm_eps = 1e-05
masked_score = -1e30
root_half = 0.7071067811865476
inv_root_tau = 0.3989422804014327

MESH_ID = pl.DeviceIdType.MESH
PARTS = 4
UNITS = 256
QUERIES = 256
PAIR = 2 * HEAD_DIM
scale_val = HEAD_DIM ** (-0.5)
low = jnp.bfloat16
f32 = jnp.float32


def mm(a, b):
    return jnp.dot(a, b, preferred_element_type=f32)


def mm_nt(a, b):
    return lax.dot_general(a, b, (((1,), (1,)), ((), ())), preferred_element_type=f32)


def mm_tn(a, b):
    return lax.dot_general(a, b, (((0,), (0,)), ((), ())), preferred_element_type=f32)


def normalize(values, axis=-1):
    mean_val = jnp.mean(values, axis=axis, keepdims=True)
    centered = values - mean_val
    variance = jnp.mean(centered * centered, axis=axis, keepdims=True)
    inv_std = lax.rsqrt(variance + norm_eps)
    return (centered * inv_std, inv_std)


def norm_back(grad_normed, normed, inv_std, gain_vec, axis=-1):
    scaled = grad_normed * gain_vec
    mean_grad = jnp.mean(scaled, axis=axis, keepdims=True)
    mean_cross = jnp.mean(scaled * normed, axis=axis, keepdims=True)
    return inv_std * (scaled - mean_grad - normed * mean_cross)


def gelu_parts(pre):
    bell = jnp.exp(-0.5 * pre * pre)
    den = 1.0 + (0.3275911 * root_half) * jnp.abs(pre)
    t = pl.reciprocal(den, approx=True)
    t = t * (2.0 - den * t)
    tail = t * (
        0.5 * 0.254829592
        + t * (0.5 * -0.284496736 + t * (0.5 * 1.421413741 + t * (0.5 * -1.453152027 + t * (0.5 * 1.061405429))))
    )
    tail = tail * bell
    phi = jnp.where(pre >= 0.0, 1.0 - tail, tail)
    return pre * phi, phi + pre * (inv_root_tau * bell)


def greet(me_d, me_e, n):
    barrier = pltpu.get_barrier_semaphore()

    def signal(i, carry):
        pl.semaphore_signal(barrier, inc=1, device_id=(me_d, me_e ^ i), device_id_type=MESH_ID)
        return carry

    lax.fori_loop(1, n, signal, 0)
    pl.semaphore_signal(barrier, inc=1, device_id=(1 - me_d, me_e), device_id_type=MESH_ID)
    pl.semaphore_wait(barrier, n)


def start_kernel(
    n,
    cap,
    hidden,
    grad_out,
    buckets,
    expert_of,
    lengths,
    gain,
    bias,
    w_qkv_hbm,
    w_out_hbm,
    sent,
    grads,
    grads_pair,
    live,
    attn_in_t,
    tokens_t,
    queries_t,
    keys_t,
    values,
    attended_t,
    inv_sums,
    slot_row,
    expos,
    arrived,
    w_qkv,
    w_out,
    grad_v,
    proj,
    values_t,
    allow,
    tokens,
    expo_v,
    sent_v,
    counts_out,
    counts_in,
    sem_send,
    sem_recv,
    sem_count_send,
    sem_count_recv,
    sem_pair,
    sem_load,
    sem_store,
    sem_turn,
):
    me_d = lax.axis_index("dp")
    me_e = lax.axis_index("expert")
    partner = (1 - me_d, me_e)
    rows, width = arrived.shape
    toks = buckets.shape[0]
    lanes = expert_of.shape[0]

    def slot_copy(i):
        peer = me_e ^ i
        return pltpu.make_async_remote_copy(
            src_ref=hidden.at[pl.ds(pl.multiple_of(peer * cap, cap), cap)],
            dst_ref=arrived.at[pl.ds(pl.multiple_of(me_e * cap, cap), cap)],
            send_sem=sem_send.at[i],
            recv_sem=sem_recv.at[i],
            device_id=(me_d, peer),
            device_id_type=MESH_ID,
        )

    def own_slots():
        here = pl.ds(pl.multiple_of(me_e * cap, cap), cap)
        return pltpu.make_async_copy(hidden.at[here], arrived.at[here], sem_recv.at[0])

    def count_copy(i):
        return pltpu.make_async_remote_copy(
            src_ref=counts_out,
            dst_ref=counts_in.at[me_e],
            send_sem=sem_count_send.at[i],
            recv_sem=sem_count_recv.at[i],
            device_id=(me_d, me_e ^ i),
            device_id_type=MESH_ID,
        )

    grad_load = pltpu.make_async_copy(grad_out, grad_v, sem_load.at[0])
    qkv_load = pltpu.make_async_copy(w_qkv_hbm, w_qkv, sem_load.at[1])
    out_load = pltpu.make_async_copy(w_out_hbm, w_out, sem_load.at[2])
    grad_store = pltpu.make_async_copy(grad_v, grads, sem_store.at[0])
    grad_pair = pltpu.make_async_remote_copy(
        src_ref=grad_v,
        dst_ref=grads_pair,
        send_sem=sem_pair.at[0],
        recv_sem=sem_pair.at[1],
        device_id=partner,
        device_id_type=MESH_ID,
    )

    def start_slots(i, carry):
        slot_copy(i).start()
        return carry

    grad_load.start()
    greet(me_d, me_e, n)

    @pl.when(me_d == 0)
    def _():
        lax.fori_loop(1, n, start_slots, 0)

    own_slots().start()
    qkv_load.start()
    out_load.start()

    lane_ids = lax.broadcasted_iota(jnp.int32, (toks, lanes), 1)
    bucket_hot = (buckets[...] == lane_ids).astype(f32).astype(low)
    serves = (expert_of[...] == lax.broadcasted_iota(jnp.int32, (lanes, lanes), 1)).astype(f32).astype(low)
    expert_hot = mm(bucket_hot, serves)
    row_ids = lax.broadcasted_iota(jnp.int32, (toks, toks), 0)
    col_ids = lax.broadcasted_iota(jnp.int32, (toks, toks), 1)
    earlier = (col_ids < row_ids).astype(f32).astype(low)
    before = mm(earlier, expert_hot.astype(low))
    slot = jnp.sum(expert_hot * (before + (lane_ids * cap).astype(f32)), axis=1, keepdims=True)
    counts_out[...] = jnp.broadcast_to(jnp.sum(expert_hot, axis=0, keepdims=True), counts_out.shape)
    counts_in[me_e] = counts_out[...]

    def start_counts(i, carry):
        count_copy(i).start()
        return carry

    lax.fori_loop(1, n, start_counts, 0)
    slot_row[...] = jnp.broadcast_to(slot, (toks, lanes)).T[0:8, :].astype(jnp.int32)
    ends = jnp.zeros((1, toks), jnp.int32)
    begin = jnp.zeros((1, toks), jnp.int32)
    places = lax.broadcasted_iota(jnp.int32, (1, toks), 1)
    for s in range(lengths.shape[1]):
        ends = ends + lengths[0:1, s : s + 1]
        begin = jnp.where(places >= ends, ends, begin)
    allow[...] = jnp.where(jnp.logical_and(row_ids <= col_ids, row_ids >= begin), 0.0, masked_score)

    def wait_counts(i, carry):
        count_copy(i).wait()
        return carry

    lax.fori_loop(1, n, wait_counts, 0)
    grad_load.wait()

    def mark(s, carry):
        here = pl.ds(pl.multiple_of(s * cap, cap), cap)
        mine = lax.broadcasted_iota(jnp.int32, (1, lanes), 1) == me_e
        count = jnp.sum(jnp.where(mine, counts_in[s, 0:1, :], 0.0), axis=1, keepdims=True)
        taken = (lax.broadcasted_iota(jnp.int32, (cap, 1), 0).astype(f32) < count).astype(f32)
        live[here, :] = taken
        grad_v[here, :] = (grad_v[here, :].astype(f32) * taken).astype(low)
        return carry

    lax.fori_loop(0, n, mark, 0)
    grad_store.start()
    grad_pair.start()

    @pl.when(me_d == 0)
    def _():
        def wait_sent(i, carry):
            slot_copy(i).wait_send()
            return carry

        lax.fori_loop(1, n, wait_sent, 0)
        pl.semaphore_signal(sem_turn, inc=1, device_id=partner, device_id_type=MESH_ID)

    @pl.when(me_d == 1)
    def _():
        pl.semaphore_wait(sem_turn, 1)
        lax.fori_loop(1, n, start_slots, 0)

    own_slots().wait()

    def wait_slots(i, carry):
        slot_copy(i).wait_recv()
        return carry

    lax.fori_loop(1, n, wait_slots, 0)

    pick = (slot.astype(jnp.int32) == lax.broadcasted_iota(jnp.int32, (toks, rows), 1)).astype(f32).astype(low)
    tokens[...] = mm(pick, arrived[...])
    normed, _ = normalize(tokens[...])
    attn_in = (normed * gain[...] + bias[...]).astype(low)
    tokens_t[...] = tokens[...].T.astype(low)
    attn_in_t[...] = attn_in.T
    qkv_load.wait()
    step = width // 4
    for c in range(3 * width // step):
        here = slice(c * step, (c + 1) * step)
        part = mm(attn_in, w_qkv[:, here])
        if c * step < width:
            part = part.astype(low).astype(f32) * scale_val
        proj[:, here] = part.astype(low)
    queries_t[...] = proj[:, 0:width].T
    keys_t[...] = proj[:, width : 2 * width].T
    values[...] = proj[:, 2 * width : 3 * width]
    values_t[...] = proj[:, 2 * width : 3 * width].T

    def pair_store(p):
        here = pl.ds(pl.multiple_of(2 * p, 2), 2)
        return pltpu.make_async_copy(expo_v.at[here], expos.at[here], sem_store.at[2 + p])

    def head_pair(p, carry):
        first = pl.multiple_of(p * PAIR, PAIR)
        in_first = lax.broadcasted_iota(jnp.int32, (1, PAIR), 1) < HEAD_DIM
        for h in range(2):
            mine = in_first if h == 0 else jnp.logical_not(in_first)
            head_rows = pl.ds(pl.multiple_of(first + h * HEAD_DIM, HEAD_DIM), HEAD_DIM)
            for q in range(toks // QUERIES):
                upto = (q + 1) * QUERIES
                here = slice(q * QUERIES, upto)
                query = jnp.where(mine, proj[here, pl.ds(first, PAIR)], jnp.zeros((), low))
                scores = mm_nt(proj[0:upto, pl.ds(pl.multiple_of(width + first, PAIR), PAIR)], query)
                scores = scores + allow[0:upto, here]
                expo = jnp.exp(scores - jnp.max(scores, axis=0, keepdims=True))
                inv = 1.0 / jnp.sum(expo, axis=0, keepdims=True)
                expo = expo.astype(low)
                expo_v[2 * p + h, 0:upto, here] = expo
                if upto < toks:
                    expo_v[2 * p + h, upto:toks, here] = jnp.zeros((toks - upto, QUERIES), low)
                out = mm(values_t[head_rows, 0:upto], expo)
                attended_t[head_rows, here] = (out * inv).astype(low)
                inv_sums[2 * p + h, :, here] = jnp.broadcast_to(inv, (8, QUERIES))
        pair_store(p).start()
        return carry

    lax.fori_loop(0, HEADS // 2, head_pair, 0)
    out_load.wait()
    residual = (tokens[...] + mm_tn(attended_t[...], w_out[...])).astype(low)
    place = (slot_row[0:1, :] == lax.broadcasted_iota(jnp.int32, (rows, toks), 0)).astype(f32).astype(low)
    sent_v[...] = mm(place, residual).astype(low)
    sent_store = pltpu.make_async_copy(sent_v, sent, sem_store.at[1])
    sent_store.start()

    def wait_pairs(p, carry):
        pair_store(p).wait()
        return carry

    lax.fori_loop(0, HEADS // 2, wait_pairs, 0)
    grad_store.wait()
    grad_pair.wait()

    @pl.when(me_d == 1)
    def _():
        def wait_sent(i, carry):
            slot_copy(i).wait_send()
            return carry

        lax.fori_loop(1, n, wait_sent, 0)

    sent_store.wait()


def starting(hidden, grad_out, buckets, expert_of, lengths, gain, bias, w_qkv, w_out):
    n = lax.axis_size("expert")
    rows, width = hidden.shape
    toks = buckets.shape[0]
    lanes = 128
    vm = pl.BlockSpec(memory_space=pltpu.VMEM)
    hbm = pl.BlockSpec(memory_space=pl.ANY)
    shape = jax.ShapeDtypeStruct
    expert_of = jnp.pad(expert_of, (0, lanes - n), constant_values=-1)[:, None]
    return pl.pallas_call(
        functools.partial(start_kernel, n, rows // n),
        out_shape=(
            shape((rows, width), low),
            shape((rows, width), low),
            shape((rows, width), low),
            shape((rows, 1), f32),
            shape((width, toks), low),
            shape((width, toks), low),
            shape((width, toks), low),
            shape((width, toks), low),
            shape((toks, width), low),
            shape((width, toks), low),
            shape((HEADS, 8, toks), f32),
            shape((8, toks), jnp.int32),
            shape((HEADS, toks, toks), low),
        ),
        in_specs=[hbm, hbm, vm, vm, vm, vm, vm, hbm, hbm],
        out_specs=(hbm, hbm, hbm, vm, vm, vm, vm, vm, vm, vm, vm, vm, hbm),
        scratch_shapes=[
            pltpu.VMEM((rows, width), low),
            pltpu.VMEM(w_qkv.shape, low),
            pltpu.VMEM(w_out.shape, low),
            pltpu.VMEM((rows, width), low),
            pltpu.VMEM((toks, 3 * width), low),
            pltpu.VMEM((width, toks), low),
            pltpu.VMEM((toks, toks), f32),
            pltpu.VMEM((toks, width), f32),
            pltpu.VMEM((HEADS, toks, toks), low),
            pltpu.VMEM((rows, width), low),
            pltpu.VMEM((8, lanes), f32),
            pltpu.VMEM((n, 8, lanes), f32),
            pltpu.SemaphoreType.DMA((n,)),
            pltpu.SemaphoreType.DMA((n,)),
            pltpu.SemaphoreType.DMA((n,)),
            pltpu.SemaphoreType.DMA((n,)),
            pltpu.SemaphoreType.DMA((2,)),
            pltpu.SemaphoreType.DMA((3,)),
            pltpu.SemaphoreType.DMA((2 + HEADS // 2,)),
            pltpu.SemaphoreType.REGULAR,
        ],
        compiler_params=pltpu.CompilerParams(
            collective_id=3, has_side_effects=True, vmem_limit_bytes=60 * 1024 * 1024
        ),
    )(hidden, grad_out, buckets, expert_of, lengths, gain, bias, w_qkv, w_out)


def attention_back_kernel(
    returned_hbm,
    slot_row,
    attn_in_hbm,
    tokens_hbm,
    queries_hbm,
    keys_hbm,
    values_hbm,
    attended_hbm,
    inv_sums,
    expos,
    w_qkv_hbm,
    w_out_hbm,
    gain,
    grad_norm2,
    grad_up_in,
    grad_down_in,
    hidden_in,
    sent,
    terms,
    grad_up,
    grad_down,
    hidden_out,
    returned,
    attn_in_t,
    tokens_t,
    queries_t,
    keys_t,
    values,
    attended_t,
    w_qkv,
    w_out,
    expo_v,
    grad_att_t,
    grad_h,
    grad_proj_t,
    terms_v,
    sent_v,
    held_up,
    held_down,
    held_out,
    sem_load,
    sem_expo,
    sem_store,
):
    rows, width = returned.shape
    toks = slot_row.shape[1]
    loads = [
        pltpu.make_async_copy(a, b, sem_load.at[i])
        for i, (a, b) in enumerate(
            (
                (returned_hbm, returned),
                (w_out_hbm, w_out),
                (attended_hbm, attended_t),
                (queries_hbm, queries_t),
                (keys_hbm, keys_t),
                (values_hbm, values),
                (w_qkv_hbm, w_qkv),
                (attn_in_hbm, attn_in_t),
                (tokens_hbm, tokens_t),
            )
        )
    ]

    def move(k, p, store):
        source, target, held = (
            (grad_up_in, grad_up, held_up),
            (grad_down_in, grad_down, held_down),
            (hidden_in, hidden_out, held_out),
        )[k]
        size = held.shape[1]
        here = pl.ds(pl.multiple_of(p * size, size), size)
        slot = lax.rem(p, 2)
        if store:
            return pltpu.make_async_copy(held.at[slot], target.at[here], sem_store.at[3 + k, slot])
        return pltpu.make_async_copy(source.at[here], held.at[slot], sem_store.at[k, slot])

    def expo_load(p):
        here = pl.ds(pl.multiple_of(2 * p, 2), 2)
        return pltpu.make_async_copy(expos.at[here], expo_v.at[here], sem_expo.at[p])

    for i in range(6):
        loads[i].start()

    def start_expo(p, carry):
        expo_load(p).start()
        return carry

    lax.fori_loop(0, HEADS // 2, start_expo, 0)
    for i in range(6, len(loads)):
        loads[i].start()
    place = (slot_row[0:1, :] == lax.broadcasted_iota(jnp.int32, (rows, toks), 0)).astype(f32).astype(low)
    loads[0].wait()
    grad_h[...] = mm_tn(place, returned[...]).astype(low)
    loads[1].wait()
    loads[2].wait()
    grad_att_t[...] = mm_nt(w_out[...], grad_h[...]).astype(low)
    terms_v[:, 3 * width : 4 * width] = mm(attended_t[...], grad_h[...]).astype(low)
    for i in range(3, 6):
        loads[i].wait()
    for k in range(3):
        move(k, 0, False).start()

    def head_pair(p, carry):
        first = pl.multiple_of(p * PAIR, PAIR)
        expo_load(p).wait()
        for k in range(3):
            move(k, p, False).wait()
            move(k, p, True).start()

        @pl.when(p > 0)
        def _():
            for k in range(3):
                move(k, p - 1, True).wait()

        @pl.when(p < HEADS // 2 - 1)
        def _():
            for k in range(3):
                move(k, p + 1, False).start()

        in_first = lax.broadcasted_iota(jnp.int32, (1, PAIR), 1) < HEAD_DIM
        pair_rows = pl.ds(first, PAIR)
        inv_pair = jnp.concatenate(
            [jnp.broadcast_to(inv_sums[2 * p + h, 0:1, :], (HEAD_DIM, toks)) for h in range(2)], axis=0
        )
        grad_pair = grad_att_t[pair_rows, :].astype(f32)
        cross = grad_pair * attended_t[pair_rows, :].astype(f32) * inv_pair
        scaled = (grad_pair * inv_pair).astype(low)
        for h in range(2):
            mine = in_first if h == 0 else jnp.logical_not(in_first)
            head_rows = pl.ds(pl.multiple_of(first + h * HEAD_DIM, HEAD_DIM), HEAD_DIM)
            in_pair = slice(h * HEAD_DIM, (h + 1) * HEAD_DIM)
            row_dot = jnp.sum(cross[in_pair], axis=0, keepdims=True)
            value = jnp.where(mine, values[:, pair_rows], jnp.zeros((), low))
            grad_key, grad_value = None, None
            for q in reversed(range(toks // QUERIES)):
                upto = (q + 1) * QUERIES
                here = slice(q * QUERIES, upto)
                expo = expo_v[2 * p + h, 0:upto, here]
                grad_prob = mm(value[0:upto], scaled[:, here])
                grad_score = (expo.astype(f32) * (grad_prob - row_dot[:, here])).astype(low)
                grad_proj_t[head_rows, here] = (mm(keys_t[head_rows, 0:upto], grad_score) * scale_val).astype(low)
                key_term = mm_nt(queries_t[head_rows, here], grad_score)
                value_term = mm_nt(scaled[in_pair, here], expo)
                if grad_key is None:
                    grad_key, grad_value = key_term, value_term
                else:
                    grad_key = jnp.concatenate([grad_key[:, 0:upto] + key_term, grad_key[:, upto:]], axis=1)
                    grad_value = jnp.concatenate([grad_value[:, 0:upto] + value_term, grad_value[:, upto:]], axis=1)
            key_rows = pl.ds(pl.multiple_of(width + first + h * HEAD_DIM, HEAD_DIM), HEAD_DIM)
            value_rows = pl.ds(pl.multiple_of(2 * width + first + h * HEAD_DIM, HEAD_DIM), HEAD_DIM)
            grad_proj_t[key_rows, :] = grad_key.astype(low)
            grad_proj_t[value_rows, :] = grad_value.astype(low)
        return carry

    lax.fori_loop(0, HEADS // 2, head_pair, 0)
    for i in range(6, len(loads)):
        loads[i].wait()
    grad_attn_t = mm(w_qkv[...], grad_proj_t[...])
    normed_t, inv_std = normalize(tokens_t[...].astype(f32), axis=0)
    terms_v[:, 4 * width :] = jnp.concatenate(
        [
            jnp.sum(grad_attn_t * normed_t, axis=1, keepdims=True),
            jnp.sum(grad_attn_t, axis=1, keepdims=True),
            grad_norm2[...].T[:, 0:2],
            jnp.zeros((width, terms_v.shape[1] - 4 * width - 4), f32),
        ],
        axis=1,
    ).astype(low)
    result = grad_h[...].astype(f32).T + norm_back(grad_attn_t, normed_t, inv_std, gain[...], axis=0)
    sent_v[...] = mm_nt(place, result.astype(low)).astype(low)
    sent_store = pltpu.make_async_copy(sent_v, sent, sem_store.at[6, 0])
    sent_store.start()
    step = width // 4
    for c in range(3 * width // step):
        here = slice(c * step, (c + 1) * step)
        terms_v[:, here] = mm_nt(attn_in_t[...], grad_proj_t[here, :]).astype(low)
    terms_store = pltpu.make_async_copy(terms_v, terms, sem_store.at[6, 1])
    terms_store.start()
    sent_store.wait()
    terms_store.wait()
    for k in range(3):
        move(k, HEADS // 2 - 1, True).wait()


def attention_back(returned, slot_row, attn_in_t, tokens_t, queries_t, keys_t, values, attended_t, inv_sums, expos, w_qkv, w_out, gain, grad_norm2, grad_up, grad_down, hidden_out):
    rows, width = returned.shape
    toks = slot_row.shape[1]
    vm = pl.BlockSpec(memory_space=pltpu.VMEM)
    hbm = pl.BlockSpec(memory_space=pl.ANY)
    shape = jax.ShapeDtypeStruct
    wide = 4 * width + 128
    return pl.pallas_call(
        attention_back_kernel,
        out_shape=(
            shape((rows, width), low),
            shape((width, wide), low),
            shape(grad_up.shape, f32),
            shape(grad_down.shape, f32),
            shape(hidden_out.shape, low),
        ),
        in_specs=[hbm, vm, hbm, hbm, hbm, hbm, hbm, hbm, vm, hbm, hbm, hbm, vm, vm, hbm, hbm, hbm],
        out_specs=(hbm, hbm, hbm, hbm, hbm),
        scratch_shapes=[
            pltpu.VMEM((rows, width), low),
            pltpu.VMEM((width, toks), low),
            pltpu.VMEM((width, toks), low),
            pltpu.VMEM((width, toks), low),
            pltpu.VMEM((width, toks), low),
            pltpu.VMEM((toks, width), low),
            pltpu.VMEM((width, toks), low),
            pltpu.VMEM(w_qkv.shape, low),
            pltpu.VMEM(w_out.shape, low),
            pltpu.VMEM((HEADS, toks, toks), low),
            pltpu.VMEM((width, toks), low),
            pltpu.VMEM((toks, width), low),
            pltpu.VMEM((3 * width, toks), low),
            pltpu.VMEM((width, wide), low),
            pltpu.VMEM((rows, width), low),
            pltpu.VMEM((2, grad_up.shape[0] * 2 // HEADS, grad_up.shape[1]), f32),
            pltpu.VMEM((2, grad_down.shape[0] * 2 // HEADS, grad_down.shape[1]), f32),
            pltpu.VMEM((2, rows * 2 // HEADS, width), low),
            pltpu.SemaphoreType.DMA((9,)),
            pltpu.SemaphoreType.DMA((HEADS // 2,)),
            pltpu.SemaphoreType.DMA((7, 2)),
        ],
        compiler_params=pltpu.CompilerParams(has_side_effects=True, vmem_limit_bytes=60 * 1024 * 1024),
    )(returned, slot_row, attn_in_t, tokens_t, queries_t, keys_t, values, attended_t, inv_sums, expos, w_qkv, w_out, gain, grad_norm2, grad_up, grad_down, hidden_out)


def expert_kernel(
    n,
    cap,
    sent,
    grads,
    grads_pair,
    live,
    up_hbm,
    up_bias,
    down_hbm,
    down_bias,
    gain,
    bias,
    returned,
    hidden_out,
    grad_up,
    grad_down,
    grad_bup,
    grad_bdown,
    grad_norm,
    rows_in,
    ffn_in,
    grad_rows,
    up,
    down,
    act,
    pre_grad,
    pre_tile,
    hid_tile,
    part_out,
    part_in,
    back,
    tile,
    tile_down,
    sem_send,
    sem_recv,
    sem_back_send,
    sem_back_recv,
    sem_pair,
    sem_load,
    sem_store,
):
    me_d = lax.axis_index("dp")
    me_e = lax.axis_index("expert")
    rows = rows_in.shape[0]
    width = rows_in.shape[1]
    units = up.shape[1]
    block = rows // PARTS
    many = n // PARTS
    partner = (1 - me_d, me_e)

    def base_of(part):
        return pl.multiple_of(((me_e // many) ^ part) * block, block)

    def slot_copy(i):
        peer = me_e ^ i
        return pltpu.make_async_remote_copy(
            src_ref=sent.at[pl.ds(pl.multiple_of(peer * cap, cap), cap)],
            dst_ref=rows_in.at[pl.ds(pl.multiple_of(me_e * cap, cap), cap)],
            send_sem=sem_send.at[i],
            recv_sem=sem_recv.at[i],
            device_id=(me_d, peer),
            device_id_type=MESH_ID,
        )

    def own_slots():
        own = pl.ds(pl.multiple_of(me_e * cap, cap), cap)
        return pltpu.make_async_copy(sent.at[own], rows_in.at[own], sem_recv.at[0])

    def back_copy(i):
        peer = me_e ^ i
        return pltpu.make_async_remote_copy(
            src_ref=back.at[pl.ds(pl.multiple_of(peer * cap, cap), cap)],
            dst_ref=returned.at[pl.ds(pl.multiple_of(me_e * cap, cap), cap)],
            send_sem=sem_back_send.at[i],
            recv_sem=sem_back_recv.at[i],
            device_id=(me_d, peer),
            device_id_type=MESH_ID,
        )

    def own_back():
        own = pl.ds(pl.multiple_of(me_e * cap, cap), cap)
        return pltpu.make_async_copy(back.at[own], returned.at[own], sem_back_recv.at[0])

    def pair_copy(src, dst, kind, part):
        return pltpu.make_async_remote_copy(
            src_ref=src,
            dst_ref=dst,
            send_sem=sem_pair.at[kind - 1, 0, part],
            recv_sem=sem_pair.at[kind - 1, 1, part],
            device_id=partner,
            device_id_type=MESH_ID,
        )

    def ffn_pair(part):
        return pair_copy(
            ffn_in.at[part, pl.ds(0, block)], ffn_in.at[part, pl.ds(block, block)], 1, part
        )

    def part_pair(part):
        return pair_copy(part_out.at[part], part_in.at[part], 2, part)

    def out_pair(part):
        return pair_copy(part_out.at[PARTS + part], part_in.at[PARTS + part], 3, part)

    def grads_load(part, k):
        return pltpu.make_async_copy(
            (grads, grads_pair)[k].at[pl.ds(base_of(part), block)],
            grad_rows.at[part, pl.ds(k * block, block)],
            sem_load.at[2 + k * PARTS + part],
        )

    up_load = pltpu.make_async_copy(up_hbm, up, sem_load.at[0])
    down_load = pltpu.make_async_copy(down_hbm, down, sem_load.at[1])

    greet(me_d, me_e, n)
    own_slots().start()
    for part in range(PARTS):
        grads_load(part, 0).start()
        grads_load(part, 1).start()
    down_load.start()
    up_load.start()

    def start_slots(i, carry):
        slot_copy(i).start()
        return carry

    lax.fori_loop(1, n, start_slots, 0)
    grad_norm[...] = jnp.zeros_like(grad_norm)
    down_load.wait()
    up_load.wait()

    def stats(base):
        x = rows_in[pl.ds(base, block), :].astype(jnp.float32)
        return normalize(x)

    def work(part, carry):
        base = base_of(part)

        @pl.when(part == 0)
        def _():
            own_slots().wait()

        @pl.when(part > 0)
        def _():
            slot_copy(part * many).wait()

        def wait_slots(j, c):
            slot_copy(part * many + j).wait()
            return c

        lax.fori_loop(1, many, wait_slots, 0)
        normed, _ = stats(base)
        ffn_in[part, 0:block, :] = (normed * gain[...] + bias[...]).astype(jnp.bfloat16)
        ffn_pair(part).start()
        grads_load(part, 0).wait()
        grads_load(part, 1).wait()
        ffn_pair(part).wait()

        def hidden(f, c):
            cols = pl.ds(pl.multiple_of(f * UNITS, UNITS), UNITS)
            pre = mm(ffn_in[part], up[:, cols]) + up_bias[:, cols]
            hid = mm_nt(grad_rows[part], down[cols, :])
            a, slope = gelu_parts(pre)
            act[part, :, cols] = a.astype(jnp.bfloat16)
            pre_grad[part, :, cols] = (hid * slope).astype(jnp.bfloat16)
            return c

        lax.fori_loop(0, units // UNITS, hidden, 0)
        part_out[part] = mm_nt(pre_grad[part, block:, :], up[...]).astype(jnp.bfloat16)
        part_pair(part).start()
        mine = mm_nt(pre_grad[part, 0:block, :], up[...])
        part_pair(part).wait()
        grad_ffn = mine + part_in[part].astype(jnp.float32)
        normed, inv_std = stats(base)
        grad_norm[0:1, :] += jnp.sum(grad_ffn * normed, axis=0, keepdims=True)
        grad_norm[1:2, :] += jnp.sum(grad_ffn, axis=0, keepdims=True)
        result = grad_rows[part, 0:block, :].astype(jnp.float32) + norm_back(
            grad_ffn, normed, inv_std, gain[...]
        )
        back[pl.ds(base, block), :] = result.astype(jnp.bfloat16)

        @pl.when(part == 0)
        def _():
            own_back().start()

        @pl.when(part > 0)
        def _():
            back_copy(part * many).start()

        def start_back(j, c):
            back_copy(part * many + j).start()
            return c

        lax.fori_loop(1, many, start_back, 0)
        return carry

    lax.fori_loop(0, PARTS, work, 0)

    def output(part, carry):
        part_out[PARTS + part] = mm(act[part, block:, :], down[...]).astype(jnp.bfloat16)
        out_pair(part).start()
        return carry

    lax.fori_loop(0, PARTS, output, 0)

    def output_own(part, carry):
        base = base_of(part)
        here = pl.ds(base, block)
        mine = mm(act[part, 0:block, :], down[...])
        out_pair(part).wait()
        total = rows_in[here, :].astype(jnp.float32) + mine + part_in[PARTS + part].astype(jnp.float32) + down_bias[...]
        rows_in[here, :] = (total * live[here, :]).astype(jnp.bfloat16)
        pltpu.make_async_copy(rows_in.at[here], hidden_out.at[here], sem_store.at[part]).start()
        return carry

    lax.fori_loop(0, PARTS, output_own, 0)

    ones = jnp.ones((8, PARTS * 2 * block), jnp.bfloat16)
    all_act = act.reshape(PARTS * 2 * block, units)
    all_pre = pre_grad.reshape(PARTS * 2 * block, units)
    all_in = ffn_in.reshape(PARTS * 2 * block, width)
    all_grad = grad_rows.reshape(PARTS * 2 * block, width)
    grad_bup[...] = mm(ones, all_pre[...])
    grad_bdown[...] = mm(ones, all_grad[...])

    def up_store(f, slot):
        cols = pl.ds(pl.multiple_of(f * UNITS, UNITS), UNITS)
        return pltpu.make_async_copy(tile.at[slot], grad_up.at[:, cols], sem_store.at[PARTS + slot])

    def down_store(f, slot):
        cols = pl.ds(pl.multiple_of(f * UNITS, UNITS), UNITS)
        return pltpu.make_async_copy(
            tile_down.at[slot], grad_down.at[cols, :], sem_store.at[PARTS + 2 + slot]
        )

    def weights(f, carry):
        slot = lax.rem(f, 2)
        cols = pl.ds(pl.multiple_of(f * UNITS, UNITS), UNITS)

        @pl.when(f >= 2)
        def _():
            up_store(f, slot).wait()
            down_store(f, slot).wait()

        tile[slot] = mm_tn(all_in[...], all_pre[:, cols])
        up_store(f, slot).start()
        tile_down[slot] = mm_tn(all_act[:, cols], all_grad[...])
        down_store(f, slot).start()
        return carry

    lax.fori_loop(0, units // UNITS, weights, 0)
    for slot in range(2):
        up_store(0, slot).wait()
        down_store(0, slot).wait()
    for part in range(PARTS):
        pltpu.make_async_copy(
            rows_in.at[pl.ds(0, block)], hidden_out.at[pl.ds(0, block)], sem_store.at[part]
        ).wait()
    own_back().wait()

    def wait_back(i, carry):
        back_copy(i).wait()
        return carry

    lax.fori_loop(1, n, wait_back, 0)


def expert_block(sent, grads, grads_pair, live, up, up_bias, down, down_bias, gain, bias):
    n = lax.axis_size("expert")
    rows, width = sent.shape
    units = up.shape[1]
    cap = rows // n
    block = rows // PARTS
    vm = pl.BlockSpec(memory_space=pltpu.VMEM)
    hbm = pl.BlockSpec(memory_space=pl.ANY)
    return pl.pallas_call(
        functools.partial(expert_kernel, n, cap),
        out_shape=(
            jax.ShapeDtypeStruct((rows, width), low),
            jax.ShapeDtypeStruct((rows, width), low),
            jax.ShapeDtypeStruct((width, units), f32),
            jax.ShapeDtypeStruct((units, width), f32),
            jax.ShapeDtypeStruct((8, units), f32),
            jax.ShapeDtypeStruct((8, width), f32),
            jax.ShapeDtypeStruct((8, width), f32),
        ),
        in_specs=[hbm, hbm, hbm, vm, hbm, vm, hbm, vm, vm, vm],
        out_specs=(hbm, hbm, hbm, hbm, vm, vm, vm),
        scratch_shapes=[
            pltpu.VMEM((rows, width), low),
            pltpu.VMEM((PARTS, 2 * block, width), low),
            pltpu.VMEM((PARTS, 2 * block, width), low),
            pltpu.VMEM((width, units), low),
            pltpu.VMEM((units, width), low),
            pltpu.VMEM((PARTS, 2 * block, units), low),
            pltpu.VMEM((PARTS, 2 * block, units), low),
            pltpu.VMEM((2, 2 * block, UNITS), f32),
            pltpu.VMEM((2, 2 * block, UNITS), f32),
            pltpu.VMEM((2 * PARTS, block, width), low),
            pltpu.VMEM((2 * PARTS, block, width), low),
            pltpu.VMEM((rows, width), low),
            pltpu.VMEM((2, width, UNITS), f32),
            pltpu.VMEM((2, UNITS, width), f32),
            pltpu.SemaphoreType.DMA((n,)),
            pltpu.SemaphoreType.DMA((n,)),
            pltpu.SemaphoreType.DMA((n,)),
            pltpu.SemaphoreType.DMA((n,)),
            pltpu.SemaphoreType.DMA((3, 2, PARTS)),
            pltpu.SemaphoreType.DMA((2 + 2 * PARTS,)),
            pltpu.SemaphoreType.DMA((PARTS + 4,)),
        ],
        compiler_params=pltpu.CompilerParams(
            collective_id=1, has_side_effects=True, vmem_limit_bytes=60 * 1024 * 1024
        ),
    )(sent, grads, grads_pair, live, up, up_bias, down, down_bias, gain, bias)


STREAMS = 3


def ending_kernel(n, cap, sent, terms, grad_in, sums, own, total, landed, sem_send, sem_recv, sem_own, sem_pair, sem_step):
    me_d = lax.axis_index("dp")
    me_e = lax.axis_index("expert")
    partner = (1 - me_d, me_e)
    bits = n.bit_length() - 1
    half = n // 2
    wide = total.shape[-1]
    orders = []
    for s in range(STREAMS):
        first = s % bits
        orders.append([first] + [b for b in range(bits) if b != first])

    def cols(s):
        return pl.ds(s * wide, wide)

    def offset(s, p):
        k = 0
        for j, b in enumerate(orders[s]):
            k = k + lax.rem(p // (1 << (bits - 1 - j)), 2) * (1 << b)
        return k

    def slot_copy(i):
        peer = me_e ^ i
        return pltpu.make_async_remote_copy(
            src_ref=sent.at[pl.ds(pl.multiple_of(peer * cap, cap), cap)],
            dst_ref=grad_in.at[pl.ds(pl.multiple_of(me_e * cap, cap), cap)],
            send_sem=sem_send.at[i],
            recv_sem=sem_recv.at[i],
            device_id=(me_d, peer),
            device_id_type=MESH_ID,
        )

    def own_slots():
        here = pl.ds(pl.multiple_of(me_e * cap, cap), cap)
        return pltpu.make_async_copy(sent.at[here], grad_in.at[here], sem_recv.at[0])

    def pair_copy(s, p):
        return pltpu.make_async_remote_copy(
            src_ref=terms.at[(1 - me_d) * n + (me_e ^ offset(s, p)), :, cols(s)],
            dst_ref=landed.at[s, p],
            send_sem=sem_pair.at[0, s, p // half],
            recv_sem=sem_pair.at[1, s, p // half],
            device_id=partner,
            device_id_type=MESH_ID,
        )

    def pair_whole(s, q):
        here = landed.at[s, pl.ds(q * half, half)]
        return pltpu.make_async_remote_copy(
            src_ref=here,
            dst_ref=here,
            send_sem=sem_pair.at[0, s, q],
            recv_sem=sem_pair.at[1, s, q],
            device_id=partner,
            device_id_type=MESH_ID,
        )

    def step_copy(s, j):
        size = n >> (j + 1)
        start = n + sum(n >> (i + 1) for i in range(j))
        return (
            pltpu.make_async_remote_copy(
                src_ref=total.at[s, pl.ds(size, size)],
                dst_ref=landed.at[s, pl.ds(start, size)],
                send_sem=sem_step.at[0, s, j],
                recv_sem=sem_step.at[1, s, j],
                device_id=(me_d, me_e ^ (1 << orders[s][j])),
                device_id_type=MESH_ID,
            ),
            size,
            start,
        )

    greet(me_d, me_e, n)
    own_load = pltpu.make_async_copy(terms.at[pl.ds(me_d * n, n)], own, sem_own.at[0])
    own_load.start()
    own_slots().start()
    for q in (1, 0):
        for s in range(STREAMS):

            def start_pair(p, carry, s=s):
                pair_copy(s, p).start()
                return carry

            lax.fori_loop(q * half, q * half + half, start_pair, 0)

    def start_slots(i, carry):
        slot_copy(i).start()
        return carry

    lax.fori_loop(1, n, start_slots, 0)
    own_load.wait()
    for q in (1, 0):
        for s in range(STREAMS):
            pair_whole(s, q).wait()

            def add_pair(p, carry, s=s):
                mine = own[me_e ^ offset(s, p), :, cols(s)].astype(jnp.float32)
                total[s, p] = (mine + landed[s, p].astype(jnp.float32)).astype(jnp.bfloat16)
                return carry

            lax.fori_loop(q * half, q * half + half, add_pair, 0)
            if q == 1:
                step_copy(s, 0)[0].start()
    for j in range(bits):
        for s in range(STREAMS):
            copy, size, start = step_copy(s, j)
            copy.wait()
            if size > 1:

                def add_step(p, carry, s=s, start=start):
                    both = total[s, p].astype(jnp.float32) + landed[s, start + p].astype(jnp.float32)
                    total[s, p] = both.astype(jnp.bfloat16)
                    return carry

                lax.fori_loop(0, size, add_step, 0)
                step_copy(s, j + 1)[0].start()
            else:
                sums[:, cols(s)] = total[s, 0].astype(jnp.float32) + landed[s, start].astype(jnp.float32)
    own_slots().wait()

    def wait_slots(i, carry):
        slot_copy(i).wait()
        return carry

    lax.fori_loop(1, n, wait_slots, 0)


def ending(sent, terms):
    n = lax.axis_size("expert")
    rows, width = sent.shape
    owners, each, wide = terms.shape
    bits = n.bit_length() - 1
    hbm = pl.BlockSpec(memory_space=pl.ANY)
    return pl.pallas_call(
        functools.partial(ending_kernel, n, rows // n),
        out_shape=(
            jax.ShapeDtypeStruct((rows, width), low),
            jax.ShapeDtypeStruct((each, wide), jnp.float32),
        ),
        in_specs=[hbm, hbm],
        out_specs=(hbm, pl.BlockSpec(memory_space=pltpu.VMEM)),
        scratch_shapes=[
            pltpu.VMEM((n, each, wide), low),
            pltpu.VMEM((STREAMS, n, each, wide // STREAMS), low),
            pltpu.VMEM((STREAMS, 2 * n, each, wide // STREAMS), low),
            pltpu.SemaphoreType.DMA((n,)),
            pltpu.SemaphoreType.DMA((n,)),
            pltpu.SemaphoreType.DMA((1,)),
            pltpu.SemaphoreType.DMA((2, STREAMS, 2)),
            pltpu.SemaphoreType.DMA((2, STREAMS, bits)),
        ],
        compiler_params=pltpu.CompilerParams(
            collective_id=2, has_side_effects=True, vmem_limit_bytes=60 * 1024 * 1024
        ),
    )(sent, terms)


def on_device(
    hidden_in,
    buckets,
    expert_of_bucket,
    lengths,
    norm1_gain,
    norm1_bias,
    w_qkv,
    w_out,
    norm2_gain,
    norm2_bias,
    w_up,
    b_up,
    w_down,
    b_down,
    grad_out,
):
    width = hidden_in.shape[1]
    (
        sent,
        grads,
        grads_pair,
        live,
        attn_in_t,
        tokens_t,
        queries_t,
        keys_t,
        values,
        attended_t,
        inv_sums,
        slot_row,
        expos,
    ) = starting(
        hidden_in, grad_out, buckets, expert_of_bucket, lengths, norm1_gain[None], norm1_bias[None], w_qkv, w_out
    )
    returned, hidden_out, grad_up, grad_down, grad_bup, grad_bdown, grad_norm2 = expert_block(
        sent, grads, grads_pair, live, w_up[0], b_up, w_down[0], b_down, norm2_gain[None], norm2_bias[None]
    )
    sent_grad, terms, grad_up, grad_down, hidden_out = attention_back(
        returned,
        slot_row,
        attn_in_t,
        tokens_t,
        queries_t,
        keys_t,
        values,
        attended_t,
        inv_sums,
        expos,
        w_qkv,
        w_out,
        norm1_gain[:, None],
        grad_norm2,
        grad_up,
        grad_down,
        hidden_out,
    )
    owners = lax.axis_size("dp") * lax.axis_size("expert")
    grad_in, sums = ending(sent_grad, terms.reshape(owners, width // owners, terms.shape[1]))
    half = width // lax.axis_size("dp")
    return (
        hidden_out,
        grad_in,
        sums[:, : 3 * width],
        sums[:, 3 * width : 4 * width],
        sums[:, 4 * width],
        sums[:, 4 * width + 1],
        sums[:, 4 * width + 2],
        sums[:, 4 * width + 3],
        grad_up[None],
        grad_bup[0][None],
        grad_down[None],
        lax.dynamic_slice_in_dim(grad_bdown[0], lax.axis_index("dp") * half, half)[None],
    )


def solution(mesh):
    return jax.shard_map(
        on_device,
        mesh=mesh,
        in_specs=(
            P(("dp", "expert"), None),
            P(("dp", "expert"), None),
            P(),
            P(("dp", "expert"), None),
            P(),
            P(),
            P(),
            P(),
            P(),
            P(),
            P("expert", None, "dp"),
            P("expert", "dp"),
            P("expert", "dp", None),
            P("expert", None),
            P(("dp", "expert"), None),
        ),
        out_specs=(
            P(("dp", "expert"), None),
            P(("dp", "expert"), None),
            P(("dp", "expert"), None),
            P(("dp", "expert"), None),
            P(("dp", "expert")),
            P(("dp", "expert")),
            P(("dp", "expert")),
            P(("dp", "expert")),
            P("expert", None, "dp"),
            P("expert", "dp"),
            P("expert", "dp", None),
            P("expert", "dp"),
        ),
        check_vma=False,
    )
```

```python
import functools

import jax
import jax.numpy as jnp
from jax import lax
from jax.experimental import pallas as pl
from jax.experimental.pallas import tpu as pltpu
from jax.sharding import PartitionSpec as P

HEADS = 16
HEAD_DIM = 64


norm_eps = 1e-05
masked_score = -1e30
root_half = 0.7071067811865476
inv_root_tau = 0.3989422804014327

MESH_ID = pl.DeviceIdType.MESH
PARTS = 4
UNITS = 256
WIDE = 512
LANES = 128
MOVES = 8
QUERIES = 256
PAIR = 2 * HEAD_DIM
scale_val = HEAD_DIM ** (-0.5)
low = jnp.bfloat16
f32 = jnp.float32


def mm(a, b):
    return jnp.dot(a, b, preferred_element_type=f32)


def mm_nt(a, b):
    return lax.dot_general(a, b, (((1,), (1,)), ((), ())), preferred_element_type=f32)


def mm_tn(a, b):
    return lax.dot_general(a, b, (((0,), (0,)), ((), ())), preferred_element_type=f32)


def normalize(values, axis=-1):
    mean_val = jnp.mean(values, axis=axis, keepdims=True)
    centered = values - mean_val
    variance = jnp.mean(centered * centered, axis=axis, keepdims=True)
    inv_std = lax.rsqrt(variance + norm_eps)
    return (centered * inv_std, inv_std)


def norm_back(grad_normed, normed, inv_std, gain_vec, axis=-1):
    scaled = grad_normed * gain_vec
    mean_grad = jnp.mean(scaled, axis=axis, keepdims=True)
    mean_cross = jnp.mean(scaled * normed, axis=axis, keepdims=True)
    return inv_std * (scaled - mean_grad - normed * mean_cross)


def gelu_parts(pre):
    bell = jnp.exp(-0.5 * pre * pre)
    den = 1.0 + (0.3275911 * root_half) * jnp.abs(pre)
    t = pl.reciprocal(den, approx=True)
    t = t * (2.0 - den * t)
    tail = t * (
        0.5 * 0.254829592
        + t * (0.5 * -0.284496736 + t * (0.5 * 1.421413741 + t * (0.5 * -1.453152027 + t * (0.5 * 1.061405429))))
    )
    tail = tail * bell
    phi = jnp.where(pre >= 0.0, 1.0 - tail, tail)
    return pre * phi, phi + pre * (inv_root_tau * bell)


STREAMS = 3


def greet_peers(me_d, me_e, n):
    barrier = pltpu.get_barrier_semaphore()

    def signal(i, carry):
        pl.semaphore_signal(barrier, inc=1, device_id=(me_d, me_e ^ i), device_id_type=MESH_ID)
        return carry

    lax.fori_loop(1, n, signal, 0)


def greet_partner(me_d, me_e):
    pl.semaphore_signal(
        pltpu.get_barrier_semaphore(), inc=1, device_id=(1 - me_d, me_e), device_id_type=MESH_ID
    )


def greet(me_d, me_e, n):
    greet_peers(me_d, me_e, n)
    greet_partner(me_d, me_e)
    pl.semaphore_wait(pltpu.get_barrier_semaphore(), n)


def staged(units, *stages):
    held = [None] * len(units)
    for step in range(len(units) + len(stages) - 1):
        for k, stage in enumerate(stages):
            i = step - k
            if 0 <= i < len(units):
                held[i] = stage(units[i]) if k == 0 else stage(units[i], held[i])


def start_kernel(
    n,
    cap,
    hidden,
    grad_out,
    buckets,
    expert_of,
    lengths,
    gain,
    bias,
    w_qkv_hbm,
    w_out_hbm,
    down_hbm,
    sent,
    grads,
    grads_pair,
    hids,
    live,
    attn_in_hbm,
    tokens_hbm,
    queries_hbm,
    keys_hbm,
    values_hbm,
    attended_hbm,
    inv_sums,
    slot_row,
    expos,
    arrived,
    w_qkv,
    w_out,
    down,
    grad_v,
    grad_p,
    hid_v,
    attn_in_t,
    tokens_t,
    queries_t,
    keys_t,
    values,
    attended_t,
    proj,
    values_t,
    allow,
    tokens,
    expo_v,
    sent_v,
    counts_out,
    counts_in,
    sem_send,
    sem_recv,
    sem_count_send,
    sem_count_recv,
    sem_pair,
    sem_load,
    sem_store,
    sem_turn,
):
    me_d = lax.axis_index("dp")
    me_e = lax.axis_index("expert")
    partner = (1 - me_d, me_e)
    rows, width = arrived.shape
    toks = buckets.shape[1]
    lanes = counts_out.shape[1]

    def slot_copy(i):
        peer = me_e ^ i
        return pltpu.make_async_remote_copy(
            src_ref=hidden.at[pl.ds(pl.multiple_of(peer * cap, cap), cap)],
            dst_ref=arrived.at[pl.ds(pl.multiple_of(me_e * cap, cap), cap)],
            send_sem=sem_send.at[i],
            recv_sem=sem_recv.at[i],
            device_id=(me_d, peer),
            device_id_type=MESH_ID,
        )

    def own_slots():
        here = pl.ds(pl.multiple_of(me_e * cap, cap), cap)
        return pltpu.make_async_copy(hidden.at[here], arrived.at[here], sem_recv.at[0])

    def count_copy(i):
        return pltpu.make_async_remote_copy(
            src_ref=counts_out,
            dst_ref=counts_in.at[me_e],
            send_sem=sem_count_send.at[i],
            recv_sem=sem_count_recv.at[i],
            device_id=(me_d, me_e ^ i),
            device_id_type=MESH_ID,
        )

    grad_load = pltpu.make_async_copy(grad_out, grad_v, sem_load.at[0])
    qkv_load = pltpu.make_async_copy(w_qkv_hbm, w_qkv, sem_load.at[1])
    out_load = pltpu.make_async_copy(w_out_hbm, w_out, sem_load.at[2])
    down_load = pltpu.make_async_copy(down_hbm, down, sem_load.at[3])
    pair_grads_store = pltpu.make_async_copy(grad_p, grads_pair, sem_store.at[2])
    keep = [
        pltpu.make_async_copy(a, b, sem_store.at[3 + i])
        for i, (a, b) in enumerate(
            (
                (attn_in_t, attn_in_hbm),
                (tokens_t, tokens_hbm),
                (queries_t, queries_hbm),
                (keys_t, keys_hbm),
                (values, values_hbm),
                (attended_t, attended_hbm),
            )
        )
    ]

    def hid_store(k):
        return pltpu.make_async_copy(hid_v.at[k], hids.at[k], sem_store.at[9 + k])

    def hidden_grad(k, grad_ref):
        def tile(i, carry):
            here = pl.ds(pl.multiple_of((i // 2) * WIDE, WIDE), WIDE)
            some = pl.ds(pl.multiple_of(lax.rem(i, 2) * (rows // 2), rows // 2), rows // 2)
            hid_v[k, some, here] = mm_nt(grad_ref[some, :], down[here, :]).astype(low)
            return carry

        lax.fori_loop(0, 2 * (down.shape[0] // WIDE), tile, 0)
        hid_store(k).start()

    grad_store = pltpu.make_async_copy(grad_v, grads, sem_store.at[0])
    grad_pair = pltpu.make_async_remote_copy(
        src_ref=grad_v,
        dst_ref=grad_p,
        send_sem=sem_pair.at[0],
        recv_sem=sem_pair.at[1],
        device_id=partner,
        device_id_type=MESH_ID,
    )

    def start_slots(i, carry):
        slot_copy(i).start()
        return carry

    grad_load.start()
    down_load.start()
    greet(me_d, me_e, n)

    @pl.when(me_d == 0)
    def _():
        lax.fori_loop(n // 2, n, start_slots, 0)

    lax.fori_loop(1, n // 2, start_slots, 0)
    own_slots().start()
    qkv_load.start()
    out_load.start()

    lane_ids = lax.broadcasted_iota(jnp.int32, (toks, lanes), 1)
    bucket = jnp.broadcast_to(buckets[...], (lanes, toks)).T[:, 0:n]
    bucket_hot = (bucket == lane_ids[:, 0:n]).astype(f32).astype(low)
    serves_t = (expert_of[...] == lax.broadcasted_iota(jnp.int32, (lanes, n), 0)).astype(f32).astype(low)
    expert_hot = mm_nt(bucket_hot, serves_t)
    row_ids = lax.broadcasted_iota(jnp.int32, (toks, toks), 0)
    col_ids = lax.broadcasted_iota(jnp.int32, (toks, toks), 1)
    earlier = (col_ids < row_ids).astype(f32).astype(low)
    before = mm(earlier, expert_hot.astype(low))
    slot = jnp.sum(expert_hot * (before + (lane_ids * cap).astype(f32)), axis=1, keepdims=True)
    counts_out[...] = jnp.broadcast_to(jnp.sum(expert_hot, axis=0, keepdims=True), counts_out.shape)
    counts_in[me_e] = counts_out[...]

    def start_counts(i, carry):
        count_copy(i).start()
        return carry

    lax.fori_loop(1, n, start_counts, 0)
    slot_row[...] = jnp.broadcast_to(slot, (toks, lanes)).T[0:8, :].astype(jnp.int32)
    ends = jnp.zeros((1, toks), jnp.int32)
    begin = jnp.zeros((1, toks), jnp.int32)
    places = lax.broadcasted_iota(jnp.int32, (1, toks), 1)
    for s in range(lengths.shape[1]):
        ends = ends + lengths[0:1, s : s + 1]
        begin = jnp.where(places >= ends, ends, begin)
    allow[...] = jnp.where(jnp.logical_and(row_ids <= col_ids, row_ids >= begin), 0.0, masked_score)

    def wait_counts(i, carry):
        count_copy(i).wait()
        return carry

    lax.fori_loop(1, n, wait_counts, 0)
    grad_load.wait()

    def mark(s, carry):
        here = pl.ds(pl.multiple_of(s * cap, cap), cap)
        mine = lax.broadcasted_iota(jnp.int32, (1, lanes), 1) == me_e
        count = jnp.sum(jnp.where(mine, counts_in[s, 0:1, :], 0.0), axis=1, keepdims=True)
        taken = (lax.broadcasted_iota(jnp.int32, (cap, 1), 0).astype(f32) < count).astype(f32)
        live[here, :] = taken
        grad_v[here, :] = (grad_v[here, :].astype(f32) * taken).astype(low)
        return carry

    lax.fori_loop(0, n, mark, 0)
    grad_store.start()
    grad_pair.start()
    @pl.when(me_d == 0)
    def _():
        def wait_sent(i, carry):
            slot_copy(i).wait_send()
            return carry

        lax.fori_loop(n // 2, n, wait_sent, 0)
        pl.semaphore_signal(sem_turn, inc=1, device_id=partner, device_id_type=MESH_ID)

    @pl.when(me_d == 1)
    def _():
        pl.semaphore_wait(sem_turn, 1)
        lax.fori_loop(n // 2, n, start_slots, 0)

    down_load.wait()
    hidden_grad(0, grad_v)
    grad_pair.wait()
    pair_grads_store.start()
    hidden_grad(1, grad_p)

    own_slots().wait()

    def wait_slots(i, carry):
        slot_copy(i).wait_recv()
        return carry

    lax.fori_loop(1, n, wait_slots, 0)

    pick = (slot.astype(jnp.int32) == lax.broadcasted_iota(jnp.int32, (toks, rows), 1)).astype(f32).astype(low)
    tokens[...] = mm(pick, arrived[...])
    normed, _ = normalize(tokens[...])
    attn_in = (normed * gain[...] + bias[...]).astype(low)
    tokens_t[...] = tokens[...].T.astype(low)
    keep[1].start()
    attn_in_t[...] = attn_in.T
    keep[0].start()
    qkv_load.wait()
    step = width // 4
    for c in range(3 * width // step):
        here = slice(c * step, (c + 1) * step)
        part = mm(attn_in, w_qkv[:, here])
        if c * step < width:
            part = part.astype(low).astype(f32) * scale_val
        proj[:, here] = part.astype(low)
    values_t[...] = proj[:, 2 * width : 3 * width].T

    def expo_store(g):
        here = pl.ds(pl.multiple_of(4 * g, 4), 4)
        return pltpu.make_async_copy(expo_v.at[here], expos.at[here], sem_store.at[11 + g])

    in_first = lax.broadcasted_iota(jnp.int32, (1, PAIR), 1) < HEAD_DIM

    def head_group(g, carry):
        units = [
            (2 * g + pair, h, q) for pair in range(2) for h in range(2) for q in range(toks // QUERIES)
        ]

        def score(unit):
            p, h, q = unit
            first = pl.multiple_of(p * PAIR, PAIR)
            upto = (q + 1) * QUERIES
            here = slice(q * QUERIES, upto)
            mine = in_first if h == 0 else jnp.logical_not(in_first)
            query = jnp.where(mine, proj[here, pl.ds(first, PAIR)], jnp.zeros((), low))
            scores = mm_nt(proj[0:upto, pl.ds(pl.multiple_of(width + first, PAIR), PAIR)], query)
            return scores + allow[0:upto, here]

        def soft(unit, scores):
            expo = jnp.exp(scores - jnp.max(scores, axis=0, keepdims=True))
            inv = 1.0 / jnp.sum(expo, axis=0, keepdims=True)
            return expo.astype(low), inv

        def attend(unit, held):
            p, h, q = unit
            expo, inv = held
            upto = (q + 1) * QUERIES
            here = slice(q * QUERIES, upto)
            head_rows = pl.ds(pl.multiple_of(p * PAIR + h * HEAD_DIM, HEAD_DIM), HEAD_DIM)
            expo_v[2 * p + h, 0:upto, here] = expo
            if upto < toks:
                expo_v[2 * p + h, upto:toks, here] = jnp.zeros((toks - upto, QUERIES), low)
            out = mm(values_t[head_rows, 0:upto], expo)
            attended_t[head_rows, here] = (out * inv).astype(low)
            inv_sums[2 * p + h, :, here] = jnp.broadcast_to(inv, (8, QUERIES))

        staged(units, score, soft, attend)
        expo_store(g).start()
        return carry

    lax.fori_loop(0, HEADS // 4, head_group, 0)
    queries_t[...] = proj[:, 0:width].T
    keys_t[...] = proj[:, width : 2 * width].T
    values[...] = proj[:, 2 * width : 3 * width]
    for i in range(2, 6):
        keep[i].start()
    out_load.wait()
    residual = (tokens[...] + mm_tn(attended_t[...], w_out[...])).astype(low)
    place = (slot_row[0:1, :] == lax.broadcasted_iota(jnp.int32, (rows, toks), 0)).astype(f32).astype(low)
    sent_v[...] = mm(place, residual).astype(low)
    sent_store = pltpu.make_async_copy(sent_v, sent, sem_store.at[1])
    sent_store.start()

    for g in range(HEADS // 4):
        expo_store(g).wait()
    for copy in keep:
        copy.wait()
    grad_store.wait()
    pair_grads_store.wait()
    hid_store(0).wait()
    hid_store(1).wait()

    def wait_sent(i, carry):
        slot_copy(i).wait_send()
        return carry

    lax.fori_loop(1, n // 2, wait_sent, 0)

    @pl.when(me_d == 1)
    def _():
        lax.fori_loop(n // 2, n, wait_sent, 0)

    sent_store.wait()


def starting(hidden, grad_out, buckets, expert_of, lengths, gain, bias, w_qkv, w_out, down):
    n = lax.axis_size("expert")
    rows, width = hidden.shape
    toks = buckets.shape[1]
    units = down.shape[0]
    lanes = 128
    vm = pl.BlockSpec(memory_space=pltpu.VMEM)
    hbm = pl.BlockSpec(memory_space=pl.ANY)
    shape = jax.ShapeDtypeStruct
    return pl.pallas_call(
        functools.partial(start_kernel, n, rows // n),
        out_shape=(
            shape((rows, width), low),
            shape((rows, width), low),
            shape((rows, width), low),
            shape((2, rows, units), low),
            shape((rows, 1), f32),
            shape((width, toks), low),
            shape((width, toks), low),
            shape((width, toks), low),
            shape((width, toks), low),
            shape((toks, width), low),
            shape((width, toks), low),
            shape((HEADS, 8, toks), f32),
            shape((8, toks), jnp.int32),
            shape((HEADS, toks, toks), low),
        ),
        in_specs=[hbm, hbm, vm, vm, vm, vm, vm, hbm, hbm, hbm],
        out_specs=(hbm, hbm, hbm, hbm, vm, hbm, hbm, hbm, hbm, hbm, hbm, vm, vm, hbm),
        scratch_shapes=[
            pltpu.VMEM((rows, width), low),
            pltpu.VMEM(w_qkv.shape, low),
            pltpu.VMEM(w_out.shape, low),
            pltpu.VMEM(down.shape, low),
            pltpu.VMEM((rows, width), low),
            pltpu.VMEM((rows, width), low),
            pltpu.VMEM((2, rows, units), low),
            pltpu.VMEM((width, toks), low),
            pltpu.VMEM((width, toks), low),
            pltpu.VMEM((width, toks), low),
            pltpu.VMEM((width, toks), low),
            pltpu.VMEM((toks, width), low),
            pltpu.VMEM((width, toks), low),
            pltpu.VMEM((toks, 3 * width), low),
            pltpu.VMEM((width, toks), low),
            pltpu.VMEM((toks, toks), f32),
            pltpu.VMEM((toks, width), f32),
            pltpu.VMEM((HEADS, toks, toks), low),
            pltpu.VMEM((rows, width), low),
            pltpu.VMEM((8, lanes), f32),
            pltpu.VMEM((n, 8, lanes), f32),
            pltpu.SemaphoreType.DMA((n,)),
            pltpu.SemaphoreType.DMA((n,)),
            pltpu.SemaphoreType.DMA((n,)),
            pltpu.SemaphoreType.DMA((n,)),
            pltpu.SemaphoreType.DMA((2,)),
            pltpu.SemaphoreType.DMA((4,)),
            pltpu.SemaphoreType.DMA((11 + HEADS // 4,)),
            pltpu.SemaphoreType.REGULAR,
        ],
        compiler_params=pltpu.CompilerParams(
            collective_id=3, has_side_effects=True, vmem_limit_bytes=60 * 1024 * 1024
        ),
    )(hidden, grad_out, buckets, expert_of, lengths, gain, bias, w_qkv, w_out, down)


def attention_back_kernel(
    returned_hbm,
    slot_row,
    tokens_hbm,
    queries_hbm,
    keys_hbm,
    values_hbm,
    attended_hbm,
    inv_sums,
    expos,
    w_qkv_hbm,
    w_out_hbm,
    gain,
    grad_norm2,
    grad_bup_in,
    grad_bdown_in,
    grad_up_in,
    grad_down_in,
    hidden_in,
    sent,
    grad_h_hbm,
    grad_proj_hbm,
    norm_terms,
    grad_bup,
    grad_bdown,
    grad_up,
    grad_down,
    hidden_out,
    returned,
    tokens_t,
    queries_t,
    keys_t,
    values,
    attended_t,
    w_qkv,
    w_out,
    expo_v,
    grad_att_t,
    grad_h,
    grad_proj_t,
    sent_v,
    held_up,
    held_down,
    held_out,
    sem_load,
    sem_expo,
    sem_store,
    sem_move,
):
    rows, width = returned.shape
    toks = slot_row.shape[1]
    loads = [
        pltpu.make_async_copy(a, b, sem_load.at[i])
        for i, (a, b) in enumerate(
            (
                (returned_hbm, returned),
                (w_out_hbm, w_out),
                (attended_hbm, attended_t),
                (values_hbm, values),
                (keys_hbm, keys_t),
                (queries_hbm, queries_t),
                (w_qkv_hbm, w_qkv),
                (tokens_hbm, tokens_t),
            )
        )
    ]

    def move(k, p, store):
        source, target, held = (
            (grad_up_in, grad_up, held_up),
            (grad_down_in, grad_down, held_down),
            (hidden_in, hidden_out, held_out),
        )[k]
        size = held.shape[1]
        here = pl.ds(pl.multiple_of(p * size, size), size)
        slot = lax.rem(p, 2)
        if store:
            return pltpu.make_async_copy(held.at[slot], target.at[here], sem_move.at[3 + k, slot])
        return pltpu.make_async_copy(source.at[here], held.at[slot], sem_move.at[k, slot])

    def tick(p):
        for k in range(3):
            move(k, p, False).wait()
            move(k, p, True).start()

        @pl.when(p > 0)
        def _():
            for k in range(3):
                move(k, p - 1, True).wait()

        @pl.when(p < MOVES - 1)
        def _():
            for k in range(3):
                move(k, p + 1, False).start()

    def expo_load(g):
        here = pl.ds(pl.multiple_of(4 * g, 4), 4)
        return pltpu.make_async_copy(expos.at[here], expo_v.at[here], sem_expo.at[g])

    for i in range(6):
        loads[i].start()
    for g in range(HEADS // 4):
        expo_load(g).start()
    for k in range(3):
        move(k, 0, False).start()
    for i in range(6, len(loads)):
        loads[i].start()
    grad_bup[...] = grad_bup_in[...]
    part = grad_bdown.shape[1]
    first_half = lax.axis_index("dp") == 0
    grad_bdown[...] = jnp.where(first_half, grad_bdown_in[:, 0:part], grad_bdown_in[:, part : 2 * part])
    place = (slot_row[0:1, :] == lax.broadcasted_iota(jnp.int32, (rows, toks), 0)).astype(f32).astype(low)
    loads[0].wait()
    grad_h[...] = mm_tn(place, returned[...]).astype(low)
    grad_h_store = pltpu.make_async_copy(grad_h, grad_h_hbm, sem_store.at[0])
    grad_h_store.start()
    tick(0)
    loads[1].wait()
    grad_att_t[...] = mm_nt(w_out[...], grad_h[...]).astype(low)
    tick(1)
    for i in range(2, 6):
        loads[i].wait()
    in_first = lax.broadcasted_iota(jnp.int32, (1, PAIR), 1) < HEAD_DIM

    def head_group(g, carry):
        expo_load(g).wait()
        ready = {}
        sums = {}
        for pair in range(2):
            p = 2 * g + pair
            pair_rows = pl.ds(pl.multiple_of(p * PAIR, PAIR), PAIR)
            inv_pair = jnp.concatenate(
                [jnp.broadcast_to(inv_sums[2 * p + h, 0:1, :], (HEAD_DIM, toks)) for h in range(2)], axis=0
            )
            grad_pair = grad_att_t[pair_rows, :].astype(f32)
            cross = grad_pair * attended_t[pair_rows, :].astype(f32) * inv_pair
            scaled = (grad_pair * inv_pair).astype(low)
            for h in range(2):
                in_pair = slice(h * HEAD_DIM, (h + 1) * HEAD_DIM)
                ready[pair, h] = (jnp.sum(cross[in_pair], axis=0, keepdims=True), scaled)
        units = [
            (pair, h, q) for pair in range(2) for h in range(2) for q in reversed(range(toks // QUERIES))
        ]

        def probs_back(unit):
            pair, h, q = unit
            upto = (q + 1) * QUERIES
            here = slice(q * QUERIES, upto)
            first = pl.multiple_of((2 * g + pair) * PAIR, PAIR)
            mine = in_first if h == 0 else jnp.logical_not(in_first)
            value = jnp.where(mine, values[0:upto, pl.ds(first, PAIR)], jnp.zeros((), low))
            return mm(value, ready[pair, h][1][:, here])

        def scores_back(unit, grad_prob):
            pair, h, q = unit
            upto = (q + 1) * QUERIES
            here = slice(q * QUERIES, upto)
            expo = expo_v[4 * g + 2 * pair + h, 0:upto, here]
            return expo, (expo.astype(f32) * (grad_prob - ready[pair, h][0][:, here])).astype(low)

        def heads_back(unit, held):
            pair, h, q = unit
            expo, grad_score = held
            upto = (q + 1) * QUERIES
            here = slice(q * QUERIES, upto)
            first = pl.multiple_of((2 * g + pair) * PAIR + h * HEAD_DIM, HEAD_DIM)
            head_rows = pl.ds(first, HEAD_DIM)
            key_rows = pl.ds(pl.multiple_of(width + first, HEAD_DIM), HEAD_DIM)
            value_rows = pl.ds(pl.multiple_of(2 * width + first, HEAD_DIM), HEAD_DIM)
            grad_proj_t[head_rows, here] = (mm(keys_t[head_rows, 0:upto], grad_score) * scale_val).astype(low)
            key_term = mm_nt(queries_t[head_rows, here], grad_score)
            value_term = mm_nt(ready[pair, h][1][h * HEAD_DIM : (h + 1) * HEAD_DIM, here], expo)
            if upto < toks:
                key_more, value_more = sums[pair, h]
                key_term = jnp.concatenate([key_more[:, 0:upto] + key_term, key_more[:, upto:]], axis=1)
                value_term = jnp.concatenate([value_more[:, 0:upto] + value_term, value_more[:, upto:]], axis=1)
            sums[pair, h] = (key_term, value_term)
            if q == 0:
                grad_proj_t[key_rows, :] = key_term.astype(low)
                grad_proj_t[value_rows, :] = value_term.astype(low)

        staged(units, probs_back, scores_back, heads_back)
        tick(2 + g)
        return carry

    lax.fori_loop(0, HEADS // 4, head_group, 0)
    grad_proj_store = pltpu.make_async_copy(grad_proj_t, grad_proj_hbm, sem_store.at[1])
    grad_proj_store.start()
    for i in range(6, len(loads)):
        loads[i].wait()
    grad_attn_t = mm(w_qkv[...], grad_proj_t[...])
    tick(6)
    normed_t, inv_std = normalize(tokens_t[...].astype(f32), axis=0)
    gain_col = jnp.broadcast_to(gain[...], (LANES, width)).T[:, 0:1]
    norm_terms[...] = jnp.concatenate(
        [
            jnp.sum(grad_attn_t * normed_t, axis=1, keepdims=True),
            jnp.sum(grad_attn_t, axis=1, keepdims=True),
            grad_norm2[...].T[:, 0:2],
            jnp.zeros((width, LANES - 4), f32),
        ],
        axis=1,
    )
    result = grad_h[...].astype(f32).T + norm_back(grad_attn_t, normed_t, inv_std, gain_col, axis=0)
    sent_v[...] = mm_nt(place, result.astype(low)).astype(low)
    sent_store = pltpu.make_async_copy(sent_v, sent, sem_store.at[2])
    sent_store.start()
    tick(7)
    for k in range(3):
        move(k, MOVES - 1, True).wait()
    grad_h_store.wait()
    grad_proj_store.wait()
    sent_store.wait()


def attention_back(returned, slot_row, tokens_t, queries_t, keys_t, values, attended_t, inv_sums, expos, w_qkv, w_out, gain, grad_norm2, grad_bup, grad_bdown, grad_up, grad_down, hidden_out):
    rows, width = returned.shape
    toks = slot_row.shape[1]
    vm = pl.BlockSpec(memory_space=pltpu.VMEM)
    hbm = pl.BlockSpec(memory_space=pl.ANY)
    shape = jax.ShapeDtypeStruct
    return pl.pallas_call(
        attention_back_kernel,
        out_shape=(
            shape((rows, width), low),
            shape((toks, width), low),
            shape((3 * width, toks), low),
            shape((width, LANES), f32),
            shape(grad_bup.shape, f32),
            shape((1, width // lax.axis_size("dp")), f32),
            shape(grad_up.shape, f32),
            shape(grad_down.shape, f32),
            shape(hidden_out.shape, low),
        ),
        in_specs=[hbm, vm, hbm, hbm, hbm, hbm, hbm, vm, hbm, hbm, hbm, vm, vm, vm, vm, hbm, hbm, hbm],
        out_specs=(hbm, hbm, hbm, vm, vm, vm, hbm, hbm, hbm),
        scratch_shapes=[
            pltpu.VMEM((rows, width), low),
            pltpu.VMEM((width, toks), low),
            pltpu.VMEM((width, toks), low),
            pltpu.VMEM((width, toks), low),
            pltpu.VMEM((toks, width), low),
            pltpu.VMEM((width, toks), low),
            pltpu.VMEM(w_qkv.shape, low),
            pltpu.VMEM(w_out.shape, low),
            pltpu.VMEM((HEADS, toks, toks), low),
            pltpu.VMEM((width, toks), low),
            pltpu.VMEM((toks, width), low),
            pltpu.VMEM((3 * width, toks), low),
            pltpu.VMEM((rows, width), low),
            pltpu.VMEM((2, grad_up.shape[0] // MOVES, grad_up.shape[1]), f32),
            pltpu.VMEM((2, grad_down.shape[0] // MOVES, grad_down.shape[1]), f32),
            pltpu.VMEM((2, rows // MOVES, width), low),
            pltpu.SemaphoreType.DMA((8,)),
            pltpu.SemaphoreType.DMA((HEADS // 4,)),
            pltpu.SemaphoreType.DMA((3,)),
            pltpu.SemaphoreType.DMA((6, 2)),
        ],
        compiler_params=pltpu.CompilerParams(has_side_effects=True, vmem_limit_bytes=60 * 1024 * 1024),
    )(returned, slot_row, tokens_t, queries_t, keys_t, values, attended_t, inv_sums, expos, w_qkv, w_out, gain, grad_norm2, grad_bup, grad_bdown, grad_up, grad_down, hidden_out)


def expert_kernel(
    n,
    cap,
    sent,
    grads,
    grads_pair,
    hids,
    live,
    up_hbm,
    up_bias,
    down_hbm,
    down_bias,
    gain,
    bias,
    returned,
    hidden_out,
    grad_up,
    grad_down,
    grad_bup,
    grad_bdown,
    grad_norm,
    rows_in,
    ffn_in,
    grad_rows,
    up,
    down,
    act,
    pre_grad,
    part_out,
    part_in,
    back,
    tile,
    tile_down,
    sem_send,
    sem_recv,
    sem_back_send,
    sem_back_recv,
    sem_pair,
    sem_load,
    sem_store,
):
    me_d = lax.axis_index("dp")
    me_e = lax.axis_index("expert")
    rows = rows_in.shape[0]
    width = rows_in.shape[1]
    units = up.shape[1]
    block = rows // PARTS
    many = n // PARTS
    partner = (1 - me_d, me_e)

    def base_of(part):
        return pl.multiple_of(((me_e // many) ^ part) * block, block)

    def slot_copy(i):
        peer = me_e ^ i
        return pltpu.make_async_remote_copy(
            src_ref=sent.at[pl.ds(pl.multiple_of(peer * cap, cap), cap)],
            dst_ref=rows_in.at[pl.ds(pl.multiple_of(me_e * cap, cap), cap)],
            send_sem=sem_send.at[i],
            recv_sem=sem_recv.at[i],
            device_id=(me_d, peer),
            device_id_type=MESH_ID,
        )

    def own_slots():
        own = pl.ds(pl.multiple_of(me_e * cap, cap), cap)
        return pltpu.make_async_copy(sent.at[own], rows_in.at[own], sem_recv.at[0])

    def back_copy(i):
        peer = me_e ^ i
        return pltpu.make_async_remote_copy(
            src_ref=back.at[pl.ds(pl.multiple_of(peer * cap, cap), cap)],
            dst_ref=returned.at[pl.ds(pl.multiple_of(me_e * cap, cap), cap)],
            send_sem=sem_back_send.at[i],
            recv_sem=sem_back_recv.at[i],
            device_id=(me_d, peer),
            device_id_type=MESH_ID,
        )

    def own_back():
        own = pl.ds(pl.multiple_of(me_e * cap, cap), cap)
        return pltpu.make_async_copy(back.at[own], returned.at[own], sem_back_recv.at[0])

    def pair_copy(src, dst, kind, part):
        return pltpu.make_async_remote_copy(
            src_ref=src,
            dst_ref=dst,
            send_sem=sem_pair.at[kind - 1, 0, part],
            recv_sem=sem_pair.at[kind - 1, 1, part],
            device_id=partner,
            device_id_type=MESH_ID,
        )

    def ffn_pair(part):
        return pair_copy(
            ffn_in.at[part, pl.ds(0, block)], ffn_in.at[part, pl.ds(block, block)], 1, part
        )

    def part_pair(part):
        return pair_copy(part_out.at[part], part_in.at[part], 2, part)

    def out_pair(part):
        return pair_copy(part_out.at[PARTS + part], part_in.at[PARTS + part], 3, part)

    def grads_load(part, k):
        return pltpu.make_async_copy(
            (grads, grads_pair)[k].at[pl.ds(base_of(part), block)],
            grad_rows.at[part, pl.ds(k * block, block)],
            sem_load.at[2 + k * PARTS + part],
        )

    up_load = pltpu.make_async_copy(up_hbm, up, sem_load.at[0])
    down_load = pltpu.make_async_copy(down_hbm, down, sem_load.at[1])

    def hid_load(part, k):
        return pltpu.make_async_copy(
            hids.at[k, pl.ds(base_of(part), block)],
            pre_grad.at[part, pl.ds(k * block, block)],
            sem_load.at[2 + (2 + k) * PARTS + part],
        )

    up_load.start()
    for part in range(PARTS):
        for k in range(2):
            hid_load(part, k).start()
            grads_load(part, k).start()
    down_load.start()
    own_slots().start()
    barrier = pltpu.get_barrier_semaphore()
    greet_peers(me_d, me_e, n)

    @pl.when(me_d == 0)
    def _():
        pl.semaphore_wait(barrier, n - 1)
        greet_partner(me_d, me_e)

    @pl.when(me_d == 1)
    def _():
        pl.semaphore_wait(barrier, n)
        greet_partner(me_d, me_e)

    def start_slots(i, carry):
        slot_copy(i).start()
        return carry

    lax.fori_loop(1, n, start_slots, 0)
    grad_norm[...] = jnp.zeros_like(grad_norm)
    up_load.wait()
    down_load.wait()

    @pl.when(me_d == 0)
    def _():
        pl.semaphore_wait(barrier, 1)

    def stats(base):
        x = rows_in[pl.ds(base, block), :].astype(f32)
        return normalize(x)

    def work(part, carry):
        base = base_of(part)

        @pl.when(part == 0)
        def _():
            own_slots().wait()

        @pl.when(part > 0)
        def _():
            slot_copy(part * many).wait()

        def wait_slots(j, c):
            slot_copy(part * many + j).wait()
            return c

        lax.fori_loop(1, many, wait_slots, 0)
        normed, _ = stats(base)
        ffn_in[part, 0:block, :] = (normed * gain[...] + bias[...]).astype(low)
        ffn_pair(part).start()
        for k in range(2):
            hid_load(part, k).wait()
            grads_load(part, k).wait()
        tiles = [pl.ds(f * WIDE, WIDE) for f in range(units // WIDE)]

        def hidden(k):
            some = pl.ds(k * block, block)

            def before(cols):
                return mm(ffn_in[part, some, :], up[:, cols]) + up_bias[:, cols]

            def after(cols, pre):
                a, slope = gelu_parts(pre)
                act[part, some, cols] = a.astype(low)
                pre_grad[part, some, cols] = (pre_grad[part, some, cols].astype(f32) * slope).astype(low)

            staged(tiles, before, after)

        hidden(0)
        ffn_pair(part).wait()
        hidden(1)
        part_out[part] = mm_nt(pre_grad[part, block:, :], up[...]).astype(low)
        part_pair(part).start()
        mine = mm_nt(pre_grad[part, 0:block, :], up[...])
        part_out[PARTS + part] = mm(act[part, block:, :], down[...]).astype(low)
        out_pair(part).start()
        part_pair(part).wait()
        grad_ffn = mine + part_in[part].astype(f32)
        normed, inv_std = stats(base)
        grad_norm[0:1, :] += jnp.sum(grad_ffn * normed, axis=0, keepdims=True)
        grad_norm[1:2, :] += jnp.sum(grad_ffn, axis=0, keepdims=True)
        result = grad_rows[part, 0:block, :].astype(f32) + norm_back(
            grad_ffn, normed, inv_std, gain[...]
        )
        back[pl.ds(base, block), :] = result.astype(low)

        @pl.when(part == 0)
        def _():
            own_back().start()

        @pl.when(part > 0)
        def _():
            back_copy(part * many).start()

        def start_back(j, c):
            back_copy(part * many + j).start()
            return c

        lax.fori_loop(1, many, start_back, 0)
        return carry

    lax.fori_loop(0, PARTS, work, 0)

    def output_own(part, carry):
        base = base_of(part)
        here = pl.ds(base, block)
        mine = mm(act[part, 0:block, :], down[...])
        out_pair(part).wait()
        total = rows_in[here, :].astype(f32) + mine + part_in[PARTS + part].astype(f32) + down_bias[...]
        rows_in[here, :] = (total * live[here, :]).astype(low)
        pltpu.make_async_copy(rows_in.at[here], hidden_out.at[here], sem_store.at[part]).start()
        return carry

    lax.fori_loop(0, PARTS, output_own, 0)

    ones = jnp.ones((8, PARTS * 2 * block), low)
    all_act = act.reshape(PARTS * 2 * block, units)
    all_pre = pre_grad.reshape(PARTS * 2 * block, units)
    all_in = ffn_in.reshape(PARTS * 2 * block, width)
    all_grad = grad_rows.reshape(PARTS * 2 * block, width)
    grad_bup[...] = mm(ones, all_pre[...])[0:1]
    grad_bdown[...] = mm(ones, all_grad[...])[0:1]

    def up_store(f, slot):
        cols = pl.ds(pl.multiple_of(f * UNITS, UNITS), UNITS)
        return pltpu.make_async_copy(tile.at[slot], grad_up.at[:, cols], sem_store.at[PARTS + slot])

    def down_store(f, slot):
        cols = pl.ds(pl.multiple_of(f * UNITS, UNITS), UNITS)
        return pltpu.make_async_copy(
            tile_down.at[slot], grad_down.at[cols, :], sem_store.at[PARTS + 2 + slot]
        )

    def weights(f, carry):
        slot = lax.rem(f, 2)
        cols = pl.ds(pl.multiple_of(f * UNITS, UNITS), UNITS)

        @pl.when(f >= 2)
        def _():
            up_store(f, slot).wait()
            down_store(f, slot).wait()

        tile[slot] = mm_tn(all_in[...], all_pre[:, cols])
        up_store(f, slot).start()
        tile_down[slot] = mm_tn(all_act[:, cols], all_grad[...])
        down_store(f, slot).start()
        return carry

    lax.fori_loop(0, units // UNITS, weights, 0)
    for slot in range(2):
        up_store(0, slot).wait()
        down_store(0, slot).wait()
    for part in range(PARTS):
        pltpu.make_async_copy(
            rows_in.at[pl.ds(0, block)], hidden_out.at[pl.ds(0, block)], sem_store.at[part]
        ).wait()
    own_back().wait()

    def wait_back(i, carry):
        back_copy(i).wait()
        return carry

    lax.fori_loop(1, n, wait_back, 0)


def expert_block(sent, grads, grads_pair, hids, live, up, up_bias, down, down_bias, gain, bias):
    n = lax.axis_size("expert")
    rows, width = sent.shape
    units = up.shape[1]
    cap = rows // n
    block = rows // PARTS
    vm = pl.BlockSpec(memory_space=pltpu.VMEM)
    hbm = pl.BlockSpec(memory_space=pl.ANY)
    return pl.pallas_call(
        functools.partial(expert_kernel, n, cap),
        out_shape=(
            jax.ShapeDtypeStruct((rows, width), low),
            jax.ShapeDtypeStruct((rows, width), low),
            jax.ShapeDtypeStruct((width, units), f32),
            jax.ShapeDtypeStruct((units, width), f32),
            jax.ShapeDtypeStruct((1, units), f32),
            jax.ShapeDtypeStruct((1, width), f32),
            jax.ShapeDtypeStruct((8, width), f32),
        ),
        in_specs=[hbm, hbm, hbm, hbm, vm, hbm, vm, hbm, vm, vm, vm],
        out_specs=(hbm, hbm, hbm, hbm, vm, vm, vm),
        scratch_shapes=[
            pltpu.VMEM((rows, width), low),
            pltpu.VMEM((PARTS, 2 * block, width), low),
            pltpu.VMEM((PARTS, 2 * block, width), low),
            pltpu.VMEM((width, units), low),
            pltpu.VMEM((units, width), low),
            pltpu.VMEM((PARTS, 2 * block, units), low),
            pltpu.VMEM((PARTS, 2 * block, units), low),
            pltpu.VMEM((2 * PARTS, block, width), low),
            pltpu.VMEM((2 * PARTS, block, width), low),
            pltpu.VMEM((rows, width), low),
            pltpu.VMEM((2, width, UNITS), f32),
            pltpu.VMEM((2, UNITS, width), f32),
            pltpu.SemaphoreType.DMA((n,)),
            pltpu.SemaphoreType.DMA((n,)),
            pltpu.SemaphoreType.DMA((n,)),
            pltpu.SemaphoreType.DMA((n,)),
            pltpu.SemaphoreType.DMA((3, 2, PARTS)),
            pltpu.SemaphoreType.DMA((2 + 4 * PARTS,)),
            pltpu.SemaphoreType.DMA((PARTS + 4,)),
        ],
        compiler_params=pltpu.CompilerParams(
            collective_id=1, has_side_effects=True, vmem_limit_bytes=60 * 1024 * 1024
        ),
    )(sent, grads, grads_pair, hids, live, up, up_bias, down, down_bias, gain, bias)


STREAMS = 3


def ending_kernel(
    n,
    cap,
    chunks,
    sent,
    attn_in_hbm,
    grad_proj_hbm,
    attended_hbm,
    grad_h_hbm,
    norm_terms,
    grad_in,
    grad_qkv,
    grad_wout,
    grad_norms,
    attn_in_t,
    grad_proj_t,
    attended_t,
    grad_h,
    made,
    total,
    landed,
    sem_send,
    sem_recv,
    sem_load,
    sem_pair,
    sem_step,
):
    me_d = lax.axis_index("dp")
    me_e = lax.axis_index("expert")
    partner = (1 - me_d, me_e)
    bits = n.bit_length() - 1
    half = n // 2
    width = grad_h.shape[1]
    each = made.shape[1]

    def offset(order, p):
        k = 0
        for j, b in enumerate(order):
            k = k + lax.rem(p // (1 << (bits - 1 - j)), 2) * (1 << b)
        return k

    def slot_copy(i):
        peer = me_e ^ i
        return pltpu.make_async_remote_copy(
            src_ref=sent.at[pl.ds(pl.multiple_of(peer * cap, cap), cap)],
            dst_ref=grad_in.at[pl.ds(pl.multiple_of(me_e * cap, cap), cap)],
            send_sem=sem_send.at[i],
            recv_sem=sem_recv.at[i],
            device_id=(me_d, peer),
            device_id_type=MESH_ID,
        )

    def own_slots():
        here = pl.ds(pl.multiple_of(me_e * cap, cap), cap)
        return pltpu.make_async_copy(sent.at[here], grad_in.at[here], sem_recv.at[0])

    def pair_copy(c, q):
        size = chunks[c][2]
        here = pl.ds(q * half, half)
        return pltpu.make_async_remote_copy(
            src_ref=total.at[c, 1, here, :, 0:size],
            dst_ref=landed.at[c, here, :, 0:size],
            send_sem=sem_pair.at[0, c, q],
            recv_sem=sem_pair.at[1, c, q],
            device_id=partner,
            device_id_type=MESH_ID,
        )

    def step_copy(c, j):
        order, _, size = chunks[c]
        many = n >> (j + 1)
        start = n + sum(n >> (i + 1) for i in range(j))
        return pltpu.make_async_remote_copy(
            src_ref=total.at[c, 0, pl.ds(many, many), :, 0:size],
            dst_ref=landed.at[c, pl.ds(start, many), :, 0:size],
            send_sem=sem_step.at[0, c, j],
            recv_sem=sem_step.at[1, c, j],
            device_id=(me_d, me_e ^ (1 << order[j])),
            device_id_type=MESH_ID,
        ), many, start

    loads = [
        pltpu.make_async_copy(a, b, sem_load.at[i])
        for i, (a, b) in enumerate(
            (
                (attn_in_hbm, attn_in_t),
                (grad_proj_hbm, grad_proj_t),
                (attended_hbm, attended_t),
                (grad_h_hbm, grad_h),
            )
        )
    ]
    for load in loads:
        load.start()
    own_slots().start()
    greet(me_d, me_e, n)

    def start_slots(i, carry):
        slot_copy(n - i).start()
        return carry

    lax.fori_loop(1, n, start_slots, 0)
    for load in loads:
        load.wait()

    def pieces(c):
        _, begin, size = chunks[c]
        edges = (0, 3 * width, 4 * width, 4 * width + LANES)
        for kind in range(3):
            a, b = max(begin, edges[kind]), min(begin + size, edges[kind + 1])
            if a < b:
                yield kind, slice(a - edges[kind], b - edges[kind]), slice(a - begin, b - begin)

    for c, (order, _, size) in enumerate(chunks):
        for kind, source, target in pieces(c):
            if kind == 0:
                term = mm_nt(attn_in_t[...], grad_proj_t[source, :])
            elif kind == 1:
                term = mm(attended_t[...], grad_h[:, source])
            else:
                term = norm_terms[...]
            made[:, :, target] = term.reshape(made.shape[0], each, term.shape[1])

        def arrange(p, carry, c=c, order=order, size=size):
            owner = me_e ^ offset(order, p)
            total[c, 0, p, :, 0:size] = made[me_d * n + owner, :, 0:size].astype(low)
            total[c, 1, p, :, 0:size] = made[(1 - me_d) * n + owner, :, 0:size].astype(low)
            return carry

        lax.fori_loop(0, n, arrange, 0)
        pair_copy(c, 1).start()
        pair_copy(c, 0).start()

    def add(c, p, q):
        size = chunks[c][2]
        both = total[c, 0, p, :, 0:size].astype(f32) + landed[c, q, :, 0:size].astype(f32)
        return both

    for q in (1, 0):
        for c in range(len(chunks)):
            pair_copy(c, q).wait()

            def add_pair(p, carry, c=c):
                total[c, 0, p, :, 0 : chunks[c][2]] = add(c, p, p).astype(low)
                return carry

            lax.fori_loop(q * half, q * half + half, add_pair, 0)
            if q == 1:
                step_copy(c, 0)[0].start()
    for j in range(bits):
        for c in range(len(chunks)):
            copy, many, start = step_copy(c, j)
            copy.wait()
            if many > 1:

                def add_step(p, carry, c=c, start=start):
                    total[c, 0, p, :, 0 : chunks[c][2]] = add(c, p, start + p).astype(low)
                    return carry

                lax.fori_loop(0, many, add_step, 0)
                step_copy(c, j + 1)[0].start()
            else:
                both = add(c, 0, start)
                for kind, target, source in pieces(c):
                    (grad_qkv, grad_wout, grad_norms)[kind][:, target] = both[:, source]
    own_slots().wait()

    def wait_slots(i, carry):
        slot_copy(i).wait()
        return carry

    lax.fori_loop(1, n, wait_slots, 0)


def ending(sent, attn_in_t, grad_proj_t, attended_t, grad_h, norm_terms):
    n = lax.axis_size("expert")
    owners = n * lax.axis_size("dp")
    rows, width = sent.shape
    each = width // owners
    bits = n.bit_length() - 1
    tiles = 4 * width // LANES + 1
    count = 2 * STREAMS
    chunks = []
    begin = 0
    for c in range(count):
        size = (tiles // count + (1 if c < tiles % count else 0)) * LANES
        turn = [(c + k) % STREAMS for k in range(STREAMS)]
        chunks.append((turn + list(range(STREAMS, bits)), begin, size))
        begin += size
    widest = max(size for _, _, size in chunks)
    vm = pl.BlockSpec(memory_space=pltpu.VMEM)
    hbm = pl.BlockSpec(memory_space=pl.ANY)
    shape = jax.ShapeDtypeStruct
    return pl.pallas_call(
        functools.partial(ending_kernel, n, rows // n, tuple(chunks)),
        out_shape=(
            shape((rows, width), low),
            shape((each, 3 * width), f32),
            shape((each, width), f32),
            shape((each, LANES), f32),
        ),
        in_specs=[hbm, hbm, hbm, hbm, hbm, vm],
        out_specs=(hbm, vm, vm, vm),
        scratch_shapes=[
            pltpu.VMEM(attn_in_t.shape, low),
            pltpu.VMEM(grad_proj_t.shape, low),
            pltpu.VMEM(attended_t.shape, low),
            pltpu.VMEM(grad_h.shape, low),
            pltpu.VMEM((owners, each, widest), f32),
            pltpu.VMEM((count, 2, n, each, widest), low),
            pltpu.VMEM((count, 2 * n, each, widest), low),
            pltpu.SemaphoreType.DMA((n,)),
            pltpu.SemaphoreType.DMA((n,)),
            pltpu.SemaphoreType.DMA((4,)),
            pltpu.SemaphoreType.DMA((2, count, 2)),
            pltpu.SemaphoreType.DMA((2, count, bits)),
        ],
        compiler_params=pltpu.CompilerParams(
            collective_id=2, has_side_effects=True, vmem_limit_bytes=60 * 1024 * 1024
        ),
    )(sent, attn_in_t, grad_proj_t, attended_t, grad_h, norm_terms)


def on_device(
    hidden_in,
    buckets,
    expert_of_bucket,
    lengths,
    norm1_gain,
    norm1_bias,
    w_qkv,
    w_out,
    norm2_gain,
    norm2_bias,
    w_up,
    b_up,
    w_down,
    b_down,
    grad_out,
):
    (
        sent,
        grads,
        grads_pair,
        hids,
        live,
        attn_in_t,
        tokens_t,
        queries_t,
        keys_t,
        values,
        attended_t,
        inv_sums,
        slot_row,
        expos,
    ) = starting(
        hidden_in,
        grad_out,
        buckets.reshape(1, -1),
        expert_of_bucket[None],
        lengths,
        norm1_gain[None],
        norm1_bias[None],
        w_qkv,
        w_out,
        w_down[0],
    )
    returned, hidden_out, grad_up, grad_down, grad_bup, grad_bdown, grad_norm2 = expert_block(
        sent, grads, grads_pair, hids, live, w_up[0], b_up, w_down[0], b_down, norm2_gain[None], norm2_bias[None]
    )
    sent_grad, grad_h, grad_proj_t, norm_terms, grad_bup, grad_bdown, grad_up, grad_down, hidden_out = attention_back(
        returned,
        slot_row,
        tokens_t,
        queries_t,
        keys_t,
        values,
        attended_t,
        inv_sums,
        expos,
        w_qkv,
        w_out,
        norm1_gain[None],
        grad_norm2,
        grad_bup,
        grad_bdown,
        grad_up,
        grad_down,
        hidden_out,
    )
    grad_in, grad_qkv, grad_wout, grad_norms = ending(
        sent_grad, attn_in_t, grad_proj_t, attended_t, grad_h, norm_terms
    )
    return (
        hidden_out,
        grad_in,
        grad_qkv,
        grad_wout,
        grad_norms[:, 0],
        grad_norms[:, 1],
        grad_norms[:, 2],
        grad_norms[:, 3],
        grad_up[None],
        grad_bup,
        grad_down[None],
        grad_bdown,
    )


def solution(mesh):
    return jax.shard_map(
        on_device,
        mesh=mesh,
        in_specs=(
            P(("dp", "expert"), None),
            P(("dp", "expert"), None),
            P(),
            P(("dp", "expert"), None),
            P(),
            P(),
            P(),
            P(),
            P(),
            P(),
            P("expert", None, "dp"),
            P("expert", "dp"),
            P("expert", "dp", None),
            P("expert", None),
            P(("dp", "expert"), None),
        ),
        out_specs=(
            P(("dp", "expert"), None),
            P(("dp", "expert"), None),
            P(("dp", "expert"), None),
            P(("dp", "expert"), None),
            P(("dp", "expert")),
            P(("dp", "expert")),
            P(("dp", "expert")),
            P(("dp", "expert")),
            P("expert", None, "dp"),
            P("expert", "dp"),
            P("expert", "dp", None),
            P("expert", "dp"),
        ),
        check_vma=False,
    )
```

```python
import functools

import jax
import jax.numpy as jnp
from jax import lax
from jax.experimental import pallas as pl
from jax.experimental.pallas import tpu as pltpu
from jax.sharding import PartitionSpec as P

HEADS = 16
HEAD_DIM = 64


norm_eps = 1e-05
masked_score = -1e30
root_half = 0.7071067811865476
inv_root_tau = 0.3989422804014327

MESH_ID = pl.DeviceIdType.MESH
PARTS = 4
UNITS = 256
WIDE = 512
LANES = 128
MOVES = 8
QUERIES = 256
PAIR = 2 * HEAD_DIM
scale_val = HEAD_DIM ** (-0.5)
low = jnp.bfloat16
f32 = jnp.float32


def mm(a, b):
    return jnp.dot(a, b, preferred_element_type=f32)


def mm_nt(a, b):
    return lax.dot_general(a, b, (((1,), (1,)), ((), ())), preferred_element_type=f32)


def mm_tn(a, b):
    return lax.dot_general(a, b, (((0,), (0,)), ((), ())), preferred_element_type=f32)


def normalize(values, axis=-1):
    mean_val = jnp.mean(values, axis=axis, keepdims=True)
    centered = values - mean_val
    variance = jnp.mean(centered * centered, axis=axis, keepdims=True)
    inv_std = lax.rsqrt(variance + norm_eps)
    return (centered * inv_std, inv_std)


def norm_back(grad_normed, normed, inv_std, gain_vec, axis=-1):
    scaled = grad_normed * gain_vec
    mean_grad = jnp.mean(scaled, axis=axis, keepdims=True)
    mean_cross = jnp.mean(scaled * normed, axis=axis, keepdims=True)
    return inv_std * (scaled - mean_grad - normed * mean_cross)


def gelu_parts(pre):
    bell = jnp.exp(-0.5 * pre * pre)
    den = 1.0 + (0.3275911 * root_half) * jnp.abs(pre)
    t = pl.reciprocal(den, approx=True)
    t = t * (2.0 - den * t)
    tail = t * (
        0.5 * 0.254829592
        + t * (0.5 * -0.284496736 + t * (0.5 * 1.421413741 + t * (0.5 * -1.453152027 + t * (0.5 * 1.061405429))))
    )
    tail = tail * bell
    phi = jnp.where(pre >= 0.0, 1.0 - tail, tail)
    return pre * phi, phi + pre * (inv_root_tau * bell)


STREAMS = 2
GROUPS = 3


def greet_peers(me_d, me_e, n):
    barrier = pltpu.get_barrier_semaphore()

    def signal(i, carry):
        pl.semaphore_signal(barrier, inc=1, device_id=(me_d, me_e ^ i), device_id_type=MESH_ID)
        return carry

    lax.fori_loop(1, n, signal, 0)


def greet_partner(me_d, me_e):
    pl.semaphore_signal(
        pltpu.get_barrier_semaphore(), inc=1, device_id=(1 - me_d, me_e), device_id_type=MESH_ID
    )


def greet(me_d, me_e, n):
    greet_peers(me_d, me_e, n)
    greet_partner(me_d, me_e)
    pl.semaphore_wait(pltpu.get_barrier_semaphore(), n)


def staged(units, *stages):
    held = [None] * len(units)
    for step in range(len(units) + len(stages) - 1):
        for k, stage in enumerate(stages):
            i = step - k
            if 0 <= i < len(units):
                held[i] = stage(units[i]) if k == 0 else stage(units[i], held[i])


def start_kernel(
    n,
    cap,
    hidden,
    grad_out,
    buckets,
    expert_of,
    lengths,
    gain,
    bias,
    w_qkv_hbm,
    w_out_hbm,
    down_hbm,
    sent,
    grads,
    hids,
    live,
    attn_in_hbm,
    tokens_hbm,
    queries_hbm,
    keys_hbm,
    values_hbm,
    attended_hbm,
    inv_sums,
    slot_row,
    expos,
    arrived,
    w_qkv,
    w_out,
    down,
    grad_raw,
    grad_v,
    grad_p,
    hid_v,
    attn_in_t,
    tokens_t,
    queries_t,
    keys_t,
    values,
    attended_t,
    attn_in_v,
    proj,
    values_t,
    allow,
    tokens,
    expo_v,
    sent_v,
    counts_out,
    counts_in,
    sem_send,
    sem_recv,
    sem_count_send,
    sem_count_recv,
    sem_pair,
    sem_load,
    sem_store,
    sem_turn,
):
    me_d = lax.axis_index("dp")
    me_e = lax.axis_index("expert")
    partner = (1 - me_d, me_e)
    rows, width = arrived.shape
    toks = buckets.shape[1]
    lanes = counts_out.shape[1]

    def slot_copy(i):
        peer = me_e ^ i
        return pltpu.make_async_remote_copy(
            src_ref=hidden.at[pl.ds(pl.multiple_of(peer * cap, cap), cap)],
            dst_ref=arrived.at[pl.ds(pl.multiple_of(me_e * cap, cap), cap)],
            send_sem=sem_send.at[i],
            recv_sem=sem_recv.at[i],
            device_id=(me_d, peer),
            device_id_type=MESH_ID,
        )

    def own_slots():
        here = pl.ds(pl.multiple_of(me_e * cap, cap), cap)
        return pltpu.make_async_copy(hidden.at[here], arrived.at[here], sem_recv.at[0])

    def count_copy(i):
        return pltpu.make_async_remote_copy(
            src_ref=counts_out,
            dst_ref=counts_in.at[me_e],
            send_sem=sem_count_send.at[i],
            recv_sem=sem_count_recv.at[i],
            device_id=(me_d, me_e ^ i),
            device_id_type=MESH_ID,
        )

    grad_load = pltpu.make_async_copy(grad_out, grad_raw, sem_load.at[0])
    qkv_load = pltpu.make_async_copy(w_qkv_hbm, w_qkv, sem_load.at[1])
    out_load = pltpu.make_async_copy(w_out_hbm, w_out, sem_load.at[2])
    down_load = pltpu.make_async_copy(down_hbm, down, sem_load.at[3])
    pair_grads_store = pltpu.make_async_copy(grad_p, grads.at[1], sem_store.at[2])
    keep = [
        pltpu.make_async_copy(a, b, sem_store.at[3 + i])
        for i, (a, b) in enumerate(
            (
                (attn_in_t, attn_in_hbm),
                (tokens_t, tokens_hbm),
                (queries_t, queries_hbm),
                (keys_t, keys_hbm),
                (values, values_hbm),
                (attended_t, attended_hbm),
            )
        )
    ]

    def hid_store(k):
        return pltpu.make_async_copy(hid_v.at[k], hids.at[k], sem_store.at[9 + k])

    def hidden_grad(k, grad_ref):
        def tile(i, carry):
            here = pl.ds(pl.multiple_of((i // 2) * WIDE, WIDE), WIDE)
            some = pl.ds(pl.multiple_of(lax.rem(i, 2) * (rows // 2), rows // 2), rows // 2)
            hid_v[k, some, here] = mm_nt(grad_ref[some, :], down[here, :]).astype(low)
            return carry

        lax.fori_loop(0, 2 * (down.shape[0] // WIDE), tile, 0)
        hid_store(k).start()

    grad_store = pltpu.make_async_copy(grad_v, grads.at[0], sem_store.at[0])
    grad_pair = pltpu.make_async_remote_copy(
        src_ref=grad_v,
        dst_ref=grad_p,
        send_sem=sem_pair.at[0],
        recv_sem=sem_pair.at[1],
        device_id=partner,
        device_id_type=MESH_ID,
    )

    def start_slots(i, carry):
        slot_copy(i).start()
        return carry

    grad_load.start()

    @pl.when(me_d == 1)
    def _():
        down_load.start()

    greet(me_d, me_e, n)

    lax.fori_loop(1, n // 2, start_slots, 0)

    @pl.when(me_d == 0)
    def _():
        lax.fori_loop(n // 2, n, start_slots, 0)

    own_slots().start()
    qkv_load.start()
    out_load.start()

    lane_ids = lax.broadcasted_iota(jnp.int32, (toks, lanes), 1)
    bucket = jnp.broadcast_to(buckets[...], (lanes, toks)).T[:, 0:n]
    bucket_hot = (bucket == lane_ids[:, 0:n]).astype(f32).astype(low)
    serves_t = (expert_of[...] == lax.broadcasted_iota(jnp.int32, (lanes, n), 0)).astype(f32).astype(low)
    expert_hot = mm_nt(bucket_hot, serves_t)
    row_ids = lax.broadcasted_iota(jnp.int32, (toks, toks), 0)
    col_ids = lax.broadcasted_iota(jnp.int32, (toks, toks), 1)
    earlier = (col_ids < row_ids).astype(f32).astype(low)
    before = mm(earlier, expert_hot.astype(low))
    slot = jnp.sum(expert_hot * (before + (lane_ids * cap).astype(f32)), axis=1, keepdims=True)
    counts_out[...] = jnp.broadcast_to(jnp.sum(expert_hot, axis=0, keepdims=True), counts_out.shape)
    counts_in[me_e] = counts_out[...]

    def start_counts(i, carry):
        count_copy(i).start()
        return carry

    lax.fori_loop(1, n, start_counts, 0)
    slot_row[...] = jnp.broadcast_to(slot, (toks, lanes)).T[0:8, :].astype(jnp.int32)
    ends = jnp.zeros((1, toks), jnp.int32)
    begin = jnp.zeros((1, toks), jnp.int32)
    places = lax.broadcasted_iota(jnp.int32, (1, toks), 1)
    for s in range(lengths.shape[1]):
        ends = ends + lengths[0:1, s : s + 1]
        begin = jnp.where(places >= ends, ends, begin)
    allow[...] = jnp.where(jnp.logical_and(row_ids <= col_ids, row_ids >= begin), 0.0, masked_score)

    def wait_counts(i, carry):
        count_copy(i).wait()
        return carry

    lax.fori_loop(1, n, wait_counts, 0)
    grad_load.wait()

    def mark(s, carry):
        here = pl.ds(pl.multiple_of(s * cap, cap), cap)
        mine = lax.broadcasted_iota(jnp.int32, (1, lanes), 1) == me_e
        count = jnp.sum(jnp.where(mine, counts_in[s, 0:1, :], 0.0), axis=1, keepdims=True)
        taken = (lax.broadcasted_iota(jnp.int32, (cap, 1), 0).astype(f32) < count).astype(f32)
        live[here, :] = taken
        grad_v[here, :] = (grad_raw[here, :].astype(f32) * taken).astype(low)
        return carry

    lax.fori_loop(0, n, mark, 0)
    grad_store.start()
    grad_pair.start()
    @pl.when(me_d == 0)
    def _():
        def wait_sent(i, carry):
            slot_copy(i).wait_send()
            return carry

        lax.fori_loop(n // 2, n, wait_sent, 0)
        pl.semaphore_signal(sem_turn, inc=1, device_id=partner, device_id_type=MESH_ID)

    @pl.when(me_d == 1)
    def _():
        pl.semaphore_wait(sem_turn, 1)
        lax.fori_loop(n // 2, n, start_slots, 0)

    grad_pair.wait()
    pair_grads_store.start()

    @pl.when(me_d == 1)
    def _():
        down_load.wait()
        hidden_grad(0, grad_v)
        hidden_grad(1, grad_p)


    own_slots().wait()

    def wait_slots(i, carry):
        slot_copy(i).wait_recv()
        return carry

    lax.fori_loop(1, n, wait_slots, 0)

    pick = (slot.astype(jnp.int32) == lax.broadcasted_iota(jnp.int32, (toks, rows), 1)).astype(f32).astype(low)
    tokens[...] = mm(pick, arrived[...])
    normed, _ = normalize(tokens[...])
    attn_in = (normed * gain[...] + bias[...]).astype(low)
    attn_in_v[...] = attn_in
    qkv_load.wait()
    step = width // 4
    for c in range(3 * width // step):
        here = slice(c * step, (c + 1) * step)
        part = mm(attn_in, w_qkv[:, here])
        if c * step < width:
            part = part.astype(low).astype(f32) * scale_val
        proj[:, here] = part.astype(low)
    values_t[...] = proj[:, 2 * width : 3 * width].T

    def expo_store(g):
        here = pl.ds(pl.multiple_of(4 * g, 4), 4)
        return pltpu.make_async_copy(expo_v.at[here], expos.at[here], sem_store.at[11 + g])

    in_first = lax.broadcasted_iota(jnp.int32, (1, PAIR), 1) < HEAD_DIM

    def head_group(g, carry):
        units = [
            (2 * g + pair, h, q) for pair in range(2) for h in range(2) for q in range(toks // QUERIES)
        ]

        def score(unit):
            p, h, q = unit
            first = pl.multiple_of(p * PAIR, PAIR)
            upto = (q + 1) * QUERIES
            here = slice(q * QUERIES, upto)
            mine = in_first if h == 0 else jnp.logical_not(in_first)
            query = jnp.where(mine, proj[here, pl.ds(first, PAIR)], jnp.zeros((), low))
            scores = mm_nt(proj[0:upto, pl.ds(pl.multiple_of(width + first, PAIR), PAIR)], query)
            return scores + allow[0:upto, here]

        def soft(unit, scores):
            expo = jnp.exp(scores - jnp.max(scores, axis=0, keepdims=True))
            inv = 1.0 / jnp.sum(expo, axis=0, keepdims=True)
            return expo.astype(low), inv

        def attend(unit, held):
            p, h, q = unit
            expo, inv = held
            upto = (q + 1) * QUERIES
            here = slice(q * QUERIES, upto)
            head_rows = pl.ds(pl.multiple_of(p * PAIR + h * HEAD_DIM, HEAD_DIM), HEAD_DIM)
            expo_v[2 * p + h, 0:upto, here] = expo
            if upto < toks:
                expo_v[2 * p + h, upto:toks, here] = jnp.zeros((toks - upto, QUERIES), low)
            out = mm(values_t[head_rows, 0:upto], expo)
            attended_t[head_rows, here] = (out * inv).astype(low)
            inv_sums[2 * p + h, :, here] = jnp.broadcast_to(inv, (8, QUERIES))

        staged(units, score, soft, attend)
        here = pl.ds(pl.multiple_of(g * 2 * PAIR, 2 * PAIR), 2 * PAIR)
        queries_t[here, :] = proj[:, here].T
        keys_t[here, :] = proj[:, pl.ds(pl.multiple_of(width + g * 2 * PAIR, 2 * PAIR), 2 * PAIR)].T
        values[:, here] = proj[:, pl.ds(pl.multiple_of(2 * width + g * 2 * PAIR, 2 * PAIR), 2 * PAIR)]
        tokens_t[here, :] = tokens[:, here].T.astype(low)
        attn_in_t[here, :] = attn_in_v[:, here].T
        expo_store(g).start()
        return carry

    lax.fori_loop(0, HEADS // 4, head_group, 0)
    for copy in keep:
        copy.start()
    out_load.wait()
    residual = (tokens[...] + mm_tn(attended_t[...], w_out[...])).astype(low)
    place = (slot_row[0:1, :] == lax.broadcasted_iota(jnp.int32, (rows, toks), 0)).astype(f32).astype(low)
    sent_v[...] = mm(place, residual).astype(low)
    sent_store = pltpu.make_async_copy(sent_v, sent, sem_store.at[1])
    sent_store.start()

    for g in range(HEADS // 4):
        expo_store(g).wait()
    for copy in keep:
        copy.wait()
    grad_store.wait()
    pair_grads_store.wait()

    @pl.when(me_d == 1)
    def _():
        hid_store(0).wait()
        hid_store(1).wait()


    def wait_sent(i, carry):
        slot_copy(i).wait_send()
        return carry

    lax.fori_loop(1, n // 2, wait_sent, 0)

    @pl.when(me_d == 1)
    def _():
        lax.fori_loop(n // 2, n, wait_sent, 0)

    sent_store.wait()


def starting(hidden, grad_out, buckets, expert_of, lengths, gain, bias, w_qkv, w_out, down):
    n = lax.axis_size("expert")
    rows, width = hidden.shape
    toks = buckets.shape[1]
    units = down.shape[0]
    lanes = 128
    vm = pl.BlockSpec(memory_space=pltpu.VMEM)
    hbm = pl.BlockSpec(memory_space=pl.ANY)
    shape = jax.ShapeDtypeStruct
    return pl.pallas_call(
        functools.partial(start_kernel, n, rows // n),
        out_shape=(
            shape((rows, width), low),
            shape((2, rows, width), low),
            shape((2, rows, units), low),
            shape((rows, 1), f32),
            shape((width, toks), low),
            shape((width, toks), low),
            shape((width, toks), low),
            shape((width, toks), low),
            shape((toks, width), low),
            shape((width, toks), low),
            shape((HEADS, 8, toks), f32),
            shape((8, toks), jnp.int32),
            shape((HEADS, toks, toks), low),
        ),
        in_specs=[hbm, hbm, vm, vm, vm, vm, vm, hbm, hbm, hbm],
        out_specs=(hbm, hbm, hbm, vm, hbm, hbm, hbm, hbm, hbm, hbm, vm, vm, hbm),
        scratch_shapes=[
            pltpu.VMEM((rows, width), low),
            pltpu.VMEM(w_qkv.shape, low),
            pltpu.VMEM(w_out.shape, low),
            pltpu.VMEM(down.shape, low),
            pltpu.VMEM((rows, width), low),
            pltpu.VMEM((rows, width), low),
            pltpu.VMEM((rows, width), low),
            pltpu.VMEM((2, rows, units), low),
            pltpu.VMEM((width, toks), low),
            pltpu.VMEM((width, toks), low),
            pltpu.VMEM((width, toks), low),
            pltpu.VMEM((width, toks), low),
            pltpu.VMEM((toks, width), low),
            pltpu.VMEM((width, toks), low),
            pltpu.VMEM((toks, width), low),
            pltpu.VMEM((toks, 3 * width), low),
            pltpu.VMEM((width, toks), low),
            pltpu.VMEM((toks, toks), f32),
            pltpu.VMEM((toks, width), f32),
            pltpu.VMEM((HEADS, toks, toks), low),
            pltpu.VMEM((rows, width), low),
            pltpu.VMEM((8, lanes), f32),
            pltpu.VMEM((n, 8, lanes), f32),
            pltpu.SemaphoreType.DMA((n,)),
            pltpu.SemaphoreType.DMA((n,)),
            pltpu.SemaphoreType.DMA((n,)),
            pltpu.SemaphoreType.DMA((n,)),
            pltpu.SemaphoreType.DMA((2,)),
            pltpu.SemaphoreType.DMA((4,)),
            pltpu.SemaphoreType.DMA((11 + HEADS // 4,)),
            pltpu.SemaphoreType.REGULAR,
        ],
        compiler_params=pltpu.CompilerParams(
            collective_id=3, has_side_effects=True, vmem_limit_bytes=60 * 1024 * 1024
        ),
    )(hidden, grad_out, buckets, expert_of, lengths, gain, bias, w_qkv, w_out, down)


def attention_back_kernel(
    returned_hbm,
    slot_row,
    tokens_hbm,
    queries_hbm,
    keys_hbm,
    values_hbm,
    attended_hbm,
    inv_sums,
    expos,
    w_qkv_hbm,
    w_out_hbm,
    gain,
    grad_norm2,
    grad_bup_in,
    grad_bdown_in,
    grad_up_in,
    grad_down_in,
    hidden_in,
    sent,
    grad_h_hbm,
    grad_proj_hbm,
    norm_terms,
    grad_bup,
    grad_bdown,
    grad_up,
    grad_down,
    hidden_out,
    returned,
    tokens_t,
    queries_t,
    keys_t,
    values,
    attended_t,
    w_qkv,
    w_out,
    expo_v,
    grad_att_t,
    grad_h,
    grad_proj_t,
    sent_v,
    taken_up,
    taken_down,
    taken_out,
    held_up,
    held_down,
    held_out,
    sem_load,
    sem_expo,
    sem_store,
    sem_move,
):
    rows, width = returned.shape
    toks = slot_row.shape[1]
    loads = [
        pltpu.make_async_copy(a, b, sem_load.at[i])
        for i, (a, b) in enumerate(
            (
                (returned_hbm, returned),
                (w_out_hbm, w_out),
                (attended_hbm, attended_t),
                (values_hbm, values),
                (keys_hbm, keys_t),
                (queries_hbm, queries_t),
                (w_qkv_hbm, w_qkv),
                (tokens_hbm, tokens_t),
            )
        )
    ]

    def move(k, p, store):
        source, target, taken, held = (
            (grad_up_in, grad_up, taken_up, held_up),
            (grad_down_in, grad_down, taken_down, held_down),
            (hidden_in, hidden_out, taken_out, held_out),
        )[k]
        size = held.shape[1]
        here = pl.ds(pl.multiple_of(p * size, size), size)
        slot = lax.rem(p, 2)
        if store:
            return pltpu.make_async_copy(held.at[slot], target.at[here], sem_move.at[3 + k, slot])
        return pltpu.make_async_copy(source.at[here], taken.at[slot], sem_move.at[k, slot])

    def tick(p):
        slot = lax.rem(p, 2)
        for k in range(3):
            move(k, p, False).wait()

        @pl.when(p > 1)
        def _():
            for k in range(3):
                move(k, p - 2, True).wait()

        held_up[slot] = taken_up[slot].astype(f32)
        held_down[slot] = taken_down[slot].astype(f32)
        held_out[slot] = taken_out[slot]
        for k in range(3):
            move(k, p, True).start()

        @pl.when(p < MOVES - 2)
        def _():
            for k in range(3):
                move(k, p + 2, False).start()

    def expo_load(g):
        here = pl.ds(pl.multiple_of(4 * g, 4), 4)
        return pltpu.make_async_copy(expos.at[here], expo_v.at[here], sem_expo.at[g])

    for i in range(2):
        loads[i].start()
    grad_bup[...] = grad_bup_in[...]
    part = grad_bdown.shape[1]
    first_half = lax.axis_index("dp") == 0
    grad_bdown[...] = jnp.where(first_half, grad_bdown_in[:, 0:part], grad_bdown_in[:, part : 2 * part])
    place = (slot_row[0:1, :] == lax.broadcasted_iota(jnp.int32, (rows, toks), 0)).astype(f32).astype(low)
    loads[0].wait()
    for i in range(2, 6):
        loads[i].start()
    expo_load(0).start()
    for p in range(2):
        for k in range(3):
            move(k, p, False).start()
    for g in range(1, HEADS // 4):
        expo_load(g).start()
    for i in range(6, len(loads)):
        loads[i].start()
    grad_h[...] = mm_tn(place, returned[...]).astype(low)
    grad_h_store = pltpu.make_async_copy(grad_h, grad_h_hbm, sem_store.at[0])
    grad_h_store.start()
    tick(0)
    loads[1].wait()
    grad_att_t[...] = mm_nt(w_out[...], grad_h[...]).astype(low)
    tick(1)
    for i in range(2, 6):
        loads[i].wait()
    in_first = lax.broadcasted_iota(jnp.int32, (1, PAIR), 1) < HEAD_DIM

    def head_group(g, carry):
        expo_load(g).wait()
        ready = {}
        sums = {}
        for pair in range(2):
            p = 2 * g + pair
            pair_rows = pl.ds(pl.multiple_of(p * PAIR, PAIR), PAIR)
            inv_pair = jnp.concatenate(
                [jnp.broadcast_to(inv_sums[2 * p + h, 0:1, :], (HEAD_DIM, toks)) for h in range(2)], axis=0
            )
            grad_pair = grad_att_t[pair_rows, :].astype(f32)
            cross = grad_pair * attended_t[pair_rows, :].astype(f32) * inv_pair
            scaled = (grad_pair * inv_pair).astype(low)
            for h in range(2):
                in_pair = slice(h * HEAD_DIM, (h + 1) * HEAD_DIM)
                ready[pair, h] = (jnp.sum(cross[in_pair], axis=0, keepdims=True), scaled)
        units = [
            (pair, h, q) for pair in range(2) for h in range(2) for q in reversed(range(toks // QUERIES))
        ]

        def probs_back(unit):
            pair, h, q = unit
            upto = (q + 1) * QUERIES
            here = slice(q * QUERIES, upto)
            first = pl.multiple_of((2 * g + pair) * PAIR, PAIR)
            mine = in_first if h == 0 else jnp.logical_not(in_first)
            value = jnp.where(mine, values[0:upto, pl.ds(first, PAIR)], jnp.zeros((), low))
            return mm(value, ready[pair, h][1][:, here])

        def scores_back(unit, grad_prob):
            pair, h, q = unit
            upto = (q + 1) * QUERIES
            here = slice(q * QUERIES, upto)
            expo = expo_v[4 * g + 2 * pair + h, 0:upto, here]
            return expo, (expo.astype(f32) * (grad_prob - ready[pair, h][0][:, here])).astype(low)

        def heads_back(unit, held):
            pair, h, q = unit
            expo, grad_score = held
            upto = (q + 1) * QUERIES
            here = slice(q * QUERIES, upto)
            first = pl.multiple_of((2 * g + pair) * PAIR + h * HEAD_DIM, HEAD_DIM)
            head_rows = pl.ds(first, HEAD_DIM)
            key_rows = pl.ds(pl.multiple_of(width + first, HEAD_DIM), HEAD_DIM)
            value_rows = pl.ds(pl.multiple_of(2 * width + first, HEAD_DIM), HEAD_DIM)
            grad_proj_t[head_rows, here] = (mm(keys_t[head_rows, 0:upto], grad_score) * scale_val).astype(low)
            key_term = mm_nt(queries_t[head_rows, here], grad_score)
            value_term = mm_nt(ready[pair, h][1][h * HEAD_DIM : (h + 1) * HEAD_DIM, here], expo)
            if upto < toks:
                key_more, value_more = sums[pair, h]
                key_term = jnp.concatenate([key_more[:, 0:upto] + key_term, key_more[:, upto:]], axis=1)
                value_term = jnp.concatenate([value_more[:, 0:upto] + value_term, value_more[:, upto:]], axis=1)
            sums[pair, h] = (key_term, value_term)
            if q == 0:
                grad_proj_t[key_rows, :] = key_term.astype(low)
                grad_proj_t[value_rows, :] = value_term.astype(low)

        staged(units, probs_back, scores_back, heads_back)
        tick(2 + g)
        return carry

    lax.fori_loop(0, HEADS // 4, head_group, 0)
    grad_proj_store = pltpu.make_async_copy(grad_proj_t, grad_proj_hbm, sem_store.at[1])
    grad_proj_store.start()
    for i in range(6, len(loads)):
        loads[i].wait()
    grad_attn_t = mm(w_qkv[...], grad_proj_t[...])
    tick(6)
    normed_t, inv_std = normalize(tokens_t[...].astype(f32), axis=0)
    gain_col = jnp.broadcast_to(gain[...], (LANES, width)).T[:, 0:1]
    norm_terms[...] = jnp.concatenate(
        [
            jnp.sum(grad_attn_t * normed_t, axis=1, keepdims=True),
            jnp.sum(grad_attn_t, axis=1, keepdims=True),
            grad_norm2[...].T[:, 0:2],
            jnp.zeros((width, LANES - 4), f32),
        ],
        axis=1,
    )
    result = grad_h[...].astype(f32).T + norm_back(grad_attn_t, normed_t, inv_std, gain_col, axis=0)
    sent_v[...] = mm_nt(place, result.astype(low)).astype(low)
    sent_store = pltpu.make_async_copy(sent_v, sent, sem_store.at[2])
    sent_store.start()
    tick(7)
    for p in range(MOVES - 2, MOVES):
        for k in range(3):
            move(k, p, True).wait()
    grad_h_store.wait()
    grad_proj_store.wait()
    sent_store.wait()


def attention_back(returned, slot_row, tokens_t, queries_t, keys_t, values, attended_t, inv_sums, expos, w_qkv, w_out, gain, grad_norm2, grad_bup, grad_bdown, grad_up, grad_down, hidden_out):
    rows, width = returned.shape
    toks = slot_row.shape[1]
    vm = pl.BlockSpec(memory_space=pltpu.VMEM)
    hbm = pl.BlockSpec(memory_space=pl.ANY)
    shape = jax.ShapeDtypeStruct
    return pl.pallas_call(
        attention_back_kernel,
        out_shape=(
            shape((rows, width), low),
            shape((toks, width), low),
            shape((3 * width, toks), low),
            shape((width, LANES), f32),
            shape(grad_bup.shape, f32),
            shape((1, width // lax.axis_size("dp")), f32),
            shape(grad_up.shape, f32),
            shape(grad_down.shape, f32),
            shape(hidden_out.shape, low),
        ),
        in_specs=[hbm, vm, hbm, hbm, hbm, hbm, hbm, vm, hbm, hbm, hbm, vm, vm, vm, vm, hbm, hbm, hbm],
        out_specs=(hbm, hbm, hbm, vm, vm, vm, hbm, hbm, hbm),
        scratch_shapes=[
            pltpu.VMEM((rows, width), low),
            pltpu.VMEM((width, toks), low),
            pltpu.VMEM((width, toks), low),
            pltpu.VMEM((width, toks), low),
            pltpu.VMEM((toks, width), low),
            pltpu.VMEM((width, toks), low),
            pltpu.VMEM(w_qkv.shape, low),
            pltpu.VMEM(w_out.shape, low),
            pltpu.VMEM((HEADS, toks, toks), low),
            pltpu.VMEM((width, toks), low),
            pltpu.VMEM((toks, width), low),
            pltpu.VMEM((3 * width, toks), low),
            pltpu.VMEM((rows, width), low),
            pltpu.VMEM((2, grad_up.shape[0] // MOVES, grad_up.shape[1]), low),
            pltpu.VMEM((2, grad_down.shape[0] // MOVES, grad_down.shape[1]), low),
            pltpu.VMEM((2, rows // MOVES, width), low),
            pltpu.VMEM((2, grad_up.shape[0] // MOVES, grad_up.shape[1]), f32),
            pltpu.VMEM((2, grad_down.shape[0] // MOVES, grad_down.shape[1]), f32),
            pltpu.VMEM((2, rows // MOVES, width), low),
            pltpu.SemaphoreType.DMA((8,)),
            pltpu.SemaphoreType.DMA((HEADS // 4,)),
            pltpu.SemaphoreType.DMA((3,)),
            pltpu.SemaphoreType.DMA((6, 2)),
        ],
        compiler_params=pltpu.CompilerParams(has_side_effects=True, vmem_limit_bytes=60 * 1024 * 1024),
    )(returned, slot_row, tokens_t, queries_t, keys_t, values, attended_t, inv_sums, expos, w_qkv, w_out, gain, grad_norm2, grad_bup, grad_bdown, grad_up, grad_down, hidden_out)


def expert_kernel(
    n,
    cap,
    sent,
    grads,
    hids,
    live,
    up_hbm,
    up_bias,
    down_hbm,
    down_bias,
    gain,
    bias,
    returned,
    hidden_out,
    grad_up,
    grad_down,
    grad_bup,
    grad_bdown,
    grad_norm,
    rows_in,
    ffn_in,
    grad_rows,
    up,
    down,
    hid,
    act,
    pre_grad,
    part_out,
    part_in,
    back,
    mine,
    tile,
    tile_down,
    sem_send,
    sem_recv,
    sem_back_send,
    sem_back_recv,
    sem_pair,
    sem_load,
    sem_store,
):
    me_d = lax.axis_index("dp")
    me_e = lax.axis_index("expert")
    rows = rows_in.shape[0]
    width = rows_in.shape[1]
    units = up.shape[1]
    block = rows // PARTS
    many = n // PARTS
    partner = (1 - me_d, me_e)

    def base_of(part):
        return pl.multiple_of(((me_e // many) ^ part) * block, block)

    def slot_copy(i):
        peer = me_e ^ i
        return pltpu.make_async_remote_copy(
            src_ref=sent.at[pl.ds(pl.multiple_of(peer * cap, cap), cap)],
            dst_ref=rows_in.at[pl.ds(pl.multiple_of(me_e * cap, cap), cap)],
            send_sem=sem_send.at[i],
            recv_sem=sem_recv.at[i],
            device_id=(me_d, peer),
            device_id_type=MESH_ID,
        )

    def own_slots():
        own = pl.ds(pl.multiple_of(me_e * cap, cap), cap)
        return pltpu.make_async_copy(sent.at[own], rows_in.at[own], sem_recv.at[0])

    def back_copy(i):
        peer = me_e ^ i
        return pltpu.make_async_remote_copy(
            src_ref=back.at[pl.ds(pl.multiple_of(peer * cap, cap), cap)],
            dst_ref=returned.at[pl.ds(pl.multiple_of(me_e * cap, cap), cap)],
            send_sem=sem_back_send.at[i],
            recv_sem=sem_back_recv.at[i],
            device_id=(me_d, peer),
            device_id_type=MESH_ID,
        )

    def own_back():
        own = pl.ds(pl.multiple_of(me_e * cap, cap), cap)
        return pltpu.make_async_copy(back.at[own], returned.at[own], sem_back_recv.at[0])

    def pair_copy(src, dst, kind, part):
        return pltpu.make_async_remote_copy(
            src_ref=src,
            dst_ref=dst,
            send_sem=sem_pair.at[kind - 1, 0, part],
            recv_sem=sem_pair.at[kind - 1, 1, part],
            device_id=partner,
            device_id_type=MESH_ID,
        )

    def ffn_pair(part):
        return pair_copy(ffn_in.at[part, 0], ffn_in.at[part, 1], 1, part)

    def part_pair(part):
        return pair_copy(part_out.at[part], part_in.at[part], 2, part)

    def out_pair(part):
        return pair_copy(part_out.at[PARTS + part], part_in.at[PARTS + part], 3, part)

    def hid_load(unit):
        part, k = part_of(unit), core_of(unit)
        here = pl.ds(base_of(part), block)
        return pltpu.make_async_copy(hids.at[k, here], hid.at[part, k], sem_load.at[2 + unit])

    def grads_load(unit):
        part, k = part_of(unit), core_of(unit)
        here = pl.ds(base_of(part), block)
        return pltpu.make_async_copy(grads.at[k, here], grad_rows.at[part, k], sem_load.at[2 + 2 * PARTS + unit])

    def part_of(unit):
        return lax.rem(unit, PARTS)

    def core_of(unit):
        return me_d ^ (unit // PARTS)

    up_load = pltpu.make_async_copy(up_hbm, up, sem_load.at[0])
    down_load = pltpu.make_async_copy(down_hbm, down, sem_load.at[1])
    own_slots().start()

    @pl.when(me_d == 0)
    def _():
        down_load.start()
        for unit in range(2 * PARTS):
            grads_load(unit).start()
        up_load.start()

    @pl.when(me_d == 1)
    def _():
        up_load.start()
        hid_load(0).start()
        grads_load(0).start()

    barrier = pltpu.get_barrier_semaphore()
    greet_peers(me_d, me_e, n)

    @pl.when(me_d == 0)
    def _():
        pl.semaphore_wait(barrier, n - 1)
        greet_partner(me_d, me_e)

    @pl.when(me_d == 1)
    def _():
        pl.semaphore_wait(barrier, n)
        greet_partner(me_d, me_e)

    def start_slots(i, carry):
        slot_copy(i).start()
        return carry

    lax.fori_loop(1, n, start_slots, 0)
    grad_norm[...] = jnp.zeros_like(grad_norm)
    up_load.wait()

    @pl.when(me_d == 1)
    def _():
        down_load.start()
        for unit in range(1, 2 * PARTS):
            hid_load(unit).start()
            grads_load(unit).start()


    def stats(base):
        return normalize(rows_in[pl.ds(base, block), :].astype(f32))

    def arrive(part):
        @pl.when(part == 0)
        def _():
            own_slots().wait()

        @pl.when(part > 0)
        def _():
            slot_copy(part * many).wait()

        def wait_slots(j, c):
            slot_copy(part * many + j).wait()
            return c

        lax.fori_loop(1, many, wait_slots, 0)
        normed, _ = stats(base_of(part))
        ffn_in[part, 0] = (normed * gain[...] + bias[...]).astype(low)

    @pl.when(me_d == 0)
    def _():
        def arrive_all(part, carry):
            arrive(part)

            @pl.when(part == 0)
            def _():
                pl.semaphore_wait(barrier, 1)

            ffn_pair(part).start()
            return carry

        def hidden_grad(unit, carry):
            part, k = part_of(unit), core_of(unit)
            grads_load(unit).wait()
            hid[part, k] = mm_nt(grad_rows[part, k], down[...]).astype(low)
            return carry

        down_load.wait()
        lax.fori_loop(0, 2 * PARTS, hidden_grad, 0)
        lax.fori_loop(0, PARTS, arrive_all, 0)

    def hidden(part, k):
        def before(cols):
            return mm(ffn_in[part, k], up[:, cols]) + up_bias[:, cols]

        def after(cols, pre):
            a, slope = gelu_parts(pre)
            act[part, k, :, cols] = a.astype(low)
            pre_grad[part, k, :, cols] = (hid[part, k, :, cols].astype(f32) * slope).astype(low)

        staged([pl.ds(f * WIDE, WIDE) for f in range(units // WIDE)], before, after)

    def send_back(unit):
        part = part_of(unit)
        base = base_of(part)
        part_pair(part).wait_recv()
        grad_ffn = mine[lax.rem(unit, 2)] + part_in[part].astype(f32)
        normed, inv_std = stats(base)
        grad_norm[0:1, :] += jnp.sum(grad_ffn * normed, axis=0, keepdims=True)
        grad_norm[1:2, :] += jnp.sum(grad_ffn, axis=0, keepdims=True)
        result = grad_rows[part, 0].astype(f32) + norm_back(grad_ffn, normed, inv_std, gain[...])
        back[pl.ds(base, block), :] = result.astype(low)

        @pl.when(part == 0)
        def _():
            own_back().start()

        @pl.when(part > 0)
        def _():
            back_copy(part * many).start()

        def start_back(j, c):
            back_copy(part * many + j).start()
            return c

        lax.fori_loop(1, many, start_back, 0)

    def work(unit, carry):
        part, k = part_of(unit), core_of(unit)
        ahead = unit + 1 - PARTS

        @pl.when((me_d == 1) & (ahead >= 0) & (ahead < PARTS))
        def _():
            arrive(ahead)
            ffn_pair(ahead).start()

        @pl.when(k == 1)
        def _():
            ffn_pair(part).wait_recv()

        @pl.when(me_d == 1)
        def _():
            hid_load(unit).wait()
            grads_load(unit).wait()

        hidden(part, k)
        slot = lax.rem(unit, 2)
        mine[slot] = mm_nt(pre_grad[part, k], up[...])

        @pl.when((unit == 0) & (me_d == 1))
        def _():
            down_load.wait()

        @pl.when(k == 1)
        def _():
            part_out[part] = mine[slot].astype(low)
            part_pair(part).start()
            part_out[PARTS + part] = mm(act[part, 1], down[...]).astype(low)
            out_pair(part).start()

        @pl.when((unit > 0) & (core_of(unit - 1) == 0))
        def _():
            send_back(unit - 1)

        return carry

    lax.fori_loop(0, 2 * PARTS, work, 0)

    @pl.when(me_d == 1)
    def _():
        send_back(2 * PARTS - 1)

    def output_own(part, carry):
        base = base_of(part)
        here = pl.ds(base, block)
        product = mm(act[part, 0], down[...])
        out_pair(part).wait_recv()
        total = rows_in[here, :].astype(f32) + product + part_in[PARTS + part].astype(f32) + down_bias[...]
        rows_in[here, :] = (total * live[here, :]).astype(low)
        pltpu.make_async_copy(rows_in.at[here], hidden_out.at[here], sem_store.at[part]).start()
        return carry

    lax.fori_loop(0, PARTS, output_own, 0)

    ones = jnp.ones((8, PARTS * 2 * block), low)
    all_act = act.reshape(PARTS * 2 * block, units)
    all_pre = pre_grad.reshape(PARTS * 2 * block, units)
    all_in = ffn_in.reshape(PARTS * 2 * block, width)
    all_grad = grad_rows.reshape(PARTS * 2 * block, width)
    grad_bup[...] = mm(ones, all_pre[...])[0:1]
    grad_bdown[...] = mm(ones, all_grad[...])[0:1]

    def up_store(f, slot):
        cols = pl.ds(pl.multiple_of(f * UNITS, UNITS), UNITS)
        return pltpu.make_async_copy(tile.at[slot], grad_up.at[:, cols], sem_store.at[PARTS + slot])

    def down_store(f, slot):
        cols = pl.ds(pl.multiple_of(f * UNITS, UNITS), UNITS)
        return pltpu.make_async_copy(
            tile_down.at[slot], grad_down.at[cols, :], sem_store.at[PARTS + 2 + slot]
        )

    def weights(f, carry):
        slot = lax.rem(f, 2)
        cols = pl.ds(pl.multiple_of(f * UNITS, UNITS), UNITS)

        @pl.when(f >= 2)
        def _():
            up_store(f, slot).wait()
            down_store(f, slot).wait()

        tile[slot] = mm_tn(all_in[...], all_pre[:, cols]).astype(low)
        up_store(f, slot).start()
        tile_down[slot] = mm_tn(all_act[:, cols], all_grad[...]).astype(low)
        down_store(f, slot).start()
        return carry

    lax.fori_loop(0, units // UNITS, weights, 0)
    for slot in range(2):
        up_store(0, slot).wait()
        down_store(0, slot).wait()
    for part in range(PARTS):
        pltpu.make_async_copy(
            rows_in.at[pl.ds(0, block)], hidden_out.at[pl.ds(0, block)], sem_store.at[part]
        ).wait()
    own_back().wait()
    for part in range(PARTS):
        ffn_pair(part).wait_send()
        part_pair(part).wait_send()
        out_pair(part).wait_send()

    def wait_back(i, carry):
        back_copy(i).wait()
        return carry

    lax.fori_loop(1, n, wait_back, 0)


def expert_block(sent, grads, hids, live, up, up_bias, down, down_bias, gain, bias):
    n = lax.axis_size("expert")
    rows, width = sent.shape
    units = up.shape[1]
    cap = rows // n
    block = rows // PARTS
    vm = pl.BlockSpec(memory_space=pltpu.VMEM)
    hbm = pl.BlockSpec(memory_space=pl.ANY)
    return pl.pallas_call(
        functools.partial(expert_kernel, n, cap),
        out_shape=(
            jax.ShapeDtypeStruct((rows, width), low),
            jax.ShapeDtypeStruct((rows, width), low),
            jax.ShapeDtypeStruct((width, units), low),
            jax.ShapeDtypeStruct((units, width), low),
            jax.ShapeDtypeStruct((1, units), f32),
            jax.ShapeDtypeStruct((1, width), f32),
            jax.ShapeDtypeStruct((8, width), f32),
        ),
        in_specs=[hbm, hbm, hbm, vm, hbm, vm, hbm, vm, vm, vm],
        out_specs=(hbm, hbm, hbm, hbm, vm, vm, vm),
        scratch_shapes=[
            pltpu.VMEM((rows, width), low),
            pltpu.VMEM((PARTS, 2, block, width), low),
            pltpu.VMEM((PARTS, 2, block, width), low),
            pltpu.VMEM((width, units), low),
            pltpu.VMEM((units, width), low),
            pltpu.VMEM((PARTS, 2, block, units), low),
            pltpu.VMEM((PARTS, 2, block, units), low),
            pltpu.VMEM((PARTS, 2, block, units), low),
            pltpu.VMEM((2 * PARTS, block, width), low),
            pltpu.VMEM((2 * PARTS, block, width), low),
            pltpu.VMEM((rows, width), low),
            pltpu.VMEM((2, block, width), f32),
            pltpu.VMEM((2, width, UNITS), low),
            pltpu.VMEM((2, UNITS, width), low),
            pltpu.SemaphoreType.DMA((n,)),
            pltpu.SemaphoreType.DMA((n,)),
            pltpu.SemaphoreType.DMA((n,)),
            pltpu.SemaphoreType.DMA((n,)),
            pltpu.SemaphoreType.DMA((3, 2, PARTS)),
            pltpu.SemaphoreType.DMA((2 + 4 * PARTS,)),
            pltpu.SemaphoreType.DMA((PARTS + 4,)),
        ],
        compiler_params=pltpu.CompilerParams(
            collective_id=1, has_side_effects=True, vmem_limit_bytes=62 * 1024 * 1024
        ),
    )(sent, grads, hids, live, up, up_bias, down, down_bias, gain, bias)


STREAMS = 2
GROUPS = 3


def ending_kernel(
    n,
    cap,
    chunks,
    sent,
    attn_in_hbm,
    grad_proj_hbm,
    attended_hbm,
    grad_h_hbm,
    norm_terms,
    grad_in,
    grad_qkv,
    grad_wout,
    grad_norms,
    attn_in_t,
    grad_proj_t,
    attended_t,
    grad_h,
    made,
    total,
    landed,
    sem_send,
    sem_recv,
    sem_load,
    sem_pair,
    sem_step,
):
    me_d = lax.axis_index("dp")
    me_e = lax.axis_index("expert")
    partner = (1 - me_d, me_e)
    bits = n.bit_length() - 1
    half = n // 2
    width = grad_h.shape[1]
    each = made.shape[1]

    def offset(order, p):
        k = 0
        for j, b in enumerate(order):
            k = k + lax.rem(p // (1 << (bits - 1 - j)), 2) * (1 << b)
        return k

    def slot_copy(i):
        peer = me_e ^ i
        return pltpu.make_async_remote_copy(
            src_ref=sent.at[pl.ds(pl.multiple_of(peer * cap, cap), cap)],
            dst_ref=grad_in.at[pl.ds(pl.multiple_of(me_e * cap, cap), cap)],
            send_sem=sem_send.at[i],
            recv_sem=sem_recv.at[i],
            device_id=(me_d, peer),
            device_id_type=MESH_ID,
        )

    def own_slots():
        here = pl.ds(pl.multiple_of(me_e * cap, cap), cap)
        return pltpu.make_async_copy(sent.at[here], grad_in.at[here], sem_recv.at[0])

    def pair_copy(c, q):
        size = chunks[c][2]
        here = pl.ds(q * half, half)
        return pltpu.make_async_remote_copy(
            src_ref=total.at[c, 1, here, :, 0:size],
            dst_ref=landed.at[c, here, :, 0:size],
            send_sem=sem_pair.at[0, c, q],
            recv_sem=sem_pair.at[1, c, q],
            device_id=partner,
            device_id_type=MESH_ID,
        )

    def step_copy(c, j):
        order, _, size = chunks[c]
        many = n >> (j + 1)
        start = n + sum(n >> (i + 1) for i in range(j))
        return pltpu.make_async_remote_copy(
            src_ref=total.at[c, 0, pl.ds(many, many), :, 0:size],
            dst_ref=landed.at[c, pl.ds(start, many), :, 0:size],
            send_sem=sem_step.at[0, c, j],
            recv_sem=sem_step.at[1, c, j],
            device_id=(me_d, me_e ^ (1 << order[j])),
            device_id_type=MESH_ID,
        ), many, start

    loads = [
        pltpu.make_async_copy(a, b, sem_load.at[i])
        for i, (a, b) in enumerate(
            (
                (attn_in_hbm, attn_in_t),
                (grad_proj_hbm, grad_proj_t),
                (attended_hbm, attended_t),
                (grad_h_hbm, grad_h),
            )
        )
    ]
    for load in loads:
        load.start()
    own_slots().start()
    greet(me_d, me_e, n)

    def start_slots(i, carry):
        slot_copy(i).start()
        return carry

    lax.fori_loop(1, n, start_slots, 0)
    for load in loads:
        load.wait()

    def pieces(c):
        _, begin, size = chunks[c]
        edges = (0, 3 * width, 4 * width, 4 * width + LANES)
        for kind in range(3):
            a, b = max(begin, edges[kind]), min(begin + size, edges[kind + 1])
            if a < b:
                yield kind, slice(a - edges[kind], b - edges[kind]), slice(a - begin, b - begin)

    def make(c):
        order, _, size = chunks[c]
        for kind, source, target in pieces(c):
            if kind == 0:
                term = mm_nt(attn_in_t[...], grad_proj_t[source, :])
            elif kind == 1:
                term = mm(attended_t[...], grad_h[:, source])
            else:
                term = norm_terms[...]
            made[:, :, target] = term.reshape(made.shape[0], each, term.shape[1])

        def arrange(p, carry):
            owner = me_e ^ offset(order, p)
            total[c, 0, p, :, 0:size] = made[me_d * n + owner, :, 0:size].astype(low)
            total[c, 1, p, :, 0:size] = made[(1 - me_d) * n + owner, :, 0:size].astype(low)
            return carry

        lax.fori_loop(0, n, arrange, 0)
        pair_copy(c, 1).start()
        pair_copy(c, 0).start()

    def add(c, p, q):
        size = chunks[c][2]
        return total[c, 0, p, :, 0:size].astype(f32) + landed[c, q, :, 0:size].astype(f32)

    def add_all(c, first, many, start):
        def add_one(p, carry):
            total[c, 0, p, :, 0 : chunks[c][2]] = add(c, p, start + p).astype(low)
            return carry

        lax.fori_loop(first, first + many, add_one, 0)

    def stage(c, j):
        if j == 0:
            pair_copy(c, 1).wait()
            add_all(c, half, half, 0)
            step_copy(c, 0)[0].start()
            pair_copy(c, 0).wait()
            add_all(c, 0, half, 0)
            return
        copy, many, start = step_copy(c, j - 1)
        copy.wait()
        if many > 1:
            add_all(c, 0, many, start)
            step_copy(c, j)[0].start()
        else:
            both = add(c, 0, start)
            for kind, target, source in pieces(c):
                (grad_qkv, grad_wout, grad_norms)[kind][:, target] = both[:, source]

    groups = len(chunks) // STREAMS
    for wave in range(groups + bits + 1):
        for g in range(groups):
            for c in range(g * STREAMS, (g + 1) * STREAMS):
                if wave == g:
                    make(c)
                if 0 <= wave - 1 - g <= bits:
                    stage(c, wave - 1 - g)
    own_slots().wait()

    def wait_slots(i, carry):
        slot_copy(i).wait()
        return carry

    lax.fori_loop(1, n, wait_slots, 0)


def ending(sent, attn_in_t, grad_proj_t, attended_t, grad_h, norm_terms):
    n = lax.axis_size("expert")
    owners = n * lax.axis_size("dp")
    rows, width = sent.shape
    each = width // owners
    bits = n.bit_length() - 1
    tiles = 4 * width // LANES + 1
    count = GROUPS * STREAMS
    chunks = []
    begin = 0
    for c in range(count):
        size = (tiles // count + (1 if c < tiles % count else 0)) * LANES
        turn = [(c + k) % STREAMS for k in range(STREAMS)]
        chunks.append((turn + list(range(STREAMS, bits)), begin, size))
        begin += size
    widest = max(size for _, _, size in chunks)
    vm = pl.BlockSpec(memory_space=pltpu.VMEM)
    hbm = pl.BlockSpec(memory_space=pl.ANY)
    shape = jax.ShapeDtypeStruct
    return pl.pallas_call(
        functools.partial(ending_kernel, n, rows // n, tuple(chunks)),
        out_shape=(
            shape((rows, width), low),
            shape((each, 3 * width), f32),
            shape((each, width), f32),
            shape((each, LANES), f32),
        ),
        in_specs=[hbm, hbm, hbm, hbm, hbm, vm],
        out_specs=(hbm, vm, vm, vm),
        scratch_shapes=[
            pltpu.VMEM(attn_in_t.shape, low),
            pltpu.VMEM(grad_proj_t.shape, low),
            pltpu.VMEM(attended_t.shape, low),
            pltpu.VMEM(grad_h.shape, low),
            pltpu.VMEM((owners, each, widest), f32),
            pltpu.VMEM((count, 2, n, each, widest), low),
            pltpu.VMEM((count, 2 * n, each, widest), low),
            pltpu.SemaphoreType.DMA((n,)),
            pltpu.SemaphoreType.DMA((n,)),
            pltpu.SemaphoreType.DMA((4,)),
            pltpu.SemaphoreType.DMA((2, count, 2)),
            pltpu.SemaphoreType.DMA((2, count, bits)),
        ],
        compiler_params=pltpu.CompilerParams(
            collective_id=2, has_side_effects=True, vmem_limit_bytes=60 * 1024 * 1024
        ),
    )(sent, attn_in_t, grad_proj_t, attended_t, grad_h, norm_terms)


def on_device(
    hidden_in,
    buckets,
    expert_of_bucket,
    lengths,
    norm1_gain,
    norm1_bias,
    w_qkv,
    w_out,
    norm2_gain,
    norm2_bias,
    w_up,
    b_up,
    w_down,
    b_down,
    grad_out,
):
    (
        sent,
        grads,
        hids,
        live,
        attn_in_t,
        tokens_t,
        queries_t,
        keys_t,
        values,
        attended_t,
        inv_sums,
        slot_row,
        expos,
    ) = starting(
        hidden_in,
        grad_out,
        buckets.reshape(1, -1),
        expert_of_bucket[None],
        lengths,
        norm1_gain[None],
        norm1_bias[None],
        w_qkv,
        w_out,
        w_down[0],
    )
    returned, hidden_out, grad_up, grad_down, grad_bup, grad_bdown, grad_norm2 = expert_block(
        sent, grads, hids, live, w_up[0], b_up, w_down[0], b_down, norm2_gain[None], norm2_bias[None]
    )
    sent_grad, grad_h, grad_proj_t, norm_terms, grad_bup, grad_bdown, grad_up, grad_down, hidden_out = attention_back(
        returned,
        slot_row,
        tokens_t,
        queries_t,
        keys_t,
        values,
        attended_t,
        inv_sums,
        expos,
        w_qkv,
        w_out,
        norm1_gain[None],
        grad_norm2,
        grad_bup,
        grad_bdown,
        grad_up,
        grad_down,
        hidden_out,
    )
    grad_in, grad_qkv, grad_wout, grad_norms = ending(
        sent_grad, attn_in_t, grad_proj_t, attended_t, grad_h, norm_terms
    )
    return (
        hidden_out,
        grad_in,
        grad_qkv,
        grad_wout,
        grad_norms[:, 0],
        grad_norms[:, 1],
        grad_norms[:, 2],
        grad_norms[:, 3],
        grad_up[None],
        grad_bup,
        grad_down[None],
        grad_bdown,
    )


def solution(mesh):
    return jax.shard_map(
        on_device,
        mesh=mesh,
        in_specs=(
            P(("dp", "expert"), None),
            P(("dp", "expert"), None),
            P(),
            P(("dp", "expert"), None),
            P(),
            P(),
            P(),
            P(),
            P(),
            P(),
            P("expert", None, "dp"),
            P("expert", "dp"),
            P("expert", "dp", None),
            P("expert", None),
            P(("dp", "expert"), None),
        ),
        out_specs=(
            P(("dp", "expert"), None),
            P(("dp", "expert"), None),
            P(("dp", "expert"), None),
            P(("dp", "expert"), None),
            P(("dp", "expert")),
            P(("dp", "expert")),
            P(("dp", "expert")),
            P(("dp", "expert")),
            P("expert", None, "dp"),
            P("expert", "dp"),
            P("expert", "dp", None),
            P("expert", "dp"),
        ),
        check_vma=False,
    )
```

```python
import functools

import jax
import jax.numpy as jnp
from jax import lax
from jax.experimental import pallas as pl
from jax.experimental.pallas import tpu as pltpu
from jax.sharding import PartitionSpec as P

HEADS = 16
HEAD_DIM = 64


norm_eps = 1e-05
masked_score = -1e30
root_half = 0.7071067811865476
inv_root_tau = 0.3989422804014327

MESH_ID = pl.DeviceIdType.MESH
PARTS = 4
UNITS = 256
WIDE = 512
LANES = 128
QUERIES = 256
PAIR = 2 * HEAD_DIM
scale_val = HEAD_DIM ** (-0.5)
low = jnp.bfloat16
f32 = jnp.float32


def mm(a, b):
    return jnp.dot(a, b, preferred_element_type=f32)


def mm_nt(a, b):
    return lax.dot_general(a, b, (((1,), (1,)), ((), ())), preferred_element_type=f32)


def mm_tn(a, b):
    return lax.dot_general(a, b, (((0,), (0,)), ((), ())), preferred_element_type=f32)


def normalize(values, axis=-1):
    mean_val = jnp.mean(values, axis=axis, keepdims=True)
    centered = values - mean_val
    variance = jnp.mean(centered * centered, axis=axis, keepdims=True)
    inv_std = lax.rsqrt(variance + norm_eps)
    return (centered * inv_std, inv_std)


def norm_back(grad_normed, normed, inv_std, gain_vec, axis=-1):
    scaled = grad_normed * gain_vec
    mean_grad = jnp.mean(scaled, axis=axis, keepdims=True)
    mean_cross = jnp.mean(scaled * normed, axis=axis, keepdims=True)
    return inv_std * (scaled - mean_grad - normed * mean_cross)


def gelu_parts(pre):
    bell = jnp.exp(-0.5 * pre * pre)
    den = 1.0 + (0.3275911 * root_half) * jnp.abs(pre)
    t = pl.reciprocal(den, approx=True)
    t = t * (2.0 - den * t)
    tail = t * (
        0.5 * 0.254829592
        + t * (0.5 * -0.284496736 + t * (0.5 * 1.421413741 + t * (0.5 * -1.453152027 + t * (0.5 * 1.061405429))))
    )
    tail = tail * bell
    phi = jnp.where(pre >= 0.0, 1.0 - tail, tail)
    return pre * phi, phi + pre * (inv_root_tau * bell)


def greet_peers(me_d, me_e, n):
    barrier = pltpu.get_barrier_semaphore()

    def signal(i, carry):
        pl.semaphore_signal(barrier, inc=1, device_id=(me_d, me_e ^ i), device_id_type=MESH_ID)
        return carry

    lax.fori_loop(1, n, signal, 0)


def greet_partner(me_d, me_e):
    pl.semaphore_signal(
        pltpu.get_barrier_semaphore(), inc=1, device_id=(1 - me_d, me_e), device_id_type=MESH_ID
    )


def staged(units, *stages):
    held = [None] * len(units)
    for step in range(len(units) + len(stages) - 1):
        for k, stage in enumerate(stages):
            i = step - k
            if 0 <= i < len(units):
                held[i] = stage(units[i]) if k == 0 else stage(units[i], held[i])


def start_kernel(
    n,
    cap,
    hidden,
    grad_out,
    buckets,
    expert_of,
    lengths,
    gain,
    bias,
    w_qkv_hbm,
    w_out_hbm,
    down_hbm,
    sent,
    grads,
    hids,
    live,
    attn_in_hbm,
    tokens_hbm,
    queries_hbm,
    keys_hbm,
    values_hbm,
    attended_hbm,
    inv_sums,
    slot_row,
    expos,
    arrived,
    w_qkv,
    w_out,
    down,
    grad_raw,
    grad_v,
    grad_p,
    hid_v,
    attn_in_t,
    tokens_t,
    queries_t,
    keys_t,
    values,
    attended_t,
    attn_in_v,
    proj,
    values_t,
    allow,
    tokens,
    expo_v,
    sent_v,
    counts_out,
    counts_in,
    sem_send,
    sem_recv,
    sem_count_send,
    sem_count_recv,
    sem_pair,
    sem_load,
    sem_store,
    sem_keep,
    sem_turn,
):
    me_d = lax.axis_index("dp")
    me_e = lax.axis_index("expert")
    partner = (1 - me_d, me_e)
    rows, width = arrived.shape
    toks = buckets.shape[1]
    lanes = counts_out.shape[1]

    def slot_copy(i):
        peer = me_e ^ i
        return pltpu.make_async_remote_copy(
            src_ref=hidden.at[pl.ds(pl.multiple_of(peer * cap, cap), cap)],
            dst_ref=arrived.at[pl.ds(pl.multiple_of(me_e * cap, cap), cap)],
            send_sem=sem_send.at[i],
            recv_sem=sem_recv.at[i],
            device_id=(me_d, peer),
            device_id_type=MESH_ID,
        )

    def own_slots():
        here = pl.ds(pl.multiple_of(me_e * cap, cap), cap)
        return pltpu.make_async_copy(hidden.at[here], arrived.at[here], sem_recv.at[0])

    def count_copy(i):
        return pltpu.make_async_remote_copy(
            src_ref=counts_out,
            dst_ref=counts_in.at[me_e],
            send_sem=sem_count_send.at[i],
            recv_sem=sem_count_recv.at[i],
            device_id=(me_d, me_e ^ i),
            device_id_type=MESH_ID,
        )

    grad_load = pltpu.make_async_copy(grad_out, grad_raw, sem_load.at[0])
    qkv_load = pltpu.make_async_copy(w_qkv_hbm, w_qkv, sem_load.at[1])
    out_load = pltpu.make_async_copy(w_out_hbm, w_out, sem_load.at[2])
    down_load = pltpu.make_async_copy(down_hbm, down, sem_load.at[3])
    pair_grads_store = pltpu.make_async_copy(grad_p, grads.at[1], sem_store.at[2])
    def keep(i, g):
        source, target = (
            (attn_in_t, attn_in_hbm),
            (tokens_t, tokens_hbm),
            (queries_t, queries_hbm),
            (keys_t, keys_hbm),
            (attended_t, attended_hbm),
            (values, values_hbm),
        )[i]
        here = pl.ds(pl.multiple_of(g * 2 * PAIR, 2 * PAIR), 2 * PAIR)
        if i == 5:
            return pltpu.make_async_copy(source.at[:, here], target.at[:, here], sem_keep.at[i, g])
        return pltpu.make_async_copy(source.at[here], target.at[here], sem_keep.at[i, g])

    def hid_store(k):
        return pltpu.make_async_copy(hid_v.at[k], hids.at[k], sem_store.at[3 + k])

    def hidden_grad(k, grad_ref):
        def tile(i, carry):
            here = pl.ds(pl.multiple_of((i // 2) * WIDE, WIDE), WIDE)
            some = pl.ds(pl.multiple_of(lax.rem(i, 2) * (rows // 2), rows // 2), rows // 2)
            hid_v[k, some, here] = mm_nt(grad_ref[some, :], down[here, :]).astype(low)
            return carry

        lax.fori_loop(0, 2 * (down.shape[0] // WIDE), tile, 0)
        hid_store(k).start()

    grad_store = pltpu.make_async_copy(grad_v, grads.at[0], sem_store.at[0])
    grad_pair = pltpu.make_async_remote_copy(
        src_ref=grad_v,
        dst_ref=grad_p,
        send_sem=sem_pair.at[0],
        recv_sem=sem_pair.at[1],
        device_id=partner,
        device_id_type=MESH_ID,
    )

    def start_slots(i, carry):
        slot_copy(i).start()
        return carry

    grad_load.start()

    @pl.when(me_d == 1)
    def _():
        down_load.start()

    greet_peers(me_d, me_e, n)
    greet_partner(me_d, me_e)
    lane_ids = lax.broadcasted_iota(jnp.int32, (toks, lanes), 1)
    bucket = jnp.broadcast_to(buckets[...], (lanes, toks)).T[:, 0:n]
    bucket_hot = (bucket == lane_ids[:, 0:n]).astype(f32).astype(low)
    serves_t = (expert_of[...] == lax.broadcasted_iota(jnp.int32, (lanes, n), 0)).astype(f32).astype(low)
    expert_hot = mm_nt(bucket_hot, serves_t)
    counts_out[...] = jnp.broadcast_to(jnp.sum(expert_hot, axis=0, keepdims=True), counts_out.shape)
    counts_in[me_e] = counts_out[...]

    def start_counts(i, carry):
        count_copy(i).start()
        return carry

    pl.semaphore_wait(pltpu.get_barrier_semaphore(), n)
    lax.fori_loop(1, n, start_counts, 0)
    lax.fori_loop(1, n // 2, start_slots, 0)

    @pl.when(me_d == 0)
    def _():
        lax.fori_loop(n // 2, n, start_slots, 0)

    own_slots().start()
    qkv_load.start()
    out_load.start()

    row_ids = lax.broadcasted_iota(jnp.int32, (toks, toks), 0)
    col_ids = lax.broadcasted_iota(jnp.int32, (toks, toks), 1)
    earlier = (col_ids < row_ids).astype(f32).astype(low)
    before = mm(earlier, expert_hot.astype(low))
    slot = jnp.sum(expert_hot * (before + (lane_ids * cap).astype(f32)), axis=1, keepdims=True)
    slot_row[...] = jnp.broadcast_to(slot, (toks, lanes)).T[0:8, :].astype(jnp.int32)
    ends = jnp.zeros((1, toks), jnp.int32)
    begin = jnp.zeros((1, toks), jnp.int32)
    places = lax.broadcasted_iota(jnp.int32, (1, toks), 1)
    for s in range(lengths.shape[1]):
        ends = ends + lengths[0:1, s : s + 1]
        begin = jnp.where(places >= ends, ends, begin)
    allow[...] = jnp.where(jnp.logical_and(row_ids <= col_ids, row_ids >= begin), 0.0, masked_score)

    def wait_counts(i, carry):
        count_copy(i).wait()
        return carry

    lax.fori_loop(1, n, wait_counts, 0)
    grad_load.wait()

    def mark(s, carry):
        here = pl.ds(pl.multiple_of(s * cap, cap), cap)
        mine = lax.broadcasted_iota(jnp.int32, (1, lanes), 1) == me_e
        count = jnp.sum(jnp.where(mine, counts_in[s, 0:1, :], 0.0), axis=1, keepdims=True)
        taken = (lax.broadcasted_iota(jnp.int32, (cap, 1), 0).astype(f32) < count).astype(f32)
        live[here, :] = taken
        grad_v[here, :] = (grad_raw[here, :].astype(f32) * taken).astype(low)
        return carry

    lax.fori_loop(0, n, mark, 0)
    grad_store.start()
    grad_pair.start()
    @pl.when(me_d == 0)
    def _():
        def wait_sent(i, carry):
            slot_copy(i).wait_send()
            return carry

        lax.fori_loop(n // 2, n, wait_sent, 0)
        pl.semaphore_signal(sem_turn, inc=1, device_id=partner, device_id_type=MESH_ID)

    @pl.when(me_d == 1)
    def _():
        pl.semaphore_wait(sem_turn, 1)
        lax.fori_loop(n // 2, n, start_slots, 0)

    grad_pair.wait()
    pair_grads_store.start()

    @pl.when(me_d == 1)
    def _():
        down_load.wait()
        hidden_grad(0, grad_v)
        hidden_grad(1, grad_p)


    own_slots().wait()

    def wait_slots(i, carry):
        slot_copy(i).wait_recv()
        return carry

    lax.fori_loop(1, n, wait_slots, 0)

    pick = (slot.astype(jnp.int32) == lax.broadcasted_iota(jnp.int32, (toks, rows), 1)).astype(f32).astype(low)
    tokens[...] = mm(pick, arrived[...])
    normed, _ = normalize(tokens[...])
    attn_in = (normed * gain[...] + bias[...]).astype(low)
    attn_in_v[...] = attn_in
    qkv_load.wait()
    step = width // 4
    for c in range(3 * width // step):
        here = slice(c * step, (c + 1) * step)
        part = mm(attn_in, w_qkv[:, here])
        if c * step < width:
            part = part.astype(low).astype(f32) * scale_val
        proj[:, here] = part.astype(low)
    values_t[...] = proj[:, 2 * width : 3 * width].T

    def expo_store(g):
        here = pl.ds(pl.multiple_of(4 * g, 4), 4)
        return pltpu.make_async_copy(expo_v.at[here], expos.at[here], sem_store.at[5 + g])

    in_first = lax.broadcasted_iota(jnp.int32, (1, PAIR), 1) < HEAD_DIM

    def head_group(g, carry):
        units = [
            (2 * g + pair, h, q) for pair in range(2) for h in range(2) for q in range(toks // QUERIES)
        ]

        def score(unit):
            p, h, q = unit
            first = pl.multiple_of(p * PAIR, PAIR)
            upto = (q + 1) * QUERIES
            here = slice(q * QUERIES, upto)
            mine = in_first if h == 0 else jnp.logical_not(in_first)
            query = jnp.where(mine, proj[here, pl.ds(first, PAIR)], jnp.zeros((), low))
            scores = mm_nt(proj[0:upto, pl.ds(pl.multiple_of(width + first, PAIR), PAIR)], query)
            return scores + allow[0:upto, here]

        def soft(unit, scores):
            expo = jnp.exp(scores - jnp.max(scores, axis=0, keepdims=True))
            inv = 1.0 / jnp.sum(expo, axis=0, keepdims=True)
            return expo.astype(low), inv

        def attend(unit, held):
            p, h, q = unit
            expo, inv = held
            upto = (q + 1) * QUERIES
            here = slice(q * QUERIES, upto)
            head_rows = pl.ds(pl.multiple_of(p * PAIR + h * HEAD_DIM, HEAD_DIM), HEAD_DIM)
            expo_v[2 * p + h, 0:upto, here] = expo
            if upto < toks:
                expo_v[2 * p + h, upto:toks, here] = jnp.zeros((toks - upto, QUERIES), low)
            out = mm(values_t[head_rows, 0:upto], expo)
            attended_t[head_rows, here] = (out * inv).astype(low)
            inv_sums[2 * p + h, :, here] = jnp.broadcast_to(inv, (8, QUERIES))

        staged(units, score, soft, attend)
        here = pl.ds(pl.multiple_of(g * 2 * PAIR, 2 * PAIR), 2 * PAIR)
        queries_t[here, :] = proj[:, here].T
        keys_t[here, :] = proj[:, pl.ds(pl.multiple_of(width + g * 2 * PAIR, 2 * PAIR), 2 * PAIR)].T
        values[:, here] = proj[:, pl.ds(pl.multiple_of(2 * width + g * 2 * PAIR, 2 * PAIR), 2 * PAIR)]
        tokens_t[here, :] = tokens[:, here].T.astype(low)
        attn_in_t[here, :] = attn_in_v[:, here].T
        expo_store(g).start()
        for i in range(6):
            keep(i, g).start()
        return carry

    lax.fori_loop(0, HEADS // 4, head_group, 0)
    out_load.wait()
    residual = (tokens[...] + mm_tn(attended_t[...], w_out[...])).astype(low)
    place = (slot_row[0:1, :] == lax.broadcasted_iota(jnp.int32, (rows, toks), 0)).astype(f32).astype(low)
    sent_v[...] = mm(place, residual).astype(low)
    sent_store = pltpu.make_async_copy(sent_v, sent, sem_store.at[1])
    sent_store.start()

    for g in range(HEADS // 4):
        expo_store(g).wait()
        for i in range(6):
            keep(i, g).wait()
    grad_store.wait()
    pair_grads_store.wait()

    @pl.when(me_d == 1)
    def _():
        hid_store(0).wait()
        hid_store(1).wait()


    def wait_sent(i, carry):
        slot_copy(i).wait_send()
        return carry

    lax.fori_loop(1, n // 2, wait_sent, 0)

    @pl.when(me_d == 1)
    def _():
        lax.fori_loop(n // 2, n, wait_sent, 0)

    sent_store.wait()


def starting(hidden, grad_out, buckets, expert_of, lengths, gain, bias, w_qkv, w_out, down):
    n = lax.axis_size("expert")
    rows, width = hidden.shape
    toks = buckets.shape[1]
    units = down.shape[0]
    lanes = 128
    vm = pl.BlockSpec(memory_space=pltpu.VMEM)
    hbm = pl.BlockSpec(memory_space=pl.ANY)
    shape = jax.ShapeDtypeStruct
    return pl.pallas_call(
        functools.partial(start_kernel, n, rows // n),
        out_shape=(
            shape((rows, width), low),
            shape((2, rows, width), low),
            shape((2, rows, units), low),
            shape((rows, 1), f32),
            shape((width, toks), low),
            shape((width, toks), low),
            shape((width, toks), low),
            shape((width, toks), low),
            shape((toks, width), low),
            shape((width, toks), low),
            shape((HEADS, 8, toks), f32),
            shape((8, toks), jnp.int32),
            shape((HEADS, toks, toks), low),
        ),
        in_specs=[hbm, hbm, vm, vm, vm, vm, vm, hbm, hbm, hbm],
        out_specs=(hbm, hbm, hbm, vm, hbm, hbm, hbm, hbm, hbm, hbm, vm, vm, hbm),
        scratch_shapes=[
            pltpu.VMEM((rows, width), low),
            pltpu.VMEM(w_qkv.shape, low),
            pltpu.VMEM(w_out.shape, low),
            pltpu.VMEM(down.shape, low),
            pltpu.VMEM((rows, width), low),
            pltpu.VMEM((rows, width), low),
            pltpu.VMEM((rows, width), low),
            pltpu.VMEM((2, rows, units), low),
            pltpu.VMEM((width, toks), low),
            pltpu.VMEM((width, toks), low),
            pltpu.VMEM((width, toks), low),
            pltpu.VMEM((width, toks), low),
            pltpu.VMEM((toks, width), low),
            pltpu.VMEM((width, toks), low),
            pltpu.VMEM((toks, width), low),
            pltpu.VMEM((toks, 3 * width), low),
            pltpu.VMEM((width, toks), low),
            pltpu.VMEM((toks, toks), f32),
            pltpu.VMEM((toks, width), f32),
            pltpu.VMEM((HEADS, toks, toks), low),
            pltpu.VMEM((rows, width), low),
            pltpu.VMEM((8, lanes), f32),
            pltpu.VMEM((n, 8, lanes), f32),
            pltpu.SemaphoreType.DMA((n,)),
            pltpu.SemaphoreType.DMA((n,)),
            pltpu.SemaphoreType.DMA((n,)),
            pltpu.SemaphoreType.DMA((n,)),
            pltpu.SemaphoreType.DMA((2,)),
            pltpu.SemaphoreType.DMA((4,)),
            pltpu.SemaphoreType.DMA((5 + HEADS // 4,)),
            pltpu.SemaphoreType.DMA((6, HEADS // 4)),
            pltpu.SemaphoreType.REGULAR,
        ],
        compiler_params=pltpu.CompilerParams(
            collective_id=3, has_side_effects=True, vmem_limit_bytes=60 * 1024 * 1024
        ),
    )(hidden, grad_out, buckets, expert_of, lengths, gain, bias, w_qkv, w_out, down)


def expert_kernel(
    n,
    cap,
    sent,
    grads,
    hids,
    live,
    up_hbm,
    up_bias,
    down_hbm,
    down_bias,
    gain,
    bias,
    returned,
    hidden_out,
    grad_up,
    grad_down,
    grad_bup,
    grad_bdown,
    grad_norm,
    rows_in,
    ffn_in,
    grad_rows,
    up,
    down,
    hid,
    act,
    pre_grad,
    part_out,
    part_in,
    back,
    mine,
    tile,
    tile_down,
    sem_send,
    sem_recv,
    sem_back_send,
    sem_back_recv,
    sem_pair,
    sem_load,
    sem_store,
):
    me_d = lax.axis_index("dp")
    me_e = lax.axis_index("expert")
    rows = rows_in.shape[0]
    width = rows_in.shape[1]
    units = up.shape[1]
    block = rows // PARTS
    many = n // PARTS
    partner = (1 - me_d, me_e)

    def base_of(part):
        return pl.multiple_of(((me_e // many) ^ part) * block, block)

    def slot_copy(i):
        peer = me_e ^ i
        return pltpu.make_async_remote_copy(
            src_ref=sent.at[pl.ds(pl.multiple_of(peer * cap, cap), cap)],
            dst_ref=rows_in.at[pl.ds(pl.multiple_of(me_e * cap, cap), cap)],
            send_sem=sem_send.at[i],
            recv_sem=sem_recv.at[i],
            device_id=(me_d, peer),
            device_id_type=MESH_ID,
        )

    def own_slots():
        own = pl.ds(pl.multiple_of(me_e * cap, cap), cap)
        return pltpu.make_async_copy(sent.at[own], rows_in.at[own], sem_recv.at[0])

    def back_copy(i):
        peer = me_e ^ i
        return pltpu.make_async_remote_copy(
            src_ref=back.at[pl.ds(pl.multiple_of(peer * cap, cap), cap)],
            dst_ref=returned.at[pl.ds(pl.multiple_of(me_e * cap, cap), cap)],
            send_sem=sem_back_send.at[i],
            recv_sem=sem_back_recv.at[i],
            device_id=(me_d, peer),
            device_id_type=MESH_ID,
        )

    def own_back():
        own = pl.ds(pl.multiple_of(me_e * cap, cap), cap)
        return pltpu.make_async_copy(back.at[own], returned.at[own], sem_back_recv.at[0])

    def pair_copy(src, dst, kind, part):
        return pltpu.make_async_remote_copy(
            src_ref=src,
            dst_ref=dst,
            send_sem=sem_pair.at[kind - 1, 0, part],
            recv_sem=sem_pair.at[kind - 1, 1, part],
            device_id=partner,
            device_id_type=MESH_ID,
        )

    def ffn_pair(part):
        return pair_copy(ffn_in.at[part, 0], ffn_in.at[part, 1], 1, part)

    def part_pair(part):
        return pair_copy(part_out.at[part], part_in.at[part], 2, part)

    def out_pair(part):
        return pair_copy(part_out.at[PARTS + part], part_in.at[PARTS + part], 3, part)

    def hid_load(unit):
        part, k = part_of(unit), core_of(unit)
        here = pl.ds(base_of(part), block)
        return pltpu.make_async_copy(hids.at[k, here], hid.at[part, k], sem_load.at[2 + unit])

    def grads_load(unit):
        part, k = part_of(unit), core_of(unit)
        here = pl.ds(base_of(part), block)
        return pltpu.make_async_copy(grads.at[k, here], grad_rows.at[part, k], sem_load.at[2 + 2 * PARTS + unit])

    def part_of(unit):
        return lax.rem(unit, PARTS)

    def core_of(unit):
        return me_d ^ (unit // PARTS)

    up_load = pltpu.make_async_copy(up_hbm, up, sem_load.at[0])
    down_load = pltpu.make_async_copy(down_hbm, down, sem_load.at[1])
    own_slots().start()

    @pl.when(me_d == 0)
    def _():
        down_load.start()
        for unit in range(2 * PARTS):
            grads_load(unit).start()
        up_load.start()

    @pl.when(me_d == 1)
    def _():
        up_load.start()
        hid_load(0).start()
        grads_load(0).start()

    barrier = pltpu.get_barrier_semaphore()
    greet_peers(me_d, me_e, n)

    @pl.when(me_d == 0)
    def _():
        pl.semaphore_wait(barrier, n - 1)
        greet_partner(me_d, me_e)

    @pl.when(me_d == 1)
    def _():
        pl.semaphore_wait(barrier, n)
        greet_partner(me_d, me_e)

    def start_slots(i, carry):
        slot_copy(i).start()
        return carry

    lax.fori_loop(1, n, start_slots, 0)
    grad_norm[...] = jnp.zeros_like(grad_norm)
    up_load.wait()

    @pl.when(me_d == 1)
    def _():
        down_load.start()
        for unit in range(1, 2 * PARTS):
            hid_load(unit).start()
            grads_load(unit).start()


    def stats(base):
        return normalize(rows_in[pl.ds(base, block), :].astype(f32))

    def arrive(part):
        @pl.when(part == 0)
        def _():
            own_slots().wait()

        @pl.when(part > 0)
        def _():
            slot_copy(part * many).wait()

        def wait_slots(j, c):
            slot_copy(part * many + j).wait()
            return c

        lax.fori_loop(1, many, wait_slots, 0)
        normed, _ = stats(base_of(part))
        ffn_in[part, 0] = (normed * gain[...] + bias[...]).astype(low)

    @pl.when(me_d == 0)
    def _():
        def arrive_all(part, carry):
            arrive(part)

            @pl.when(part == 0)
            def _():
                pl.semaphore_wait(barrier, 1)

            ffn_pair(part).start()
            return carry

        def hidden_grad(unit, carry):
            part, k = part_of(unit), core_of(unit)
            grads_load(unit).wait()
            hid[part, k] = mm_nt(grad_rows[part, k], down[...]).astype(low)
            return carry

        down_load.wait()
        lax.fori_loop(0, 2 * PARTS, hidden_grad, 0)
        lax.fori_loop(0, PARTS, arrive_all, 0)

    def hidden(part, k):
        def before(cols):
            return mm(ffn_in[part, k], up[:, cols]) + up_bias[:, cols]

        def after(cols, pre):
            a, slope = gelu_parts(pre)
            act[part, k, :, cols] = a.astype(low)
            pre_grad[part, k, :, cols] = (hid[part, k, :, cols].astype(f32) * slope).astype(low)

        staged([pl.ds(f * WIDE, WIDE) for f in range(units // WIDE)], before, after)

    def send_back(unit):
        part = part_of(unit)
        base = base_of(part)
        part_pair(part).wait_recv()
        grad_ffn = mine[lax.rem(unit, 2)] + part_in[part].astype(f32)
        normed, inv_std = stats(base)
        grad_norm[0:1, :] += jnp.sum(grad_ffn * normed, axis=0, keepdims=True)
        grad_norm[1:2, :] += jnp.sum(grad_ffn, axis=0, keepdims=True)
        result = grad_rows[part, 0].astype(f32) + norm_back(grad_ffn, normed, inv_std, gain[...])
        back[pl.ds(base, block), :] = result.astype(low)

        @pl.when(part == 0)
        def _():
            own_back().start()

        @pl.when(part > 0)
        def _():
            back_copy(part * many).start()

        def start_back(j, c):
            back_copy(part * many + j).start()
            return c

        lax.fori_loop(1, many, start_back, 0)

    def work(unit, carry):
        part, k = part_of(unit), core_of(unit)
        ahead = unit + 1 - PARTS

        @pl.when((me_d == 1) & (ahead >= 0) & (ahead < PARTS))
        def _():
            arrive(ahead)
            ffn_pair(ahead).start()

        @pl.when(k == 1)
        def _():
            ffn_pair(part).wait_recv()

        @pl.when(me_d == 1)
        def _():
            hid_load(unit).wait()
            grads_load(unit).wait()

        hidden(part, k)
        slot = lax.rem(unit, 2)
        mine[slot] = mm_nt(pre_grad[part, k], up[...])

        @pl.when((unit == 0) & (me_d == 1))
        def _():
            down_load.wait()

        @pl.when(k == 1)
        def _():
            part_out[part] = mine[slot].astype(low)
            part_pair(part).start()
            part_out[PARTS + part] = mm(act[part, 1], down[...]).astype(low)
            out_pair(part).start()

        @pl.when((unit > 0) & (core_of(unit - 1) == 0))
        def _():
            send_back(unit - 1)

        return carry

    lax.fori_loop(0, 2 * PARTS, work, 0)

    @pl.when(me_d == 1)
    def _():
        send_back(2 * PARTS - 1)

    def output_own(part, carry):
        base = base_of(part)
        here = pl.ds(base, block)
        product = mm(act[part, 0], down[...])
        out_pair(part).wait_recv()
        total = rows_in[here, :].astype(f32) + product + part_in[PARTS + part].astype(f32) + down_bias[...]
        rows_in[here, :] = (total * live[here, :]).astype(low)
        pltpu.make_async_copy(rows_in.at[here], hidden_out.at[here], sem_store.at[part]).start()
        return carry

    lax.fori_loop(0, PARTS, output_own, 0)

    ones = jnp.ones((8, PARTS * 2 * block), low)
    all_act = act.reshape(PARTS * 2 * block, units)
    all_pre = pre_grad.reshape(PARTS * 2 * block, units)
    all_in = ffn_in.reshape(PARTS * 2 * block, width)
    all_grad = grad_rows.reshape(PARTS * 2 * block, width)
    grad_bup[...] = mm(ones, all_pre[...])[0:1]
    grad_bdown[...] = mm(ones, all_grad[...])[0:1]

    def up_store(f, slot):
        cols = pl.ds(pl.multiple_of(f * UNITS, UNITS), UNITS)
        return pltpu.make_async_copy(tile.at[slot], grad_up.at[:, cols], sem_store.at[PARTS + slot])

    def down_store(f, slot):
        cols = pl.ds(pl.multiple_of(f * UNITS, UNITS), UNITS)
        return pltpu.make_async_copy(
            tile_down.at[slot], grad_down.at[cols, :], sem_store.at[PARTS + 2 + slot]
        )

    def weights(f, carry):
        slot = lax.rem(f, 2)
        cols = pl.ds(pl.multiple_of(f * UNITS, UNITS), UNITS)

        @pl.when(f >= 2)
        def _():
            up_store(f, slot).wait()
            down_store(f, slot).wait()

        tile[slot] = mm_tn(all_in[...], all_pre[:, cols]).astype(low)
        up_store(f, slot).start()
        tile_down[slot] = mm_tn(all_act[:, cols], all_grad[...]).astype(low)
        down_store(f, slot).start()
        return carry

    lax.fori_loop(0, units // UNITS, weights, 0)
    for slot in range(2):
        up_store(0, slot).wait()
        down_store(0, slot).wait()
    for part in range(PARTS):
        pltpu.make_async_copy(
            rows_in.at[pl.ds(0, block)], hidden_out.at[pl.ds(0, block)], sem_store.at[part]
        ).wait()
    own_back().wait()
    for part in range(PARTS):
        ffn_pair(part).wait_send()
        part_pair(part).wait_send()
        out_pair(part).wait_send()

    def wait_back(i, carry):
        back_copy(i).wait()
        return carry

    lax.fori_loop(1, n, wait_back, 0)


def expert_block(sent, grads, hids, live, up, up_bias, down, down_bias, gain, bias):
    n = lax.axis_size("expert")
    rows, width = sent.shape
    units = up.shape[1]
    cap = rows // n
    block = rows // PARTS
    vm = pl.BlockSpec(memory_space=pltpu.VMEM)
    hbm = pl.BlockSpec(memory_space=pl.ANY)
    return pl.pallas_call(
        functools.partial(expert_kernel, n, cap),
        out_shape=(
            jax.ShapeDtypeStruct((rows, width), low),
            jax.ShapeDtypeStruct((rows, width), low),
            jax.ShapeDtypeStruct((width, units), low),
            jax.ShapeDtypeStruct((units, width), low),
            jax.ShapeDtypeStruct((1, units), f32),
            jax.ShapeDtypeStruct((1, width), f32),
            jax.ShapeDtypeStruct((8, width), f32),
        ),
        in_specs=[hbm, hbm, hbm, vm, hbm, vm, hbm, vm, vm, vm],
        out_specs=(hbm, hbm, hbm, hbm, vm, vm, vm),
        scratch_shapes=[
            pltpu.VMEM((rows, width), low),
            pltpu.VMEM((PARTS, 2, block, width), low),
            pltpu.VMEM((PARTS, 2, block, width), low),
            pltpu.VMEM((width, units), low),
            pltpu.VMEM((units, width), low),
            pltpu.VMEM((PARTS, 2, block, units), low),
            pltpu.VMEM((PARTS, 2, block, units), low),
            pltpu.VMEM((PARTS, 2, block, units), low),
            pltpu.VMEM((2 * PARTS, block, width), low),
            pltpu.VMEM((2 * PARTS, block, width), low),
            pltpu.VMEM((rows, width), low),
            pltpu.VMEM((2, block, width), f32),
            pltpu.VMEM((2, width, UNITS), low),
            pltpu.VMEM((2, UNITS, width), low),
            pltpu.SemaphoreType.DMA((n,)),
            pltpu.SemaphoreType.DMA((n,)),
            pltpu.SemaphoreType.DMA((n,)),
            pltpu.SemaphoreType.DMA((n,)),
            pltpu.SemaphoreType.DMA((3, 2, PARTS)),
            pltpu.SemaphoreType.DMA((2 + 4 * PARTS,)),
            pltpu.SemaphoreType.DMA((PARTS + 4,)),
        ],
        compiler_params=pltpu.CompilerParams(
            collective_id=1, has_side_effects=True, vmem_limit_bytes=62 * 1024 * 1024
        ),
    )(sent, grads, hids, live, up, up_bias, down, down_bias, gain, bias)


def closing_kernel(
    n,
    cap,
    chunks,
    returned_hbm,
    slot_row,
    attn_in_hbm,
    tokens_hbm,
    queries_hbm,
    keys_hbm,
    values_hbm,
    attended_hbm,
    inv_sums,
    expos,
    w_qkv_hbm,
    w_out_hbm,
    gain,
    grad_norm2,
    grad_in,
    grad_qkv,
    grad_wout,
    grad_norms,
    returned,
    attn_in_t,
    tokens_t,
    queries_t,
    keys_t,
    values,
    attended_t,
    w_qkv,
    w_out,
    expo_v,
    grad_att_t,
    grad_h,
    grad_proj_t,
    sent_v,
    norm_terms,
    made,
    *rest,
):
    count = len(chunks)
    totals, landeds = rest[:count], rest[count : 2 * count]
    sem_load, sem_expo, sem_send, sem_recv, sem_pair, sem_step = rest[2 * count :]
    me_d = lax.axis_index("dp")
    me_e = lax.axis_index("expert")
    partner = (1 - me_d, me_e)
    bits = n.bit_length() - 1
    half = n // 2
    rows, width = returned.shape
    toks = slot_row.shape[1]
    each = made.shape[1]
    loads = [
        pltpu.make_async_copy(a, b, sem_load.at[i])
        for i, (a, b) in enumerate(
            (
                (returned_hbm, returned),
                (w_out_hbm, w_out),
                (attended_hbm, attended_t),
                (values_hbm, values),
                (keys_hbm, keys_t),
                (queries_hbm, queries_t),
                (attn_in_hbm, attn_in_t),
                (w_qkv_hbm, w_qkv),
                (tokens_hbm, tokens_t),
            )
        )
    ]

    def expo_load(g):
        here = pl.ds(4 * g, 4)
        return pltpu.make_async_copy(expos.at[here], expo_v.at[here], sem_expo.at[g])

    def slot_copy(i):
        peer = me_e ^ i
        return pltpu.make_async_remote_copy(
            src_ref=sent_v.at[pl.ds(pl.multiple_of(peer * cap, cap), cap)],
            dst_ref=grad_in.at[pl.ds(pl.multiple_of(me_e * cap, cap), cap)],
            send_sem=sem_send.at[i],
            recv_sem=sem_recv.at[i],
            device_id=(me_d, peer),
            device_id_type=MESH_ID,
        )

    def own_slots():
        here = pl.ds(pl.multiple_of(me_e * cap, cap), cap)
        return pltpu.make_async_copy(sent_v.at[here], grad_in.at[here], sem_recv.at[0])

    def offset(order, p):
        k = 0
        for j, b in enumerate(order):
            k = k + lax.rem(p // (1 << (bits - 1 - j)), 2) * (1 << b)
        return k

    def pair_copy(c, q):
        here = pl.ds(q * half, half)
        return pltpu.make_async_remote_copy(
            src_ref=totals[c].at[1, here],
            dst_ref=landeds[c].at[here],
            send_sem=sem_pair.at[0, c, q],
            recv_sem=sem_pair.at[1, c, q],
            device_id=partner,
            device_id_type=MESH_ID,
        )

    def step_copy(c, j):
        many = n >> (j + 1)
        start = n + sum(n >> (i + 1) for i in range(j))
        copy = pltpu.make_async_remote_copy(
            src_ref=totals[c].at[0, pl.ds(many, many)],
            dst_ref=landeds[c].at[pl.ds(start, many)],
            send_sem=sem_step.at[0, c, j],
            recv_sem=sem_step.at[1, c, j],
            device_id=(me_d, me_e ^ (1 << chunks[c][0][j])),
            device_id_type=MESH_ID,
        )
        return copy, many, start

    def make(c):
        order, size, pieces = chunks[c]
        for kind, source, target in pieces:
            if kind == 0:
                term = mm_nt(attn_in_t[...], grad_proj_t[slice(*source), :])
            elif kind == 1:
                term = mm(attended_t[...], grad_h[:, slice(*source)])
            else:
                term = norm_terms[...]
            made[:, :, slice(*target)] = term.reshape(made.shape[0], each, term.shape[1])

        def arrange(p, carry):
            owner = me_e ^ offset(order, p)
            totals[c][0, p] = made[me_d * n + owner, :, 0:size].astype(low)
            totals[c][1, p] = made[(1 - me_d) * n + owner, :, 0:size].astype(low)
            return carry

        lax.fori_loop(0, n, arrange, 0)
        pair_copy(c, 1).start()
        pair_copy(c, 0).start()

    def add_all(c, first, many, start):
        def add_one(p, carry):
            both = totals[c][0, p].astype(f32) + landeds[c][start + p].astype(f32)
            totals[c][0, p] = both.astype(low)
            return carry

        lax.fori_loop(first, first + many, add_one, 0)

    def stage(c, j):
        if j == 0:
            pair_copy(c, 1).wait()
            add_all(c, half, half, 0)
            step_copy(c, 0)[0].start()
            pair_copy(c, 0).wait()
            add_all(c, 0, half, 0)
            return
        copy, many, start = step_copy(c, j - 1)
        copy.wait()
        if many > 1:
            add_all(c, 0, many, start)
            step_copy(c, j)[0].start()
        else:
            both = totals[c][0, 0].astype(f32) + landeds[c][start].astype(f32)
            for kind, source, target in chunks[c][2]:
                (grad_qkv, grad_wout, grad_norms)[kind][:, slice(*source)] = both[:, slice(*target)]

    for i in range(2):
        loads[i].start()
    greet_peers(me_d, me_e, n)
    greet_partner(me_d, me_e)
    place = (slot_row[0:1, :] == lax.broadcasted_iota(jnp.int32, (rows, toks), 0)).astype(f32).astype(low)
    loads[0].wait()
    for i in range(2, 6):
        loads[i].start()
    for g in range(HEADS // 4):
        expo_load(g).start()
    for i in range(6, len(loads)):
        loads[i].start()
    grad_h[...] = mm_tn(place, returned[...]).astype(low)
    loads[1].wait()
    grad_att_t[...] = mm_nt(w_out[...], grad_h[...]).astype(low)
    loads[2].wait()
    pl.semaphore_wait(pltpu.get_barrier_semaphore(), n)
    make(0)
    make(1)
    for i in range(3, 7):
        loads[i].wait()
    in_first = lax.broadcasted_iota(jnp.int32, (1, PAIR), 1) < HEAD_DIM

    def head_group(g):
        expo_load(g).wait()
        ready = {}
        sums = {}
        for pair in range(2):
            p = 2 * g + pair
            pair_rows = pl.ds(p * PAIR, PAIR)
            inv_pair = jnp.concatenate(
                [jnp.broadcast_to(inv_sums[2 * p + h, 0:1, :], (HEAD_DIM, toks)) for h in range(2)], axis=0
            )
            grad_pair = grad_att_t[pair_rows, :].astype(f32)
            cross = grad_pair * attended_t[pair_rows, :].astype(f32) * inv_pair
            scaled = (grad_pair * inv_pair).astype(low)
            for h in range(2):
                in_pair = slice(h * HEAD_DIM, (h + 1) * HEAD_DIM)
                ready[pair, h] = (jnp.sum(cross[in_pair], axis=0, keepdims=True), scaled)
        units = [
            (pair, h, q) for pair in range(2) for h in range(2) for q in reversed(range(toks // QUERIES))
        ]

        def probs_back(unit):
            pair, h, q = unit
            upto = (q + 1) * QUERIES
            here = slice(q * QUERIES, upto)
            mine = in_first if h == 0 else jnp.logical_not(in_first)
            value = jnp.where(mine, values[0:upto, pl.ds((2 * g + pair) * PAIR, PAIR)], jnp.zeros((), low))
            return mm(value, ready[pair, h][1][:, here])

        def scores_back(unit, grad_prob):
            pair, h, q = unit
            upto = (q + 1) * QUERIES
            here = slice(q * QUERIES, upto)
            expo = expo_v[4 * g + 2 * pair + h, 0:upto, here]
            return expo, (expo.astype(f32) * (grad_prob - ready[pair, h][0][:, here])).astype(low)

        def heads_back(unit, held):
            pair, h, q = unit
            expo, grad_score = held
            upto = (q + 1) * QUERIES
            here = slice(q * QUERIES, upto)
            first = (2 * g + pair) * PAIR + h * HEAD_DIM
            head_rows = pl.ds(first, HEAD_DIM)
            grad_proj_t[head_rows, here] = (mm(keys_t[head_rows, 0:upto], grad_score) * scale_val).astype(low)
            key_term = mm_nt(queries_t[head_rows, here], grad_score)
            value_term = mm_nt(ready[pair, h][1][h * HEAD_DIM : (h + 1) * HEAD_DIM, here], expo)
            if upto < toks:
                key_more, value_more = sums[pair, h]
                key_term = jnp.concatenate([key_more[:, 0:upto] + key_term, key_more[:, upto:]], axis=1)
                value_term = jnp.concatenate([value_more[:, 0:upto] + value_term, value_more[:, upto:]], axis=1)
            sums[pair, h] = (key_term, value_term)
            if q == 0:
                grad_proj_t[pl.ds(width + first, HEAD_DIM), :] = key_term.astype(low)
                grad_proj_t[pl.ds(2 * width + first, HEAD_DIM), :] = value_term.astype(low)

        staged(units, probs_back, scores_back, heads_back)

    groups = HEADS // 4
    head_group(0)
    make(2)
    stage(0, 0)
    stage(1, 0)
    for g in range(1, groups):
        head_group(g)
        make(2 + g)
        stage(1 + g, 0)
    for i in range(7, len(loads)):
        loads[i].wait()
    grad_attn_t = mm(w_qkv[...], grad_proj_t[...])
    stage(1 + groups, 0)
    normed_t, inv_std = normalize(tokens_t[...].astype(f32), axis=0)
    gain_col = jnp.broadcast_to(gain[...], (LANES, width)).T[:, 0:1]
    norm_terms[...] = jnp.concatenate(
        [
            jnp.sum(grad_attn_t * normed_t, axis=1, keepdims=True),
            jnp.sum(grad_attn_t, axis=1, keepdims=True),
            grad_norm2[...].T[:, 0:2],
            jnp.zeros((width, LANES - 4), f32),
        ],
        axis=1,
    )
    result = grad_h[...].astype(f32).T + norm_back(grad_attn_t, normed_t, inv_std, gain_col, axis=0)
    sent_v[...] = mm_nt(place, result.astype(low)).astype(low)
    own_slots().start()

    def start_slots(i, carry):
        slot_copy(i).start()
        return carry

    lax.fori_loop(1, n, start_slots, 0)
    make(count - 1)
    done = [1] * (count - 1) + [0]
    for wave in range(1, bits + count + 1):
        for c in range(count):
            late = c // 4
            while done[c] <= min(bits, wave - late):
                stage(c, done[c])
                done[c] += 1
    own_slots().wait()

    def wait_slots(i, carry):
        slot_copy(i).wait()
        return carry

    lax.fori_loop(1, n, wait_slots, 0)


def closing(returned, slot_row, attn_in_t, tokens_t, queries_t, keys_t, values, attended_t, inv_sums, expos, w_qkv, w_out, gain, grad_norm2):
    n = lax.axis_size("expert")
    owners = n * lax.axis_size("dp")
    rows, width = returned.shape
    toks = slot_row.shape[1]
    each = width // owners
    bits = n.bit_length() - 1
    groups = HEADS // 4
    part = width // groups
    orders = [list(range(bits)), [1, 0] + list(range(2, bits))]
    chunks = []
    for c in range(2):
        size = width // 2
        chunks.append((orders[c], size, [(1, (c * size, (c + 1) * size), (0, size))]))
    for g in range(groups):
        pieces = [
            (0, (k * width + g * part, k * width + (g + 1) * part), (k * part, (k + 1) * part)) for k in range(3)
        ]
        chunks.append((orders[g % 2], 3 * part, pieces))
    chunks.append((orders[0], LANES, [(2, (0, LANES), (0, LANES))]))
    count = len(chunks)
    widest = max(size for _, size, _ in chunks)
    vm = pl.BlockSpec(memory_space=pltpu.VMEM)
    hbm = pl.BlockSpec(memory_space=pl.ANY)
    shape = jax.ShapeDtypeStruct
    return pl.pallas_call(
        functools.partial(closing_kernel, n, rows // n, chunks),
        out_shape=(
            shape((rows, width), low),
            shape((each, 3 * width), f32),
            shape((each, width), f32),
            shape((each, LANES), f32),
        ),
        in_specs=[hbm, vm, hbm, hbm, hbm, hbm, hbm, hbm, vm, hbm, hbm, hbm, vm, vm],
        out_specs=(hbm, vm, vm, vm),
        scratch_shapes=[
            pltpu.VMEM((rows, width), low),
            pltpu.VMEM((width, toks), low),
            pltpu.VMEM((width, toks), low),
            pltpu.VMEM((width, toks), low),
            pltpu.VMEM((width, toks), low),
            pltpu.VMEM((toks, width), low),
            pltpu.VMEM((width, toks), low),
            pltpu.VMEM(w_qkv.shape, low),
            pltpu.VMEM(w_out.shape, low),
            pltpu.VMEM((HEADS, toks, toks), low),
            pltpu.VMEM((width, toks), low),
            pltpu.VMEM((toks, width), low),
            pltpu.VMEM((3 * width, toks), low),
            pltpu.VMEM((rows, width), low),
            pltpu.VMEM((width, LANES), f32),
            pltpu.VMEM((owners, each, widest), f32),
        ]
        + [pltpu.VMEM((2, n, each, size), low) for _, size, _ in chunks]
        + [pltpu.VMEM((2 * n, each, size), low) for _, size, _ in chunks]
        + [
            pltpu.SemaphoreType.DMA((9,)),
            pltpu.SemaphoreType.DMA((groups,)),
            pltpu.SemaphoreType.DMA((n,)),
            pltpu.SemaphoreType.DMA((n,)),
            pltpu.SemaphoreType.DMA((2, count, 2)),
            pltpu.SemaphoreType.DMA((2, count, bits)),
        ],
        compiler_params=pltpu.CompilerParams(
            collective_id=2, has_side_effects=True, vmem_limit_bytes=62 * 1024 * 1024
        ),
    )(returned, slot_row, attn_in_t, tokens_t, queries_t, keys_t, values, attended_t, inv_sums, expos, w_qkv, w_out, gain, grad_norm2)


def on_device(
    hidden_in,
    buckets,
    expert_of_bucket,
    lengths,
    norm1_gain,
    norm1_bias,
    w_qkv,
    w_out,
    norm2_gain,
    norm2_bias,
    w_up,
    b_up,
    w_down,
    b_down,
    grad_out,
):
    (
        sent,
        grads,
        hids,
        live,
        attn_in_t,
        tokens_t,
        queries_t,
        keys_t,
        values,
        attended_t,
        inv_sums,
        slot_row,
        expos,
    ) = starting(
        hidden_in,
        grad_out,
        buckets.reshape(1, -1),
        expert_of_bucket[None],
        lengths,
        norm1_gain[None],
        norm1_bias[None],
        w_qkv,
        w_out,
        w_down[0],
    )
    returned, hidden_out, grad_up, grad_down, grad_bup, grad_bdown, grad_norm2 = expert_block(
        sent, grads, hids, live, w_up[0], b_up, w_down[0], b_down, norm2_gain[None], norm2_bias[None]
    )
    grad_in, grad_qkv, grad_wout, grad_norms = closing(
        returned,
        slot_row,
        attn_in_t,
        tokens_t,
        queries_t,
        keys_t,
        values,
        attended_t,
        inv_sums,
        expos,
        w_qkv,
        w_out,
        norm1_gain[None],
        grad_norm2,
    )
    half = grad_bdown.shape[1] // lax.axis_size("dp")
    return (
        hidden_out,
        grad_in,
        grad_qkv,
        grad_wout,
        grad_norms[:, 0],
        grad_norms[:, 1],
        grad_norms[:, 2],
        grad_norms[:, 3],
        grad_up.astype(f32)[None],
        grad_bup,
        grad_down.astype(f32)[None],
        lax.dynamic_slice_in_dim(grad_bdown, lax.axis_index("dp") * half, half, axis=1),
    )


def solution(mesh):
    return jax.shard_map(
        on_device,
        mesh=mesh,
        in_specs=(
            P(("dp", "expert"), None),
            P(("dp", "expert"), None),
            P(),
            P(("dp", "expert"), None),
            P(),
            P(),
            P(),
            P(),
            P(),
            P(),
            P("expert", None, "dp"),
            P("expert", "dp"),
            P("expert", "dp", None),
            P("expert", None),
            P(("dp", "expert"), None),
        ),
        out_specs=(
            P(("dp", "expert"), None),
            P(("dp", "expert"), None),
            P(("dp", "expert"), None),
            P(("dp", "expert"), None),
            P(("dp", "expert")),
            P(("dp", "expert")),
            P(("dp", "expert")),
            P(("dp", "expert")),
            P("expert", None, "dp"),
            P("expert", "dp"),
            P("expert", "dp", None),
            P("expert", "dp"),
        ),
        check_vma=False,
    )
```

```python
import functools

import jax
import jax.numpy as jnp
from jax import lax
from jax.experimental import pallas as pl
from jax.experimental.pallas import tpu as pltpu
from jax.sharding import PartitionSpec as P

HEADS = 16
HEAD_DIM = 64


norm_eps = 1e-05
masked_score = -1e30
root_half = 0.7071067811865476
inv_root_tau = 0.3989422804014327

MESH_ID = pl.DeviceIdType.MESH
PARTS = 4
WIDE = 512
LANES = 128
QUERIES = 256
PAIR = 2 * HEAD_DIM
scale_val = HEAD_DIM ** (-0.5)
low = jnp.bfloat16
f32 = jnp.float32


def mm(a, b):
    return jnp.dot(a, b, preferred_element_type=f32)


def mm_nt(a, b):
    return lax.dot_general(a, b, (((1,), (1,)), ((), ())), preferred_element_type=f32)


def mm_tn(a, b):
    return lax.dot_general(a, b, (((0,), (0,)), ((), ())), preferred_element_type=f32)


def normalize(values, axis=-1):
    mean_val = jnp.mean(values, axis=axis, keepdims=True)
    centered = values - mean_val
    variance = jnp.mean(centered * centered, axis=axis, keepdims=True)
    inv_std = lax.rsqrt(variance + norm_eps)
    return (centered * inv_std, inv_std)


def norm_back(grad_normed, normed, inv_std, gain_vec, axis=-1):
    scaled = grad_normed * gain_vec
    mean_grad = jnp.mean(scaled, axis=axis, keepdims=True)
    mean_cross = jnp.mean(scaled * normed, axis=axis, keepdims=True)
    return inv_std * (scaled - mean_grad - normed * mean_cross)


def gelu_parts(pre):
    bell = jnp.exp(-0.5 * pre * pre)
    den = 1.0 + (0.3275911 * root_half) * jnp.abs(pre)
    t = pl.reciprocal(den, approx=True)
    t = t * (2.0 - den * t)
    tail = t * (
        0.5 * 0.254829592
        + t * (0.5 * -0.284496736 + t * (0.5 * 1.421413741 + t * (0.5 * -1.453152027 + t * (0.5 * 1.061405429))))
    )
    tail = tail * bell
    phi = jnp.where(pre >= 0.0, 1.0 - tail, tail)
    return pre * phi, phi + pre * (inv_root_tau * bell)


def greet_peers(me_d, me_e, n):
    barrier = pltpu.get_barrier_semaphore()

    def signal(i, carry):
        pl.semaphore_signal(barrier, inc=1, device_id=(me_d, me_e ^ i), device_id_type=MESH_ID)
        return carry

    lax.fori_loop(1, n, signal, 0)


def greet_partner(me_d, me_e):
    pl.semaphore_signal(
        pltpu.get_barrier_semaphore(), inc=1, device_id=(1 - me_d, me_e), device_id_type=MESH_ID
    )


def staged(units, *stages):
    held = [None] * len(units)
    for step in range(len(units) + len(stages) - 1):
        for k, stage in enumerate(stages):
            i = step - k
            if 0 <= i < len(units):
                held[i] = stage(units[i]) if k == 0 else stage(units[i], held[i])


def start_kernel(
    n,
    cap,
    hidden,
    grad_out,
    buckets,
    expert_of,
    lengths,
    gain,
    bias,
    w_qkv_hbm,
    w_out_hbm,
    down_hbm,
    sent,
    grads,
    hids,
    live,
    attn_in_hbm,
    tokens_hbm,
    queries_hbm,
    keys_hbm,
    values_hbm,
    attended_hbm,
    inv_sums,
    slot_row,
    expos,
    arrived,
    w_qkv,
    w_out,
    down,
    grad_raw,
    grad_v,
    grad_p,
    hid_v,
    attn_in_t,
    tokens_t,
    queries_t,
    keys_t,
    values,
    attended_t,
    attn_in_v,
    proj,
    values_t,
    allow,
    tokens,
    expo_v,
    sent_v,
    counts_out,
    counts_in,
    sem_send,
    sem_recv,
    sem_count_send,
    sem_count_recv,
    sem_pair,
    sem_load,
    sem_store,
    sem_keep,
    sem_turn,
):
    me_d = lax.axis_index("dp")
    me_e = lax.axis_index("expert")
    partner = (1 - me_d, me_e)
    rows, width = arrived.shape
    toks = buckets.shape[1]
    lanes = counts_out.shape[1]

    def slot_copy(i):
        peer = me_e ^ i
        return pltpu.make_async_remote_copy(
            src_ref=hidden.at[pl.ds(pl.multiple_of(peer * cap, cap), cap)],
            dst_ref=arrived.at[pl.ds(pl.multiple_of(me_e * cap, cap), cap)],
            send_sem=sem_send.at[i],
            recv_sem=sem_recv.at[i],
            device_id=(me_d, peer),
            device_id_type=MESH_ID,
        )

    def own_slots():
        here = pl.ds(pl.multiple_of(me_e * cap, cap), cap)
        return pltpu.make_async_copy(hidden.at[here], arrived.at[here], sem_recv.at[0])

    def count_copy(i):
        return pltpu.make_async_remote_copy(
            src_ref=counts_out,
            dst_ref=counts_in.at[me_e],
            send_sem=sem_count_send.at[i],
            recv_sem=sem_count_recv.at[i],
            device_id=(me_d, me_e ^ i),
            device_id_type=MESH_ID,
        )

    grad_load = pltpu.make_async_copy(grad_out, grad_raw, sem_load.at[0])
    qkv_load = pltpu.make_async_copy(w_qkv_hbm, w_qkv, sem_load.at[1])
    out_load = pltpu.make_async_copy(w_out_hbm, w_out, sem_load.at[2])
    down_load = pltpu.make_async_copy(down_hbm, down, sem_load.at[3])
    pair_grads_store = pltpu.make_async_copy(grad_p, grads.at[1], sem_store.at[2])
    def keep(i, g):
        source, target = (
            (attn_in_t, attn_in_hbm),
            (tokens_t, tokens_hbm),
            (queries_t, queries_hbm),
            (keys_t, keys_hbm),
            (attended_t, attended_hbm),
            (values, values_hbm),
        )[i]
        here = pl.ds(pl.multiple_of(g * 2 * PAIR, 2 * PAIR), 2 * PAIR)
        if i == 5:
            return pltpu.make_async_copy(source.at[:, here], target.at[:, here], sem_keep.at[i, g])
        return pltpu.make_async_copy(source.at[here], target.at[here], sem_keep.at[i, g])

    def hid_store(k):
        return pltpu.make_async_copy(hid_v.at[k], hids.at[k], sem_store.at[3 + k])

    def hidden_grad(k, grad_ref):
        def tile(i, carry):
            here = pl.ds(pl.multiple_of((i // 2) * WIDE, WIDE), WIDE)
            some = pl.ds(pl.multiple_of(lax.rem(i, 2) * (rows // 2), rows // 2), rows // 2)
            hid_v[k, some, here] = mm_nt(grad_ref[some, :], down[here, :]).astype(low)
            return carry

        lax.fori_loop(0, 2 * (down.shape[0] // WIDE), tile, 0)
        hid_store(k).start()

    grad_store = pltpu.make_async_copy(grad_v, grads.at[0], sem_store.at[0])
    grad_pair = pltpu.make_async_remote_copy(
        src_ref=grad_v,
        dst_ref=grad_p,
        send_sem=sem_pair.at[0],
        recv_sem=sem_pair.at[1],
        device_id=partner,
        device_id_type=MESH_ID,
    )

    def start_slots(i, carry):
        slot_copy(i).start()
        return carry

    grad_load.start()

    @pl.when(me_d == 1)
    def _():
        down_load.start()

    greet_peers(me_d, me_e, n)
    greet_partner(me_d, me_e)
    lane_ids = lax.broadcasted_iota(jnp.int32, (toks, lanes), 1)
    bucket = jnp.broadcast_to(buckets[...], (lanes, toks)).T[:, 0:n]
    bucket_hot = (bucket == lane_ids[:, 0:n]).astype(f32).astype(low)
    serves_t = (expert_of[...] == lax.broadcasted_iota(jnp.int32, (lanes, n), 0)).astype(f32).astype(low)
    expert_hot = mm_nt(bucket_hot, serves_t)
    counts_out[...] = jnp.broadcast_to(jnp.sum(expert_hot, axis=0, keepdims=True), counts_out.shape)
    counts_in[me_e] = counts_out[...]

    def start_counts(i, carry):
        count_copy(i).start()
        return carry

    pl.semaphore_wait(pltpu.get_barrier_semaphore(), n)
    lax.fori_loop(1, n, start_counts, 0)
    lax.fori_loop(1, n // 2, start_slots, 0)

    @pl.when(me_d == 0)
    def _():
        lax.fori_loop(n // 2, n, start_slots, 0)

    own_slots().start()
    qkv_load.start()
    out_load.start()

    row_ids = lax.broadcasted_iota(jnp.int32, (toks, toks), 0)
    col_ids = lax.broadcasted_iota(jnp.int32, (toks, toks), 1)
    earlier = (col_ids < row_ids).astype(f32).astype(low)
    before = mm(earlier, expert_hot.astype(low))
    slot = jnp.sum(expert_hot * (before + (lane_ids * cap).astype(f32)), axis=1, keepdims=True)
    slot_row[...] = jnp.broadcast_to(slot, (toks, lanes)).T[0:8, :].astype(jnp.int32)
    ends = jnp.zeros((1, toks), jnp.int32)
    begin = jnp.zeros((1, toks), jnp.int32)
    places = lax.broadcasted_iota(jnp.int32, (1, toks), 1)
    for s in range(lengths.shape[1]):
        ends = ends + lengths[0:1, s : s + 1]
        begin = jnp.where(places >= ends, ends, begin)
    allow[...] = jnp.where(jnp.logical_and(row_ids <= col_ids, row_ids >= begin), 0.0, masked_score)

    def wait_counts(i, carry):
        count_copy(i).wait()
        return carry

    lax.fori_loop(1, n, wait_counts, 0)
    grad_load.wait()

    def mark(s, carry):
        here = pl.ds(pl.multiple_of(s * cap, cap), cap)
        mine = lax.broadcasted_iota(jnp.int32, (1, lanes), 1) == me_e
        count = jnp.sum(jnp.where(mine, counts_in[s, 0:1, :], 0.0), axis=1, keepdims=True)
        taken = (lax.broadcasted_iota(jnp.int32, (cap, 1), 0).astype(f32) < count).astype(f32)
        live[here, :] = taken
        grad_v[here, :] = (grad_raw[here, :].astype(f32) * taken).astype(low)
        return carry

    lax.fori_loop(0, n, mark, 0)
    grad_store.start()
    grad_pair.start()
    @pl.when(me_d == 0)
    def _():
        def wait_sent(i, carry):
            slot_copy(i).wait_send()
            return carry

        lax.fori_loop(n // 2, n, wait_sent, 0)
        pl.semaphore_signal(sem_turn, inc=1, device_id=partner, device_id_type=MESH_ID)

    @pl.when(me_d == 1)
    def _():
        pl.semaphore_wait(sem_turn, 1)
        lax.fori_loop(n // 2, n, start_slots, 0)

    grad_pair.wait()
    pair_grads_store.start()

    @pl.when(me_d == 1)
    def _():
        down_load.wait()
        hidden_grad(0, grad_v)
        hidden_grad(1, grad_p)


    own_slots().wait()

    def wait_slots(i, carry):
        slot_copy(i).wait_recv()
        return carry

    lax.fori_loop(1, n, wait_slots, 0)

    pick = (slot.astype(jnp.int32) == lax.broadcasted_iota(jnp.int32, (toks, rows), 1)).astype(f32).astype(low)
    tokens[...] = mm(pick, arrived[...])
    normed, _ = normalize(tokens[...])
    attn_in = (normed * gain[...] + bias[...]).astype(low)
    attn_in_v[...] = attn_in
    qkv_load.wait()
    step = width // 4
    for c in range(3 * width // step):
        here = slice(c * step, (c + 1) * step)
        part = mm(attn_in, w_qkv[:, here])
        if c * step < width:
            part = part.astype(low).astype(f32) * scale_val
        proj[:, here] = part.astype(low)
    values_t[...] = proj[:, 2 * width : 3 * width].T

    def expo_store(g):
        here = pl.ds(pl.multiple_of(4 * g, 4), 4)
        return pltpu.make_async_copy(expo_v.at[here], expos.at[here], sem_store.at[5 + g])

    in_first = lax.broadcasted_iota(jnp.int32, (1, PAIR), 1) < HEAD_DIM

    def head_group(g, carry):
        units = [
            (2 * g + pair, h, q) for pair in range(2) for h in range(2) for q in range(toks // QUERIES)
        ]

        def score(unit):
            p, h, q = unit
            first = pl.multiple_of(p * PAIR, PAIR)
            upto = (q + 1) * QUERIES
            here = slice(q * QUERIES, upto)
            mine = in_first if h == 0 else jnp.logical_not(in_first)
            query = jnp.where(mine, proj[here, pl.ds(first, PAIR)], jnp.zeros((), low))
            scores = mm_nt(proj[0:upto, pl.ds(pl.multiple_of(width + first, PAIR), PAIR)], query)
            return scores + allow[0:upto, here]

        def soft(unit, scores):
            expo = jnp.exp(scores - jnp.max(scores, axis=0, keepdims=True))
            inv = 1.0 / jnp.sum(expo, axis=0, keepdims=True)
            return expo.astype(low), inv

        def attend(unit, held):
            p, h, q = unit
            expo, inv = held
            upto = (q + 1) * QUERIES
            here = slice(q * QUERIES, upto)
            head_rows = pl.ds(pl.multiple_of(p * PAIR + h * HEAD_DIM, HEAD_DIM), HEAD_DIM)
            expo_v[2 * p + h, 0:upto, here] = expo
            if upto < toks:
                expo_v[2 * p + h, upto:toks, here] = jnp.zeros((toks - upto, QUERIES), low)
            out = mm(values_t[head_rows, 0:upto], expo)
            attended_t[head_rows, here] = (out * inv).astype(low)
            inv_sums[2 * p + h, :, here] = jnp.broadcast_to(inv, (8, QUERIES))

        staged(units, score, soft, attend)
        here = pl.ds(pl.multiple_of(g * 2 * PAIR, 2 * PAIR), 2 * PAIR)
        queries_t[here, :] = proj[:, here].T
        keys_t[here, :] = proj[:, pl.ds(pl.multiple_of(width + g * 2 * PAIR, 2 * PAIR), 2 * PAIR)].T
        values[:, here] = proj[:, pl.ds(pl.multiple_of(2 * width + g * 2 * PAIR, 2 * PAIR), 2 * PAIR)]
        tokens_t[here, :] = tokens[:, here].T.astype(low)
        attn_in_t[here, :] = attn_in_v[:, here].T
        expo_store(g).start()
        for i in range(6):
            keep(i, g).start()
        return carry

    lax.fori_loop(0, HEADS // 4, head_group, 0)
    out_load.wait()
    residual = (tokens[...] + mm_tn(attended_t[...], w_out[...])).astype(low)
    place = (slot_row[0:1, :] == lax.broadcasted_iota(jnp.int32, (rows, toks), 0)).astype(f32).astype(low)
    sent_v[...] = mm(place, residual).astype(low)
    sent_store = pltpu.make_async_copy(sent_v, sent, sem_store.at[1])
    sent_store.start()

    for g in range(HEADS // 4):
        expo_store(g).wait()
        for i in range(6):
            keep(i, g).wait()
    grad_store.wait()
    pair_grads_store.wait()

    @pl.when(me_d == 1)
    def _():
        hid_store(0).wait()
        hid_store(1).wait()


    def wait_sent(i, carry):
        slot_copy(i).wait_send()
        return carry

    lax.fori_loop(1, n // 2, wait_sent, 0)

    @pl.when(me_d == 1)
    def _():
        lax.fori_loop(n // 2, n, wait_sent, 0)

    sent_store.wait()


def starting(hidden, grad_out, buckets, expert_of, lengths, gain, bias, w_qkv, w_out, down):
    n = lax.axis_size("expert")
    rows, width = hidden.shape
    toks = buckets.shape[1]
    units = down.shape[0]
    lanes = 128
    vm = pl.BlockSpec(memory_space=pltpu.VMEM)
    hbm = pl.BlockSpec(memory_space=pl.ANY)
    shape = jax.ShapeDtypeStruct
    return pl.pallas_call(
        functools.partial(start_kernel, n, rows // n),
        out_shape=(
            shape((rows, width), low),
            shape((2, rows, width), low),
            shape((2, rows, units), low),
            shape((rows, 1), f32),
            shape((width, toks), low),
            shape((width, toks), low),
            shape((width, toks), low),
            shape((width, toks), low),
            shape((toks, width), low),
            shape((width, toks), low),
            shape((HEADS, 8, toks), f32),
            shape((8, toks), jnp.int32),
            shape((HEADS, toks, toks), low),
        ),
        in_specs=[hbm, hbm, vm, vm, vm, vm, vm, hbm, hbm, hbm],
        out_specs=(hbm, hbm, hbm, vm, hbm, hbm, hbm, hbm, hbm, hbm, vm, vm, hbm),
        scratch_shapes=[
            pltpu.VMEM((rows, width), low),
            pltpu.VMEM(w_qkv.shape, low),
            pltpu.VMEM(w_out.shape, low),
            pltpu.VMEM(down.shape, low),
            pltpu.VMEM((rows, width), low),
            pltpu.VMEM((rows, width), low),
            pltpu.VMEM((rows, width), low),
            pltpu.VMEM((2, rows, units), low),
            pltpu.VMEM((width, toks), low),
            pltpu.VMEM((width, toks), low),
            pltpu.VMEM((width, toks), low),
            pltpu.VMEM((width, toks), low),
            pltpu.VMEM((toks, width), low),
            pltpu.VMEM((width, toks), low),
            pltpu.VMEM((toks, width), low),
            pltpu.VMEM((toks, 3 * width), low),
            pltpu.VMEM((width, toks), low),
            pltpu.VMEM((toks, toks), f32),
            pltpu.VMEM((toks, width), f32),
            pltpu.VMEM((HEADS, toks, toks), low),
            pltpu.VMEM((rows, width), low),
            pltpu.VMEM((8, lanes), f32),
            pltpu.VMEM((n, 8, lanes), f32),
            pltpu.SemaphoreType.DMA((n,)),
            pltpu.SemaphoreType.DMA((n,)),
            pltpu.SemaphoreType.DMA((n,)),
            pltpu.SemaphoreType.DMA((n,)),
            pltpu.SemaphoreType.DMA((2,)),
            pltpu.SemaphoreType.DMA((4,)),
            pltpu.SemaphoreType.DMA((5 + HEADS // 4,)),
            pltpu.SemaphoreType.DMA((6, HEADS // 4)),
            pltpu.SemaphoreType.REGULAR,
        ],
        compiler_params=pltpu.CompilerParams(
            collective_id=3, has_side_effects=True, vmem_limit_bytes=60 * 1024 * 1024
        ),
    )(hidden, grad_out, buckets, expert_of, lengths, gain, bias, w_qkv, w_out, down)


def expert_kernel(
    n,
    cap,
    sent,
    grads,
    hids,
    live,
    up_hbm,
    up_bias,
    down_hbm,
    down_bias,
    gain,
    bias,
    returned,
    hidden_out,
    grad_up,
    grad_down,
    grad_bup,
    grad_bdown,
    grad_norm,
    rows_in,
    ffn_in,
    grad_rows,
    up,
    down,
    hid,
    act,
    pre_grad,
    part_out,
    part_in,
    back,
    mine,
    tile,
    tile_down,
    sem_send,
    sem_recv,
    sem_back_send,
    sem_back_recv,
    sem_pair,
    sem_load,
    sem_store,
):
    me_d = lax.axis_index("dp")
    me_e = lax.axis_index("expert")
    rows = rows_in.shape[0]
    width = rows_in.shape[1]
    units = up.shape[1]
    block = rows // PARTS
    many = n // PARTS
    partner = (1 - me_d, me_e)

    def base_of(part):
        return pl.multiple_of(((me_e // many) ^ part) * block, block)

    def slot_copy(i):
        peer = me_e ^ i
        return pltpu.make_async_remote_copy(
            src_ref=sent.at[pl.ds(pl.multiple_of(peer * cap, cap), cap)],
            dst_ref=rows_in.at[pl.ds(pl.multiple_of(me_e * cap, cap), cap)],
            send_sem=sem_send.at[i],
            recv_sem=sem_recv.at[i],
            device_id=(me_d, peer),
            device_id_type=MESH_ID,
        )

    def own_slots():
        own = pl.ds(pl.multiple_of(me_e * cap, cap), cap)
        return pltpu.make_async_copy(sent.at[own], rows_in.at[own], sem_recv.at[0])

    def back_copy(i):
        peer = me_e ^ i
        return pltpu.make_async_remote_copy(
            src_ref=back.at[pl.ds(pl.multiple_of(peer * cap, cap), cap)],
            dst_ref=returned.at[pl.ds(pl.multiple_of(me_e * cap, cap), cap)],
            send_sem=sem_back_send.at[i],
            recv_sem=sem_back_recv.at[i],
            device_id=(me_d, peer),
            device_id_type=MESH_ID,
        )

    def own_back():
        own = pl.ds(pl.multiple_of(me_e * cap, cap), cap)
        return pltpu.make_async_copy(back.at[own], returned.at[own], sem_back_recv.at[0])

    def pair_copy(src, dst, kind, part):
        return pltpu.make_async_remote_copy(
            src_ref=src,
            dst_ref=dst,
            send_sem=sem_pair.at[kind - 1, 0, part],
            recv_sem=sem_pair.at[kind - 1, 1, part],
            device_id=partner,
            device_id_type=MESH_ID,
        )

    def ffn_pair(part):
        return pair_copy(ffn_in.at[part, 0], ffn_in.at[part, 1], 1, part)

    def part_pair(part):
        return pair_copy(part_out.at[part], part_in.at[part], 2, part)

    def out_pair(part):
        return pair_copy(part_out.at[PARTS + part], part_in.at[PARTS + part], 3, part)

    def hid_load(unit):
        part, k = part_of(unit), core_of(unit)
        here = pl.ds(base_of(part), block)
        return pltpu.make_async_copy(hids.at[k, here], hid.at[part, k], sem_load.at[2 + unit])

    def grads_load(unit):
        part, k = part_of(unit), core_of(unit)
        here = pl.ds(base_of(part), block)
        return pltpu.make_async_copy(grads.at[k, here], grad_rows.at[part, k], sem_load.at[2 + 2 * PARTS + unit])

    def part_of(unit):
        return lax.rem(unit, PARTS)

    def core_of(unit):
        return me_d ^ (unit // PARTS)

    up_load = pltpu.make_async_copy(up_hbm, up, sem_load.at[0])
    down_load = pltpu.make_async_copy(down_hbm, down, sem_load.at[1])
    own_slots().start()

    @pl.when(me_d == 0)
    def _():
        down_load.start()
        for unit in range(2 * PARTS):
            grads_load(unit).start()
        up_load.start()

    @pl.when(me_d == 1)
    def _():
        up_load.start()
        hid_load(0).start()
        grads_load(0).start()

    barrier = pltpu.get_barrier_semaphore()
    greet_peers(me_d, me_e, n)

    @pl.when(me_d == 0)
    def _():
        pl.semaphore_wait(barrier, n - 1)
        greet_partner(me_d, me_e)

    @pl.when(me_d == 1)
    def _():
        pl.semaphore_wait(barrier, n)
        greet_partner(me_d, me_e)

    def start_slots(i, carry):
        slot_copy(i).start()
        return carry

    lax.fori_loop(1, n, start_slots, 0)
    grad_norm[...] = jnp.zeros_like(grad_norm)
    up_load.wait()

    @pl.when(me_d == 1)
    def _():
        down_load.start()
        for unit in range(1, 2 * PARTS):
            hid_load(unit).start()
            grads_load(unit).start()


    def stats(base):
        return normalize(rows_in[pl.ds(base, block), :].astype(f32))

    def arrive(part):
        @pl.when(part == 0)
        def _():
            own_slots().wait()

        @pl.when(part > 0)
        def _():
            slot_copy(part * many).wait()

        def wait_slots(j, c):
            slot_copy(part * many + j).wait()
            return c

        lax.fori_loop(1, many, wait_slots, 0)
        normed, _ = stats(base_of(part))
        ffn_in[part, 0] = (normed * gain[...] + bias[...]).astype(low)

    @pl.when(me_d == 0)
    def _():
        def arrive_all(part, carry):
            arrive(part)

            @pl.when(part == 0)
            def _():
                pl.semaphore_wait(barrier, 1)

            ffn_pair(part).start()
            return carry

        def hidden_grad(unit, carry):
            part, k = part_of(unit), core_of(unit)
            grads_load(unit).wait()
            hid[part, k] = mm_nt(grad_rows[part, k], down[...]).astype(low)
            return carry

        down_load.wait()
        lax.fori_loop(0, 2 * PARTS, hidden_grad, 0)
        lax.fori_loop(0, PARTS, arrive_all, 0)

    def hidden(part, k):
        def before(cols):
            return mm(ffn_in[part, k], up[:, cols]) + up_bias[:, cols]

        def after(cols, pre):
            a, slope = gelu_parts(pre)
            act[part, k, :, cols] = a.astype(low)
            pre_grad[part, k, :, cols] = (hid[part, k, :, cols].astype(f32) * slope).astype(low)

        staged([pl.ds(f * WIDE, WIDE) for f in range(units // WIDE)], before, after)

    def send_back(unit):
        part = part_of(unit)
        base = base_of(part)
        part_pair(part).wait_recv()
        grad_ffn = mine[lax.rem(unit, 2)] + part_in[part].astype(f32)
        normed, inv_std = stats(base)
        grad_norm[0:1, :] += jnp.sum(grad_ffn * normed, axis=0, keepdims=True)
        grad_norm[1:2, :] += jnp.sum(grad_ffn, axis=0, keepdims=True)
        result = grad_rows[part, 0].astype(f32) + norm_back(grad_ffn, normed, inv_std, gain[...])
        back[pl.ds(base, block), :] = result.astype(low)

        @pl.when(part == 0)
        def _():
            own_back().start()

        @pl.when(part > 0)
        def _():
            back_copy(part * many).start()

        def start_back(j, c):
            back_copy(part * many + j).start()
            return c

        lax.fori_loop(1, many, start_back, 0)

    def work(unit, carry):
        part, k = part_of(unit), core_of(unit)
        ahead = unit + 1 - PARTS

        @pl.when((me_d == 1) & (ahead >= 0) & (ahead < PARTS))
        def _():
            arrive(ahead)
            ffn_pair(ahead).start()

        @pl.when(k == 1)
        def _():
            ffn_pair(part).wait_recv()

        @pl.when(me_d == 1)
        def _():
            hid_load(unit).wait()
            grads_load(unit).wait()

        hidden(part, k)
        slot = lax.rem(unit, 2)
        mine[slot] = mm_nt(pre_grad[part, k], up[...])

        @pl.when((unit == 0) & (me_d == 1))
        def _():
            down_load.wait()

        @pl.when(k == 1)
        def _():
            part_out[part] = mine[slot].astype(low)
            part_pair(part).start()
            part_out[PARTS + part] = mm(act[part, 1], down[...]).astype(low)
            out_pair(part).start()

        @pl.when((unit > 0) & (core_of(unit - 1) == 0))
        def _():
            send_back(unit - 1)

        return carry

    lax.fori_loop(0, 2 * PARTS, work, 0)

    @pl.when(me_d == 1)
    def _():
        send_back(2 * PARTS - 1)

    def output_own(part, carry):
        base = base_of(part)
        here = pl.ds(base, block)
        product = mm(act[part, 0], down[...])
        out_pair(part).wait_recv()
        total = rows_in[here, :].astype(f32) + product + part_in[PARTS + part].astype(f32) + down_bias[...]
        rows_in[here, :] = (total * live[here, :]).astype(low)
        pltpu.make_async_copy(rows_in.at[here], hidden_out.at[here], sem_store.at[part]).start()
        return carry

    lax.fori_loop(0, PARTS, output_own, 0)

    ones = jnp.ones((8, PARTS * 2 * block), low)
    all_act = act.reshape(PARTS * 2 * block, units)
    all_pre = pre_grad.reshape(PARTS * 2 * block, units)
    all_in = ffn_in.reshape(PARTS * 2 * block, width)
    all_grad = grad_rows.reshape(PARTS * 2 * block, width)
    grad_bup[...] = mm(ones, all_pre[...])[0:1]
    grad_bdown[...] = mm(ones, all_grad[...])[0:1]

    def up_store(f):
        cols = pl.ds(pl.multiple_of(f * WIDE, WIDE), WIDE)
        return pltpu.make_async_copy(tile, grad_up.at[:, cols], sem_store.at[PARTS])

    def down_store(f):
        cols = pl.ds(pl.multiple_of(f * WIDE, WIDE), WIDE)
        return pltpu.make_async_copy(tile_down, grad_down.at[cols, :], sem_store.at[PARTS + 1])

    def weights(f, carry):
        cols = pl.ds(pl.multiple_of(f * WIDE, WIDE), WIDE)

        @pl.when(f > 0)
        def _():
            up_store(f).wait()

        tile[...] = mm_tn(all_in[...], all_pre[:, cols]).astype(low)
        up_store(f).start()

        @pl.when(f > 0)
        def _():
            down_store(f).wait()

        tile_down[...] = mm_tn(all_act[:, cols], all_grad[...]).astype(low)
        down_store(f).start()
        return carry

    lax.fori_loop(0, units // WIDE, weights, 0)
    up_store(0).wait()
    down_store(0).wait()
    for part in range(PARTS):
        pltpu.make_async_copy(
            rows_in.at[pl.ds(0, block)], hidden_out.at[pl.ds(0, block)], sem_store.at[part]
        ).wait()
    own_back().wait()
    for part in range(PARTS):
        ffn_pair(part).wait_send()
        part_pair(part).wait_send()
        out_pair(part).wait_send()

    def wait_back(i, carry):
        back_copy(i).wait()
        return carry

    lax.fori_loop(1, n, wait_back, 0)


def expert_block(sent, grads, hids, live, up, up_bias, down, down_bias, gain, bias):
    n = lax.axis_size("expert")
    rows, width = sent.shape
    units = up.shape[1]
    cap = rows // n
    block = rows // PARTS
    vm = pl.BlockSpec(memory_space=pltpu.VMEM)
    hbm = pl.BlockSpec(memory_space=pl.ANY)
    return pl.pallas_call(
        functools.partial(expert_kernel, n, cap),
        out_shape=(
            jax.ShapeDtypeStruct((rows, width), low),
            jax.ShapeDtypeStruct((rows, width), low),
            jax.ShapeDtypeStruct((width, units), low),
            jax.ShapeDtypeStruct((units, width), low),
            jax.ShapeDtypeStruct((1, units), f32),
            jax.ShapeDtypeStruct((1, width), f32),
            jax.ShapeDtypeStruct((8, width), f32),
        ),
        in_specs=[hbm, hbm, hbm, vm, hbm, vm, hbm, vm, vm, vm],
        out_specs=(hbm, hbm, hbm, hbm, vm, vm, vm),
        scratch_shapes=[
            pltpu.VMEM((rows, width), low),
            pltpu.VMEM((PARTS, 2, block, width), low),
            pltpu.VMEM((PARTS, 2, block, width), low),
            pltpu.VMEM((width, units), low),
            pltpu.VMEM((units, width), low),
            pltpu.VMEM((PARTS, 2, block, units), low),
            pltpu.VMEM((PARTS, 2, block, units), low),
            pltpu.VMEM((PARTS, 2, block, units), low),
            pltpu.VMEM((2 * PARTS, block, width), low),
            pltpu.VMEM((2 * PARTS, block, width), low),
            pltpu.VMEM((rows, width), low),
            pltpu.VMEM((2, block, width), f32),
            pltpu.VMEM((width, WIDE), low),
            pltpu.VMEM((WIDE, width), low),
            pltpu.SemaphoreType.DMA((n,)),
            pltpu.SemaphoreType.DMA((n,)),
            pltpu.SemaphoreType.DMA((n,)),
            pltpu.SemaphoreType.DMA((n,)),
            pltpu.SemaphoreType.DMA((3, 2, PARTS)),
            pltpu.SemaphoreType.DMA((2 + 4 * PARTS,)),
            pltpu.SemaphoreType.DMA((PARTS + 2,)),
        ],
        compiler_params=pltpu.CompilerParams(
            collective_id=1, has_side_effects=True, vmem_limit_bytes=62 * 1024 * 1024
        ),
    )(sent, grads, hids, live, up, up_bias, down, down_bias, gain, bias)


def closing_kernel(
    n,
    cap,
    chunks,
    returned_hbm,
    slot_row,
    attn_in_hbm,
    tokens_hbm,
    queries_hbm,
    keys_hbm,
    values_hbm,
    attended_hbm,
    inv_sums,
    expos,
    w_qkv_hbm,
    w_out_hbm,
    gain,
    grad_norm2,
    grad_in,
    grad_qkv,
    grad_wout,
    grad_norms,
    returned,
    attn_in_t,
    tokens_t,
    queries_t,
    keys_t,
    values,
    attended_t,
    w_qkv,
    w_out,
    expo_v,
    grad_att_t,
    grad_h,
    grad_proj_t,
    sent_v,
    norm_terms,
    made,
    *rest,
):
    count = len(chunks)
    totals, landeds = rest[:count], rest[count : 2 * count]
    sem_load, sem_expo, sem_send, sem_recv, sem_pair, sem_step = rest[2 * count :]
    me_d = lax.axis_index("dp")
    me_e = lax.axis_index("expert")
    partner = (1 - me_d, me_e)
    bits = n.bit_length() - 1
    half = n // 2
    rows, width = returned.shape
    toks = slot_row.shape[1]
    each = made.shape[1]
    loads = [
        pltpu.make_async_copy(a, b, sem_load.at[i])
        for i, (a, b) in enumerate(
            (
                (returned_hbm, returned),
                (w_out_hbm, w_out),
                (attended_hbm, attended_t),
                (values_hbm, values),
                (keys_hbm, keys_t),
                (queries_hbm, queries_t),
                (attn_in_hbm, attn_in_t),
                (w_qkv_hbm, w_qkv),
                (tokens_hbm, tokens_t),
            )
        )
    ]

    def expo_load(g):
        here = pl.ds(4 * g, 4)
        return pltpu.make_async_copy(expos.at[here], expo_v.at[here], sem_expo.at[g])

    def slot_copy(i):
        peer = me_e ^ i
        return pltpu.make_async_remote_copy(
            src_ref=sent_v.at[pl.ds(pl.multiple_of(peer * cap, cap), cap)],
            dst_ref=grad_in.at[pl.ds(pl.multiple_of(me_e * cap, cap), cap)],
            send_sem=sem_send.at[i],
            recv_sem=sem_recv.at[i],
            device_id=(me_d, peer),
            device_id_type=MESH_ID,
        )

    def own_slots():
        here = pl.ds(pl.multiple_of(me_e * cap, cap), cap)
        return pltpu.make_async_copy(sent_v.at[here], grad_in.at[here], sem_recv.at[0])

    def offset(order, p):
        k = 0
        for j, b in enumerate(order):
            k = k + lax.rem(p // (1 << (bits - 1 - j)), 2) * (1 << b)
        return k

    def pair_copy(c, q):
        here = pl.ds(q * half, half)
        return pltpu.make_async_remote_copy(
            src_ref=totals[c].at[1, here],
            dst_ref=landeds[c].at[here],
            send_sem=sem_pair.at[0, c, q],
            recv_sem=sem_pair.at[1, c, q],
            device_id=partner,
            device_id_type=MESH_ID,
        )

    def step_copy(c, j):
        many = n >> (j + 1)
        start = n + sum(n >> (i + 1) for i in range(j))
        copy = pltpu.make_async_remote_copy(
            src_ref=totals[c].at[0, pl.ds(many, many)],
            dst_ref=landeds[c].at[pl.ds(start, many)],
            send_sem=sem_step.at[0, c, j],
            recv_sem=sem_step.at[1, c, j],
            device_id=(me_d, me_e ^ (1 << chunks[c][0][j])),
            device_id_type=MESH_ID,
        )
        return copy, many, start

    def make(c):
        order, size, pieces = chunks[c]
        for kind, source, target in pieces:
            if kind == 0:
                term = mm_nt(attn_in_t[...], grad_proj_t[slice(*source), :])
            elif kind == 1:
                term = mm(attended_t[...], grad_h[:, slice(*source)])
            else:
                term = norm_terms[...]
            made[:, :, slice(*target)] = term.reshape(made.shape[0], each, term.shape[1])

        def arrange(p, carry):
            owner = me_e ^ offset(order, p)
            totals[c][0, p] = made[me_d * n + owner, :, 0:size].astype(low)
            totals[c][1, p] = made[(1 - me_d) * n + owner, :, 0:size].astype(low)
            return carry

        lax.fori_loop(0, n, arrange, 0)
        pair_copy(c, 1).start()
        pair_copy(c, 0).start()

    def add_all(c, first, many, start):
        def add_one(p, carry):
            both = totals[c][0, p].astype(f32) + landeds[c][start + p].astype(f32)
            totals[c][0, p] = both.astype(low)
            return carry

        lax.fori_loop(first, first + many, add_one, 0)

    def stage(c, j):
        if j == 0:
            pair_copy(c, 1).wait()
            add_all(c, half, half, 0)
            step_copy(c, 0)[0].start()
            pair_copy(c, 0).wait()
            add_all(c, 0, half, 0)
            return
        copy, many, start = step_copy(c, j - 1)
        copy.wait()
        if many > 1:
            add_all(c, 0, many, start)
            step_copy(c, j)[0].start()
        else:
            both = totals[c][0, 0].astype(f32) + landeds[c][start].astype(f32)
            for kind, source, target in chunks[c][2]:
                (grad_qkv, grad_wout, grad_norms)[kind][:, slice(*source)] = both[:, slice(*target)]

    for i in range(2):
        loads[i].start()
    greet_peers(me_d, me_e, n)
    greet_partner(me_d, me_e)
    place = (slot_row[0:1, :] == lax.broadcasted_iota(jnp.int32, (rows, toks), 0)).astype(f32).astype(low)
    loads[0].wait()
    for i in range(2, 6):
        loads[i].start()
    for g in range(HEADS // 4):
        expo_load(g).start()
    for i in range(6, len(loads)):
        loads[i].start()
    grad_h[...] = mm_tn(place, returned[...]).astype(low)
    loads[1].wait()
    grad_att_t[...] = mm_nt(w_out[...], grad_h[...]).astype(low)
    loads[2].wait()
    pl.semaphore_wait(pltpu.get_barrier_semaphore(), n)
    make(0)
    make(1)
    for i in range(3, 7):
        loads[i].wait()
    in_first = lax.broadcasted_iota(jnp.int32, (1, PAIR), 1) < HEAD_DIM

    def head_group(g):
        expo_load(g).wait()
        ready = {}
        sums = {}
        for pair in range(2):
            p = 2 * g + pair
            pair_rows = pl.ds(p * PAIR, PAIR)
            inv_pair = jnp.concatenate(
                [jnp.broadcast_to(inv_sums[2 * p + h, 0:1, :], (HEAD_DIM, toks)) for h in range(2)], axis=0
            )
            grad_pair = grad_att_t[pair_rows, :].astype(f32)
            cross = grad_pair * attended_t[pair_rows, :].astype(f32) * inv_pair
            scaled = (grad_pair * inv_pair).astype(low)
            for h in range(2):
                in_pair = slice(h * HEAD_DIM, (h + 1) * HEAD_DIM)
                ready[pair, h] = (jnp.sum(cross[in_pair], axis=0, keepdims=True), scaled)
        units = [
            (pair, h, q) for pair in range(2) for h in range(2) for q in reversed(range(toks // QUERIES))
        ]

        def probs_back(unit):
            pair, h, q = unit
            upto = (q + 1) * QUERIES
            here = slice(q * QUERIES, upto)
            mine = in_first if h == 0 else jnp.logical_not(in_first)
            value = jnp.where(mine, values[0:upto, pl.ds((2 * g + pair) * PAIR, PAIR)], jnp.zeros((), low))
            return mm(value, ready[pair, h][1][:, here])

        def scores_back(unit, grad_prob):
            pair, h, q = unit
            upto = (q + 1) * QUERIES
            here = slice(q * QUERIES, upto)
            expo = expo_v[4 * g + 2 * pair + h, 0:upto, here]
            return expo, (expo.astype(f32) * (grad_prob - ready[pair, h][0][:, here])).astype(low)

        def heads_back(unit, held):
            pair, h, q = unit
            expo, grad_score = held
            upto = (q + 1) * QUERIES
            here = slice(q * QUERIES, upto)
            first = (2 * g + pair) * PAIR + h * HEAD_DIM
            head_rows = pl.ds(first, HEAD_DIM)
            grad_proj_t[head_rows, here] = (mm(keys_t[head_rows, 0:upto], grad_score) * scale_val).astype(low)
            key_term = mm_nt(queries_t[head_rows, here], grad_score)
            value_term = mm_nt(ready[pair, h][1][h * HEAD_DIM : (h + 1) * HEAD_DIM, here], expo)
            if upto < toks:
                key_more, value_more = sums[pair, h]
                key_term = jnp.concatenate([key_more[:, 0:upto] + key_term, key_more[:, upto:]], axis=1)
                value_term = jnp.concatenate([value_more[:, 0:upto] + value_term, value_more[:, upto:]], axis=1)
            sums[pair, h] = (key_term, value_term)
            if q == 0:
                grad_proj_t[pl.ds(width + first, HEAD_DIM), :] = key_term.astype(low)
                grad_proj_t[pl.ds(2 * width + first, HEAD_DIM), :] = value_term.astype(low)

        staged(units, probs_back, scores_back, heads_back)

    groups = HEADS // 4
    head_group(0)
    make(2)
    stage(0, 0)
    stage(1, 0)
    for g in range(1, groups):
        head_group(g)
        make(2 + g)
        stage(1 + g, 0)
    for i in range(7, len(loads)):
        loads[i].wait()
    grad_attn_t = mm(w_qkv[...], grad_proj_t[...])
    stage(1 + groups, 0)
    normed_t, inv_std = normalize(tokens_t[...].astype(f32), axis=0)
    gain_col = jnp.broadcast_to(gain[...], (LANES, width)).T[:, 0:1]
    norm_terms[...] = jnp.concatenate(
        [
            jnp.sum(grad_attn_t * normed_t, axis=1, keepdims=True),
            jnp.sum(grad_attn_t, axis=1, keepdims=True),
            grad_norm2[...].T[:, 0:2],
            jnp.zeros((width, LANES - 4), f32),
        ],
        axis=1,
    )
    result = grad_h[...].astype(f32).T + norm_back(grad_attn_t, normed_t, inv_std, gain_col, axis=0)
    sent_v[...] = mm_nt(place, result.astype(low)).astype(low)
    own_slots().start()

    def start_slots(i, carry):
        slot_copy(i).start()
        return carry

    lax.fori_loop(1, n, start_slots, 0)
    make(count - 1)
    done = [1] * (count - 1) + [0]
    for wave in range(1, bits + count + 1):
        for c in range(count):
            late = c // 4
            while done[c] <= min(bits, wave - late):
                stage(c, done[c])
                done[c] += 1
    own_slots().wait()

    def wait_slots(i, carry):
        slot_copy(i).wait()
        return carry

    lax.fori_loop(1, n, wait_slots, 0)


def closing(returned, slot_row, attn_in_t, tokens_t, queries_t, keys_t, values, attended_t, inv_sums, expos, w_qkv, w_out, gain, grad_norm2):
    n = lax.axis_size("expert")
    owners = n * lax.axis_size("dp")
    rows, width = returned.shape
    toks = slot_row.shape[1]
    each = width // owners
    bits = n.bit_length() - 1
    groups = HEADS // 4
    part = width // groups
    orders = [list(range(bits)), [1, 0] + list(range(2, bits))]
    chunks = []
    for c in range(2):
        size = width // 2
        chunks.append((orders[c], size, [(1, (c * size, (c + 1) * size), (0, size))]))
    for g in range(groups):
        pieces = [
            (0, (k * width + g * part, k * width + (g + 1) * part), (k * part, (k + 1) * part)) for k in range(3)
        ]
        chunks.append((orders[g % 2], 3 * part, pieces))
    chunks.append((orders[0], LANES, [(2, (0, LANES), (0, LANES))]))
    count = len(chunks)
    widest = max(size for _, size, _ in chunks)
    vm = pl.BlockSpec(memory_space=pltpu.VMEM)
    hbm = pl.BlockSpec(memory_space=pl.ANY)
    shape = jax.ShapeDtypeStruct
    return pl.pallas_call(
        functools.partial(closing_kernel, n, rows // n, chunks),
        out_shape=(
            shape((rows, width), low),
            shape((each, 3 * width), f32),
            shape((each, width), f32),
            shape((each, LANES), f32),
        ),
        in_specs=[hbm, vm, hbm, hbm, hbm, hbm, hbm, hbm, vm, hbm, hbm, hbm, vm, vm],
        out_specs=(hbm, vm, vm, vm),
        scratch_shapes=[
            pltpu.VMEM((rows, width), low),
            pltpu.VMEM((width, toks), low),
            pltpu.VMEM((width, toks), low),
            pltpu.VMEM((width, toks), low),
            pltpu.VMEM((width, toks), low),
            pltpu.VMEM((toks, width), low),
            pltpu.VMEM((width, toks), low),
            pltpu.VMEM(w_qkv.shape, low),
            pltpu.VMEM(w_out.shape, low),
            pltpu.VMEM((HEADS, toks, toks), low),
            pltpu.VMEM((width, toks), low),
            pltpu.VMEM((toks, width), low),
            pltpu.VMEM((3 * width, toks), low),
            pltpu.VMEM((rows, width), low),
            pltpu.VMEM((width, LANES), f32),
            pltpu.VMEM((owners, each, widest), f32),
        ]
        + [pltpu.VMEM((2, n, each, size), low) for _, size, _ in chunks]
        + [pltpu.VMEM((2 * n, each, size), low) for _, size, _ in chunks]
        + [
            pltpu.SemaphoreType.DMA((9,)),
            pltpu.SemaphoreType.DMA((groups,)),
            pltpu.SemaphoreType.DMA((n,)),
            pltpu.SemaphoreType.DMA((n,)),
            pltpu.SemaphoreType.DMA((2, count, 2)),
            pltpu.SemaphoreType.DMA((2, count, bits)),
        ],
        compiler_params=pltpu.CompilerParams(
            collective_id=2, has_side_effects=True, vmem_limit_bytes=62 * 1024 * 1024
        ),
    )(returned, slot_row, attn_in_t, tokens_t, queries_t, keys_t, values, attended_t, inv_sums, expos, w_qkv, w_out, gain, grad_norm2)


def handing_kernel(up_in, down_in, hidden_in, rows_in, qkv_in, wout_in, bup_in, bdown_in, up, down, hidden, rows, qkv, wout, bup, bdown):
    up[...] = up_in[...].astype(f32)
    down[...] = down_in[...].astype(f32)
    hidden[...] = hidden_in[...]
    rows[...] = rows_in[...]
    qkv[...] = qkv_in[...]
    wout[...] = wout_in[...]
    bup[...] = bup_in[...]
    half = bdown.shape[1]
    bdown[...] = jnp.where(lax.axis_index("dp") == 0, bdown_in[:, 0:half], bdown_in[:, half : 2 * half])


def handing(grad_up, grad_down, hidden_out, grad_in, grad_qkv, grad_wout, grad_bup, grad_bdown):
    steps = 4
    arrays = (grad_up, grad_down, hidden_out, grad_in, grad_qkv, grad_wout, grad_bup, grad_bdown)
    small = grad_bdown.shape[1] // lax.axis_size("dp")
    types = (f32, f32, low, low, f32, f32, f32, f32)

    def block(shape, cut):
        if cut:
            return pl.BlockSpec((shape[0] // steps, shape[1]), lambda i: (i, 0))
        return pl.BlockSpec(shape, lambda i: (0, 0))

    shapes = [x.shape for x in arrays[:-1]] + [(1, small)]
    return pl.pallas_call(
        handing_kernel,
        grid=(steps,),
        out_shape=tuple(jax.ShapeDtypeStruct(shape, t) for shape, t in zip(shapes, types)),
        in_specs=[block(x.shape, i < 4) for i, x in enumerate(arrays)],
        out_specs=tuple(block(shape, i < 4) for i, shape in enumerate(shapes)),
        compiler_params=pltpu.CompilerParams(vmem_limit_bytes=62 * 1024 * 1024),
    )(*arrays)


def on_device(
    hidden_in,
    buckets,
    expert_of_bucket,
    lengths,
    norm1_gain,
    norm1_bias,
    w_qkv,
    w_out,
    norm2_gain,
    norm2_bias,
    w_up,
    b_up,
    w_down,
    b_down,
    grad_out,
):
    (
        sent,
        grads,
        hids,
        live,
        attn_in_t,
        tokens_t,
        queries_t,
        keys_t,
        values,
        attended_t,
        inv_sums,
        slot_row,
        expos,
    ) = starting(
        hidden_in,
        grad_out,
        buckets.reshape(1, -1),
        expert_of_bucket[None],
        lengths,
        norm1_gain[None],
        norm1_bias[None],
        w_qkv,
        w_out,
        w_down[0],
    )
    returned, hidden_out, grad_up, grad_down, grad_bup, grad_bdown, grad_norm2 = expert_block(
        sent, grads, hids, live, w_up[0], b_up, w_down[0], b_down, norm2_gain[None], norm2_bias[None]
    )
    grad_in, grad_qkv, grad_wout, grad_norms = closing(
        returned,
        slot_row,
        attn_in_t,
        tokens_t,
        queries_t,
        keys_t,
        values,
        attended_t,
        inv_sums,
        expos,
        w_qkv,
        w_out,
        norm1_gain[None],
        grad_norm2,
    )
    grad_up, grad_down, hidden_out, grad_in, grad_qkv, grad_wout, grad_bup, grad_bdown = handing(
        grad_up, grad_down, hidden_out, grad_in, grad_qkv, grad_wout, grad_bup, grad_bdown
    )
    return (
        hidden_out,
        grad_in,
        grad_qkv,
        grad_wout,
        grad_norms[:, 0],
        grad_norms[:, 1],
        grad_norms[:, 2],
        grad_norms[:, 3],
        grad_up[None],
        grad_bup,
        grad_down[None],
        grad_bdown,
    )


def solution(mesh):
    return jax.shard_map(
        on_device,
        mesh=mesh,
        in_specs=(
            P(("dp", "expert"), None),
            P(("dp", "expert"), None),
            P(),
            P(("dp", "expert"), None),
            P(),
            P(),
            P(),
            P(),
            P(),
            P(),
            P("expert", None, "dp"),
            P("expert", "dp"),
            P("expert", "dp", None),
            P("expert", None),
            P(("dp", "expert"), None),
        ),
        out_specs=(
            P(("dp", "expert"), None),
            P(("dp", "expert"), None),
            P(("dp", "expert"), None),
            P(("dp", "expert"), None),
            P(("dp", "expert")),
            P(("dp", "expert")),
            P(("dp", "expert")),
            P(("dp", "expert")),
            P("expert", None, "dp"),
            P("expert", "dp"),
            P("expert", "dp", None),
            P("expert", "dp"),
        ),
        check_vma=False,
    )
```

```python
import functools

import jax
import jax.numpy as jnp
from jax import lax
from jax.experimental import pallas as pl
from jax.experimental.pallas import tpu as pltpu
from jax.sharding import PartitionSpec as P

HEADS = 16
HEAD_DIM = 64


norm_eps = 1e-05
masked_score = -1e30
root_half = 0.7071067811865476
inv_root_tau = 0.3989422804014327

MESH_ID = pl.DeviceIdType.MESH
PARTS = 4
WIDE = 512
LANES = 128
QUERIES = 256
PAIR = 2 * HEAD_DIM
scale_val = HEAD_DIM ** (-0.5)
low = jnp.bfloat16
f32 = jnp.float32


def mm(a, b):
    return jnp.dot(a, b, preferred_element_type=f32)


def mm_nt(a, b):
    return lax.dot_general(a, b, (((1,), (1,)), ((), ())), preferred_element_type=f32)


def mm_tn(a, b):
    return lax.dot_general(a, b, (((0,), (0,)), ((), ())), preferred_element_type=f32)


def normalize(values, axis=-1):
    mean_val = jnp.mean(values, axis=axis, keepdims=True)
    centered = values - mean_val
    variance = jnp.mean(centered * centered, axis=axis, keepdims=True)
    inv_std = lax.rsqrt(variance + norm_eps)
    return (centered * inv_std, inv_std)


def norm_back(grad_normed, normed, inv_std, gain_vec, axis=-1):
    scaled = grad_normed * gain_vec
    mean_grad = jnp.mean(scaled, axis=axis, keepdims=True)
    mean_cross = jnp.mean(scaled * normed, axis=axis, keepdims=True)
    return inv_std * (scaled - mean_grad - normed * mean_cross)


def gelu_parts(pre):
    bell = jnp.exp(-0.5 * pre * pre)
    den = 1.0 + (0.3275911 * root_half) * jnp.abs(pre)
    t = pl.reciprocal(den, approx=True)
    t = t * (2.0 - den * t)
    tail = t * (
        0.5 * 0.254829592
        + t * (0.5 * -0.284496736 + t * (0.5 * 1.421413741 + t * (0.5 * -1.453152027 + t * (0.5 * 1.061405429))))
    )
    tail = tail * bell
    phi = jnp.where(pre >= 0.0, 1.0 - tail, tail)
    return pre * phi, phi + pre * (inv_root_tau * bell)


def greet_peers(me_d, me_e, n):
    barrier = pltpu.get_barrier_semaphore()

    def signal(i, carry):
        pl.semaphore_signal(barrier, inc=1, device_id=(me_d, me_e ^ i), device_id_type=MESH_ID)
        return carry

    lax.fori_loop(1, n, signal, 0)


def greet_partner(me_d, me_e):
    pl.semaphore_signal(
        pltpu.get_barrier_semaphore(), inc=1, device_id=(1 - me_d, me_e), device_id_type=MESH_ID
    )


def staged(units, *stages):
    held = [None] * len(units)
    for step in range(len(units) + len(stages) - 1):
        for k, stage in enumerate(stages):
            i = step - k
            if 0 <= i < len(units):
                held[i] = stage(units[i]) if k == 0 else stage(units[i], held[i])


def start_kernel(
    n,
    cap,
    hidden,
    grad_out,
    buckets,
    expert_of,
    lengths,
    gain,
    bias,
    w_qkv_hbm,
    w_out_hbm,
    down_hbm,
    sent,
    grads,
    hids,
    live,
    attn_in_hbm,
    tokens_hbm,
    queries_hbm,
    keys_hbm,
    values_hbm,
    attended_hbm,
    inv_sums,
    slot_row,
    expos,
    arrived,
    w_qkv,
    w_out,
    down,
    grad_raw,
    grad_v,
    grad_p,
    hid_v,
    attn_in_t,
    tokens_t,
    queries_t,
    keys_t,
    values,
    attended_t,
    attn_in_v,
    proj,
    values_t,
    allow,
    tokens,
    expo_v,
    sent_v,
    counts_out,
    counts_in,
    sem_send,
    sem_recv,
    sem_count_send,
    sem_count_recv,
    sem_pair,
    sem_load,
    sem_store,
    sem_keep,
    sem_turn,
):
    me_d = lax.axis_index("dp")
    me_e = lax.axis_index("expert")
    partner = (1 - me_d, me_e)
    rows, width = arrived.shape
    toks = buckets.shape[1]
    lanes = counts_out.shape[1]

    def slot_copy(i):
        peer = me_e ^ i
        return pltpu.make_async_remote_copy(
            src_ref=hidden.at[pl.ds(pl.multiple_of(peer * cap, cap), cap)],
            dst_ref=arrived.at[pl.ds(pl.multiple_of(me_e * cap, cap), cap)],
            send_sem=sem_send.at[i],
            recv_sem=sem_recv.at[i],
            device_id=(me_d, peer),
            device_id_type=MESH_ID,
        )

    def own_slots():
        here = pl.ds(pl.multiple_of(me_e * cap, cap), cap)
        return pltpu.make_async_copy(hidden.at[here], arrived.at[here], sem_recv.at[0])

    def count_copy(i):
        return pltpu.make_async_remote_copy(
            src_ref=counts_out,
            dst_ref=counts_in.at[me_e],
            send_sem=sem_count_send.at[i],
            recv_sem=sem_count_recv.at[i],
            device_id=(me_d, me_e ^ i),
            device_id_type=MESH_ID,
        )

    grad_load = pltpu.make_async_copy(grad_out, grad_raw, sem_load.at[0])
    qkv_load = pltpu.make_async_copy(w_qkv_hbm, w_qkv, sem_load.at[1])
    out_load = pltpu.make_async_copy(w_out_hbm, w_out, sem_load.at[2])
    down_load = pltpu.make_async_copy(down_hbm, down, sem_load.at[3])
    pair_grads_store = pltpu.make_async_copy(grad_p, grads.at[1], sem_store.at[2])
    def keep(i, g):
        source, target = (
            (attn_in_t, attn_in_hbm),
            (tokens_t, tokens_hbm),
            (queries_t, queries_hbm),
            (keys_t, keys_hbm),
            (attended_t, attended_hbm),
            (values, values_hbm),
        )[i]
        here = pl.ds(pl.multiple_of(g * 2 * PAIR, 2 * PAIR), 2 * PAIR)
        if i == 5:
            return pltpu.make_async_copy(source.at[:, here], target.at[:, here], sem_keep.at[i, g])
        return pltpu.make_async_copy(source.at[here], target.at[here], sem_keep.at[i, g])

    def hid_store(k):
        return pltpu.make_async_copy(hid_v.at[k], hids.at[k], sem_store.at[3 + k])

    def hidden_grad(k, grad_ref):
        def tile(i, carry):
            here = pl.ds(pl.multiple_of((i // 2) * WIDE, WIDE), WIDE)
            some = pl.ds(pl.multiple_of(lax.rem(i, 2) * (rows // 2), rows // 2), rows // 2)
            hid_v[k, some, here] = mm_nt(grad_ref[some, :], down[here, :]).astype(low)
            return carry

        lax.fori_loop(0, 2 * (down.shape[0] // WIDE), tile, 0)
        hid_store(k).start()

    grad_store = pltpu.make_async_copy(grad_v, grads.at[0], sem_store.at[0])
    grad_pair = pltpu.make_async_remote_copy(
        src_ref=grad_v,
        dst_ref=grad_p,
        send_sem=sem_pair.at[0],
        recv_sem=sem_pair.at[1],
        device_id=partner,
        device_id_type=MESH_ID,
    )

    def start_slots(i, carry):
        slot_copy(i).start()
        return carry

    grad_load.start()

    @pl.when(me_d == 1)
    def _():
        down_load.start()

    greet_peers(me_d, me_e, n)
    greet_partner(me_d, me_e)
    lane_ids = lax.broadcasted_iota(jnp.int32, (toks, lanes), 1)
    bucket = jnp.broadcast_to(buckets[...], (lanes, toks)).T[:, 0:n]
    bucket_hot = (bucket == lane_ids[:, 0:n]).astype(f32).astype(low)
    serves_t = (expert_of[...] == lax.broadcasted_iota(jnp.int32, (lanes, n), 0)).astype(f32).astype(low)
    expert_hot = mm_nt(bucket_hot, serves_t)
    counts_out[...] = jnp.broadcast_to(jnp.sum(expert_hot, axis=0, keepdims=True), counts_out.shape)
    counts_in[me_e] = counts_out[...]

    def start_counts(i, carry):
        count_copy(i).start()
        return carry

    pl.semaphore_wait(pltpu.get_barrier_semaphore(), n)
    lax.fori_loop(1, n, start_counts, 0)
    lax.fori_loop(1, n // 2, start_slots, 0)

    @pl.when(me_d == 0)
    def _():
        lax.fori_loop(n // 2, n, start_slots, 0)

    own_slots().start()
    qkv_load.start()
    out_load.start()

    row_ids = lax.broadcasted_iota(jnp.int32, (toks, toks), 0)
    col_ids = lax.broadcasted_iota(jnp.int32, (toks, toks), 1)
    earlier = (col_ids < row_ids).astype(f32).astype(low)
    before = mm(earlier, expert_hot.astype(low))
    slot = jnp.sum(expert_hot * (before + (lane_ids * cap).astype(f32)), axis=1, keepdims=True)
    slot_row[...] = jnp.broadcast_to(slot, (toks, lanes)).T[0:8, :].astype(jnp.int32)
    ends = jnp.zeros((1, toks), jnp.int32)
    begin = jnp.zeros((1, toks), jnp.int32)
    places = lax.broadcasted_iota(jnp.int32, (1, toks), 1)
    for s in range(lengths.shape[1]):
        ends = ends + lengths[0:1, s : s + 1]
        begin = jnp.where(places >= ends, ends, begin)
    allow[...] = jnp.where(jnp.logical_and(row_ids <= col_ids, row_ids >= begin), 0.0, masked_score)

    def wait_counts(i, carry):
        count_copy(i).wait()
        return carry

    lax.fori_loop(1, n, wait_counts, 0)
    grad_load.wait()

    def mark(s, carry):
        here = pl.ds(pl.multiple_of(s * cap, cap), cap)
        mine = lax.broadcasted_iota(jnp.int32, (1, lanes), 1) == me_e
        count = jnp.sum(jnp.where(mine, counts_in[s, 0:1, :], 0.0), axis=1, keepdims=True)
        taken = (lax.broadcasted_iota(jnp.int32, (cap, 1), 0).astype(f32) < count).astype(f32)
        live[here, :] = taken
        grad_v[here, :] = (grad_raw[here, :].astype(f32) * taken).astype(low)
        return carry

    lax.fori_loop(0, n, mark, 0)
    grad_store.start()
    grad_pair.start()
    @pl.when(me_d == 0)
    def _():
        def wait_sent(i, carry):
            slot_copy(i).wait_send()
            return carry

        lax.fori_loop(n // 2, n, wait_sent, 0)
        pl.semaphore_signal(sem_turn, inc=1, device_id=partner, device_id_type=MESH_ID)

    @pl.when(me_d == 1)
    def _():
        pl.semaphore_wait(sem_turn, 1)
        lax.fori_loop(n // 2, n, start_slots, 0)

    grad_pair.wait()
    pair_grads_store.start()

    @pl.when(me_d == 1)
    def _():
        down_load.wait()
        hidden_grad(0, grad_v)
        hidden_grad(1, grad_p)


    own_slots().wait()

    def wait_slots(i, carry):
        slot_copy(i).wait_recv()
        return carry

    lax.fori_loop(1, n, wait_slots, 0)

    pick = (slot.astype(jnp.int32) == lax.broadcasted_iota(jnp.int32, (toks, rows), 1)).astype(f32).astype(low)
    tokens[...] = mm(pick, arrived[...])
    normed, _ = normalize(tokens[...])
    attn_in = (normed * gain[...] + bias[...]).astype(low)
    attn_in_v[...] = attn_in
    qkv_load.wait()
    step = width // 4
    for c in range(3 * width // step):
        here = slice(c * step, (c + 1) * step)
        part = mm(attn_in, w_qkv[:, here])
        if c * step < width:
            part = part.astype(low).astype(f32) * scale_val
        proj[:, here] = part.astype(low)
    values_t[...] = proj[:, 2 * width : 3 * width].T

    def expo_store(g):
        here = pl.ds(pl.multiple_of(4 * g, 4), 4)
        return pltpu.make_async_copy(expo_v.at[here], expos.at[here], sem_store.at[5 + g])

    in_first = lax.broadcasted_iota(jnp.int32, (1, PAIR), 1) < HEAD_DIM

    def head_group(g, carry):
        units = [
            (2 * g + pair, h, q) for pair in range(2) for h in range(2) for q in range(toks // QUERIES)
        ]

        def score(unit):
            p, h, q = unit
            first = pl.multiple_of(p * PAIR, PAIR)
            upto = (q + 1) * QUERIES
            here = slice(q * QUERIES, upto)
            mine = in_first if h == 0 else jnp.logical_not(in_first)
            query = jnp.where(mine, proj[here, pl.ds(first, PAIR)], jnp.zeros((), low))
            scores = mm_nt(proj[0:upto, pl.ds(pl.multiple_of(width + first, PAIR), PAIR)], query)
            return scores + allow[0:upto, here]

        def soft(unit, scores):
            expo = jnp.exp(scores - jnp.max(scores, axis=0, keepdims=True))
            inv = 1.0 / jnp.sum(expo, axis=0, keepdims=True)
            return expo.astype(low), inv

        def attend(unit, held):
            p, h, q = unit
            expo, inv = held
            upto = (q + 1) * QUERIES
            here = slice(q * QUERIES, upto)
            head_rows = pl.ds(pl.multiple_of(p * PAIR + h * HEAD_DIM, HEAD_DIM), HEAD_DIM)
            expo_v[2 * p + h, 0:upto, here] = expo
            if upto < toks:
                expo_v[2 * p + h, upto:toks, here] = jnp.zeros((toks - upto, QUERIES), low)
            out = mm(values_t[head_rows, 0:upto], expo)
            attended_t[head_rows, here] = (out * inv).astype(low)
            inv_sums[2 * p + h, :, here] = jnp.broadcast_to(inv, (8, QUERIES))

        staged(units, score, soft, attend)
        here = pl.ds(pl.multiple_of(g * 2 * PAIR, 2 * PAIR), 2 * PAIR)
        queries_t[here, :] = proj[:, here].T
        keys_t[here, :] = proj[:, pl.ds(pl.multiple_of(width + g * 2 * PAIR, 2 * PAIR), 2 * PAIR)].T
        values[:, here] = proj[:, pl.ds(pl.multiple_of(2 * width + g * 2 * PAIR, 2 * PAIR), 2 * PAIR)]
        tokens_t[here, :] = tokens[:, here].T.astype(low)
        attn_in_t[here, :] = attn_in_v[:, here].T
        expo_store(g).start()
        for i in range(6):
            keep(i, g).start()
        return carry

    lax.fori_loop(0, HEADS // 4, head_group, 0)
    out_load.wait()
    residual = (tokens[...] + mm_tn(attended_t[...], w_out[...])).astype(low)
    place = (slot_row[0:1, :] == lax.broadcasted_iota(jnp.int32, (rows, toks), 0)).astype(f32).astype(low)
    sent_v[...] = mm(place, residual).astype(low)
    sent_store = pltpu.make_async_copy(sent_v, sent, sem_store.at[1])
    sent_store.start()

    for g in range(HEADS // 4):
        expo_store(g).wait()
        for i in range(6):
            keep(i, g).wait()
    grad_store.wait()
    pair_grads_store.wait()

    @pl.when(me_d == 1)
    def _():
        hid_store(0).wait()
        hid_store(1).wait()


    def wait_sent(i, carry):
        slot_copy(i).wait_send()
        return carry

    lax.fori_loop(1, n // 2, wait_sent, 0)

    @pl.when(me_d == 1)
    def _():
        lax.fori_loop(n // 2, n, wait_sent, 0)

    sent_store.wait()


def starting(hidden, grad_out, buckets, expert_of, lengths, gain, bias, w_qkv, w_out, down):
    n = lax.axis_size("expert")
    rows, width = hidden.shape
    toks = buckets.shape[1]
    units = down.shape[0]
    lanes = 128
    vm = pl.BlockSpec(memory_space=pltpu.VMEM)
    hbm = pl.BlockSpec(memory_space=pl.ANY)
    shape = jax.ShapeDtypeStruct
    return pl.pallas_call(
        functools.partial(start_kernel, n, rows // n),
        out_shape=(
            shape((rows, width), low),
            shape((2, rows, width), low),
            shape((2, rows, units), low),
            shape((rows, 1), f32),
            shape((width, toks), low),
            shape((width, toks), low),
            shape((width, toks), low),
            shape((width, toks), low),
            shape((toks, width), low),
            shape((width, toks), low),
            shape((HEADS, 8, toks), f32),
            shape((8, toks), jnp.int32),
            shape((HEADS, toks, toks), low),
        ),
        in_specs=[hbm, hbm, vm, vm, vm, vm, vm, hbm, hbm, hbm],
        out_specs=(hbm, hbm, hbm, vm, hbm, hbm, hbm, hbm, hbm, hbm, vm, vm, hbm),
        scratch_shapes=[
            pltpu.VMEM((rows, width), low),
            pltpu.VMEM(w_qkv.shape, low),
            pltpu.VMEM(w_out.shape, low),
            pltpu.VMEM(down.shape, low),
            pltpu.VMEM((rows, width), low),
            pltpu.VMEM((rows, width), low),
            pltpu.VMEM((rows, width), low),
            pltpu.VMEM((2, rows, units), low),
            pltpu.VMEM((width, toks), low),
            pltpu.VMEM((width, toks), low),
            pltpu.VMEM((width, toks), low),
            pltpu.VMEM((width, toks), low),
            pltpu.VMEM((toks, width), low),
            pltpu.VMEM((width, toks), low),
            pltpu.VMEM((toks, width), low),
            pltpu.VMEM((toks, 3 * width), low),
            pltpu.VMEM((width, toks), low),
            pltpu.VMEM((toks, toks), f32),
            pltpu.VMEM((toks, width), f32),
            pltpu.VMEM((HEADS, toks, toks), low),
            pltpu.VMEM((rows, width), low),
            pltpu.VMEM((8, lanes), f32),
            pltpu.VMEM((n, 8, lanes), f32),
            pltpu.SemaphoreType.DMA((n,)),
            pltpu.SemaphoreType.DMA((n,)),
            pltpu.SemaphoreType.DMA((n,)),
            pltpu.SemaphoreType.DMA((n,)),
            pltpu.SemaphoreType.DMA((2,)),
            pltpu.SemaphoreType.DMA((4,)),
            pltpu.SemaphoreType.DMA((5 + HEADS // 4,)),
            pltpu.SemaphoreType.DMA((6, HEADS // 4)),
            pltpu.SemaphoreType.REGULAR,
        ],
        compiler_params=pltpu.CompilerParams(
            collective_id=3, has_side_effects=True, vmem_limit_bytes=60 * 1024 * 1024
        ),
    )(hidden, grad_out, buckets, expert_of, lengths, gain, bias, w_qkv, w_out, down)


def expert_kernel(
    n,
    cap,
    sent,
    grads,
    hids,
    live,
    up_hbm,
    up_bias,
    down_hbm,
    down_bias,
    gain,
    bias,
    returned,
    hidden_out,
    grad_up,
    grad_down,
    grad_bup,
    grad_bdown,
    grad_norm,
    rows_in,
    ffn_in,
    grad_rows,
    up,
    down,
    hid,
    act,
    pre_grad,
    part_out,
    part_in,
    back,
    mine,
    tile,
    tile_down,
    sem_send,
    sem_recv,
    sem_back_send,
    sem_back_recv,
    sem_pair,
    sem_load,
    sem_store,
):
    me_d = lax.axis_index("dp")
    me_e = lax.axis_index("expert")
    rows = rows_in.shape[0]
    width = rows_in.shape[1]
    units = up.shape[1]
    block = rows // PARTS
    many = n // PARTS
    partner = (1 - me_d, me_e)

    def base_of(part):
        return pl.multiple_of(((me_e // many) ^ part) * block, block)

    def slot_copy(i):
        peer = me_e ^ i
        return pltpu.make_async_remote_copy(
            src_ref=sent.at[pl.ds(pl.multiple_of(peer * cap, cap), cap)],
            dst_ref=rows_in.at[pl.ds(pl.multiple_of(me_e * cap, cap), cap)],
            send_sem=sem_send.at[i],
            recv_sem=sem_recv.at[i],
            device_id=(me_d, peer),
            device_id_type=MESH_ID,
        )

    def own_slots():
        own = pl.ds(pl.multiple_of(me_e * cap, cap), cap)
        return pltpu.make_async_copy(sent.at[own], rows_in.at[own], sem_recv.at[0])

    def back_copy(i):
        peer = me_e ^ i
        return pltpu.make_async_remote_copy(
            src_ref=back.at[pl.ds(pl.multiple_of(peer * cap, cap), cap)],
            dst_ref=returned.at[pl.ds(pl.multiple_of(me_e * cap, cap), cap)],
            send_sem=sem_back_send.at[i],
            recv_sem=sem_back_recv.at[i],
            device_id=(me_d, peer),
            device_id_type=MESH_ID,
        )

    def own_back():
        own = pl.ds(pl.multiple_of(me_e * cap, cap), cap)
        return pltpu.make_async_copy(back.at[own], returned.at[own], sem_back_recv.at[0])

    def pair_copy(src, dst, kind, part):
        return pltpu.make_async_remote_copy(
            src_ref=src,
            dst_ref=dst,
            send_sem=sem_pair.at[kind - 1, 0, part],
            recv_sem=sem_pair.at[kind - 1, 1, part],
            device_id=partner,
            device_id_type=MESH_ID,
        )

    def ffn_pair(part):
        return pair_copy(ffn_in.at[part, 0], ffn_in.at[part, 1], 1, part)

    def part_pair(part):
        return pair_copy(part_out.at[part], part_in.at[part], 2, part)

    def out_pair(part):
        return pair_copy(part_out.at[PARTS + part], part_in.at[PARTS + part], 3, part)

    def hid_load(unit):
        part, k = part_of(unit), core_of(unit)
        here = pl.ds(base_of(part), block)
        return pltpu.make_async_copy(hids.at[k, here], hid.at[part, k], sem_load.at[2 + unit])

    def grads_load(unit):
        part, k = part_of(unit), core_of(unit)
        here = pl.ds(base_of(part), block)
        return pltpu.make_async_copy(grads.at[k, here], grad_rows.at[part, k], sem_load.at[2 + 2 * PARTS + unit])

    def part_of(unit):
        return lax.rem(unit, PARTS)

    def core_of(unit):
        return me_d ^ (unit // PARTS)

    up_load = pltpu.make_async_copy(up_hbm, up, sem_load.at[0])
    down_load = pltpu.make_async_copy(down_hbm, down, sem_load.at[1])
    own_slots().start()

    @pl.when(me_d == 0)
    def _():
        down_load.start()
        for unit in range(2 * PARTS):
            grads_load(unit).start()
        up_load.start()

    @pl.when(me_d == 1)
    def _():
        up_load.start()
        hid_load(0).start()
        grads_load(0).start()

    barrier = pltpu.get_barrier_semaphore()
    greet_peers(me_d, me_e, n)

    @pl.when(me_d == 0)
    def _():
        pl.semaphore_wait(barrier, n - 1)
        greet_partner(me_d, me_e)

    @pl.when(me_d == 1)
    def _():
        pl.semaphore_wait(barrier, n)
        greet_partner(me_d, me_e)

    def start_slots(i, carry):
        slot_copy(i).start()
        return carry

    lax.fori_loop(1, n, start_slots, 0)
    grad_norm[...] = jnp.zeros_like(grad_norm)
    up_load.wait()

    @pl.when(me_d == 1)
    def _():
        down_load.start()
        for unit in range(1, 2 * PARTS):
            hid_load(unit).start()
            grads_load(unit).start()


    def stats(base):
        return normalize(rows_in[pl.ds(base, block), :].astype(f32))

    def arrive(part):
        @pl.when(part == 0)
        def _():
            own_slots().wait()

        @pl.when(part > 0)
        def _():
            slot_copy(part * many).wait()

        def wait_slots(j, c):
            slot_copy(part * many + j).wait()
            return c

        lax.fori_loop(1, many, wait_slots, 0)
        normed, _ = stats(base_of(part))
        ffn_in[part, 0] = (normed * gain[...] + bias[...]).astype(low)

    @pl.when(me_d == 0)
    def _():
        def arrive_all(part, carry):
            arrive(part)

            @pl.when(part == 0)
            def _():
                pl.semaphore_wait(barrier, 1)

            ffn_pair(part).start()
            return carry

        def hidden_grad(unit, carry):
            part, k = part_of(unit), core_of(unit)
            grads_load(unit).wait()
            hid[part, k] = mm_nt(grad_rows[part, k], down[...]).astype(low)
            return carry

        down_load.wait()
        lax.fori_loop(0, 2 * PARTS, hidden_grad, 0)
        lax.fori_loop(0, PARTS, arrive_all, 0)

    def hidden(part, k):
        def before(cols):
            return mm(ffn_in[part, k], up[:, cols]) + up_bias[:, cols]

        def after(cols, pre):
            a, slope = gelu_parts(pre)
            act[part, k, :, cols] = a.astype(low)
            pre_grad[part, k, :, cols] = (hid[part, k, :, cols].astype(f32) * slope).astype(low)

        staged([pl.ds(f * WIDE, WIDE) for f in range(units // WIDE)], before, after)

    def send_back(unit):
        part = part_of(unit)
        base = base_of(part)
        part_pair(part).wait_recv()
        grad_ffn = mine[lax.rem(unit, 2)] + part_in[part].astype(f32)
        normed, inv_std = stats(base)
        grad_norm[0:1, :] += jnp.sum(grad_ffn * normed, axis=0, keepdims=True)
        grad_norm[1:2, :] += jnp.sum(grad_ffn, axis=0, keepdims=True)
        result = grad_rows[part, 0].astype(f32) + norm_back(grad_ffn, normed, inv_std, gain[...])
        back[pl.ds(base, block), :] = result.astype(low)

        @pl.when(part == 0)
        def _():
            own_back().start()

        @pl.when(part > 0)
        def _():
            back_copy(part * many).start()

        def start_back(j, c):
            back_copy(part * many + j).start()
            return c

        lax.fori_loop(1, many, start_back, 0)

    def work(unit, carry):
        part, k = part_of(unit), core_of(unit)
        ahead = unit + 1 - PARTS

        @pl.when((me_d == 1) & (ahead >= 0) & (ahead < PARTS))
        def _():
            arrive(ahead)
            ffn_pair(ahead).start()

        @pl.when(k == 1)
        def _():
            ffn_pair(part).wait_recv()

        @pl.when(me_d == 1)
        def _():
            hid_load(unit).wait()
            grads_load(unit).wait()

        hidden(part, k)
        slot = lax.rem(unit, 2)
        mine[slot] = mm_nt(pre_grad[part, k], up[...])

        @pl.when((unit == 0) & (me_d == 1))
        def _():
            down_load.wait()

        @pl.when(k == 1)
        def _():
            part_out[part] = mine[slot].astype(low)
            part_pair(part).start()
            part_out[PARTS + part] = mm(act[part, 1], down[...]).astype(low)
            out_pair(part).start()

        @pl.when((unit > 0) & (core_of(unit - 1) == 0))
        def _():
            send_back(unit - 1)

        return carry

    lax.fori_loop(0, 2 * PARTS, work, 0)

    @pl.when(me_d == 1)
    def _():
        send_back(2 * PARTS - 1)

    def output_own(part, carry):
        base = base_of(part)
        here = pl.ds(base, block)
        product = mm(act[part, 0], down[...])
        out_pair(part).wait_recv()
        total = rows_in[here, :].astype(f32) + product + part_in[PARTS + part].astype(f32) + down_bias[...]
        rows_in[here, :] = (total * live[here, :]).astype(low)
        pltpu.make_async_copy(rows_in.at[here], hidden_out.at[here], sem_store.at[part]).start()
        return carry

    lax.fori_loop(0, PARTS, output_own, 0)

    ones = jnp.ones((8, PARTS * 2 * block), low)
    all_act = act.reshape(PARTS * 2 * block, units)
    all_pre = pre_grad.reshape(PARTS * 2 * block, units)
    all_in = ffn_in.reshape(PARTS * 2 * block, width)
    all_grad = grad_rows.reshape(PARTS * 2 * block, width)
    grad_bup[...] = mm(ones, all_pre[...])[0:1]
    grad_bdown[...] = mm(ones, all_grad[...])[0:1]

    def up_store(f):
        cols = pl.ds(pl.multiple_of(f * WIDE, WIDE), WIDE)
        return pltpu.make_async_copy(tile, grad_up.at[:, cols], sem_store.at[PARTS])

    def down_store(f):
        cols = pl.ds(pl.multiple_of(f * WIDE, WIDE), WIDE)
        return pltpu.make_async_copy(tile_down, grad_down.at[cols, :], sem_store.at[PARTS + 1])

    def weights(f, carry):
        cols = pl.ds(pl.multiple_of(f * WIDE, WIDE), WIDE)

        @pl.when(f > 0)
        def _():
            up_store(f).wait()

        tile[...] = mm_tn(all_in[...], all_pre[:, cols]).astype(low)
        up_store(f).start()

        @pl.when(f > 0)
        def _():
            down_store(f).wait()

        tile_down[...] = mm_tn(all_act[:, cols], all_grad[...]).astype(low)
        down_store(f).start()
        return carry

    lax.fori_loop(0, units // WIDE, weights, 0)
    up_store(0).wait()
    down_store(0).wait()
    for part in range(PARTS):
        pltpu.make_async_copy(
            rows_in.at[pl.ds(0, block)], hidden_out.at[pl.ds(0, block)], sem_store.at[part]
        ).wait()
    own_back().wait()
    for part in range(PARTS):
        ffn_pair(part).wait_send()
        part_pair(part).wait_send()
        out_pair(part).wait_send()

    def wait_back(i, carry):
        back_copy(i).wait()
        return carry

    lax.fori_loop(1, n, wait_back, 0)


def expert_block(sent, grads, hids, live, up, up_bias, down, down_bias, gain, bias):
    n = lax.axis_size("expert")
    rows, width = sent.shape
    units = up.shape[1]
    cap = rows // n
    block = rows // PARTS
    vm = pl.BlockSpec(memory_space=pltpu.VMEM)
    hbm = pl.BlockSpec(memory_space=pl.ANY)
    return pl.pallas_call(
        functools.partial(expert_kernel, n, cap),
        out_shape=(
            jax.ShapeDtypeStruct((rows, width), low),
            jax.ShapeDtypeStruct((rows, width), low),
            jax.ShapeDtypeStruct((width, units), low),
            jax.ShapeDtypeStruct((units, width), low),
            jax.ShapeDtypeStruct((1, units), f32),
            jax.ShapeDtypeStruct((1, width), f32),
            jax.ShapeDtypeStruct((8, width), f32),
        ),
        in_specs=[hbm, hbm, hbm, vm, hbm, vm, hbm, vm, vm, vm],
        out_specs=(hbm, hbm, hbm, hbm, vm, vm, vm),
        scratch_shapes=[
            pltpu.VMEM((rows, width), low),
            pltpu.VMEM((PARTS, 2, block, width), low),
            pltpu.VMEM((PARTS, 2, block, width), low),
            pltpu.VMEM((width, units), low),
            pltpu.VMEM((units, width), low),
            pltpu.VMEM((PARTS, 2, block, units), low),
            pltpu.VMEM((PARTS, 2, block, units), low),
            pltpu.VMEM((PARTS, 2, block, units), low),
            pltpu.VMEM((2 * PARTS, block, width), low),
            pltpu.VMEM((2 * PARTS, block, width), low),
            pltpu.VMEM((rows, width), low),
            pltpu.VMEM((2, block, width), f32),
            pltpu.VMEM((width, WIDE), low),
            pltpu.VMEM((WIDE, width), low),
            pltpu.SemaphoreType.DMA((n,)),
            pltpu.SemaphoreType.DMA((n,)),
            pltpu.SemaphoreType.DMA((n,)),
            pltpu.SemaphoreType.DMA((n,)),
            pltpu.SemaphoreType.DMA((3, 2, PARTS)),
            pltpu.SemaphoreType.DMA((2 + 4 * PARTS,)),
            pltpu.SemaphoreType.DMA((PARTS + 2,)),
        ],
        compiler_params=pltpu.CompilerParams(
            collective_id=1, has_side_effects=True, vmem_limit_bytes=62 * 1024 * 1024
        ),
    )(sent, grads, hids, live, up, up_bias, down, down_bias, gain, bias)


def closing_kernel(
    n,
    cap,
    chunks,
    returned_hbm,
    slot_row,
    attn_in_hbm,
    tokens_hbm,
    queries_hbm,
    keys_hbm,
    values_hbm,
    attended_hbm,
    inv_sums,
    expos,
    w_qkv_hbm,
    w_out_hbm,
    gain,
    grad_norm2,
    grad_in,
    grad_qkv,
    grad_wout,
    grad_norms,
    returned,
    attn_in_t,
    tokens_t,
    queries_t,
    keys_t,
    values,
    attended_t,
    w_qkv,
    w_out,
    expo_v,
    grad_att_t,
    grad_h,
    grad_proj_t,
    sent_v,
    norm_terms,
    made,
    *rest,
):
    count = len(chunks)
    totals, landeds = rest[:count], rest[count : 2 * count]
    sem_load, sem_expo, sem_send, sem_recv, sem_pair, sem_step = rest[2 * count :]
    me_d = lax.axis_index("dp")
    me_e = lax.axis_index("expert")
    partner = (1 - me_d, me_e)
    bits = n.bit_length() - 1
    half = n // 2
    rows, width = returned.shape
    toks = slot_row.shape[1]
    each = made.shape[1]
    loads = [
        pltpu.make_async_copy(a, b, sem_load.at[i])
        for i, (a, b) in enumerate(
            (
                (returned_hbm, returned),
                (w_out_hbm, w_out),
                (attended_hbm, attended_t),
                (values_hbm, values),
                (keys_hbm, keys_t),
                (queries_hbm, queries_t),
                (attn_in_hbm, attn_in_t),
                (w_qkv_hbm, w_qkv),
                (tokens_hbm, tokens_t),
            )
        )
    ]

    def expo_load(g):
        here = pl.ds(4 * g, 4)
        return pltpu.make_async_copy(expos.at[here], expo_v.at[here], sem_expo.at[g])

    def slot_copy(i):
        peer = me_e ^ i
        return pltpu.make_async_remote_copy(
            src_ref=sent_v.at[pl.ds(pl.multiple_of(peer * cap, cap), cap)],
            dst_ref=grad_in.at[pl.ds(pl.multiple_of(me_e * cap, cap), cap)],
            send_sem=sem_send.at[i],
            recv_sem=sem_recv.at[i],
            device_id=(me_d, peer),
            device_id_type=MESH_ID,
        )

    def own_slots():
        here = pl.ds(pl.multiple_of(me_e * cap, cap), cap)
        return pltpu.make_async_copy(sent_v.at[here], grad_in.at[here], sem_recv.at[0])

    def offset(order, p):
        k = 0
        for j, b in enumerate(order):
            k = k + lax.rem(p // (1 << (bits - 1 - j)), 2) * (1 << b)
        return k

    def pair_copy(c, q):
        here = pl.ds(q * half, half)
        return pltpu.make_async_remote_copy(
            src_ref=totals[c].at[1, here],
            dst_ref=landeds[c].at[here],
            send_sem=sem_pair.at[0, c, q],
            recv_sem=sem_pair.at[1, c, q],
            device_id=partner,
            device_id_type=MESH_ID,
        )

    def step_copy(c, j):
        many = n >> (j + 1)
        start = n + sum(n >> (i + 1) for i in range(j))
        copy = pltpu.make_async_remote_copy(
            src_ref=totals[c].at[0, pl.ds(many, many)],
            dst_ref=landeds[c].at[pl.ds(start, many)],
            send_sem=sem_step.at[0, c, j],
            recv_sem=sem_step.at[1, c, j],
            device_id=(me_d, me_e ^ (1 << chunks[c][0][j])),
            device_id_type=MESH_ID,
        )
        return copy, many, start

    def make(c):
        order, size, pieces = chunks[c]
        for kind, source, target in pieces:
            if kind == 0:
                term = mm_nt(attn_in_t[...], grad_proj_t[slice(*source), :])
            elif kind == 1:
                term = mm(attended_t[...], grad_h[:, slice(*source)])
            else:
                term = norm_terms[...]
            made[:, :, slice(*target)] = term.reshape(made.shape[0], each, term.shape[1])

        def arrange(p, carry):
            owner = me_e ^ offset(order, p)
            totals[c][0, p] = made[me_d * n + owner, :, 0:size].astype(low)
            totals[c][1, p] = made[(1 - me_d) * n + owner, :, 0:size].astype(low)
            return carry

        lax.fori_loop(0, n, arrange, 0)
        pair_copy(c, 1).start()
        pair_copy(c, 0).start()

    def add_all(c, first, many, start):
        def add_one(p, carry):
            both = totals[c][0, p].astype(f32) + landeds[c][start + p].astype(f32)
            totals[c][0, p] = both.astype(low)
            return carry

        lax.fori_loop(first, first + many, add_one, 0)

    def stage(c, j):
        if j == 0:
            pair_copy(c, 1).wait()
            add_all(c, half, half, 0)
            step_copy(c, 0)[0].start()
            pair_copy(c, 0).wait()
            add_all(c, 0, half, 0)
            return
        copy, many, start = step_copy(c, j - 1)
        copy.wait()
        if many > 1:
            add_all(c, 0, many, start)
            step_copy(c, j)[0].start()
        else:
            both = totals[c][0, 0].astype(f32) + landeds[c][start].astype(f32)
            for kind, source, target in chunks[c][2]:
                (grad_qkv, grad_wout, grad_norms)[kind][:, slice(*source)] = both[:, slice(*target)]

    for i in range(2):
        loads[i].start()
    greet_peers(me_d, me_e, n)
    greet_partner(me_d, me_e)
    place = (slot_row[0:1, :] == lax.broadcasted_iota(jnp.int32, (rows, toks), 0)).astype(f32).astype(low)
    loads[0].wait()
    for i in range(2, 6):
        loads[i].start()
    for g in range(HEADS // 4):
        expo_load(g).start()
    for i in range(6, len(loads)):
        loads[i].start()
    grad_h[...] = mm_tn(place, returned[...]).astype(low)
    loads[1].wait()
    grad_att_t[...] = mm_nt(w_out[...], grad_h[...]).astype(low)
    loads[2].wait()
    pl.semaphore_wait(pltpu.get_barrier_semaphore(), n)
    make(0)
    make(1)
    for i in range(3, 7):
        loads[i].wait()
    in_first = lax.broadcasted_iota(jnp.int32, (1, PAIR), 1) < HEAD_DIM

    def head_group(g):
        expo_load(g).wait()
        ready = {}
        sums = {}
        for pair in range(2):
            p = 2 * g + pair
            pair_rows = pl.ds(p * PAIR, PAIR)
            inv_pair = jnp.concatenate(
                [jnp.broadcast_to(inv_sums[2 * p + h, 0:1, :], (HEAD_DIM, toks)) for h in range(2)], axis=0
            )
            grad_pair = grad_att_t[pair_rows, :].astype(f32)
            cross = grad_pair * attended_t[pair_rows, :].astype(f32) * inv_pair
            scaled = (grad_pair * inv_pair).astype(low)
            for h in range(2):
                in_pair = slice(h * HEAD_DIM, (h + 1) * HEAD_DIM)
                ready[pair, h] = (jnp.sum(cross[in_pair], axis=0, keepdims=True), scaled)
        units = [
            (pair, h, q) for pair in range(2) for h in range(2) for q in reversed(range(toks // QUERIES))
        ]

        def probs_back(unit):
            pair, h, q = unit
            upto = (q + 1) * QUERIES
            here = slice(q * QUERIES, upto)
            mine = in_first if h == 0 else jnp.logical_not(in_first)
            value = jnp.where(mine, values[0:upto, pl.ds((2 * g + pair) * PAIR, PAIR)], jnp.zeros((), low))
            return mm(value, ready[pair, h][1][:, here])

        def scores_back(unit, grad_prob):
            pair, h, q = unit
            upto = (q + 1) * QUERIES
            here = slice(q * QUERIES, upto)
            expo = expo_v[4 * g + 2 * pair + h, 0:upto, here]
            return expo, (expo.astype(f32) * (grad_prob - ready[pair, h][0][:, here])).astype(low)

        def heads_back(unit, held):
            pair, h, q = unit
            expo, grad_score = held
            upto = (q + 1) * QUERIES
            here = slice(q * QUERIES, upto)
            first = (2 * g + pair) * PAIR + h * HEAD_DIM
            head_rows = pl.ds(first, HEAD_DIM)
            grad_proj_t[head_rows, here] = (mm(keys_t[head_rows, 0:upto], grad_score) * scale_val).astype(low)
            key_term = mm_nt(queries_t[head_rows, here], grad_score)
            value_term = mm_nt(ready[pair, h][1][h * HEAD_DIM : (h + 1) * HEAD_DIM, here], expo)
            if upto < toks:
                key_more, value_more = sums[pair, h]
                key_term = jnp.concatenate([key_more[:, 0:upto] + key_term, key_more[:, upto:]], axis=1)
                value_term = jnp.concatenate([value_more[:, 0:upto] + value_term, value_more[:, upto:]], axis=1)
            sums[pair, h] = (key_term, value_term)
            if q == 0:
                grad_proj_t[pl.ds(width + first, HEAD_DIM), :] = key_term.astype(low)
                grad_proj_t[pl.ds(2 * width + first, HEAD_DIM), :] = value_term.astype(low)

        staged(units, probs_back, scores_back, heads_back)

    groups = HEADS // 4
    head_group(0)
    make(2)
    stage(0, 0)
    stage(1, 0)
    for g in range(1, groups):
        head_group(g)
        make(2 + g)
        stage(1 + g, 0)
    for i in range(7, len(loads)):
        loads[i].wait()
    grad_attn_t = mm(w_qkv[...], grad_proj_t[...])
    stage(1 + groups, 0)
    normed_t, inv_std = normalize(tokens_t[...].astype(f32), axis=0)
    gain_col = jnp.broadcast_to(gain[...], (LANES, width)).T[:, 0:1]
    norm_terms[...] = jnp.concatenate(
        [
            jnp.sum(grad_attn_t * normed_t, axis=1, keepdims=True),
            jnp.sum(grad_attn_t, axis=1, keepdims=True),
            grad_norm2[...].T[:, 0:2],
            jnp.zeros((width, LANES - 4), f32),
        ],
        axis=1,
    )
    result = grad_h[...].astype(f32).T + norm_back(grad_attn_t, normed_t, inv_std, gain_col, axis=0)
    sent_v[...] = mm_nt(place, result.astype(low)).astype(low)
    own_slots().start()

    def start_slots(i, carry):
        slot_copy(i).start()
        return carry

    lax.fori_loop(1, n, start_slots, 0)
    make(count - 1)
    done = [1] * (count - 1) + [0]
    for wave in range(1, bits + count + 1):
        for c in range(count):
            late = c // 4
            while done[c] <= min(bits, wave - late):
                stage(c, done[c])
                done[c] += 1
    own_slots().wait()

    def wait_slots(i, carry):
        slot_copy(i).wait()
        return carry

    lax.fori_loop(1, n, wait_slots, 0)


def closing(returned, slot_row, attn_in_t, tokens_t, queries_t, keys_t, values, attended_t, inv_sums, expos, w_qkv, w_out, gain, grad_norm2):
    n = lax.axis_size("expert")
    owners = n * lax.axis_size("dp")
    rows, width = returned.shape
    toks = slot_row.shape[1]
    each = width // owners
    bits = n.bit_length() - 1
    groups = HEADS // 4
    part = width // groups
    orders = [list(range(bits)), [1, 0] + list(range(2, bits))]
    chunks = []
    for c in range(2):
        size = width // 2
        chunks.append((orders[c], size, [(1, (c * size, (c + 1) * size), (0, size))]))
    for g in range(groups):
        pieces = [
            (0, (k * width + g * part, k * width + (g + 1) * part), (k * part, (k + 1) * part)) for k in range(3)
        ]
        chunks.append((orders[g % 2], 3 * part, pieces))
    chunks.append((orders[0], LANES, [(2, (0, LANES), (0, LANES))]))
    count = len(chunks)
    widest = max(size for _, size, _ in chunks)
    vm = pl.BlockSpec(memory_space=pltpu.VMEM)
    hbm = pl.BlockSpec(memory_space=pl.ANY)
    shape = jax.ShapeDtypeStruct
    return pl.pallas_call(
        functools.partial(closing_kernel, n, rows // n, chunks),
        out_shape=(
            shape((rows, width), low),
            shape((each, 3 * width), f32),
            shape((each, width), f32),
            shape((each, LANES), f32),
        ),
        in_specs=[hbm, vm, hbm, hbm, hbm, hbm, hbm, hbm, vm, hbm, hbm, hbm, vm, vm],
        out_specs=(hbm, vm, vm, vm),
        scratch_shapes=[
            pltpu.VMEM((rows, width), low),
            pltpu.VMEM((width, toks), low),
            pltpu.VMEM((width, toks), low),
            pltpu.VMEM((width, toks), low),
            pltpu.VMEM((width, toks), low),
            pltpu.VMEM((toks, width), low),
            pltpu.VMEM((width, toks), low),
            pltpu.VMEM(w_qkv.shape, low),
            pltpu.VMEM(w_out.shape, low),
            pltpu.VMEM((HEADS, toks, toks), low),
            pltpu.VMEM((width, toks), low),
            pltpu.VMEM((toks, width), low),
            pltpu.VMEM((3 * width, toks), low),
            pltpu.VMEM((rows, width), low),
            pltpu.VMEM((width, LANES), f32),
            pltpu.VMEM((owners, each, widest), f32),
        ]
        + [pltpu.VMEM((2, n, each, size), low) for _, size, _ in chunks]
        + [pltpu.VMEM((2 * n, each, size), low) for _, size, _ in chunks]
        + [
            pltpu.SemaphoreType.DMA((9,)),
            pltpu.SemaphoreType.DMA((groups,)),
            pltpu.SemaphoreType.DMA((n,)),
            pltpu.SemaphoreType.DMA((n,)),
            pltpu.SemaphoreType.DMA((2, count, 2)),
            pltpu.SemaphoreType.DMA((2, count, bits)),
        ],
        compiler_params=pltpu.CompilerParams(
            collective_id=2, has_side_effects=True, vmem_limit_bytes=62 * 1024 * 1024
        ),
    )(returned, slot_row, attn_in_t, tokens_t, queries_t, keys_t, values, attended_t, inv_sums, expos, w_qkv, w_out, gain, grad_norm2)


def handing_kernel(up_in, down_in, hidden_in, rows_in, qkv_in, wout_in, bup_in, bdown_in, norms_in, up, down, hidden, rows, qkv, wout, bup, bdown, *norms):
    up[...] = up_in[...].astype(f32)
    down[...] = down_in[...].astype(f32)
    hidden[...] = hidden_in[...]
    rows[...] = rows_in[...]
    qkv[...] = qkv_in[...]
    wout[...] = wout_in[...]
    bup[...] = bup_in[...]
    norms_t = norms_in[...].T
    for i, norm in enumerate(norms):
        norm[...] = norms_t[i : i + 1, :]
    half = bdown.shape[1]
    bdown[...] = jnp.where(lax.axis_index("dp") == 0, bdown_in[:, 0:half], bdown_in[:, half : 2 * half])


def handing(grad_up, grad_down, hidden_out, grad_in, grad_qkv, grad_wout, grad_bup, grad_bdown, grad_norms):
    steps = 4
    arrays = (grad_up, grad_down, hidden_out, grad_in, grad_qkv, grad_wout, grad_bup, grad_bdown, grad_norms)
    small = grad_bdown.shape[1] // lax.axis_size("dp")
    types = (f32, f32, low, low) + (f32,) * 8

    def block(shape, cut):
        if cut:
            return pl.BlockSpec((shape[0] // steps, shape[1]), lambda i: (i, 0))
        return pl.BlockSpec(shape, lambda i: (0, 0))

    shapes = [x.shape for x in arrays[:-2]] + [(1, small)] + [(1, grad_norms.shape[0])] * 4
    return pl.pallas_call(
        handing_kernel,
        grid=(steps,),
        out_shape=tuple(jax.ShapeDtypeStruct(shape, t) for shape, t in zip(shapes, types)),
        in_specs=[block(x.shape, i < 4) for i, x in enumerate(arrays)],
        out_specs=tuple(block(shape, i < 4) for i, shape in enumerate(shapes)),
        compiler_params=pltpu.CompilerParams(vmem_limit_bytes=62 * 1024 * 1024),
    )(*arrays)


def on_device(
    hidden_in,
    buckets,
    expert_of_bucket,
    lengths,
    norm1_gain,
    norm1_bias,
    w_qkv,
    w_out,
    norm2_gain,
    norm2_bias,
    w_up,
    b_up,
    w_down,
    b_down,
    grad_out,
):
    (
        sent,
        grads,
        hids,
        live,
        attn_in_t,
        tokens_t,
        queries_t,
        keys_t,
        values,
        attended_t,
        inv_sums,
        slot_row,
        expos,
    ) = starting(
        hidden_in,
        grad_out,
        buckets.reshape(1, -1),
        expert_of_bucket[None],
        lengths,
        norm1_gain[None],
        norm1_bias[None],
        w_qkv,
        w_out,
        w_down[0],
    )
    returned, hidden_out, grad_up, grad_down, grad_bup, grad_bdown, grad_norm2 = expert_block(
        sent, grads, hids, live, w_up[0], b_up, w_down[0], b_down, norm2_gain[None], norm2_bias[None]
    )
    grad_in, grad_qkv, grad_wout, grad_norms = closing(
        returned,
        slot_row,
        attn_in_t,
        tokens_t,
        queries_t,
        keys_t,
        values,
        attended_t,
        inv_sums,
        expos,
        w_qkv,
        w_out,
        norm1_gain[None],
        grad_norm2,
    )
    grad_up, grad_down, hidden_out, grad_in, grad_qkv, grad_wout, grad_bup, grad_bdown, *norms = handing(
        grad_up, grad_down, hidden_out, grad_in, grad_qkv, grad_wout, grad_bup, grad_bdown, grad_norms
    )
    return (
        hidden_out,
        grad_in,
        grad_qkv,
        grad_wout,
        *(norm.reshape(-1) for norm in norms),
        grad_up[None],
        grad_bup,
        grad_down[None],
        grad_bdown,
    )


def solution(mesh):
    return jax.shard_map(
        on_device,
        mesh=mesh,
        in_specs=(
            P(("dp", "expert"), None),
            P(("dp", "expert"), None),
            P(),
            P(("dp", "expert"), None),
            P(),
            P(),
            P(),
            P(),
            P(),
            P(),
            P("expert", None, "dp"),
            P("expert", "dp"),
            P("expert", "dp", None),
            P("expert", None),
            P(("dp", "expert"), None),
        ),
        out_specs=(
            P(("dp", "expert"), None),
            P(("dp", "expert"), None),
            P(("dp", "expert"), None),
            P(("dp", "expert"), None),
            P(("dp", "expert")),
            P(("dp", "expert")),
            P(("dp", "expert")),
            P(("dp", "expert")),
            P("expert", None, "dp"),
            P("expert", "dp"),
            P("expert", "dp", None),
            P("expert", "dp"),
        ),
        check_vma=False,
    )
```

```python
import functools

import jax
import jax.numpy as jnp
from jax import lax
from jax.experimental import pallas as pl
from jax.experimental.pallas import tpu as pltpu
from jax.sharding import PartitionSpec as P

HEADS = 16
HEAD_DIM = 64


norm_eps = 1e-05
masked_score = -1e30
root_half = 0.7071067811865476
inv_root_tau = 0.3989422804014327

MESH_ID = pl.DeviceIdType.MESH
PARTS = 4
WIDE = 512
LANES = 128
QUERIES = 256
PAIR = 2 * HEAD_DIM
scale_val = HEAD_DIM ** (-0.5)
low = jnp.bfloat16
f32 = jnp.float32


def mm(a, b):
    return jnp.dot(a, b, preferred_element_type=f32)


def mm_nt(a, b):
    return lax.dot_general(a, b, (((1,), (1,)), ((), ())), preferred_element_type=f32)


def mm_tn(a, b):
    return lax.dot_general(a, b, (((0,), (0,)), ((), ())), preferred_element_type=f32)


def normalize(values, axis=-1):
    mean_val = jnp.mean(values, axis=axis, keepdims=True)
    centered = values - mean_val
    variance = jnp.mean(centered * centered, axis=axis, keepdims=True)
    inv_std = lax.rsqrt(variance + norm_eps)
    return (centered * inv_std, inv_std)


def norm_back(grad_normed, normed, inv_std, gain_vec, axis=-1):
    scaled = grad_normed * gain_vec
    mean_grad = jnp.mean(scaled, axis=axis, keepdims=True)
    mean_cross = jnp.mean(scaled * normed, axis=axis, keepdims=True)
    return inv_std * (scaled - mean_grad - normed * mean_cross)


def gelu_parts(pre):
    bell = jnp.exp(-0.5 * pre * pre)
    den = 1.0 + (0.3275911 * root_half) * jnp.abs(pre)
    t = pl.reciprocal(den, approx=True)
    t = t * (2.0 - den * t)
    tail = t * (
        0.5 * 0.254829592
        + t * (0.5 * -0.284496736 + t * (0.5 * 1.421413741 + t * (0.5 * -1.453152027 + t * (0.5 * 1.061405429))))
    )
    tail = tail * bell
    phi = jnp.where(pre >= 0.0, 1.0 - tail, tail)
    return pre * phi, phi + pre * (inv_root_tau * bell)


def greet_peers(me_d, me_e, n):
    barrier = pltpu.get_barrier_semaphore()

    def signal(i, carry):
        pl.semaphore_signal(barrier, inc=1, device_id=(me_d, me_e ^ i), device_id_type=MESH_ID)
        return carry

    lax.fori_loop(1, n, signal, 0)


def greet_partner(me_d, me_e):
    pl.semaphore_signal(
        pltpu.get_barrier_semaphore(), inc=1, device_id=(1 - me_d, me_e), device_id_type=MESH_ID
    )


def staged(units, *stages):
    held = [None] * len(units)
    for step in range(len(units) + len(stages) - 1):
        for k, stage in enumerate(stages):
            i = step - k
            if 0 <= i < len(units):
                held[i] = stage(units[i]) if k == 0 else stage(units[i], held[i])


def start_kernel(
    n,
    cap,
    hidden,
    grad_out,
    buckets,
    expert_of,
    lengths,
    gain,
    bias,
    w_qkv_hbm,
    w_out_hbm,
    down_hbm,
    sent,
    grads,
    hids,
    live,
    attn_in_hbm,
    tokens_hbm,
    queries_hbm,
    keys_hbm,
    values_hbm,
    attended_hbm,
    inv_sums,
    slot_row,
    expos,
    arrived,
    w_qkv,
    w_out,
    down,
    grad_raw,
    grad_v,
    grad_p,
    hid_v,
    attn_in_t,
    tokens_t,
    queries_t,
    keys_t,
    values,
    attended_t,
    attn_in_v,
    proj,
    values_t,
    allow,
    tokens,
    expo_v,
    sent_v,
    counts_out,
    counts_in,
    sem_send,
    sem_recv,
    sem_count_send,
    sem_count_recv,
    sem_pair,
    sem_load,
    sem_store,
    sem_keep,
    sem_turn,
):
    me_d = lax.axis_index("dp")
    me_e = lax.axis_index("expert")
    partner = (1 - me_d, me_e)
    rows, width = arrived.shape
    toks = buckets.shape[1]
    lanes = counts_out.shape[1]

    def slot_copy(i):
        peer = me_e ^ i
        return pltpu.make_async_remote_copy(
            src_ref=hidden.at[pl.ds(pl.multiple_of(peer * cap, cap), cap)],
            dst_ref=arrived.at[pl.ds(pl.multiple_of(me_e * cap, cap), cap)],
            send_sem=sem_send.at[i],
            recv_sem=sem_recv.at[i],
            device_id=(me_d, peer),
            device_id_type=MESH_ID,
        )

    def own_slots():
        here = pl.ds(pl.multiple_of(me_e * cap, cap), cap)
        return pltpu.make_async_copy(hidden.at[here], arrived.at[here], sem_recv.at[0])

    def count_copy(i):
        return pltpu.make_async_remote_copy(
            src_ref=counts_out,
            dst_ref=counts_in.at[me_e],
            send_sem=sem_count_send.at[i],
            recv_sem=sem_count_recv.at[i],
            device_id=(me_d, me_e ^ i),
            device_id_type=MESH_ID,
        )

    grad_load = pltpu.make_async_copy(grad_out, grad_raw, sem_load.at[0])
    qkv_load = pltpu.make_async_copy(w_qkv_hbm, w_qkv, sem_load.at[1])
    out_load = pltpu.make_async_copy(w_out_hbm, w_out, sem_load.at[2])
    down_load = pltpu.make_async_copy(down_hbm, down, sem_load.at[3])
    pair_grads_store = pltpu.make_async_copy(grad_p, grads.at[1], sem_store.at[2])
    def keep(i, g):
        source, target = (
            (attn_in_t, attn_in_hbm),
            (tokens_t, tokens_hbm),
            (queries_t, queries_hbm),
            (keys_t, keys_hbm),
            (attended_t, attended_hbm),
            (values, values_hbm),
        )[i]
        here = pl.ds(pl.multiple_of(g * 4 * PAIR, 4 * PAIR), 4 * PAIR)
        if i == 5:
            return pltpu.make_async_copy(source.at[:, here], target.at[:, here], sem_keep.at[i, g])
        return pltpu.make_async_copy(source.at[here], target.at[here], sem_keep.at[i, g])

    def hid_store(k):
        return pltpu.make_async_copy(hid_v.at[k], hids.at[k], sem_store.at[3 + k])

    def hidden_grad(k, grad_ref):
        def tile(i, carry):
            here = pl.ds(pl.multiple_of((i // 2) * WIDE, WIDE), WIDE)
            some = pl.ds(pl.multiple_of(lax.rem(i, 2) * (rows // 2), rows // 2), rows // 2)
            hid_v[k, some, here] = mm_nt(grad_ref[some, :], down[here, :]).astype(low)
            return carry

        lax.fori_loop(0, 2 * (down.shape[0] // WIDE), tile, 0)
        hid_store(k).start()

    grad_store = pltpu.make_async_copy(grad_v, grads.at[0], sem_store.at[0])
    grad_pair = pltpu.make_async_remote_copy(
        src_ref=grad_v,
        dst_ref=grad_p,
        send_sem=sem_pair.at[0],
        recv_sem=sem_pair.at[1],
        device_id=partner,
        device_id_type=MESH_ID,
    )

    def start_slots(i, carry):
        slot_copy(i).start()
        return carry

    grad_load.start()

    @pl.when(me_d == 1)
    def _():
        down_load.start()

    greet_peers(me_d, me_e, n)
    greet_partner(me_d, me_e)
    lane_ids = lax.broadcasted_iota(jnp.int32, (toks, lanes), 1)
    bucket = jnp.broadcast_to(buckets[...], (lanes, toks)).T[:, 0:n]
    bucket_hot = (bucket == lane_ids[:, 0:n]).astype(f32).astype(low)
    serves_t = (expert_of[...] == lax.broadcasted_iota(jnp.int32, (lanes, n), 0)).astype(f32).astype(low)
    expert_hot = mm_nt(bucket_hot, serves_t)
    counts_out[...] = jnp.broadcast_to(jnp.sum(expert_hot, axis=0, keepdims=True), counts_out.shape)
    counts_in[me_e] = counts_out[...]

    def start_counts(i, carry):
        count_copy(i).start()
        return carry

    pl.semaphore_wait(pltpu.get_barrier_semaphore(), n)
    lax.fori_loop(1, n, start_counts, 0)
    lax.fori_loop(1, n // 2, start_slots, 0)

    @pl.when(me_d == 0)
    def _():
        lax.fori_loop(n // 2, n, start_slots, 0)

    own_slots().start()
    qkv_load.start()
    out_load.start()

    row_ids = lax.broadcasted_iota(jnp.int32, (toks, toks), 0)
    col_ids = lax.broadcasted_iota(jnp.int32, (toks, toks), 1)
    earlier = (col_ids < row_ids).astype(f32).astype(low)
    before = mm(earlier, expert_hot.astype(low))
    slot = jnp.sum(expert_hot * (before + (lane_ids * cap).astype(f32)), axis=1, keepdims=True)
    slot_row[...] = jnp.broadcast_to(slot, (toks, lanes)).T[0:8, :].astype(jnp.int32)
    ends = jnp.zeros((1, toks), jnp.int32)
    begin = jnp.zeros((1, toks), jnp.int32)
    places = lax.broadcasted_iota(jnp.int32, (1, toks), 1)
    for s in range(lengths.shape[1]):
        ends = ends + lengths[0:1, s : s + 1]
        begin = jnp.where(places >= ends, ends, begin)
    allow[...] = jnp.where(jnp.logical_and(row_ids <= col_ids, row_ids >= begin), 0.0, masked_score)

    def wait_counts(i, carry):
        count_copy(i).wait()
        return carry

    lax.fori_loop(1, n, wait_counts, 0)
    grad_load.wait()

    def mark(s, carry):
        here = pl.ds(pl.multiple_of(s * cap, cap), cap)
        mine = lax.broadcasted_iota(jnp.int32, (1, lanes), 1) == me_e
        count = jnp.sum(jnp.where(mine, counts_in[s, 0:1, :], 0.0), axis=1, keepdims=True)
        taken = (lax.broadcasted_iota(jnp.int32, (cap, 1), 0).astype(f32) < count).astype(f32)
        live[here, :] = taken
        grad_v[here, :] = (grad_raw[here, :].astype(f32) * taken).astype(low)
        return carry

    lax.fori_loop(0, n, mark, 0)
    grad_store.start()
    grad_pair.start()
    @pl.when(me_d == 0)
    def _():
        def wait_sent(i, carry):
            slot_copy(i).wait_send()
            return carry

        lax.fori_loop(n // 2, n, wait_sent, 0)
        pl.semaphore_signal(sem_turn, inc=1, device_id=partner, device_id_type=MESH_ID)

    @pl.when(me_d == 1)
    def _():
        pl.semaphore_wait(sem_turn, 1)
        lax.fori_loop(n // 2, n, start_slots, 0)

    grad_pair.wait()
    pair_grads_store.start()

    @pl.when(me_d == 1)
    def _():
        down_load.wait()
        hidden_grad(0, grad_v)
        hidden_grad(1, grad_p)


    own_slots().wait()

    def wait_slots(i, carry):
        slot_copy(i).wait_recv()
        return carry

    lax.fori_loop(1, n, wait_slots, 0)

    pick = (slot.astype(jnp.int32) == lax.broadcasted_iota(jnp.int32, (toks, rows), 1)).astype(f32).astype(low)
    tokens[...] = mm(pick, arrived[...])
    normed, _ = normalize(tokens[...])
    attn_in = (normed * gain[...] + bias[...]).astype(low)
    attn_in_v[...] = attn_in
    qkv_load.wait()
    step = width // 4
    for c in range(3 * width // step):
        here = slice(c * step, (c + 1) * step)
        part = mm(attn_in, w_qkv[:, here])
        if c * step < width:
            part = part.astype(low).astype(f32) * scale_val
        proj[:, here] = part.astype(low)
    values_t[...] = proj[:, 2 * width : 3 * width].T

    def expo_store(g):
        here = pl.ds(pl.multiple_of(8 * g, 8), 8)
        return pltpu.make_async_copy(expo_v.at[here], expos.at[here], sem_store.at[5 + g])

    in_first = lax.broadcasted_iota(jnp.int32, (1, PAIR), 1) < HEAD_DIM

    def head_group(g, carry):
        units = [
            (4 * g + pair, h, q) for pair in range(4) for h in range(2) for q in range(toks // QUERIES)
        ]

        def score(unit):
            p, h, q = unit
            first = pl.multiple_of(p * PAIR, PAIR)
            upto = (q + 1) * QUERIES
            here = slice(q * QUERIES, upto)
            mine = in_first if h == 0 else jnp.logical_not(in_first)
            query = jnp.where(mine, proj[here, pl.ds(first, PAIR)], jnp.zeros((), low))
            scores = mm_nt(proj[0:upto, pl.ds(pl.multiple_of(width + first, PAIR), PAIR)], query)
            return scores + allow[0:upto, here]

        def soft(unit, scores):
            expo = jnp.exp(scores - jnp.max(scores, axis=0, keepdims=True))
            inv = 1.0 / jnp.sum(expo, axis=0, keepdims=True)
            return expo.astype(low), inv

        def attend(unit, held):
            p, h, q = unit
            expo, inv = held
            upto = (q + 1) * QUERIES
            here = slice(q * QUERIES, upto)
            head_rows = pl.ds(pl.multiple_of(p * PAIR + h * HEAD_DIM, HEAD_DIM), HEAD_DIM)
            expo_v[2 * p + h, 0:upto, here] = expo
            if upto < toks:
                expo_v[2 * p + h, upto:toks, here] = jnp.zeros((toks - upto, QUERIES), low)
            out = mm(values_t[head_rows, 0:upto], expo)
            attended_t[head_rows, here] = (out * inv).astype(low)
            inv_sums[2 * p + h, :, here] = jnp.broadcast_to(inv, (8, QUERIES))

        staged(units, score, soft, attend)
        here = pl.ds(pl.multiple_of(g * 4 * PAIR, 4 * PAIR), 4 * PAIR)
        queries_t[here, :] = proj[:, here].T
        keys_t[here, :] = proj[:, pl.ds(pl.multiple_of(width + g * 4 * PAIR, 4 * PAIR), 4 * PAIR)].T
        values[:, here] = proj[:, pl.ds(pl.multiple_of(2 * width + g * 4 * PAIR, 4 * PAIR), 4 * PAIR)]
        tokens_t[here, :] = tokens[:, here].T.astype(low)
        attn_in_t[here, :] = attn_in_v[:, here].T
        expo_store(g).start()
        for i in range(6):
            keep(i, g).start()
        return carry

    lax.fori_loop(0, HEADS // 8, head_group, 0)
    out_load.wait()
    residual = (tokens[...] + mm_tn(attended_t[...], w_out[...])).astype(low)
    place = (slot_row[0:1, :] == lax.broadcasted_iota(jnp.int32, (rows, toks), 0)).astype(f32).astype(low)
    sent_v[...] = mm(place, residual).astype(low)
    sent_store = pltpu.make_async_copy(sent_v, sent, sem_store.at[1])
    sent_store.start()

    for g in range(HEADS // 8):
        expo_store(g).wait()
        for i in range(6):
            keep(i, g).wait()
    grad_store.wait()
    pair_grads_store.wait()

    @pl.when(me_d == 1)
    def _():
        hid_store(0).wait()
        hid_store(1).wait()


    def wait_sent(i, carry):
        slot_copy(i).wait_send()
        return carry

    lax.fori_loop(1, n // 2, wait_sent, 0)

    @pl.when(me_d == 1)
    def _():
        lax.fori_loop(n // 2, n, wait_sent, 0)

    sent_store.wait()


def starting(hidden, grad_out, buckets, expert_of, lengths, gain, bias, w_qkv, w_out, down):
    n = lax.axis_size("expert")
    rows, width = hidden.shape
    toks = buckets.shape[1]
    units = down.shape[0]
    lanes = 128
    vm = pl.BlockSpec(memory_space=pltpu.VMEM)
    hbm = pl.BlockSpec(memory_space=pl.ANY)
    shape = jax.ShapeDtypeStruct
    return pl.pallas_call(
        functools.partial(start_kernel, n, rows // n),
        out_shape=(
            shape((rows, width), low),
            shape((2, rows, width), low),
            shape((2, rows, units), low),
            shape((rows, 1), f32),
            shape((width, toks), low),
            shape((width, toks), low),
            shape((width, toks), low),
            shape((width, toks), low),
            shape((toks, width), low),
            shape((width, toks), low),
            shape((HEADS, 8, toks), f32),
            shape((8, toks), jnp.int32),
            shape((HEADS, toks, toks), low),
        ),
        in_specs=[hbm, hbm, vm, vm, vm, vm, vm, hbm, hbm, hbm],
        out_specs=(hbm, hbm, hbm, vm, hbm, hbm, hbm, hbm, hbm, hbm, vm, vm, hbm),
        scratch_shapes=[
            pltpu.VMEM((rows, width), low),
            pltpu.VMEM(w_qkv.shape, low),
            pltpu.VMEM(w_out.shape, low),
            pltpu.VMEM(down.shape, low),
            pltpu.VMEM((rows, width), low),
            pltpu.VMEM((rows, width), low),
            pltpu.VMEM((rows, width), low),
            pltpu.VMEM((2, rows, units), low),
            pltpu.VMEM((width, toks), low),
            pltpu.VMEM((width, toks), low),
            pltpu.VMEM((width, toks), low),
            pltpu.VMEM((width, toks), low),
            pltpu.VMEM((toks, width), low),
            pltpu.VMEM((width, toks), low),
            pltpu.VMEM((toks, width), low),
            pltpu.VMEM((toks, 3 * width), low),
            pltpu.VMEM((width, toks), low),
            pltpu.VMEM((toks, toks), f32),
            pltpu.VMEM((toks, width), f32),
            pltpu.VMEM((HEADS, toks, toks), low),
            pltpu.VMEM((rows, width), low),
            pltpu.VMEM((8, lanes), f32),
            pltpu.VMEM((n, 8, lanes), f32),
            pltpu.SemaphoreType.DMA((n,)),
            pltpu.SemaphoreType.DMA((n,)),
            pltpu.SemaphoreType.DMA((n,)),
            pltpu.SemaphoreType.DMA((n,)),
            pltpu.SemaphoreType.DMA((2,)),
            pltpu.SemaphoreType.DMA((4,)),
            pltpu.SemaphoreType.DMA((5 + HEADS // 4,)),
            pltpu.SemaphoreType.DMA((6, HEADS // 4)),
            pltpu.SemaphoreType.REGULAR,
        ],
        compiler_params=pltpu.CompilerParams(
            collective_id=3, has_side_effects=True, vmem_limit_bytes=60 * 1024 * 1024
        ),
    )(hidden, grad_out, buckets, expert_of, lengths, gain, bias, w_qkv, w_out, down)


def expert_kernel(
    n,
    cap,
    sent,
    grads,
    hids,
    live,
    up_hbm,
    up_bias,
    down_hbm,
    down_bias,
    gain,
    bias,
    returned,
    hidden_out,
    grad_up,
    grad_down,
    grad_bup,
    grad_bdown,
    grad_norm,
    rows_in,
    ffn_in,
    grad_rows,
    up,
    down,
    hid,
    act,
    pre_grad,
    part_out,
    part_in,
    back,
    mine,
    tile,
    tile_down,
    sem_send,
    sem_recv,
    sem_back_send,
    sem_back_recv,
    sem_pair,
    sem_load,
    sem_store,
):
    me_d = lax.axis_index("dp")
    me_e = lax.axis_index("expert")
    rows = rows_in.shape[0]
    width = rows_in.shape[1]
    units = up.shape[1]
    block = rows // PARTS
    many = n // PARTS
    partner = (1 - me_d, me_e)

    def base_of(part):
        return pl.multiple_of(((me_e // many) ^ part) * block, block)

    def slot_copy(i):
        peer = me_e ^ i
        return pltpu.make_async_remote_copy(
            src_ref=sent.at[pl.ds(pl.multiple_of(peer * cap, cap), cap)],
            dst_ref=rows_in.at[pl.ds(pl.multiple_of(me_e * cap, cap), cap)],
            send_sem=sem_send.at[i],
            recv_sem=sem_recv.at[i],
            device_id=(me_d, peer),
            device_id_type=MESH_ID,
        )

    def own_slots():
        own = pl.ds(pl.multiple_of(me_e * cap, cap), cap)
        return pltpu.make_async_copy(sent.at[own], rows_in.at[own], sem_recv.at[0])

    def back_copy(i):
        peer = me_e ^ i
        return pltpu.make_async_remote_copy(
            src_ref=back.at[pl.ds(pl.multiple_of(peer * cap, cap), cap)],
            dst_ref=returned.at[pl.ds(pl.multiple_of(me_e * cap, cap), cap)],
            send_sem=sem_back_send.at[i],
            recv_sem=sem_back_recv.at[i],
            device_id=(me_d, peer),
            device_id_type=MESH_ID,
        )

    def own_back():
        own = pl.ds(pl.multiple_of(me_e * cap, cap), cap)
        return pltpu.make_async_copy(back.at[own], returned.at[own], sem_back_recv.at[0])

    def pair_copy(src, dst, kind, part):
        return pltpu.make_async_remote_copy(
            src_ref=src,
            dst_ref=dst,
            send_sem=sem_pair.at[kind - 1, 0, part],
            recv_sem=sem_pair.at[kind - 1, 1, part],
            device_id=partner,
            device_id_type=MESH_ID,
        )

    def ffn_pair(part):
        return pair_copy(ffn_in.at[part, 0], ffn_in.at[part, 1], 1, part)

    def part_pair(part):
        return pair_copy(part_out.at[part], part_in.at[part], 2, part)

    def out_pair(part):
        return pair_copy(part_out.at[PARTS + part], part_in.at[PARTS + part], 3, part)

    def hid_load(unit):
        part, k = part_of(unit), core_of(unit)
        here = pl.ds(base_of(part), block)
        return pltpu.make_async_copy(hids.at[k, here], hid.at[part, k], sem_load.at[2 + unit])

    def grads_load(unit):
        part, k = part_of(unit), core_of(unit)
        here = pl.ds(base_of(part), block)
        return pltpu.make_async_copy(grads.at[k, here], grad_rows.at[part, k], sem_load.at[2 + 2 * PARTS + unit])

    def part_of(unit):
        return lax.rem(unit, PARTS)

    def core_of(unit):
        return me_d ^ (unit // PARTS)

    up_load = pltpu.make_async_copy(up_hbm, up, sem_load.at[0])
    down_load = pltpu.make_async_copy(down_hbm, down, sem_load.at[1])
    own_slots().start()

    @pl.when(me_d == 0)
    def _():
        down_load.start()
        for unit in range(2 * PARTS):
            grads_load(unit).start()
        up_load.start()

    @pl.when(me_d == 1)
    def _():
        up_load.start()
        hid_load(0).start()
        grads_load(0).start()

    barrier = pltpu.get_barrier_semaphore()
    greet_peers(me_d, me_e, n)

    @pl.when(me_d == 0)
    def _():
        pl.semaphore_wait(barrier, n - 1)
        greet_partner(me_d, me_e)

    @pl.when(me_d == 1)
    def _():
        pl.semaphore_wait(barrier, n)
        greet_partner(me_d, me_e)

    def start_slots(i, carry):
        slot_copy(i).start()
        return carry

    lax.fori_loop(1, n, start_slots, 0)
    grad_norm[...] = jnp.zeros_like(grad_norm)
    up_load.wait()

    @pl.when(me_d == 1)
    def _():
        down_load.start()
        for unit in range(1, 2 * PARTS):
            hid_load(unit).start()
            grads_load(unit).start()


    def stats(base):
        return normalize(rows_in[pl.ds(base, block), :].astype(f32))

    def arrive(part):
        @pl.when(part == 0)
        def _():
            own_slots().wait()

        @pl.when(part > 0)
        def _():
            slot_copy(part * many).wait()

        def wait_slots(j, c):
            slot_copy(part * many + j).wait()
            return c

        lax.fori_loop(1, many, wait_slots, 0)
        normed, _ = stats(base_of(part))
        ffn_in[part, 0] = (normed * gain[...] + bias[...]).astype(low)

    @pl.when(me_d == 0)
    def _():
        def arrive_all(part, carry):
            arrive(part)

            @pl.when(part == 0)
            def _():
                pl.semaphore_wait(barrier, 1)

            ffn_pair(part).start()
            return carry

        def hidden_grad(unit, carry):
            part, k = part_of(unit), core_of(unit)
            grads_load(unit).wait()
            hid[part, k] = mm_nt(grad_rows[part, k], down[...]).astype(low)
            return carry

        down_load.wait()
        lax.fori_loop(0, 2 * PARTS, hidden_grad, 0)
        lax.fori_loop(0, PARTS, arrive_all, 0)

    def hidden(part, k):
        def before(cols):
            return mm(ffn_in[part, k], up[:, cols]) + up_bias[:, cols]

        def after(cols, pre):
            a, slope = gelu_parts(pre)
            act[part, k, :, cols] = a.astype(low)
            pre_grad[part, k, :, cols] = (hid[part, k, :, cols].astype(f32) * slope).astype(low)

        staged([pl.ds(f * WIDE, WIDE) for f in range(units // WIDE)], before, after)

    def send_back(unit):
        part = part_of(unit)
        base = base_of(part)
        part_pair(part).wait_recv()
        grad_ffn = mine[lax.rem(unit, 2)] + part_in[part].astype(f32)
        normed, inv_std = stats(base)
        grad_norm[0:1, :] += jnp.sum(grad_ffn * normed, axis=0, keepdims=True)
        grad_norm[1:2, :] += jnp.sum(grad_ffn, axis=0, keepdims=True)
        result = grad_rows[part, 0].astype(f32) + norm_back(grad_ffn, normed, inv_std, gain[...])
        back[pl.ds(base, block), :] = result.astype(low)

        @pl.when(part == 0)
        def _():
            own_back().start()

        @pl.when(part > 0)
        def _():
            back_copy(part * many).start()

        def start_back(j, c):
            back_copy(part * many + j).start()
            return c

        lax.fori_loop(1, many, start_back, 0)

    def work(unit, carry):
        part, k = part_of(unit), core_of(unit)
        ahead = unit + 1 - PARTS

        @pl.when((me_d == 1) & (ahead >= 0) & (ahead < PARTS))
        def _():
            arrive(ahead)
            ffn_pair(ahead).start()

        @pl.when(k == 1)
        def _():
            ffn_pair(part).wait_recv()

        @pl.when(me_d == 1)
        def _():
            hid_load(unit).wait()
            grads_load(unit).wait()

        hidden(part, k)
        slot = lax.rem(unit, 2)
        mine[slot] = mm_nt(pre_grad[part, k], up[...])

        @pl.when((unit == 0) & (me_d == 1))
        def _():
            down_load.wait()

        @pl.when(k == 1)
        def _():
            part_out[part] = mine[slot].astype(low)
            part_pair(part).start()
            part_out[PARTS + part] = mm(act[part, 1], down[...]).astype(low)
            out_pair(part).start()

        @pl.when((unit > 0) & (core_of(unit - 1) == 0))
        def _():
            send_back(unit - 1)

        return carry

    lax.fori_loop(0, 2 * PARTS, work, 0)

    @pl.when(me_d == 1)
    def _():
        send_back(2 * PARTS - 1)

    def output_own(part, carry):
        base = base_of(part)
        here = pl.ds(base, block)
        product = mm(act[part, 0], down[...])
        out_pair(part).wait_recv()
        total = rows_in[here, :].astype(f32) + product + part_in[PARTS + part].astype(f32) + down_bias[...]
        rows_in[here, :] = (total * live[here, :]).astype(low)
        pltpu.make_async_copy(rows_in.at[here], hidden_out.at[here], sem_store.at[part]).start()
        return carry

    lax.fori_loop(0, PARTS, output_own, 0)

    ones = jnp.ones((8, PARTS * 2 * block), low)
    all_act = act.reshape(PARTS * 2 * block, units)
    all_pre = pre_grad.reshape(PARTS * 2 * block, units)
    all_in = ffn_in.reshape(PARTS * 2 * block, width)
    all_grad = grad_rows.reshape(PARTS * 2 * block, width)
    grad_bup[...] = mm(ones, all_pre[...])[0:1]
    grad_bdown[...] = mm(ones, all_grad[...])[0:1]

    def up_store(f):
        cols = pl.ds(pl.multiple_of(f * WIDE, WIDE), WIDE)
        return pltpu.make_async_copy(tile, grad_up.at[:, cols], sem_store.at[PARTS])

    def down_store(f):
        cols = pl.ds(pl.multiple_of(f * WIDE, WIDE), WIDE)
        return pltpu.make_async_copy(tile_down, grad_down.at[cols, :], sem_store.at[PARTS + 1])

    def weights(f, carry):
        cols = pl.ds(pl.multiple_of(f * WIDE, WIDE), WIDE)

        @pl.when(f > 0)
        def _():
            up_store(f).wait()

        tile[...] = mm_tn(all_in[...], all_pre[:, cols]).astype(low)
        up_store(f).start()

        @pl.when(f > 0)
        def _():
            down_store(f).wait()

        tile_down[...] = mm_tn(all_act[:, cols], all_grad[...]).astype(low)
        down_store(f).start()
        return carry

    lax.fori_loop(0, units // WIDE, weights, 0)
    up_store(0).wait()
    down_store(0).wait()
    for part in range(PARTS):
        pltpu.make_async_copy(
            rows_in.at[pl.ds(0, block)], hidden_out.at[pl.ds(0, block)], sem_store.at[part]
        ).wait()
    own_back().wait()
    for part in range(PARTS):
        ffn_pair(part).wait_send()
        part_pair(part).wait_send()
        out_pair(part).wait_send()

    def wait_back(i, carry):
        back_copy(i).wait()
        return carry

    lax.fori_loop(1, n, wait_back, 0)


def expert_block(sent, grads, hids, live, up, up_bias, down, down_bias, gain, bias):
    n = lax.axis_size("expert")
    rows, width = sent.shape
    units = up.shape[1]
    cap = rows // n
    block = rows // PARTS
    vm = pl.BlockSpec(memory_space=pltpu.VMEM)
    hbm = pl.BlockSpec(memory_space=pl.ANY)
    return pl.pallas_call(
        functools.partial(expert_kernel, n, cap),
        out_shape=(
            jax.ShapeDtypeStruct((rows, width), low),
            jax.ShapeDtypeStruct((rows, width), low),
            jax.ShapeDtypeStruct((width, units), low),
            jax.ShapeDtypeStruct((units, width), low),
            jax.ShapeDtypeStruct((1, units), f32),
            jax.ShapeDtypeStruct((1, width), f32),
            jax.ShapeDtypeStruct((8, width), f32),
        ),
        in_specs=[hbm, hbm, hbm, vm, hbm, vm, hbm, vm, vm, vm],
        out_specs=(hbm, hbm, hbm, hbm, vm, vm, vm),
        scratch_shapes=[
            pltpu.VMEM((rows, width), low),
            pltpu.VMEM((PARTS, 2, block, width), low),
            pltpu.VMEM((PARTS, 2, block, width), low),
            pltpu.VMEM((width, units), low),
            pltpu.VMEM((units, width), low),
            pltpu.VMEM((PARTS, 2, block, units), low),
            pltpu.VMEM((PARTS, 2, block, units), low),
            pltpu.VMEM((PARTS, 2, block, units), low),
            pltpu.VMEM((2 * PARTS, block, width), low),
            pltpu.VMEM((2 * PARTS, block, width), low),
            pltpu.VMEM((rows, width), low),
            pltpu.VMEM((2, block, width), f32),
            pltpu.VMEM((width, WIDE), low),
            pltpu.VMEM((WIDE, width), low),
            pltpu.SemaphoreType.DMA((n,)),
            pltpu.SemaphoreType.DMA((n,)),
            pltpu.SemaphoreType.DMA((n,)),
            pltpu.SemaphoreType.DMA((n,)),
            pltpu.SemaphoreType.DMA((3, 2, PARTS)),
            pltpu.SemaphoreType.DMA((2 + 4 * PARTS,)),
            pltpu.SemaphoreType.DMA((PARTS + 2,)),
        ],
        compiler_params=pltpu.CompilerParams(
            collective_id=1, has_side_effects=True, vmem_limit_bytes=62 * 1024 * 1024
        ),
    )(sent, grads, hids, live, up, up_bias, down, down_bias, gain, bias)


def closing_kernel(
    n,
    cap,
    chunks,
    returned_hbm,
    slot_row,
    attn_in_hbm,
    tokens_hbm,
    queries_hbm,
    keys_hbm,
    values_hbm,
    attended_hbm,
    inv_sums,
    expos,
    w_qkv_hbm,
    w_out_hbm,
    gain,
    grad_norm2,
    grad_in,
    grad_qkv,
    grad_wout,
    grad_norms,
    returned,
    attn_in_t,
    tokens_t,
    queries_t,
    keys_t,
    values,
    attended_t,
    w_qkv,
    w_out,
    expo_v,
    grad_att_t,
    grad_h,
    grad_proj_t,
    sent_v,
    norm_terms,
    made,
    *rest,
):
    count = len(chunks)
    totals, landeds = rest[:count], rest[count : 2 * count]
    sem_load, sem_expo, sem_send, sem_recv, sem_pair, sem_step = rest[2 * count :]
    me_d = lax.axis_index("dp")
    me_e = lax.axis_index("expert")
    partner = (1 - me_d, me_e)
    bits = n.bit_length() - 1
    half = n // 2
    rows, width = returned.shape
    toks = slot_row.shape[1]
    each = made.shape[1]
    loads = [
        pltpu.make_async_copy(a, b, sem_load.at[i])
        for i, (a, b) in enumerate(
            (
                (returned_hbm, returned),
                (w_out_hbm, w_out),
                (attended_hbm, attended_t),
                (values_hbm, values),
                (keys_hbm, keys_t),
                (queries_hbm, queries_t),
                (attn_in_hbm, attn_in_t),
                (w_qkv_hbm, w_qkv),
                (tokens_hbm, tokens_t),
            )
        )
    ]

    def expo_load(g):
        here = pl.ds(4 * g, 4)
        return pltpu.make_async_copy(expos.at[here], expo_v.at[here], sem_expo.at[g])

    def slot_copy(i):
        peer = me_e ^ i
        return pltpu.make_async_remote_copy(
            src_ref=sent_v.at[pl.ds(pl.multiple_of(peer * cap, cap), cap)],
            dst_ref=grad_in.at[pl.ds(pl.multiple_of(me_e * cap, cap), cap)],
            send_sem=sem_send.at[i],
            recv_sem=sem_recv.at[i],
            device_id=(me_d, peer),
            device_id_type=MESH_ID,
        )

    def own_slots():
        here = pl.ds(pl.multiple_of(me_e * cap, cap), cap)
        return pltpu.make_async_copy(sent_v.at[here], grad_in.at[here], sem_recv.at[0])

    def offset(order, p):
        k = 0
        for j, b in enumerate(order):
            k = k + lax.rem(p // (1 << (bits - 1 - j)), 2) * (1 << b)
        return k

    def pair_copy(c, q):
        here = pl.ds(q * half, half)
        return pltpu.make_async_remote_copy(
            src_ref=totals[c].at[1, here],
            dst_ref=landeds[c].at[here],
            send_sem=sem_pair.at[0, c, q],
            recv_sem=sem_pair.at[1, c, q],
            device_id=partner,
            device_id_type=MESH_ID,
        )

    def step_copy(c, j):
        many = n >> (j + 1)
        start = n + sum(n >> (i + 1) for i in range(j))
        copy = pltpu.make_async_remote_copy(
            src_ref=totals[c].at[0, pl.ds(many, many)],
            dst_ref=landeds[c].at[pl.ds(start, many)],
            send_sem=sem_step.at[0, c, j],
            recv_sem=sem_step.at[1, c, j],
            device_id=(me_d, me_e ^ (1 << chunks[c][0][j])),
            device_id_type=MESH_ID,
        )
        return copy, many, start

    def make(c):
        order, size, pieces = chunks[c]
        for kind, source, target in pieces:
            if kind == 0:
                term = mm_nt(attn_in_t[...], grad_proj_t[slice(*source), :])
            elif kind == 1:
                term = mm(attended_t[...], grad_h[:, slice(*source)])
            else:
                term = norm_terms[...]
            made[:, :, slice(*target)] = term.reshape(made.shape[0], each, term.shape[1])

        def arrange(p, carry):
            owner = me_e ^ offset(order, p)
            totals[c][0, p] = made[me_d * n + owner, :, 0:size].astype(low)
            totals[c][1, p] = made[(1 - me_d) * n + owner, :, 0:size].astype(low)
            return carry

        lax.fori_loop(0, n, arrange, 0)
        pair_copy(c, 1).start()
        pair_copy(c, 0).start()

    def add_all(c, first, many, start):
        def add_one(p, carry):
            both = totals[c][0, p].astype(f32) + landeds[c][start + p].astype(f32)
            totals[c][0, p] = both.astype(low)
            return carry

        lax.fori_loop(first, first + many, add_one, 0)

    def stage(c, j):
        if j == 0:
            pair_copy(c, 1).wait()
            add_all(c, half, half, 0)
            step_copy(c, 0)[0].start()
            pair_copy(c, 0).wait()
            add_all(c, 0, half, 0)
            return
        copy, many, start = step_copy(c, j - 1)
        copy.wait()
        if many > 1:
            add_all(c, 0, many, start)
            step_copy(c, j)[0].start()
        else:
            both = totals[c][0, 0].astype(f32) + landeds[c][start].astype(f32)
            for kind, source, target in chunks[c][2]:
                (grad_qkv, grad_wout, grad_norms)[kind][:, slice(*source)] = both[:, slice(*target)]

    for i in range(2):
        loads[i].start()
    greet_peers(me_d, me_e, n)
    greet_partner(me_d, me_e)
    place = (slot_row[0:1, :] == lax.broadcasted_iota(jnp.int32, (rows, toks), 0)).astype(f32).astype(low)
    loads[0].wait()
    for i in range(2, 6):
        loads[i].start()
    for g in range(HEADS // 4):
        expo_load(g).start()
    for i in range(6, len(loads)):
        loads[i].start()
    grad_h[...] = mm_tn(place, returned[...]).astype(low)
    loads[1].wait()
    grad_att_t[...] = mm_nt(w_out[...], grad_h[...]).astype(low)
    loads[2].wait()
    pl.semaphore_wait(pltpu.get_barrier_semaphore(), n)
    make(0)
    make(1)
    for i in range(3, 7):
        loads[i].wait()
    in_first = lax.broadcasted_iota(jnp.int32, (1, PAIR), 1) < HEAD_DIM

    def head_group(g):
        expo_load(g).wait()
        ready = {}
        sums = {}
        for pair in range(2):
            p = 2 * g + pair
            pair_rows = pl.ds(p * PAIR, PAIR)
            inv_pair = jnp.concatenate(
                [jnp.broadcast_to(inv_sums[2 * p + h, 0:1, :], (HEAD_DIM, toks)) for h in range(2)], axis=0
            )
            grad_pair = grad_att_t[pair_rows, :].astype(f32)
            cross = grad_pair * attended_t[pair_rows, :].astype(f32) * inv_pair
            scaled = (grad_pair * inv_pair).astype(low)
            for h in range(2):
                in_pair = slice(h * HEAD_DIM, (h + 1) * HEAD_DIM)
                ready[pair, h] = (jnp.sum(cross[in_pair], axis=0, keepdims=True), scaled)
        units = [
            (pair, h, q) for pair in range(2) for h in range(2) for q in reversed(range(toks // QUERIES))
        ]

        def probs_back(unit):
            pair, h, q = unit
            upto = (q + 1) * QUERIES
            here = slice(q * QUERIES, upto)
            mine = in_first if h == 0 else jnp.logical_not(in_first)
            value = jnp.where(mine, values[0:upto, pl.ds((2 * g + pair) * PAIR, PAIR)], jnp.zeros((), low))
            return mm(value, ready[pair, h][1][:, here])

        def scores_back(unit, grad_prob):
            pair, h, q = unit
            upto = (q + 1) * QUERIES
            here = slice(q * QUERIES, upto)
            expo = expo_v[4 * g + 2 * pair + h, 0:upto, here]
            return expo, (expo.astype(f32) * (grad_prob - ready[pair, h][0][:, here])).astype(low)

        def heads_back(unit, held):
            pair, h, q = unit
            expo, grad_score = held
            upto = (q + 1) * QUERIES
            here = slice(q * QUERIES, upto)
            first = (2 * g + pair) * PAIR + h * HEAD_DIM
            head_rows = pl.ds(first, HEAD_DIM)
            grad_proj_t[head_rows, here] = (mm(keys_t[head_rows, 0:upto], grad_score) * scale_val).astype(low)
            key_term = mm_nt(queries_t[head_rows, here], grad_score)
            value_term = mm_nt(ready[pair, h][1][h * HEAD_DIM : (h + 1) * HEAD_DIM, here], expo)
            if upto < toks:
                key_more, value_more = sums[pair, h]
                key_term = jnp.concatenate([key_more[:, 0:upto] + key_term, key_more[:, upto:]], axis=1)
                value_term = jnp.concatenate([value_more[:, 0:upto] + value_term, value_more[:, upto:]], axis=1)
            sums[pair, h] = (key_term, value_term)
            if q == 0:
                grad_proj_t[pl.ds(width + first, HEAD_DIM), :] = key_term.astype(low)
                grad_proj_t[pl.ds(2 * width + first, HEAD_DIM), :] = value_term.astype(low)

        staged(units, probs_back, scores_back, heads_back)

    groups = HEADS // 4
    head_group(0)
    make(2)
    stage(0, 0)
    stage(1, 0)
    for g in range(1, groups):
        head_group(g)
        make(2 + g)
        stage(1 + g, 0)
    for i in range(7, len(loads)):
        loads[i].wait()
    grad_attn_t = mm(w_qkv[...], grad_proj_t[...])
    stage(1 + groups, 0)
    normed_t, inv_std = normalize(tokens_t[...].astype(f32), axis=0)
    gain_col = jnp.broadcast_to(gain[...], (LANES, width)).T[:, 0:1]
    norm_terms[...] = jnp.concatenate(
        [
            jnp.sum(grad_attn_t * normed_t, axis=1, keepdims=True),
            jnp.sum(grad_attn_t, axis=1, keepdims=True),
            grad_norm2[...].T[:, 0:2],
            jnp.zeros((width, LANES - 4), f32),
        ],
        axis=1,
    )
    result = grad_h[...].astype(f32).T + norm_back(grad_attn_t, normed_t, inv_std, gain_col, axis=0)
    sent_v[...] = mm_nt(place, result.astype(low)).astype(low)
    own_slots().start()

    def start_slots(i, carry):
        slot_copy(i).start()
        return carry

    lax.fori_loop(1, n, start_slots, 0)
    make(count - 1)
    done = [1] * (count - 1) + [0]
    for wave in range(1, bits + count + 1):
        for c in range(count):
            late = c // 4
            while done[c] <= min(bits, wave - late):
                stage(c, done[c])
                done[c] += 1
    own_slots().wait()

    def wait_slots(i, carry):
        slot_copy(i).wait()
        return carry

    lax.fori_loop(1, n, wait_slots, 0)


def closing(returned, slot_row, attn_in_t, tokens_t, queries_t, keys_t, values, attended_t, inv_sums, expos, w_qkv, w_out, gain, grad_norm2):
    n = lax.axis_size("expert")
    owners = n * lax.axis_size("dp")
    rows, width = returned.shape
    toks = slot_row.shape[1]
    each = width // owners
    bits = n.bit_length() - 1
    groups = HEADS // 4
    part = width // groups
    orders = [list(range(bits)), [1, 0] + list(range(2, bits))]
    chunks = []
    for c in range(2):
        size = width // 2
        chunks.append((orders[c], size, [(1, (c * size, (c + 1) * size), (0, size))]))
    for g in range(groups):
        pieces = [
            (0, (k * width + g * part, k * width + (g + 1) * part), (k * part, (k + 1) * part)) for k in range(3)
        ]
        chunks.append((orders[g % 2], 3 * part, pieces))
    chunks.append((orders[0], LANES, [(2, (0, LANES), (0, LANES))]))
    count = len(chunks)
    widest = max(size for _, size, _ in chunks)
    vm = pl.BlockSpec(memory_space=pltpu.VMEM)
    hbm = pl.BlockSpec(memory_space=pl.ANY)
    shape = jax.ShapeDtypeStruct
    return pl.pallas_call(
        functools.partial(closing_kernel, n, rows // n, chunks),
        out_shape=(
            shape((rows, width), low),
            shape((each, 3 * width), f32),
            shape((each, width), f32),
            shape((each, LANES), f32),
        ),
        in_specs=[hbm, vm, hbm, hbm, hbm, hbm, hbm, hbm, vm, hbm, hbm, hbm, vm, vm],
        out_specs=(hbm, vm, vm, vm),
        scratch_shapes=[
            pltpu.VMEM((rows, width), low),
            pltpu.VMEM((width, toks), low),
            pltpu.VMEM((width, toks), low),
            pltpu.VMEM((width, toks), low),
            pltpu.VMEM((width, toks), low),
            pltpu.VMEM((toks, width), low),
            pltpu.VMEM((width, toks), low),
            pltpu.VMEM(w_qkv.shape, low),
            pltpu.VMEM(w_out.shape, low),
            pltpu.VMEM((HEADS, toks, toks), low),
            pltpu.VMEM((width, toks), low),
            pltpu.VMEM((toks, width), low),
            pltpu.VMEM((3 * width, toks), low),
            pltpu.VMEM((rows, width), low),
            pltpu.VMEM((width, LANES), f32),
            pltpu.VMEM((owners, each, widest), f32),
        ]
        + [pltpu.VMEM((2, n, each, size), low) for _, size, _ in chunks]
        + [pltpu.VMEM((2 * n, each, size), low) for _, size, _ in chunks]
        + [
            pltpu.SemaphoreType.DMA((9,)),
            pltpu.SemaphoreType.DMA((groups,)),
            pltpu.SemaphoreType.DMA((n,)),
            pltpu.SemaphoreType.DMA((n,)),
            pltpu.SemaphoreType.DMA((2, count, 2)),
            pltpu.SemaphoreType.DMA((2, count, bits)),
        ],
        compiler_params=pltpu.CompilerParams(
            collective_id=2, has_side_effects=True, vmem_limit_bytes=62 * 1024 * 1024
        ),
    )(returned, slot_row, attn_in_t, tokens_t, queries_t, keys_t, values, attended_t, inv_sums, expos, w_qkv, w_out, gain, grad_norm2)


def handing_kernel(up_in, down_in, hidden_in, rows_in, qkv_in, wout_in, bup_in, bdown_in, norms_in, up, down, hidden, rows, qkv, wout, bup, bdown, *norms):
    up[...] = up_in[...].astype(f32)
    down[...] = down_in[...].astype(f32)
    hidden[...] = hidden_in[...]
    rows[...] = rows_in[...]
    qkv[...] = qkv_in[...]
    wout[...] = wout_in[...]
    bup[...] = bup_in[...]
    norms_t = norms_in[...].T
    for i, norm in enumerate(norms):
        norm[...] = norms_t[i : i + 1, :]
    half = bdown.shape[1]
    bdown[...] = jnp.where(lax.axis_index("dp") == 0, bdown_in[:, 0:half], bdown_in[:, half : 2 * half])


def handing(grad_up, grad_down, hidden_out, grad_in, grad_qkv, grad_wout, grad_bup, grad_bdown, grad_norms):
    steps = 4
    arrays = (grad_up, grad_down, hidden_out, grad_in, grad_qkv, grad_wout, grad_bup, grad_bdown, grad_norms)
    small = grad_bdown.shape[1] // lax.axis_size("dp")
    types = (f32, f32, low, low) + (f32,) * 8

    def block(shape, cut):
        if cut:
            return pl.BlockSpec((shape[0] // steps, shape[1]), lambda i: (i, 0))
        return pl.BlockSpec(shape, lambda i: (0, 0))

    shapes = [x.shape for x in arrays[:-2]] + [(1, small)] + [(1, grad_norms.shape[0])] * 4
    return pl.pallas_call(
        handing_kernel,
        grid=(steps,),
        out_shape=tuple(jax.ShapeDtypeStruct(shape, t) for shape, t in zip(shapes, types)),
        in_specs=[block(x.shape, i < 4) for i, x in enumerate(arrays)],
        out_specs=tuple(block(shape, i < 4) for i, shape in enumerate(shapes)),
        compiler_params=pltpu.CompilerParams(vmem_limit_bytes=62 * 1024 * 1024),
    )(*arrays)


def on_device(
    hidden_in,
    buckets,
    expert_of_bucket,
    lengths,
    norm1_gain,
    norm1_bias,
    w_qkv,
    w_out,
    norm2_gain,
    norm2_bias,
    w_up,
    b_up,
    w_down,
    b_down,
    grad_out,
):
    (
        sent,
        grads,
        hids,
        live,
        attn_in_t,
        tokens_t,
        queries_t,
        keys_t,
        values,
        attended_t,
        inv_sums,
        slot_row,
        expos,
    ) = starting(
        hidden_in,
        grad_out,
        buckets.reshape(1, -1),
        expert_of_bucket[None],
        lengths,
        norm1_gain[None],
        norm1_bias[None],
        w_qkv,
        w_out,
        w_down[0],
    )
    returned, hidden_out, grad_up, grad_down, grad_bup, grad_bdown, grad_norm2 = expert_block(
        sent, grads, hids, live, w_up[0], b_up, w_down[0], b_down, norm2_gain[None], norm2_bias[None]
    )
    grad_in, grad_qkv, grad_wout, grad_norms = closing(
        returned,
        slot_row,
        attn_in_t,
        tokens_t,
        queries_t,
        keys_t,
        values,
        attended_t,
        inv_sums,
        expos,
        w_qkv,
        w_out,
        norm1_gain[None],
        grad_norm2,
    )
    grad_up, grad_down, hidden_out, grad_in, grad_qkv, grad_wout, grad_bup, grad_bdown, *norms = handing(
        grad_up, grad_down, hidden_out, grad_in, grad_qkv, grad_wout, grad_bup, grad_bdown, grad_norms
    )
    return (
        hidden_out,
        grad_in,
        grad_qkv,
        grad_wout,
        *(norm.reshape(-1) for norm in norms),
        grad_up[None],
        grad_bup,
        grad_down[None],
        grad_bdown,
    )


def solution(mesh):
    return jax.shard_map(
        on_device,
        mesh=mesh,
        in_specs=(
            P(("dp", "expert"), None),
            P(("dp", "expert"), None),
            P(),
            P(("dp", "expert"), None),
            P(),
            P(),
            P(),
            P(),
            P(),
            P(),
            P("expert", None, "dp"),
            P("expert", "dp"),
            P("expert", "dp", None),
            P("expert", None),
            P(("dp", "expert"), None),
        ),
        out_specs=(
            P(("dp", "expert"), None),
            P(("dp", "expert"), None),
            P(("dp", "expert"), None),
            P(("dp", "expert"), None),
            P(("dp", "expert")),
            P(("dp", "expert")),
            P(("dp", "expert")),
            P(("dp", "expert")),
            P("expert", None, "dp"),
            P("expert", "dp"),
            P("expert", "dp", None),
            P("expert", "dp"),
        ),
        check_vma=False,
    )
```
